128 devices in a mesh: shard: 16 (over x, y_hi, core), ctx: 4 (over z), tp: 2 (over y_lo).
Axes of the slice: x: 4, y: 4 (y_hi: 2, y_lo: 2; y = y_hi * 2 + y_lo), z: 4, core: 2. Of those that a mesh axis runs over, the one named last changes fastest.
Arguments:
- tokens: bfloat16 [8192, 2048], P(('shard', 'ctx')), may hold values from -6 to 6
- seg_lengths: int32 [16, 13], P('shard'), may hold values from 16 to 128, as said below
- seg_parents: int32 [16, 13], P('shard'), may hold values from 0 to 4, as said below
- gain_in: bfloat16 [2048], P('shard'), may hold values from 0.5 to 1.5
- w_query: bfloat16 [2048, 2048], P('shard', 'tp'), may hold values from -0.125 to 0.125
- w_key: bfloat16 [2048, 1024], P('shard', 'tp'), may hold values from -0.125 to 0.125
- w_value: bfloat16 [2048, 1024], P('shard', 'tp'), may hold values from -0.125 to 0.125
- w_gate_attn: bfloat16 [2048, 2048], P('shard', 'tp'), may hold values from -0.125 to 0.125
- w_out: bfloat16 [2048, 2048], P('tp', 'shard'), may hold values from -2 to 2
- gain_query: bfloat16 [128], P('shard'), may hold values from 0.5 to 1.5
- gain_key: bfloat16 [128], P('shard'), may hold values from 0.5 to 1.5
- gain_mid: bfloat16 [2048], P('shard'), may hold values from 0.5 to 1.5
- w_gate: bfloat16 [2048, 6144], P('shard', 'tp'), may hold values from -0.125 to 0.125
- w_up: bfloat16 [2048, 6144], P('shard', 'tp'), may hold values from -0.125 to 0.125
- w_down: bfloat16 [6144, 2048], P('tp', 'shard'), may hold values from -0.078125 to 0.078125
- cotangent: bfloat16 [8192, 2048], P(('shard', 'ctx')), may hold values from -6 to 6
Outputs:
- layer_out: float32 [8192, 2048], P(('shard', 'ctx'))
- input_grad: float32 [8192, 2048], P(('shard', 'ctx'))
- grad_gain_in: float32 [2048], P('shard')
- grad_query: float32 [2048, 2048], P('shard', 'tp')
- grad_key: float32 [2048, 1024], P('shard', 'tp')
- grad_value: float32 [2048, 1024], P('shard', 'tp')
- grad_gate_attn: float32 [2048, 2048], P('shard', 'tp')
- grad_out: float32 [2048, 2048], P('tp', 'shard')
- grad_gain_query: float32 [128], P('shard')
- grad_gain_key: float32 [128], P('shard')
- grad_gain_mid: float32 [2048], P('shard')
- grad_gate: float32 [2048, 6144], P('shard', 'tp')
- grad_up: float32 [2048, 6144], P('shard', 'tp')
- grad_down: float32 [6144, 2048], P('tp', 'shard')
The draws below stay inside these ranges and needn't reach their ends.
Inputs may be any that keep to these rules, and one draw needn't show every extreme that they name: `seg_lengths`: each row describes one tree of 512 tokens; segment 0 (the trunk) has 128 tokens, segments 1 to 4 are branches, 5 to 12 leaves; a row sums to 512, and some segment has exactly 16. `seg_parents`: segment 0 and every branch have parent 0; every leaf has a branch as parent, each branch exactly two leaves.
All inputs are finite; a program needn't handle non-finite values.
Results may differ from the reference program's by a relative error of at most 0.025.
Values may be sent and summed in bfloat16 or wider, within the bound.
No kernel may reach another device: no remote copies, remote signals or barrier semaphores. Data moves between devices by JAX's collectives and lax.ppermute only.
A program may use at most 256 MiB of HBM per device.

```python
import math
import jax
import jax.numpy as jnp
from jax import lax

D = 2048
HQ = 16
HK = 8
HD = 128
FF = 6144
TREE_LEN = 512
TREES = 16
TOKENS = 8192


def draw_seg_lengths(key, part):
    base_len = TREE_LEN // 16
    spread = base_len // 2
    swings = jax.random.randint(jax.random.fold_in(key, 11), (TREES, 5), -spread, spread + 1)
    swings = jnp.concatenate([jnp.full((TREES, 1), spread, jnp.int32), swings.astype(jnp.int32)], axis=1)
    pairs = jnp.stack([base_len + swings, base_len - swings], axis=-1).reshape(TREES, 12)
    trunk = jnp.full((TREES, 1), 4 * base_len, jnp.int32)
    return jnp.concatenate([trunk, pairs], axis=1).astype(jnp.int32)


def draw_seg_parents(key, part):
    subkeys = jax.random.split(jax.random.fold_in(key, 23), TREES)
    orders = jax.vmap(lambda subkey: jax.random.permutation(subkey, 8))(subkeys)
    leaves = 1 + orders.astype(jnp.int32) % 4
    heads = jnp.zeros((TREES, 5), jnp.int32)
    return jnp.concatenate([heads, leaves], axis=1).astype(jnp.int32)


def block_levels(own_key, shape, cuts, smallest, top_value):
    level = 1.0
    for axis_at, blocks in cuts:
        draws = jax.random.uniform(jax.random.fold_in(jax.random.fold_in(own_key, 6), axis_at), (blocks,), jnp.float32, smallest / len(cuts), top_value / len(cuts))
        level = level * jnp.repeat(jnp.exp(draws), shape[axis_at] // blocks).reshape((-1,) + (1,) * (len(shape) - 1 - axis_at))
    return level


def normal_values(key, shape, scale, bound, cuts=(), held_as=jnp.bfloat16):
    drawn = jax.random.normal(key, shape, jnp.float32) * scale
    if len(cuts) > 0:
        drawn = block_levels(key, shape, cuts, -0.22, 0.18) * drawn
    return jnp.clip(drawn, min=-bound, max=bound).astype(held_as)


def setup_inputs(seed: int = 0) -> dict:
    splits = jax.random.split(jax.random.key(seed), 17)
    return {
        "tokens": normal_values(splits[0], (TOKENS, D), 1.0, 6.0, ((0, 64),)),
        "seg_lengths": draw_seg_lengths(jax.random.fold_in(splits[16], 71), 0),
        "seg_parents": draw_seg_parents(jax.random.fold_in(splits[16], 71), 0),
        "gain_in": jnp.clip(1.0 + 0.1 * jax.random.normal(splits[3], (D,), jnp.float32), 0.5, 1.5).astype(jnp.bfloat16),
        "w_query": normal_values(splits[4], (D, HQ * HD), D ** -0.5, 0.125, ((0, 16), (1, 2))),
        "w_key": normal_values(splits[5], (D, HK * HD), D ** -0.5, 0.125, ((0, 16), (1, 2))),
        "w_value": normal_values(splits[6], (D, HK * HD), D ** -0.5, 0.125, ((0, 16), (1, 2))),
        "w_gate_attn": normal_values(splits[7], (D, HQ * HD), D ** -0.5, 0.125, ((0, 16), (1, 2))),
        "w_out": normal_values(splits[8], (HQ * HD, D), (max(HQ * HD // 256, 4)) ** -0.5, 2.0, ((0, 2), (1, 16))),
        "gain_query": jnp.clip(1.0 + 0.1 * jax.random.normal(splits[9], (HD,), jnp.float32), 0.5, 1.5).astype(jnp.bfloat16),
        "gain_key": jnp.clip(1.0 + 0.1 * jax.random.normal(splits[10], (HD,), jnp.float32), 0.5, 1.5).astype(jnp.bfloat16),
        "gain_mid": jnp.clip(1.0 + 0.1 * jax.random.normal(splits[11], (D,), jnp.float32), 0.5, 1.5).astype(jnp.bfloat16),
        "w_gate": normal_values(splits[12], (D, FF), D ** -0.5, 0.125, ((0, 16), (1, 2))),
        "w_up": normal_values(splits[13], (D, FF), D ** -0.5, 0.125, ((0, 16), (1, 2))),
        "w_down": normal_values(splits[14], (FF, D), FF ** -0.5, 0.078125, ((0, 2), (1, 16))),
        "cotangent": normal_values(splits[15], (TOKENS, D), 1.0, 6.0, ((0, 64),)),
    }


EPS = 1e-06
BASE = 1000000.0
NEG = -1e+30

@jax.custom_vjp
def low(v):
    return lax.optimization_barrier(v.astype(jnp.bfloat16)).astype(jnp.float32)

@jax.custom_vjp
def low_back(v):
    return v

def low_keep(v):
    return (low(v), None)

def low_pass(kept, grad):
    return (grad,)

def back_keep(v):
    return (v, None)

def back_low(kept, grad):
    return (low(grad),)
low.defvjp(low_keep, low_pass)
low_back.defvjp(back_keep, back_low)

def matmul_high(left, right):
    return jnp.dot(left, right, precision=lax.Precision.HIGHEST, preferred_element_type=jnp.float32)

def rms_scale(inputs):
    return lax.rsqrt(lax.optimization_barrier(jnp.mean(inputs * inputs, axis=-1, keepdims=True)) + EPS)

def lookup(onehot, table):
    return lax.optimization_barrier(jnp.sum(onehot * table[None, :], axis=1))

def tree_layout(lengths, parents, places):
    labels = jnp.arange(lengths.shape[0], dtype=jnp.int32)
    ends = jnp.cumsum(lengths).astype(jnp.int32)
    starts = ends - lengths
    parent_hot = (parents[:, None] == labels[None, :]).astype(jnp.int32)
    grand = lookup(parent_hot, parents)
    parent_len = lookup(parent_hot, lengths)
    grand_hot = (grand[:, None] == labels[None, :]).astype(jnp.int32)
    grand_len = lookup(grand_hot, lengths)
    before = jnp.where(labels == 0, 0, parent_len + jnp.where(parents == 0, 0, grand_len))
    segment = lax.optimization_barrier(jnp.sum((places[:, None] >= ends[None, :]).astype(jnp.int32), axis=1))
    token_hot = (segment[:, None] == labels[None, :]).astype(jnp.int32)
    position = places - lookup(token_hot, starts) + lookup(token_hot, before)
    return (segment, lookup(token_hot, parents), lookup(token_hot, grand), position)

def rope_tables(position, columns):
    halfway = columns // 2
    frequency = jnp.exp(jnp.arange(halfway, dtype=jnp.float32) * (-2.0 * math.log(BASE) / columns))
    angles = position.astype(jnp.float32)[:, None] * frequency[None, :]
    angles = jnp.concatenate([angles, angles], axis=1)
    return (jnp.cos(angles)[:, None, :], jnp.sin(angles)[:, None, :])

def turn_half(inputs):
    halfway = inputs.shape[-1] // 2
    return jnp.concatenate([-inputs[..., halfway:], inputs[..., :halfway]], axis=-1)

def rotate(inputs, cosine_table, sine_table):
    return inputs * cosine_table + turn_half(inputs) * sine_table

def tree_forward(weights, tokens_tree, lengths, parents):
    gain_in, w_query, w_key, w_value, w_gate_attn, w_out, gain_query, gain_key, gain_mid, w_gate, w_up, w_down = weights
    length = tokens_tree.shape[0]
    group = HQ // HK
    scale = 1.0 / math.sqrt(HD)
    places = jnp.arange(length, dtype=jnp.int32)
    segment, parent_seg, grand_seg, position = tree_layout(lengths, parents, places)
    allowed = ((segment[None, :] == segment[:, None]) | (segment[None, :] == parent_seg[:, None]) | (segment[None, :] == grand_seg[:, None])) & (places[None, :] <= places[:, None])
    cosine_table, sine_table = rope_tables(position, HD)
    normed = low(tokens_tree * rms_scale(tokens_tree) * gain_in)
    queries = low_back(matmul_high(normed, w_query)).reshape(length, HQ, HD)
    keys_pre = low_back(matmul_high(normed, w_key)).reshape(length, HK, HD)
    values = low(low_back(matmul_high(normed, w_value))).reshape(length, HK, HD)
    gate_pre = low_back(matmul_high(normed, w_gate_attn)).reshape(length, HQ, HD)
    queries = low(rotate(queries * rms_scale(queries) * gain_query, cosine_table, sine_table))
    keys_rot = low(rotate(keys_pre * rms_scale(keys_pre) * gain_key, cosine_table, sine_table))
    queries = queries.reshape(length, HK, group, HD)
    scores = low_back(jnp.einsum('tgrd,jgd->tgrj', queries, keys_rot, precision=lax.Precision.HIGHEST) * scale)
    scores = jnp.where(allowed[:, None, None, :], scores, NEG)
    probs = jnp.exp(scores - lax.optimization_barrier(jnp.max(scores, axis=-1, keepdims=True)))
    probs = probs / lax.optimization_barrier(jnp.sum(probs, axis=-1, keepdims=True))
    attended = low_back(jnp.einsum('tgrj,jgd->tgrd', low(probs), values, precision=lax.Precision.HIGHEST))
    attended = attended.reshape(length, HQ, HD)
    gated = low(attended * jax.nn.sigmoid(gate_pre)).reshape(length, HQ * HD)
    middle = tokens_tree + low_back(matmul_high(gated, w_out))
    normed_mid = low(middle * rms_scale(middle) * gain_mid)
    gate_val = low_back(matmul_high(normed_mid, w_gate))
    up_val = low_back(matmul_high(normed_mid, w_up))
    hidden = low(jax.nn.silu(gate_val) * up_val)
    return middle + low_back(matmul_high(hidden, w_down))

def reference(tokens, seg_lengths, seg_parents, gain_in, w_query, w_key, w_value, w_gate_attn, w_out, gain_query, gain_key, gain_mid, w_gate, w_up, w_down, cotangent):
    weights = tuple((weight_item.astype(jnp.float32) for weight_item in (gain_in, w_query, w_key, w_value, w_gate_attn, w_out, gain_query, gain_key, gain_mid, w_gate, w_up, w_down)))
    trees = seg_lengths.shape[0]
    inputs = tokens.astype(jnp.float32).reshape(trees, -1, D)
    layer = jax.checkpoint(tree_forward)

    def forward(weight_set, inputs_all):

        def step_tree(carry, pieces):
            return (carry, layer(weight_set, pieces[0], pieces[1], pieces[2]))
        carry_out, outputs_all = lax.scan(step_tree, jnp.zeros((), jnp.float32), (inputs_all, seg_lengths, seg_parents))
        return outputs_all
    outputs, pullback = jax.vjp(forward, weights, inputs)
    weight_grads, input_grads = pullback(cotangent.astype(jnp.float32).reshape(inputs.shape))
    return (outputs.reshape(-1, D), input_grads.reshape(-1, D), weight_grads[0], weight_grads[1], weight_grads[2], weight_grads[3], weight_grads[4], weight_grads[5], weight_grads[6], weight_grads[7], weight_grads[8], weight_grads[9], weight_grads[10], weight_grads[11])
```

```python
import math

import jax
import jax.numpy as jnp
from jax import lax
from jax.sharding import PartitionSpec as P

HD = 128
EPS = 1e-06
BASE = 1000000.0
NEG = -1e30
F32 = jnp.float32
BF16 = jnp.bfloat16
PLANE = ("shard", "tp")


def lookup(onehot, table):
    return jnp.sum(onehot * table[None, :], axis=1)


def tree_layout(lengths, parents, places):
    labels = jnp.arange(lengths.shape[0], dtype=jnp.int32)
    ends = jnp.cumsum(lengths)
    starts = ends - lengths
    parent_hot = (parents[:, None] == labels[None, :]).astype(jnp.int32)
    grand = lookup(parent_hot, parents)
    parent_len = lookup(parent_hot, lengths)
    grand_hot = (grand[:, None] == labels[None, :]).astype(jnp.int32)
    grand_len = lookup(grand_hot, lengths)
    before = jnp.where(labels == 0, 0, parent_len + jnp.where(parents == 0, 0, grand_len))
    segment = jnp.sum((places[:, None] >= ends[None, :]).astype(jnp.int32), axis=1)
    token_hot = (segment[:, None] == labels[None, :]).astype(jnp.int32)
    position = places - lookup(token_hot, starts) + lookup(token_hot, before)
    return (segment, lookup(token_hot, parents), lookup(token_hot, grand), position)


def rope_tables(position, columns):
    halfway = columns // 2
    frequency = jnp.exp(jnp.arange(halfway, dtype=F32) * (-2.0 * math.log(BASE) / columns))
    angles = position.astype(F32)[:, None] * frequency[None, :]
    angles = jnp.concatenate([angles, angles], axis=1)
    return (jnp.cos(angles)[:, None, :], jnp.sin(angles)[:, None, :])


def rotate(inputs, cosine_table, sine_table):
    halfway = inputs.shape[-1] // 2
    turned = jnp.concatenate([-inputs[..., halfway:], inputs[..., :halfway]], axis=-1)
    return inputs * cosine_table + turned * sine_table


def turn_back(grads, cosine_table, sine_table):
    scaled = grads * sine_table
    halfway = grads.shape[-1] // 2
    return grads * cosine_table + jnp.concatenate(
        [scaled[..., halfway:], -scaled[..., :halfway]], axis=-1
    )


def rms_scale(inputs):
    return lax.rsqrt(jnp.mean(inputs * inputs, axis=-1, keepdims=True) + EPS)


def dot(left, right):
    return jnp.dot(left, right, preferred_element_type=F32)


def dot_rows(left, right):
    return lax.dot_general(left, right, (((0,), (0,)), ((), ())), preferred_element_type=F32)


def dot_back(left, right):
    return lax.dot_general(left, right, (((1,), (1,)), ((), ())), preferred_element_type=F32)


def make_shards(mesh):
    n_shard, n_ctx, n_tp = mesh.shape["shard"], mesh.shape["ctx"], mesh.shape["tp"]
    pairs = n_shard // 2

    def joint(pair, core, tp):
        return (pair * 2 + core) * n_tp + tp

    core_perm = [(i, i ^ 1) for i in range(n_shard)]
    planes = [
        [joint(pair, core, tp) for pair in range(pairs) for tp in range(n_tp)] for core in range(2)
    ]
    swap_perm = [
        edge
        for pair in range(pairs)
        for edge in (
            (joint(pair, 1, 0), joint(pair, 0, 1)),
            (joint(pair, 0, 1), joint(pair, 1, 0)),
        )
    ]
    across_perm = [(joint(pair, t, t), joint(pair, t, 1 - t)) for pair in range(pairs) for t in range(2)]

    def core_swap(value):
        return lax.ppermute(value, "shard", core_perm)

    def ctx_gather(value):
        wide = jnp.broadcast_to(value[None], (n_ctx,) + value.shape)
        return lax.all_to_all(wide, "ctx", 0, 0).reshape((-1,) + value.shape[1:])

    def ctx_scatter(value):
        split = value.reshape((n_ctx, value.shape[0] // n_ctx) + value.shape[1:])
        return jnp.sum(lax.all_to_all(split, "ctx", 0, 0).astype(F32), axis=0)

    def gather_tree(own):
        mine = ctx_gather(own)
        return jnp.concatenate([mine, core_swap(mine)], axis=0)

    def scatter_tree(part):
        half = part.shape[0] // 2
        received = core_swap(part[half:].astype(BF16))
        return ctx_scatter((part[:half] + received.astype(F32)).astype(BF16))

    def plane_gather(value):
        return lax.all_gather(value, PLANE, axis=0, tiled=True, axis_index_groups=planes)

    def plane_scatter(value):
        return lax.psum_scatter(
            value.astype(BF16), PLANE, scatter_dimension=0, tiled=True, axis_index_groups=planes
        )

    def shards(
        tokens,
        seg_lengths,
        seg_parents,
        gain_in,
        w_query,
        w_key,
        w_value,
        w_gate_attn,
        w_out,
        gain_query,
        gain_key,
        gain_mid,
        w_gate,
        w_up,
        w_down,
        cotangent,
    ):
        core = lax.axis_index("shard") % 2
        tp = lax.axis_index("tp")
        ctx = lax.axis_index("ctx")
        native = core == tp
        rows = tokens.shape[0] // 2
        scale = 1.0 / math.sqrt(HD)

        def swapped(value):
            return jnp.where(native, value, lax.ppermute(value, PLANE, swap_perm))

        def quarter(weight, axis):
            size = weight.shape[axis] // n_ctx
            return lax.dynamic_slice_in_dim(weight, ctx * size, size, axis)

        gain_one = gain_in.astype(F32)[:, None]
        gain_two = gain_mid.astype(F32)[:, None]
        first = jnp.concatenate(
            [quarter(w, 1) for w in (w_query, w_key, w_value, w_gate_attn)], axis=1
        )
        first = (first.astype(F32) * gain_one).astype(BF16)
        second = jnp.concatenate([quarter(w_gate, 1), quarter(w_up, 1)], axis=1)
        second = (second.astype(F32) * gain_two).astype(BF16)
        w1 = plane_gather(swapped(first))
        w_out_t = plane_gather(swapped(quarter(w_out, 0).T))
        w2 = plane_gather(swapped(second))
        w_down_t = plane_gather(swapped(quarter(w_down, 0).T))
        head_gains = lax.all_gather(
            jnp.concatenate([gain_query[None], gain_key[None]], axis=0), "shard", axis=1, tiled=True
        ).astype(F32)
        gain_q, gain_k = head_gains[0], head_gains[1]

        both = jnp.stack([tokens, cotangent])
        keep = lax.dynamic_slice_in_dim(both, core * rows, rows, 1)
        give = lax.dynamic_slice_in_dim(both, (1 - core) * rows, rows, 1)
        own = jnp.where(native, keep, core_swap(give))
        tree = jnp.concatenate([seg_lengths, seg_parents], axis=0)
        tree = jnp.where(native, tree, core_swap(tree))
        own_x, own_cot = own[0], own[1]
        x_all = gather_tree(own_x)
        cot_all = gather_tree(own_cot)

        length = x_all.shape[0]
        half_at = jnp.where(jnp.arange(2) == 0, core, 1 - core) * rows
        places = (
            half_at[:, None, None]
            + jnp.arange(n_ctx, dtype=jnp.int32)[None, :, None] * (2 * rows)
            + jnp.arange(rows, dtype=jnp.int32)[None, None, :]
        ).reshape(-1)
        segment, parent_seg, grand_seg, position = tree_layout(tree[0], tree[1], places)
        allowed = (
            (segment[None, :] == segment[:, None])
            | (segment[None, :] == parent_seg[:, None])
            | (segment[None, :] == grand_seg[:, None])
        ) & (places[None, :] <= places[:, None])
        cosine_table, sine_table = rope_tables(position, HD)

        x_f = x_all.astype(F32)
        xn = (x_f * rms_scale(x_f)).astype(BF16)
        qkvg = dot(xn, w1)
        q_pre = qkvg[:, : 2 * HD].reshape(length, 2, HD)
        k_pre = qkvg[:, 2 * HD : 3 * HD].reshape(length, 1, HD)
        value = qkvg[:, 3 * HD : 4 * HD].astype(BF16)
        gate_pre = qkvg[:, 4 * HD :].reshape(length, 2, HD)
        factor_q, factor_k = rms_scale(q_pre), rms_scale(k_pre)
        query = rotate(q_pre * factor_q * gain_q, cosine_table, sine_table).astype(BF16)
        key = rotate(k_pre * factor_k * gain_k, cosine_table, sine_table).astype(BF16)[:, 0]
        scores = jnp.einsum("trd,jd->rtj", query, key, preferred_element_type=F32) * scale
        scores = jnp.where(allowed[None], scores, NEG)
        probs = jnp.exp(scores - jnp.max(scores, axis=-1, keepdims=True))
        probs = probs / jnp.sum(probs, axis=-1, keepdims=True)
        probs_low = probs.astype(BF16)
        attended = jnp.einsum("rtj,jd->trd", probs_low, value, preferred_element_type=F32)
        sigmoid_gate = jax.nn.sigmoid(gate_pre)
        gated = (attended * sigmoid_gate).astype(BF16).reshape(length, 2 * HD)
        own_x_f = own_x.astype(F32)
        middle = own_x_f + scatter_tree(dot_back(gated, w_out_t))
        factor_two = rms_scale(middle)
        un = gather_tree((middle * factor_two).astype(BF16))

        gate_up = dot(un, w2)
        units = w_down_t.shape[1]
        gate_val, up_val = gate_up[:, :units], gate_up[:, units:]
        sig = jax.nn.sigmoid(gate_val)
        hidden = (gate_val * sig * up_val).astype(BF16)
        d_hidden = dot(cot_all, w_down_t)
        d_gate = (d_hidden * up_val * sig * (1.0 + gate_val * (1.0 - sig))).astype(BF16)
        d_up = (d_hidden * gate_val * sig).astype(BF16)
        d_gate_up = jnp.concatenate([d_gate, d_up], axis=1)
        layer_own = middle + scatter_tree(dot_back(hidden, w_down_t))
        d_un = scatter_tree(dot_back(d_gate_up, w2))
        d_middle = (
            own_cot.astype(F32)
            + factor_two * d_un
            - middle * factor_two**3 * jnp.mean(d_un * middle, axis=-1, keepdims=True)
        )
        mid_terms = jnp.sum(d_un * middle * factor_two, axis=0)
        d_middle_low = gather_tree(d_middle.astype(BF16))
        grad_ffn = plane_scatter(
            jnp.concatenate([dot_rows(un, d_gate_up), dot_rows(cot_all, hidden)], axis=1)
        )

        d_gated = dot(d_middle_low, w_out_t).reshape(length, 2, HD)
        d_attended = (d_gated * sigmoid_gate).astype(BF16)
        d_gate_pre = (d_gated * attended * sigmoid_gate * (1.0 - sigmoid_gate)).astype(BF16)
        d_probs = jnp.einsum("trd,jd->rtj", d_attended, value, preferred_element_type=F32)
        d_scores = (probs * (d_probs - jnp.sum(probs * d_probs, axis=-1, keepdims=True))).astype(BF16)
        d_query = jnp.einsum("rtj,jd->trd", d_scores, key, preferred_element_type=F32) * scale
        d_key = jnp.einsum("rtj,trd->jd", d_scores, query, preferred_element_type=F32) * scale
        d_value = jnp.einsum("rtj,trd->jd", probs_low, d_attended, preferred_element_type=F32)
        d_qhead = turn_back(d_query, cosine_table, sine_table)
        d_khead = turn_back(d_key[:, None], cosine_table, sine_table)
        q_terms = jnp.sum(d_qhead * q_pre * factor_q, axis=(0, 1))
        k_terms = jnp.sum(d_khead * k_pre * factor_k, axis=(0, 1))

        def head_back(grads, inputs, factor, gain):
            scaled = gain * grads
            return factor * scaled - inputs * factor**3 * jnp.mean(
                scaled * inputs, axis=-1, keepdims=True
            )

        d_q_pre = head_back(d_qhead, q_pre, factor_q, gain_q).astype(BF16).reshape(length, -1)
        d_k_pre = head_back(d_khead, k_pre, factor_k, gain_k).astype(BF16).reshape(length, -1)
        d_qkvg = jnp.concatenate(
            [d_q_pre, d_k_pre, d_value.astype(BF16), d_gate_pre.reshape(length, -1)], axis=1
        )
        d_xn = scatter_tree(dot_back(d_qkvg, w1))
        factor_one = rms_scale(own_x_f)
        input_own = (
            d_middle
            + factor_one * d_xn
            - own_x_f * factor_one**3 * jnp.mean(d_xn * own_x_f, axis=-1, keepdims=True)
        )
        in_terms = jnp.sum(d_xn * own_x_f * factor_one, axis=0)

        def spread(terms):
            per = terms.shape[0] // n_shard
            wide = jnp.pad(terms.reshape(n_shard, per), ((0, 0), (0, HD - per)))
            return wide.reshape(-1)

        columns = jnp.stack([in_terms, mid_terms, spread(q_terms), spread(k_terms)], axis=1)
        columns = jnp.pad(columns, ((0, 0), (0, HD - 4)))
        grad_attn = plane_scatter(
            jnp.concatenate(
                [dot_rows(xn, d_qkvg), dot_rows(d_middle_low, gated), columns], axis=1
            )
        )
        gains_part = grad_attn[:, -HD:]
        gains_part = (gains_part.astype(F32) + core_swap(gains_part).astype(F32)).astype(BF16)
        grad_attn = jnp.concatenate([grad_attn[:, :-HD], gains_part], axis=1)

        def owners(block):
            block = swapped(block)
            wide = jnp.broadcast_to(block[None], (n_ctx,) + block.shape)
            return lax.all_to_all(wide, "ctx", 0, 0).astype(F32)

        def side(parts):
            return parts.transpose(1, 0, 2).reshape(parts.shape[1], -1)

        def down(parts):
            return parts.transpose(0, 2, 1).reshape(-1, parts.shape[1])

        ffn = owners(grad_ffn)
        grad_gate = side(ffn[:, :, :units]) * gain_two
        grad_up = side(ffn[:, :, units : 2 * units]) * gain_two
        grad_down = down(ffn[:, :, 2 * units :])
        attn = owners(grad_attn)
        grad_query = side(attn[:, :, : 2 * HD]) * gain_one
        grad_key = side(attn[:, :, 2 * HD : 3 * HD]) * gain_one
        grad_value = side(attn[:, :, 3 * HD : 4 * HD]) * gain_one
        grad_gate_attn = side(attn[:, :, 4 * HD : 6 * HD]) * gain_one
        grad_out = down(attn[:, :, 6 * HD : 8 * HD])
        gains = jnp.sum(attn[:, :, 8 * HD :], axis=0)
        head_rows = gain_query.shape[0]

        def finish(part):
            low = part.astype(BF16)
            sibling = core_swap(low)
            full = jnp.where(
                core == 0,
                jnp.concatenate([low, sibling], axis=0),
                jnp.concatenate([sibling, low], axis=0),
            )
            return jnp.where(native, full, lax.ppermute(full, PLANE, across_perm)).astype(F32)

        return (
            finish(layer_own),
            finish(input_own),
            gains[:, 0] / gain_one[:, 0],
            grad_query,
            grad_key,
            grad_value,
            grad_gate_attn,
            grad_out,
            gains[:head_rows, 2],
            gains[:head_rows, 3],
            gains[:, 1] / gain_two[:, 0],
            grad_gate,
            grad_up,
            grad_down,
        )

    return shards


def solution(mesh):
    return jax.shard_map(
        make_shards(mesh),
        mesh=mesh,
        in_specs=(
            P(("shard", "ctx"), None),
            P("shard", None),
            P("shard", None),
            P("shard"),
            P("shard", "tp"),
            P("shard", "tp"),
            P("shard", "tp"),
            P("shard", "tp"),
            P("tp", "shard"),
            P("shard"),
            P("shard"),
            P("shard"),
            P("shard", "tp"),
            P("shard", "tp"),
            P("tp", "shard"),
            P(("shard", "ctx"), None),
        ),
        out_specs=(
            P(("shard", "ctx"), None),
            P(("shard", "ctx"), None),
            P("shard"),
            P("shard", "tp"),
            P("shard", "tp"),
            P("shard", "tp"),
            P("shard", "tp"),
            P("tp", "shard"),
            P("shard"),
            P("shard"),
            P("shard"),
            P("shard", "tp"),
            P("shard", "tp"),
            P("tp", "shard"),
        ),
        check_vma=False,
    )
```

```python
import math

import jax
import jax.numpy as jnp
from jax import lax
from jax.experimental import pallas as pl
from jax.experimental.pallas import tpu as pltpu
from jax.sharding import PartitionSpec as P

HD = 128
EPS = 1e-06
BASE = 1000000.0
NEG = -1e30
F32 = jnp.float32
BF16 = jnp.bfloat16
PLANE = ("shard", "tp")
SCALE = 1.0 / math.sqrt(HD)
VMEM = 48 << 20


def lookup(onehot, table):
    return jnp.sum(onehot * table[None, :], axis=1)


def tree_layout(lengths, parents, places):
    labels = jnp.arange(lengths.shape[0], dtype=jnp.int32)
    ends = jnp.cumsum(lengths)
    starts = ends - lengths
    parent_hot = (parents[:, None] == labels[None, :]).astype(jnp.int32)
    grand = lookup(parent_hot, parents)
    parent_len = lookup(parent_hot, lengths)
    grand_hot = (grand[:, None] == labels[None, :]).astype(jnp.int32)
    grand_len = lookup(grand_hot, lengths)
    before = jnp.where(labels == 0, 0, parent_len + jnp.where(parents == 0, 0, grand_len))
    segment = jnp.sum((places[:, None] >= ends[None, :]).astype(jnp.int32), axis=1)
    token_hot = (segment[:, None] == labels[None, :]).astype(jnp.int32)
    position = places - lookup(token_hot, starts) + lookup(token_hot, before)
    return (segment, lookup(token_hot, parents), lookup(token_hot, grand), position)


def rope_tables(position, columns):
    halfway = columns // 2
    frequency = jnp.exp(jnp.arange(halfway, dtype=F32) * (-2.0 * math.log(BASE) / columns))
    angles = position.astype(F32)[:, None] * frequency[None, :]
    angles = jnp.concatenate([angles, angles], axis=1)
    return (jnp.cos(angles), jnp.sin(angles))


def rms_scale(inputs):
    return lax.rsqrt(jnp.mean(inputs * inputs, axis=-1, keepdims=True) + EPS)


def dot(left, right):
    return jnp.dot(left, right, preferred_element_type=F32)


def dot_rows(left, right):
    return lax.dot_general(left, right, (((0,), (0,)), ((), ())), preferred_element_type=F32)


def dot_back(left, right):
    return lax.dot_general(left, right, (((1,), (1,)), ((), ())), preferred_element_type=F32)


def turn(inputs):
    halfway = inputs.shape[-1] // 2
    return jnp.concatenate([-inputs[:, halfway:], inputs[:, :halfway]], axis=-1)


def unturn(inputs):
    halfway = inputs.shape[-1] // 2
    return jnp.concatenate([inputs[:, halfway:], -inputs[:, :halfway]], axis=-1)


def head(number):
    return slice(number * HD, (number + 1) * HD)


def call(kernel, grid, in_specs, out_specs, out_shape, flops, scratch=(), moved=8 << 20):
    return pl.pallas_call(
        kernel,
        grid=grid,
        in_specs=in_specs,
        out_specs=out_specs,
        out_shape=out_shape,
        scratch_shapes=scratch,
        compiler_params=pltpu.CompilerParams(
            dimension_semantics=("arbitrary",) * len(grid), vmem_limit_bytes=VMEM
        ),
        cost_estimate=pl.CostEstimate(flops=flops, bytes_accessed=moved, transcendentals=0),
    )


def struct(shape, dtype):
    return jax.ShapeDtypeStruct(shape, dtype)


def fixed(shape):
    return pl.BlockSpec(shape, lambda i: (0,) * len(shape))


def rowed(rows, columns):
    return pl.BlockSpec((rows, columns), lambda i: (i, 0))


def project_kernel(xa, xb, w, gains, cosine, sine, xn, pre, low, gate):
    x = jnp.where(pl.program_id(0) == 0, xa[...], xb[...]).astype(F32)
    normed = (x * rms_scale(x)).astype(BF16)
    xn[...] = normed
    out = dot(normed, w[...])
    for place in range(3):
        raw = out[:, head(place)]
        pre[:, head(place)] = raw
        unit = raw * rms_scale(raw) * gains[pl.ds(place // 2, 1), :]
        low[:, head(place)] = (unit * cosine[...] + turn(unit) * sine[...]).astype(BF16)
    low[:, head(3)] = out[:, head(3)].astype(BF16)
    gate[...] = out[:, 4 * HD :]


def project(xa, xb, w, gains, cosine, sine):
    half, width = xa.shape
    return call(
        project_kernel,
        (2,),
        [
            fixed((half, width)),
            fixed((half, width)),
            fixed((width, 6 * HD)),
            fixed((2, HD)),
            rowed(half, HD),
            rowed(half, HD),
        ],
        [rowed(half, width), rowed(half, 3 * HD), rowed(half, 4 * HD), rowed(half, 2 * HD)],
        [
            struct((2 * half, width), BF16),
            struct((2 * half, 3 * HD), F32),
            struct((2 * half, 4 * HD), BF16),
            struct((2 * half, 2 * HD), F32),
        ],
        2 * 2 * half * width * 6 * HD,
    )(xa, xb, w, gains, cosine, sine)


def attend_kernel(low, gate, w_out, of_row, of_column, probs, attended, gated, mine, other):
    step = pl.program_id(0)
    half = probs.shape[1]
    rows = pl.ds(step * half, half)
    key, value = low[:, head(2)], low[:, head(3)]
    seg, par, grand, place = (of_row[rows, n : n + 1] for n in range(4))
    key_seg, key_place = of_column[0:1, :], of_column[1:2, :]
    allowed = ((key_seg == seg) | (key_seg == par) | (key_seg == grand)) & (key_place <= place)
    for number in range(2):
        scores = dot_back(low[rows, head(number)], key) * SCALE
        scores = jnp.where(allowed, scores, NEG)
        raised = jnp.exp(scores - jnp.max(scores, axis=-1, keepdims=True))
        share = raised / jnp.sum(raised, axis=-1, keepdims=True)
        probs[number] = share
        seen = dot(share.astype(BF16), value)
        attended[:, head(number)] = seen
        gated[:, head(number)] = (seen * jax.nn.sigmoid(gate[:, head(number)])).astype(BF16)
    out = dot_back(gated[...], w_out[...])

    @pl.when(step == 0)
    def _():
        mine[...] = out

    @pl.when(step == 1)
    def _():
        other[...] = out.astype(BF16)


def attend(low, gate, w, of_row, of_column):
    length = low.shape[0]
    half, width = length // 2, w.shape[0]
    return call(
        attend_kernel,
        (2,),
        [
            fixed((length, 4 * HD)),
            rowed(half, 2 * HD),
            pl.BlockSpec((width, 2 * HD), lambda i: (0, 3)),
            fixed((length, 4)),
            fixed((2, length)),
        ],
        [
            pl.BlockSpec((2, half, length), lambda i: (0, i, 0)),
            rowed(half, 2 * HD),
            rowed(half, 2 * HD),
            fixed((half, width)),
            fixed((half, width)),
        ],
        [
            struct((2, length, length), F32),
            struct((length, 2 * HD), F32),
            struct((length, 2 * HD), BF16),
            struct((half, width), F32),
            struct((half, width), BF16),
        ],
        2 * length * width * 2 * HD + 8 * length * length * HD,
    )(low, gate, w, of_row, of_column)


def feed_kernel(ua, ub, ca, cb, wg, wu, wd, hidden, d_gate, d_up, mine, other, total):
    step = pl.program_id(0)
    half = ua.shape[0]
    for number, (u, cot) in enumerate(((ua, ca), (ub, cb))):
        rows = slice(number * half, (number + 1) * half)
        gate, up = dot(u[...], wg[...]), dot(u[...], wu[...])
        d_hidden = dot(cot[...], wd[...])
        sig = jax.nn.sigmoid(gate)
        silu = gate * sig
        hidden[rows, :] = (silu * up).astype(BF16)
        dg = (d_hidden * up * sig * (1.0 + gate * (1.0 - sig))).astype(BF16)
        du = (d_hidden * silu).astype(BF16)
        d_gate[rows, :] = dg
        d_up[rows, :] = du
        term = dot_back(dg, wg[...]) + dot_back(du, wu[...])

        @pl.when(step == 0)
        def _():
            total[rows, :] = term

        @pl.when(step > 0)
        def _():
            total[rows, :] += term

    @pl.when(step == pl.num_programs(0) - 1)
    def _():
        mine[...] = total[:half, :]
        other[...] = total[half:, :].astype(BF16)


def feed(ua, ub, ca, cb, w):
    half, width = ua.shape
    chunk = 2 * HD
    parts = w.shape[1] // 3 // chunk
    column = lambda shift: pl.BlockSpec((width, chunk), lambda i: (0, shift * parts + i))
    unit = pl.BlockSpec((2 * half, chunk), lambda i: (0, i))
    units = parts * chunk
    return call(
        feed_kernel,
        (parts,),
        [fixed((half, width))] * 4 + [column(0), column(1), column(2)],
        [unit, unit, unit, fixed((half, width)), fixed((half, width))],
        [struct((2 * half, units), BF16)] * 3
        + [struct((half, width), F32), struct((half, width), BF16)],
        2 * 2 * half * width * units * 5,
        scratch=[pltpu.VMEM((2 * half, width), F32)],
    )(ua, ub, ca, cb, w, w, w)


def down_kernel(hidden, w, mine, other):
    out = dot_back(hidden[...], w[...])

    @pl.when(pl.program_id(0) == 0)
    def _():
        mine[...] = out

    @pl.when(pl.program_id(0) == 1)
    def _():
        other[...] = out.astype(BF16)


def down_product(left, w, place):
    length, units = left.shape
    half, width = length // 2, w.shape[0]
    return call(
        down_kernel,
        (2,),
        [rowed(half, units), pl.BlockSpec((width, units), lambda i: (0, place))],
        [fixed((half, width)), fixed((half, width))],
        [struct((half, width), F32), struct((half, width), BF16)],
        2 * length * width * units,
    )(left, w)


def feed_grads_kernel(ua, ub, ca, cb, d_gate, d_up, hidden, out):
    half, units = ua.shape[0], hidden.shape[1]
    pairs = ((ua, ub, d_gate), (ua, ub, d_up), (ca, cb, hidden))
    for number, (first, second, right) in enumerate(pairs):
        term = dot_rows(first[...], right[:half, :]) + dot_rows(second[...], right[half:, :])
        out[:, number * units : (number + 1) * units] = term.astype(BF16)


def feed_grads(ua, ub, ca, cb, d_gate, d_up, hidden):
    half, width = ua.shape
    units = hidden.shape[1]
    chunk = 2 * HD
    slab = pl.BlockSpec((half, chunk), lambda i: (0, i))
    return call(
        feed_grads_kernel,
        (width // chunk,),
        [slab] * 4 + [fixed((2 * half, units))] * 3,
        rowed(chunk, 3 * units),
        struct((width, 3 * units), BF16),
        2 * 2 * half * width * units * 3,
    )(ua, ub, ca, cb, d_gate, d_up, hidden)


def gate_back_kernel(da, db, w_out, gate, attended, d_attended, d_gate):
    half = da.shape[0]
    for number, low in enumerate((da, db)):
        rows = slice(number * half, (number + 1) * half)
        d_gated = dot(low[...], w_out[...])
        sig = jax.nn.sigmoid(gate[rows, :])
        d_attended[rows, :] = (d_gated * sig).astype(BF16)
        d_gate[rows, :] = (d_gated * attended[rows, :] * sig * (1.0 - sig)).astype(BF16)


def gate_back(da, db, w, gate, attended):
    half, width = da.shape
    wide = (2 * half, 2 * HD)
    return call(
        gate_back_kernel,
        (1,),
        [fixed((half, width))] * 2
        + [pl.BlockSpec((width, 2 * HD), lambda i: (0, 3)), fixed(wide), fixed(wide)],
        [fixed(wide), fixed(wide)],
        [struct(wide, BF16), struct(wide, BF16)],
        2 * 2 * half * width * 2 * HD,
    )(da, db, w, gate, attended)


def head_back(grads, inputs, gain):
    factor = rms_scale(inputs)
    scaled = gain * grads
    back = factor * scaled - inputs * factor**3 * jnp.mean(scaled * inputs, axis=-1, keepdims=True)
    return back.astype(BF16), jnp.sum(grads * inputs * factor, axis=0, keepdims=True)


def attend_back_kernel(
    probs, low, d_attended, pre, gains, cosine, sine, out, terms, d_key, d_value
):
    step = pl.program_id(0)
    half = probs.shape[1]
    start = pl.multiple_of(step * half, half)
    rows = pl.ds(start, half)
    key, value = low[:, head(2)], low[:, head(3)]
    cos_rows, sin_rows = cosine[rows, :], sine[rows, :]

    @pl.when(step == 0)
    def _():
        d_key[...] = jnp.zeros_like(d_key)
        d_value[...] = jnp.zeros_like(d_value)
        terms[...] = jnp.zeros_like(terms)

    for number in range(2):
        share = probs[number]
        d_seen = d_attended[:, head(number)]
        d_share = dot_back(d_seen, value)
        d_scores = share * (d_share - jnp.sum(share * d_share, axis=-1, keepdims=True))
        d_scores = d_scores.astype(BF16)
        d_query = dot(d_scores, key) * SCALE
        d_key[...] += dot_rows(d_scores, low[rows, head(number)])
        d_value[...] += dot_rows(share.astype(BF16), d_seen)
        grads = d_query * cos_rows + unturn(d_query * sin_rows)
        back, term = head_back(grads, pre[rows, head(number)], gains[0:1, :])
        out[rows, head(number)] = back
        terms[0:1, :] += term

    @pl.when(step == 1)
    def _():
        grads = d_key[...] * SCALE
        grads = grads * cosine[...] + unturn(grads * sine[...])
        back, term = head_back(grads, pre[:, head(2)], gains[1:2, :])
        out[:, head(2)] = back
        terms[1:2, :] = term
        out[:, head(3)] = d_value[...].astype(BF16)


def attend_back(probs, low, d_attended, pre, gains, cosine, sine):
    length = low.shape[0]
    half = length // 2
    return call(
        attend_back_kernel,
        (2,),
        [
            pl.BlockSpec((2, half, length), lambda i: (0, i, 0)),
            fixed((length, 4 * HD)),
            rowed(half, 2 * HD),
            fixed((length, 3 * HD)),
            fixed((2, HD)),
            fixed((length, HD)),
            fixed((length, HD)),
        ],
        [fixed((length, 4 * HD)), fixed((8, HD))],
        [struct((length, 4 * HD), BF16), struct((8, HD), F32)],
        20 * length * length * HD,
        scratch=[pltpu.VMEM((length, HD), F32), pltpu.VMEM((length, HD), F32)],
    )(probs, low, d_attended, pre, gains, cosine, sine)


def input_back_kernel(d_qkv, d_gate, w, mine, other):
    out = dot_back(d_qkv[...], w[:, : 4 * HD]) + dot_back(d_gate[...], w[:, 4 * HD :])

    @pl.when(pl.program_id(0) == 0)
    def _():
        mine[...] = out

    @pl.when(pl.program_id(0) == 1)
    def _():
        other[...] = out.astype(BF16)


def input_back(d_qkv, d_gate, w):
    length = d_qkv.shape[0]
    half, width = length // 2, w.shape[0]
    return call(
        input_back_kernel,
        (2,),
        [rowed(half, 4 * HD), rowed(half, 2 * HD), fixed((width, 6 * HD))],
        [fixed((half, width)), fixed((half, width))],
        [struct((half, width), F32), struct((half, width), BF16)],
        2 * length * width * 6 * HD,
    )(d_qkv, d_gate, w)


def outer_grads_kernel(xn, da, db, d_gate, gated, out):
    half = da.shape[0]
    split = d_gate.shape[1]
    out[:, :split] = dot_rows(xn[...], d_gate[...]).astype(BF16)
    term = dot_rows(da[...], gated[:half, :]) + dot_rows(db[...], gated[half:, :])
    out[:, split:] = term.astype(BF16)


def outer_grads(xn, da, db, d_gate, gated):
    half, width = da.shape
    chunk = 2 * HD
    slab = pl.BlockSpec((half, chunk), lambda i: (0, i))
    return call(
        outer_grads_kernel,
        (width // chunk,),
        [pl.BlockSpec((2 * half, chunk), lambda i: (0, i)), slab, slab]
        + [fixed((2 * half, 2 * HD))] * 2,
        rowed(chunk, 4 * HD),
        struct((width, 4 * HD), BF16),
        2 * 2 * half * width * 4 * HD,
    )(xn, da, db, d_gate, gated)


def inner_grads_kernel(xn, d_qkv, terms, out):
    term = dot_rows(xn[...], d_qkv[...]).astype(BF16)
    count, block = out.shape[0], out.shape[1] - terms.shape[1]
    for number in range(count):
        out[number, :block] = term[number * block : (number + 1) * block]
        out[number, block:] = terms[number].astype(BF16)


def inner_grads(xn, d_qkv, terms):
    length, width = xn.shape
    columns, extra = d_qkv.shape[1], terms.shape[1]
    owners = terms.shape[0]
    block = width // owners
    return call(
        inner_grads_kernel,
        (owners // 2,),
        [
            pl.BlockSpec((length, 2 * block), lambda i: (0, i)),
            fixed((length, columns)),
            pl.BlockSpec((2, extra, columns), lambda i: (i, 0, 0)),
        ],
        pl.BlockSpec((2, block + extra, columns), lambda i: (i, 0, 0)),
        struct((owners, block + extra, columns), BF16),
        2 * length * width * columns,
    )(xn, d_qkv, terms)


def middle_kernel(parts, x, middle, spread):
    total = x[...].astype(F32) + jnp.sum(parts[...].astype(F32), axis=0)
    middle[...] = total
    low = (total * rms_scale(total)).astype(BF16)
    for number in range(spread.shape[0]):
        spread[number] = low


def middle_step(parts, x):
    shape = x.shape
    return call(
        middle_kernel,
        (1,),
        [fixed(parts.shape), fixed(shape)],
        [fixed(shape), fixed(parts.shape)],
        [struct(shape, F32), struct(parts.shape, BF16)],
        1 << 20,
    )(parts, x)


def norm_back(grads, inputs):
    factor = rms_scale(inputs)
    return factor * grads - inputs * factor**3 * jnp.mean(grads * inputs, axis=-1, keepdims=True)


def d_middle_kernel(parts, middle, cot, d_middle, spread):
    grads = jnp.sum(parts[...].astype(F32), axis=0)
    total = cot[...].astype(F32) + norm_back(grads, middle[...])
    d_middle[...] = total
    for number in range(spread.shape[0]):
        spread[number] = total.astype(BF16)


def d_middle_step(parts, middle, cot):
    shape = cot.shape
    return call(
        d_middle_kernel,
        (1,),
        [fixed(parts.shape), fixed(shape), fixed(shape)],
        [fixed(shape), fixed(parts.shape)],
        [struct(shape, F32), struct(parts.shape, BF16)],
        1 << 20,
    )(parts, middle, cot)


def make_shards(mesh):
    n_shard, n_ctx, n_tp = mesh.shape["shard"], mesh.shape["ctx"], mesh.shape["tp"]
    pairs = n_shard // 2

    def joint(pair, core, tp):
        return (pair * 2 + core) * n_tp + tp

    core_perm = [(i, i ^ 1) for i in range(n_shard)]
    planes = [
        [joint(pair, core, tp) for pair in range(pairs) for tp in range(n_tp)] for core in range(2)
    ]
    swap_perm = [
        edge
        for pair in range(pairs)
        for edge in (
            (joint(pair, 1, 0), joint(pair, 0, 1)),
            (joint(pair, 0, 1), joint(pair, 1, 0)),
        )
    ]
    across_perm = [(joint(pair, t, t), joint(pair, t, 1 - t)) for pair in range(pairs) for t in range(2)]

    def core_swap(value):
        return lax.ppermute(value, "shard", core_perm)

    def ctx_exchange(value):
        return lax.all_to_all(value, "ctx", 0, 0)

    def ctx_gather(value):
        return ctx_exchange(jnp.broadcast_to(value[None], (n_ctx,) + value.shape))

    def flat(value):
        return value.reshape((-1,) + value.shape[2:])

    def tree_rows(spread):
        mine = flat(ctx_exchange(spread))
        return mine, core_swap(mine)

    def tree_sums(mine, other):
        half = (mine + core_swap(other).astype(F32)).astype(BF16)
        return ctx_exchange(half.reshape((n_ctx, -1) + half.shape[1:]))

    def plane_gather(value):
        return lax.all_gather(value, PLANE, axis=0, tiled=True, axis_index_groups=planes)

    def plane_scatter(value):
        return lax.psum_scatter(
            value, PLANE, scatter_dimension=0, tiled=True, axis_index_groups=planes
        )

    def plane_exchange(value):
        parts = lax.all_to_all(value, PLANE, 0, 0, axis_index_groups=planes)
        return jnp.sum(parts.astype(F32), axis=0)

    def shards(
        tokens,
        seg_lengths,
        seg_parents,
        gain_in,
        w_query,
        w_key,
        w_value,
        w_gate_attn,
        w_out,
        gain_query,
        gain_key,
        gain_mid,
        w_gate,
        w_up,
        w_down,
        cotangent,
    ):
        core = lax.axis_index("shard") % 2
        tp = lax.axis_index("tp")
        ctx = lax.axis_index("ctx")
        native = core == tp
        rows = tokens.shape[0] // 2

        def swapped(value):
            return jnp.where(native, value, lax.ppermute(value, PLANE, swap_perm))

        def quarter(weight, axis):
            size = weight.shape[axis] // n_ctx
            return lax.dynamic_slice_in_dim(weight, ctx * size, size, axis)

        gain_one = gain_in.astype(F32)[:, None]
        gain_two = gain_mid.astype(F32)[:, None]
        first = jnp.concatenate(
            [quarter(w, 1) for w in (w_query, w_key, w_value, w_gate_attn)], axis=1
        )
        first = (first.astype(F32) * gain_one).astype(BF16)
        first = jnp.concatenate([first, quarter(w_out, 0).T], axis=1)
        second = jnp.concatenate([quarter(w_gate, 1), quarter(w_up, 1)], axis=1)
        second = (second.astype(F32) * gain_two).astype(BF16)
        second = jnp.concatenate([second, quarter(w_down, 0).T], axis=1)
        w1 = plane_gather(swapped(first))
        w2 = plane_gather(swapped(second))
        head_gains = lax.all_gather(
            jnp.concatenate([gain_query[None], gain_key[None]], axis=0), "shard", axis=1, tiled=True
        ).astype(F32)

        both = jnp.stack([tokens, cotangent])
        keep = lax.dynamic_slice_in_dim(both, core * rows, rows, 1)
        give = lax.dynamic_slice_in_dim(both, (1 - core) * rows, rows, 1)
        own = jnp.where(native, keep, core_swap(give))
        tree = jnp.concatenate([seg_lengths, seg_parents], axis=0)
        tree = jnp.where(native, tree, core_swap(tree))
        own_x, own_cot = own[0], own[1]
        xa, xb = tree_rows(jnp.broadcast_to(own_x[None], (n_ctx,) + own_x.shape))
        ca, cb = tree_rows(jnp.broadcast_to(own_cot[None], (n_ctx,) + own_cot.shape))

        half_at = jnp.where(jnp.arange(2) == 0, core, 1 - core) * rows
        places = (
            half_at[:, None, None]
            + jnp.arange(n_ctx, dtype=jnp.int32)[None, :, None] * (2 * rows)
            + jnp.arange(rows, dtype=jnp.int32)[None, None, :]
        ).reshape(-1)
        segment, parent_seg, grand_seg, position = tree_layout(tree[0], tree[1], places)
        of_row = jnp.stack([segment, parent_seg, grand_seg, places], axis=1)
        of_column = jnp.stack([segment, places], axis=0)
        cosine, sine = rope_tables(position, HD)

        xn, pre, low, gate = project(xa, xb, w1, head_gains, cosine, sine)
        probs, attended, gated, mine, other = attend(low, gate, w1, of_row, of_column)
        middle, spread = middle_step(tree_sums(mine, other), own_x)
        ua, ub = tree_rows(spread)

        hidden, d_gate, d_up, mine, other = feed(ua, ub, ca, cb, w2)
        units = hidden.shape[1]
        grad_ffn = plane_scatter(feed_grads(ua, ub, ca, cb, d_gate, d_up, hidden))
        d_middle, spread = d_middle_step(tree_sums(mine, other), middle, own_cot)
        da, db = tree_rows(spread)
        layer_parts = tree_sums(*down_product(hidden, w2, 2))
        layer_own = middle + jnp.sum(layer_parts.astype(F32), axis=0)

        d_attended, d_gate_pre = gate_back(da, db, w1, gate, attended)
        grad_outer = plane_exchange(
            outer_grads(xn, da, db, d_gate_pre, gated).reshape(n_shard, -1, 4 * HD)
        )
        d_qkv, terms = attend_back(probs, low, d_attended, pre, head_gains, cosine, sine)

        def spread_terms(vector):
            return jnp.pad(vector.reshape(n_shard, 1, -1), ((0, 0), (0, 15), (0, 0)))

        head_rows = gain_query.shape[0]
        wide_terms = jnp.concatenate([spread_terms(terms[0]), spread_terms(terms[1])], axis=2)
        wide_terms = jnp.pad(wide_terms, ((0, 0), (0, 0), (0, 4 * HD - 2 * head_rows)))
        grad_inner = plane_exchange(inner_grads(xn, d_qkv, wide_terms))
        parts = tree_sums(*input_back(d_qkv, d_gate_pre, w1))
        input_own = d_middle + norm_back(
            jnp.sum(parts.astype(F32), axis=0), own_x.astype(F32)
        )

        def owners(block):
            return ctx_gather(swapped(block.astype(BF16))).astype(F32)

        def side(parts):
            return parts.transpose(1, 0, 2).reshape(parts.shape[1], -1)

        def down(parts):
            return parts.transpose(0, 2, 1).reshape(-1, parts.shape[1])

        size = gain_in.shape[0]
        ffn = owners(grad_ffn)
        raw_gate = side(ffn[:, :, :units])
        raw_up = side(ffn[:, :, units : 2 * units])
        grad_down = down(ffn[:, :, 2 * units :])
        outer = owners(grad_outer)
        raw_gate_attn = side(outer[:, :, : 2 * HD])
        grad_out = down(outer[:, :, 2 * HD :])
        ends = grad_inner[size:]
        ends = ends + core_swap(ends.astype(BF16)).astype(F32)
        inner = owners(jnp.concatenate([grad_inner[:size], ends], axis=0))
        raw_query = side(inner[:, :size, : 2 * HD])
        raw_key = side(inner[:, :size, 2 * HD : 3 * HD])
        raw_value = side(inner[:, :size, 3 * HD :])
        head_ends = jnp.sum(inner[:, size, : 2 * head_rows], axis=0)

        def along(weights, raws):
            total = 0.0
            for weight, raw in zip(weights, raws):
                total = total + jnp.sum(weight.astype(F32) * raw, axis=1)
            return total

        gain_terms = jnp.stack(
            [
                along(
                    (w_query, w_key, w_value, w_gate_attn),
                    (raw_query, raw_key, raw_value, raw_gate_attn),
                ),
                along((w_gate, w_up), (raw_gate, raw_up)),
            ]
        )
        gain_terms = gain_terms + lax.ppermute(gain_terms, "tp", [(0, 1), (1, 0)])

        def finish(part):
            low = part.astype(BF16)
            sibling = core_swap(low)
            full = jnp.where(
                core == 0,
                jnp.concatenate([low, sibling], axis=0),
                jnp.concatenate([sibling, low], axis=0),
            )
            return jnp.where(native, full, lax.ppermute(full, PLANE, across_perm)).astype(F32)

        return (
            finish(layer_own),
            finish(input_own),
            gain_terms[0],
            raw_query * gain_one,
            raw_key * gain_one,
            raw_value * gain_one,
            raw_gate_attn * gain_one,
            grad_out,
            head_ends[:head_rows],
            head_ends[head_rows:],
            gain_terms[1],
            raw_gate * gain_two,
            raw_up * gain_two,
            grad_down,
        )

    return shards


def solution(mesh):
    return jax.shard_map(
        make_shards(mesh),
        mesh=mesh,
        in_specs=(
            P(("shard", "ctx"), None),
            P("shard", None),
            P("shard", None),
            P("shard"),
            P("shard", "tp"),
            P("shard", "tp"),
            P("shard", "tp"),
            P("shard", "tp"),
            P("tp", "shard"),
            P("shard"),
            P("shard"),
            P("shard"),
            P("shard", "tp"),
            P("shard", "tp"),
            P("tp", "shard"),
            P(("shard", "ctx"), None),
        ),
        out_specs=(
            P(("shard", "ctx"), None),
            P(("shard", "ctx"), None),
            P("shard"),
            P("shard", "tp"),
            P("shard", "tp"),
            P("shard", "tp"),
            P("shard", "tp"),
            P("tp", "shard"),
            P("shard"),
            P("shard"),
            P("shard"),
            P("shard", "tp"),
            P("shard", "tp"),
            P("tp", "shard"),
        ),
        check_vma=False,
    )
```

```python
import math

import jax
import jax.numpy as jnp
from jax import lax
from jax.experimental import pallas as pl
from jax.experimental.pallas import tpu as pltpu
from jax.sharding import PartitionSpec as P

HD = 128
EPS = 1e-06
BASE = 1000000.0
NEG = -1e30
F32 = jnp.float32
BF16 = jnp.bfloat16
PLANE = ("shard", "tp")
SCALE = 1.0 / math.sqrt(HD)
VMEM = 48 << 20


def lookup(onehot, table):
    return jnp.sum(onehot * table[None, :], axis=1)


def tree_layout(lengths, parents, places):
    labels = jnp.arange(lengths.shape[0], dtype=jnp.int32)
    ends = jnp.cumsum(lengths)
    starts = ends - lengths
    parent_hot = (parents[:, None] == labels[None, :]).astype(jnp.int32)
    grand = lookup(parent_hot, parents)
    parent_len = lookup(parent_hot, lengths)
    grand_hot = (grand[:, None] == labels[None, :]).astype(jnp.int32)
    grand_len = lookup(grand_hot, lengths)
    before = jnp.where(labels == 0, 0, parent_len + jnp.where(parents == 0, 0, grand_len))
    segment = jnp.sum((places[:, None] >= ends[None, :]).astype(jnp.int32), axis=1)
    token_hot = (segment[:, None] == labels[None, :]).astype(jnp.int32)
    position = places - lookup(token_hot, starts) + lookup(token_hot, before)
    return (segment, lookup(token_hot, parents), lookup(token_hot, grand), position)


def rope_tables(position, columns):
    halfway = columns // 2
    frequency = jnp.exp(jnp.arange(halfway, dtype=F32) * (-2.0 * math.log(BASE) / columns))
    angles = position.astype(F32)[:, None] * frequency[None, :]
    angles = jnp.concatenate([angles, angles], axis=1)
    return (jnp.cos(angles), jnp.sin(angles))


def rms_scale(inputs):
    return lax.rsqrt(jnp.mean(inputs * inputs, axis=-1, keepdims=True) + EPS)


def dot(left, right):
    return jnp.dot(left, right, preferred_element_type=F32)


def dot_rows(left, right):
    return lax.dot_general(left, right, (((0,), (0,)), ((), ())), preferred_element_type=F32)


def dot_back(left, right):
    return lax.dot_general(left, right, (((1,), (1,)), ((), ())), preferred_element_type=F32)


def turn(inputs):
    halfway = inputs.shape[-1] // 2
    return jnp.concatenate([-inputs[:, halfway:], inputs[:, :halfway]], axis=-1)


def unturn(inputs):
    halfway = inputs.shape[-1] // 2
    return jnp.concatenate([inputs[:, halfway:], -inputs[:, :halfway]], axis=-1)


def head(number):
    return slice(number * HD, (number + 1) * HD)


def call(kernel, grid, in_specs, out_specs, out_shape, flops, scratch=(), moved=8 << 20, behind=()):
    count = len(in_specs)

    def body(*refs):
        kernel(*refs[:count], *refs[count + len(behind) :])

    built = pl.pallas_call(
        body,
        grid=grid,
        in_specs=list(in_specs) + [pl.BlockSpec(memory_space=pl.ANY)] * len(behind),
        out_specs=out_specs,
        out_shape=out_shape,
        scratch_shapes=scratch,
        compiler_params=pltpu.CompilerParams(
            dimension_semantics=("arbitrary",) * len(grid), vmem_limit_bytes=VMEM
        ),
        cost_estimate=pl.CostEstimate(flops=flops, bytes_accessed=moved, transcendentals=0),
    )
    return lambda *operands: built(*operands, *behind)


def struct(shape, dtype):
    return jax.ShapeDtypeStruct(shape, dtype)


def fixed(shape):
    return pl.BlockSpec(shape, lambda i: (0,) * len(shape))


def rowed(rows, columns):
    return pl.BlockSpec((rows, columns), lambda i: (i, 0))


def piled(shape, which):
    return pl.BlockSpec((shape[0], shape[1] // 2, shape[2]), lambda i: (0, which, 0))


def flat(value):
    return value.reshape((-1,) + value.shape[2:])


def project_kernel(xa, xb, w, ends, cosine, sine, xn, pre, low, gate, gains):
    x = flat(jnp.where(pl.program_id(0) == 0, xa[...], xb[...])).astype(F32)
    normed = (x * rms_scale(x)).astype(BF16)
    xn[...] = normed
    out = dot(normed, w[...])
    found = jnp.zeros((16, HD), F32)
    for start in range(0, ends.shape[0], HD):
        found = found + ends[start : start + 16, :].astype(F32)
    gains[...] = found
    for place in range(3):
        raw = out[:, head(place)]
        pre[:, head(place)] = raw
        unit = raw * rms_scale(raw) * found[place // 2 : place // 2 + 1, :]
        low[:, head(place)] = (unit * cosine[...] + turn(unit) * sine[...]).astype(BF16)
    low[:, head(3)] = out[:, head(3)].astype(BF16)
    gate[...] = out[:, 4 * HD :]


def project(xa, xb, w, cosine, sine):
    half, width = xa.shape[0] * xa.shape[1] // 2, xa.shape[2]
    return call(
        project_kernel,
        (2,),
        [
            piled(xa.shape, 0),
            piled(xb.shape, 0),
            fixed((width, 6 * HD)),
            pl.BlockSpec((width, HD), lambda i: (0, 8)),
            rowed(half, HD),
            rowed(half, HD),
        ],
        [
            rowed(half, width),
            rowed(half, 3 * HD),
            rowed(half, 4 * HD),
            rowed(half, 2 * HD),
            fixed((16, HD)),
        ],
        [
            struct((2 * half, width), BF16),
            struct((2 * half, 3 * HD), F32),
            struct((2 * half, 4 * HD), BF16),
            struct((2 * half, 2 * HD), F32),
            struct((16, HD), F32),
        ],
        2 * 2 * half * width * 6 * HD,
    )(xa, xb, w, w, cosine, sine)


def attend_kernel(low, gate, w_out, of_row, of_column, probs, attended, gated, mine, other):
    step = pl.program_id(0)
    half = probs.shape[1]
    rows = pl.ds(step * half, half)
    key, value = low[:, head(2)], low[:, head(3)]
    seg, par, grand, place = (of_row[rows, n : n + 1] for n in range(4))
    key_seg, key_place = of_column[0:1, :], of_column[1:2, :]
    allowed = ((key_seg == seg) | (key_seg == par) | (key_seg == grand)) & (key_place <= place)
    for number in range(2):
        scores = dot_back(low[rows, head(number)], key) * SCALE
        scores = jnp.where(allowed, scores, NEG)
        raised = jnp.exp(scores - jnp.max(scores, axis=-1, keepdims=True))
        share = raised / jnp.sum(raised, axis=-1, keepdims=True)
        probs[number] = share
        seen = dot(share.astype(BF16), value)
        attended[:, head(number)] = seen
        gated[:, head(number)] = (seen * jax.nn.sigmoid(gate[:, head(number)])).astype(BF16)
    out = dot_back(gated[...], w_out[...])

    @pl.when(step == 0)
    def _():
        mine[...] = out

    @pl.when(step == 1)
    def _():
        other[...] = out.astype(BF16)


def attend(low, gate, w, of_row, of_column):
    length = low.shape[0]
    half, width = length // 2, w.shape[0]
    return call(
        attend_kernel,
        (2,),
        [
            fixed((length, 4 * HD)),
            rowed(half, 2 * HD),
            pl.BlockSpec((width, 2 * HD), lambda i: (0, 3)),
            fixed((length, 4)),
            fixed((2, length)),
        ],
        [
            pl.BlockSpec((2, half, length), lambda i: (0, i, 0)),
            rowed(half, 2 * HD),
            rowed(half, 2 * HD),
            fixed((half, width)),
            fixed((half, width)),
        ],
        [
            struct((2, length, length), F32),
            struct((length, 2 * HD), F32),
            struct((length, 2 * HD), BF16),
            struct((half, width), F32),
            struct((half, width), BF16),
        ],
        2 * length * width * 2 * HD + 8 * length * length * HD,
    )(low, gate, w, of_row, of_column)


def feed_kernel(
    ua, ub, ca, cb, wg, wu, wd, hidden, d_gate, d_up, mine, other, total, u_all, c_all
):
    step = pl.program_id(0)
    half = ua.shape[0]

    @pl.when(step == 0)
    def _():
        u_all[:half, :] = ua[...]
        u_all[half:, :] = ub[...]
        c_all[:half, :] = flat(ca[...])
        c_all[half:, :] = flat(cb[...])

    gate, up = dot(u_all[...], wg[...]), dot(u_all[...], wu[...])
    d_hidden = dot(c_all[...], wd[...])
    sig = jax.nn.sigmoid(gate)
    silu = gate * sig
    hidden[...] = (silu * up).astype(BF16)
    dg = (d_hidden * up * sig * (1.0 + gate * (1.0 - sig))).astype(BF16)
    du = (d_hidden * silu).astype(BF16)
    d_gate[...] = dg
    d_up[...] = du
    term = dot_back(dg, wg[...]) + dot_back(du, wu[...])

    @pl.when(step == 0)
    def _():
        total[...] = term

    @pl.when(step > 0)
    def _():
        total[...] += term

    @pl.when(step == pl.num_programs(0) - 1)
    def _():
        mine[...] = total[:half, :]
        other[...] = total[half:, :].astype(BF16)


def feed(ua, ub, ca, cb, w):
    half, width = ua.shape
    chunk = 2 * HD
    parts = w.shape[1] // 3 // chunk
    column = lambda shift: pl.BlockSpec((width, chunk), lambda i: (0, shift * parts + i))
    unit = pl.BlockSpec((2 * half, chunk), lambda i: (0, i))
    units = parts * chunk
    return call(
        feed_kernel,
        (parts,),
        [fixed((half, width))] * 2
        + [piled(ca.shape, 1)] * 2
        + [column(0), column(1), column(2)],
        [unit, unit, unit, fixed((half, width)), fixed((half, width))],
        [struct((2 * half, units), BF16)] * 3
        + [struct((half, width), F32), struct((half, width), BF16)],
        2 * 2 * half * width * units * 5,
        scratch=[pltpu.VMEM((2 * half, width), F32)] + [pltpu.VMEM((2 * half, width), BF16)] * 2,
    )(ua, ub, ca, cb, w, w, w)


def down_kernel(hidden, w, mine, other):
    out = dot_back(hidden[...], w[...])

    @pl.when(pl.program_id(0) == 0)
    def _():
        mine[...] = out

    @pl.when(pl.program_id(0) == 1)
    def _():
        other[...] = out.astype(BF16)


def down_product(left, w, place, behind):
    length, units = left.shape
    half, width = length // 2, w.shape[0]
    return call(
        down_kernel,
        (2,),
        [rowed(half, units), pl.BlockSpec((width, units), lambda i: (0, place))],
        [fixed((half, width)), fixed((half, width))],
        [struct((half, width), F32), struct((half, width), BF16)],
        2 * length * width * units,
        behind=behind,
    )(left, w)


def feed_grads_kernel(ua, ub, ca, cb, d_gate, d_up, hidden, out):
    half, units = ua.shape[0], hidden.shape[1]
    pairs = ((ua, ub, d_gate), (ua, ub, d_up), (ca, cb, hidden))
    for number, (first, second, right) in enumerate(pairs):
        first, second = first[...], second[...]
        if number == 2:
            first, second = flat(first), flat(second)
        term = dot_rows(first, right[:half, :]) + dot_rows(second, right[half:, :])
        out[:, number * units : (number + 1) * units] = term.astype(BF16)


def feed_grads(ua, ub, ca, cb, d_gate, d_up, hidden, behind):
    half, width = ua.shape
    units = hidden.shape[1]
    chunk = 2 * HD
    slab = pl.BlockSpec((half, chunk), lambda i: (0, i))
    return call(
        feed_grads_kernel,
        (width // chunk,),
        [slab] * 2
        + [pl.BlockSpec((ca.shape[0], ca.shape[1] // 2, chunk), lambda i: (0, 1, i))] * 2
        + [fixed((2 * half, units))] * 3,
        rowed(chunk, 3 * units),
        struct((width, 3 * units), BF16),
        2 * 2 * half * width * units * 3,
        behind=behind,
    )(ua, ub, ca, cb, d_gate, d_up, hidden)


def gate_back_kernel(da, db, w_out, gate, attended, d_attended, d_gate):
    half = da.shape[0]
    for number, low in enumerate((da, db)):
        rows = slice(number * half, (number + 1) * half)
        d_gated = dot(low[...], w_out[...])
        sig = jax.nn.sigmoid(gate[rows, :])
        d_attended[rows, :] = (d_gated * sig).astype(BF16)
        d_gate[rows, :] = (d_gated * attended[rows, :] * sig * (1.0 - sig)).astype(BF16)


def gate_back(da, db, w, gate, attended):
    half, width = da.shape
    wide = (2 * half, 2 * HD)
    return call(
        gate_back_kernel,
        (1,),
        [fixed((half, width))] * 2
        + [pl.BlockSpec((width, 2 * HD), lambda i: (0, 3)), fixed(wide), fixed(wide)],
        [fixed(wide), fixed(wide)],
        [struct(wide, BF16), struct(wide, BF16)],
        2 * 2 * half * width * 2 * HD,
    )(da, db, w, gate, attended)


def head_back(grads, inputs, gain):
    factor = rms_scale(inputs)
    scaled = gain * grads
    back = factor * scaled - inputs * factor**3 * jnp.mean(scaled * inputs, axis=-1, keepdims=True)
    return back.astype(BF16), jnp.sum(grads * inputs * factor, axis=0, keepdims=True)


def attend_back_kernel(
    probs, low, d_attended, pre, gains, cosine, sine, out, terms, d_key, d_value
):
    step = pl.program_id(0)
    half = probs.shape[1]
    start = pl.multiple_of(step * half, half)
    rows = pl.ds(start, half)
    key, value = low[:, head(2)], low[:, head(3)]
    cos_rows, sin_rows = cosine[rows, :], sine[rows, :]

    @pl.when(step == 0)
    def _():
        d_key[...] = jnp.zeros_like(d_key)
        d_value[...] = jnp.zeros_like(d_value)
        terms[...] = jnp.zeros_like(terms)

    for number in range(2):
        share = probs[number]
        d_seen = d_attended[:, head(number)]
        d_share = dot_back(d_seen, value)
        d_scores = share * (d_share - jnp.sum(share * d_share, axis=-1, keepdims=True))
        d_scores = d_scores.astype(BF16)
        d_query = dot(d_scores, key) * SCALE
        d_key[...] += dot_rows(d_scores, low[rows, head(number)])
        d_value[...] += dot_rows(share.astype(BF16), d_seen)
        grads = d_query * cos_rows + unturn(d_query * sin_rows)
        back, term = head_back(grads, pre[rows, head(number)], gains[0:1, :])
        out[rows, head(number)] = back
        terms[0:1, :] += term

    @pl.when(step == 1)
    def _():
        grads = d_key[...] * SCALE
        grads = grads * cosine[...] + unturn(grads * sine[...])
        back, term = head_back(grads, pre[:, head(2)], gains[1:2, :])
        out[:, head(2)] = back
        terms[1:2, :] = term
        out[:, head(3)] = d_value[...].astype(BF16)


def attend_back(probs, low, d_attended, pre, gains, cosine, sine, behind):
    length = low.shape[0]
    half = length // 2
    return call(
        attend_back_kernel,
        (2,),
        [
            pl.BlockSpec((2, half, length), lambda i: (0, i, 0)),
            fixed((length, 4 * HD)),
            rowed(half, 2 * HD),
            fixed((length, 3 * HD)),
            fixed((16, HD)),
            fixed((length, HD)),
            fixed((length, HD)),
        ],
        [fixed((length, 4 * HD)), fixed((8, HD))],
        [struct((length, 4 * HD), BF16), struct((8, HD), F32)],
        20 * length * length * HD,
        scratch=[pltpu.VMEM((length, HD), F32), pltpu.VMEM((length, HD), F32)],
        behind=behind,
    )(probs, low, d_attended, pre, gains, cosine, sine)


def input_back_kernel(d_qkv, d_gate, w, mine, other):
    out = dot_back(d_qkv[...], w[:, : 4 * HD]) + dot_back(d_gate[...], w[:, 4 * HD :])

    @pl.when(pl.program_id(0) == 0)
    def _():
        mine[...] = out

    @pl.when(pl.program_id(0) == 1)
    def _():
        other[...] = out.astype(BF16)


def input_back(d_qkv, d_gate, w):
    length = d_qkv.shape[0]
    half, width = length // 2, w.shape[0]
    return call(
        input_back_kernel,
        (2,),
        [rowed(half, 4 * HD), rowed(half, 2 * HD), fixed((width, 6 * HD))],
        [fixed((half, width)), fixed((half, width))],
        [struct((half, width), F32), struct((half, width), BF16)],
        2 * length * width * 6 * HD,
    )(d_qkv, d_gate, w)


def outer_grads_kernel(xn, da, db, d_gate, gated, out):
    half = da.shape[0]
    split = d_gate.shape[1]
    out[:, :split] = dot_rows(xn[...], d_gate[...]).astype(BF16)
    term = dot_rows(da[...], gated[:half, :]) + dot_rows(db[...], gated[half:, :])
    out[:, split:] = term.astype(BF16)


def outer_grads(xn, da, db, d_gate, gated):
    half, width = da.shape
    chunk = 2 * HD
    slab = pl.BlockSpec((half, chunk), lambda i: (0, i))
    return call(
        outer_grads_kernel,
        (width // chunk,),
        [pl.BlockSpec((2 * half, chunk), lambda i: (0, i)), slab, slab]
        + [fixed((2 * half, 2 * HD))] * 2,
        rowed(chunk, 4 * HD),
        struct((width, 4 * HD), BF16),
        2 * 2 * half * width * 4 * HD,
    )(xn, da, db, d_gate, gated)


def inner_grads_kernel(xn, d_qkv, terms, out):
    term = dot_rows(xn[...], d_qkv[...]).astype(BF16)
    count, block = out.shape[0], out.shape[1] - terms.shape[1]
    for number in range(count):
        out[number, :block] = term[number * block : (number + 1) * block]
        out[number, block:] = terms[number].astype(BF16)


def inner_grads(xn, d_qkv, terms, behind):
    length, width = xn.shape
    columns, extra = d_qkv.shape[1], terms.shape[1]
    owners = terms.shape[0]
    block = width // owners
    return call(
        inner_grads_kernel,
        (owners // 2,),
        [
            pl.BlockSpec((length, 2 * block), lambda i: (0, i)),
            fixed((length, columns)),
            pl.BlockSpec((2, extra, columns), lambda i: (i, 0, 0)),
        ],
        pl.BlockSpec((2, block + extra, columns), lambda i: (i, 0, 0)),
        struct((owners, block + extra, columns), BF16),
        2 * length * width * columns,
        behind=behind,
    )(xn, d_qkv, terms)


def middle_kernel(parts, x, middle, spread):
    total = x[...].astype(F32) + jnp.sum(parts[...].astype(F32), axis=0)
    middle[...] = total
    low = (total * rms_scale(total)).astype(BF16)
    for number in range(spread.shape[0]):
        spread[number] = low


def middle_step(parts, x):
    shape = x.shape
    return call(
        middle_kernel,
        (1,),
        [fixed(parts.shape), fixed(shape)],
        [fixed(shape), fixed(parts.shape)],
        [struct(shape, F32), struct(parts.shape, BF16)],
        1 << 20,
    )(parts, x)


def norm_back(grads, inputs):
    factor = rms_scale(inputs)
    return factor * grads - inputs * factor**3 * jnp.mean(grads * inputs, axis=-1, keepdims=True)


def d_middle_kernel(parts, middle, cot, d_middle, spread):
    grads = jnp.sum(parts[...].astype(F32), axis=0)
    total = cot[...].astype(F32) + norm_back(grads, middle[...])
    d_middle[...] = total
    for number in range(spread.shape[0]):
        spread[number] = total.astype(BF16)


def d_middle_step(parts, middle, cot):
    shape = cot.shape
    return call(
        d_middle_kernel,
        (1,),
        [fixed(parts.shape), fixed(shape), fixed(shape)],
        [fixed(shape), fixed(parts.shape)],
        [struct(shape, F32), struct(parts.shape, BF16)],
        1 << 20,
    )(parts, middle, cot)


def input_step_kernel(p0, p1, p2, p3, d_middle, x, out):
    grads = sum(p[...].astype(F32) for p in (p0, p1, p2, p3))
    out[...] = (d_middle[...] + norm_back(grads, x[...].astype(F32))).astype(BF16)


def input_step(parts, d_middle, x):
    shape = x.shape
    return call(
        input_step_kernel,
        (1,),
        [fixed(shape)] * 6,
        fixed(shape),
        struct(shape, BF16),
        1 << 20,
    )(*parts, d_middle, x)


def lanes(value):
    return sum(value[:, start : start + HD] for start in range(0, value.shape[1], HD))


def pick(blocks):
    step = pl.program_id(0)
    value = blocks[0][...]
    for number in range(1, len(blocks)):
        value = jnp.where(step == number, blocks[number][...], value)
    return value.astype(F32)


def close_feed_kernel(turn_at, b0, b1, b2, b3, w_gate, w_up, gain, g_gate, g_up, g_down, sums):
    raw = pick((b0, b1, b2, b3))
    units = w_gate.shape[1]
    raw_gate, raw_up = raw[:, :units], raw[:, units : 2 * units]
    g_gate[...] = raw_gate * gain[...]
    g_up[...] = raw_up * gain[...]
    g_down[...] = raw[:, 2 * units :].T
    term = lanes(raw_gate * w_gate[...].astype(F32)) + lanes(raw_up * w_up[...].astype(F32))

    @pl.when(pl.program_id(0) == 0)
    def _():
        sums[...] = term

    @pl.when(pl.program_id(0) > 0)
    def _():
        sums[...] += term


def close_attend_kernel(
    turn_at, i0, i1, i2, i3, o0, o1, o2, o3, wq, wk, wv, wg, gain, gq, gk, gv, gg, go, sums, ends
):
    inner, outer = pick((i0, i1, i2, i3)), pick((o0, o1, o2, o3))
    block = outer.shape[0]
    scale = gain[...]
    raw_q, raw_k, raw_v = inner[:block, : 2 * HD], inner[:block, head(2)], inner[:block, head(3)]
    raw_g = outer[:, : 2 * HD]
    gq[...], gk[...], gv[...], gg[...] = raw_q * scale, raw_k * scale, raw_v * scale, raw_g * scale
    go[...] = outer[:, 2 * HD :].T
    pairs = ((raw_q, wq), (raw_k, wk), (raw_v, wv), (raw_g, wg))
    term = sum(lanes(raw * w[...].astype(F32)) for raw, w in pairs)
    last = inner[block:, :HD]

    @pl.when(pl.program_id(0) == 0)
    def _():
        sums[...] = term
        ends[...] = last

    @pl.when(pl.program_id(0) > 0)
    def _():
        sums[...] += term
        ends[...] += last


def close(kernel, turn_at, blocks, weights, gain, out_rows, extra):
    quarters = 4
    place = lambda i, at: (at[0] + quarters - i) % quarters
    whole = lambda value: pl.BlockSpec(value.shape, lambda i, at: (0, 0))
    columns = lambda w: pl.BlockSpec(
        (w.shape[0], w.shape[1] // quarters), lambda i, at: (0, place(i, at))
    )
    rows, width = out_rows
    in_specs = [whole(b) for b in blocks] + [columns(w) for w in weights] + [whole(gain)]
    out_specs = [columns(w) for w in weights]
    out_specs += [pl.BlockSpec((rows // quarters, width), lambda i, at: (place(i, at), 0))]
    out_specs += [pl.BlockSpec(shape, lambda i, at: (0, 0)) for shape in extra]
    out_shape = [struct(w.shape, F32) for w in weights] + [struct(out_rows, F32)]
    out_shape += [struct(shape, F32) for shape in extra]
    return pl.pallas_call(
        kernel,
        grid_spec=pltpu.PrefetchScalarGridSpec(
            num_scalar_prefetch=1, grid=(quarters,), in_specs=in_specs, out_specs=out_specs
        ),
        out_shape=out_shape,
        compiler_params=pltpu.CompilerParams(
            dimension_semantics=("arbitrary",), vmem_limit_bytes=VMEM
        ),
        cost_estimate=pl.CostEstimate(flops=1 << 20, bytes_accessed=8 << 20, transcendentals=0),
    )(turn_at, *blocks, *weights, gain)


def make_shards(mesh):
    n_shard, n_ctx, n_tp = mesh.shape["shard"], mesh.shape["ctx"], mesh.shape["tp"]
    pairs = n_shard // 2

    def joint(pair, core, tp):
        return (pair * 2 + core) * n_tp + tp

    core_perm = [(i, i ^ 1) for i in range(n_shard)]
    planes = [
        [joint(pair, core, tp) for pair in range(pairs) for tp in range(n_tp)] for core in range(2)
    ]
    swap_perm = [
        edge
        for pair in range(pairs)
        for edge in (
            (joint(pair, 1, 0), joint(pair, 0, 1)),
            (joint(pair, 0, 1), joint(pair, 1, 0)),
        )
    ]
    across_perm = [(joint(pair, t, t), joint(pair, t, 1 - t)) for pair in range(pairs) for t in range(2)]

    def core_swap(value):
        return lax.ppermute(value, "shard", core_perm)

    def ctx_exchange(value):
        return lax.all_to_all(value, "ctx", 0, 0)

    def ctx_turn(value, by):
        return lax.ppermute(value, "ctx", [(i, (i + by) % n_ctx) for i in range(n_ctx)])

    def tree_rows(spread):
        mine = ctx_exchange(spread)
        return mine, core_swap(mine)

    def tree_half(mine, other):
        half = (mine + core_swap(other).astype(F32)).astype(BF16)
        return half.reshape((n_ctx, -1) + half.shape[1:])

    def plane_gather(value):
        return lax.all_gather(value, PLANE, axis=0, tiled=True, axis_index_groups=planes)

    def plane_scatter(value):
        return lax.psum_scatter(
            value, PLANE, scatter_dimension=0, tiled=True, axis_index_groups=planes
        )

    def plane_exchange(value):
        parts = lax.all_to_all(value, PLANE, 0, 0, axis_index_groups=planes)
        return jnp.sum(parts.astype(F32), axis=0).astype(BF16)

    def shards(
        tokens,
        seg_lengths,
        seg_parents,
        gain_in,
        w_query,
        w_key,
        w_value,
        w_gate_attn,
        w_out,
        gain_query,
        gain_key,
        gain_mid,
        w_gate,
        w_up,
        w_down,
        cotangent,
    ):
        core = lax.axis_index("shard") % 2
        tp = lax.axis_index("tp")
        ctx = lax.axis_index("ctx")
        native = core == tp
        rows = tokens.shape[0] // 2

        def swapped(value):
            return jnp.where(native, value, lax.ppermute(value, PLANE, swap_perm))

        def quarter(weight, axis):
            size = weight.shape[axis] // n_ctx
            return lax.dynamic_slice_in_dim(weight, ctx * size, size, axis)

        gain_one = gain_in.astype(F32)[:, None]
        gain_two = gain_mid.astype(F32)[:, None]
        first = jnp.concatenate(
            [quarter(w, 1) for w in (w_query, w_key, w_value, w_gate_attn)], axis=1
        )
        first = (first.astype(F32) * gain_one).astype(BF16)
        head_rows = gain_query.shape[0]
        ends = lax.dynamic_update_slice(
            jnp.zeros((gain_in.shape[0], HD), BF16),
            jnp.stack([gain_query, gain_key]),
            (0, lax.axis_index("shard") * head_rows),
        )
        first = jnp.concatenate([first, quarter(w_out, 0).T, ends], axis=1)
        w1 = plane_gather(swapped(first))

        def half_rows(place):
            pieces = [lax.dynamic_slice_in_dim(v, place * rows, rows, 0) for v in (tokens, cotangent)]
            return jnp.concatenate(pieces, axis=0)

        own = jnp.where(native, half_rows(core), core_swap(half_rows(1 - core)))
        tree = jnp.concatenate([seg_lengths, seg_parents], axis=0)
        tree = jnp.where(native, tree, core_swap(tree))
        own_x, own_cot = own[:rows], own[rows:]
        xa, xb = tree_rows(jnp.broadcast_to(own[None], (n_ctx,) + own.shape))

        second = jnp.concatenate([quarter(w_gate, 1), quarter(w_up, 1)], axis=1)
        second = (second.astype(F32) * gain_two).astype(BF16)
        second = jnp.concatenate([second, quarter(w_down, 0).T], axis=1)
        w2 = plane_gather(swapped(second))

        half_at = jnp.where(jnp.arange(2) == 0, core, 1 - core) * rows
        places = (
            half_at[:, None, None]
            + jnp.arange(n_ctx, dtype=jnp.int32)[None, :, None] * (2 * rows)
            + jnp.arange(rows, dtype=jnp.int32)[None, None, :]
        ).reshape(-1)
        segment, parent_seg, grand_seg, position = tree_layout(tree[0], tree[1], places)
        of_row = jnp.stack([segment, parent_seg, grand_seg, places], axis=1)
        of_column = jnp.stack([segment, places], axis=0)
        cosine, sine = rope_tables(position, HD)

        xn, pre, low, gate, gains = project(xa, xb, w1, cosine, sine)
        probs, attended, gated, mine, other = attend(low, gate, w1, of_row, of_column)
        middle, spread = middle_step(ctx_exchange(tree_half(mine, other)), own_x)
        ua, ub = (flat(v) for v in tree_rows(spread))

        hidden, d_gate, d_up, mine, other = feed(ua, ub, xa, xb, w2)
        half = tree_half(mine, other)
        ffn = feed_grads(ua, ub, xa, xb, d_gate, d_up, hidden, (half,))
        d_middle, spread = d_middle_step(ctx_exchange(half), middle, own_cot)
        da, db = (flat(v) for v in tree_rows(spread))
        grad_ffn = plane_scatter(ffn)

        d_attended, d_gate_pre = gate_back(da, db, w1, gate, attended)
        outer = outer_grads(xn, da, db, d_gate_pre, gated)
        grad_outer = plane_exchange(outer.reshape(n_shard, -1, 4 * HD))
        d_qkv, terms = attend_back(probs, low, d_attended, pre, gains, cosine, sine, (outer,))
        half = tree_half(*input_back(d_qkv, d_gate_pre, w1))

        def spread_terms(vector):
            return jnp.pad(vector.reshape(n_shard, 1, -1), ((0, 0), (0, 15), (0, 0)))

        wide_terms = jnp.concatenate([spread_terms(terms[0]), spread_terms(terms[1])], axis=2)
        wide_terms = jnp.pad(wide_terms, ((0, 0), (0, 0), (0, 4 * HD - 2 * head_rows)))
        inner = inner_grads(xn, d_qkv, wide_terms, (half,))
        grad_inner = plane_exchange(inner)
        parts = [lax.dynamic_index_in_dim(half, ctx, 0, False)] + [
            ctx_turn(lax.dynamic_index_in_dim(half, (ctx + by) % n_ctx, 0, False), by)
            for by in range(1, n_ctx)
        ]
        input_own = input_step(parts, d_middle, own_x)

        layer_half = tree_half(*down_product(hidden, w2, 2, (inner,)))
        layer_own = middle + lax.psum_scatter(
            flat(layer_half), "ctx", scatter_dimension=0, tiled=True
        ).astype(F32)

        def owners(block):
            block = swapped(block)
            return [block] + [ctx_turn(block, by) for by in range(1, n_ctx)]

        turn_at = ctx.astype(jnp.int32).reshape(1)
        size = gain_in.shape[0]
        grad_gate, grad_up, grad_down, mid_sums = close(
            close_feed_kernel,
            turn_at,
            owners(grad_ffn),
            (w_gate, w_up),
            gain_two,
            w_down.shape,
            [(size, HD)],
        )
        grad_query, grad_key, grad_value, grad_gate_attn, grad_out, in_sums, head_ends = close(
            close_attend_kernel,
            turn_at,
            owners(grad_inner) + owners(grad_outer),
            (w_query, w_key, w_value, w_gate_attn),
            gain_one,
            w_out.shape,
            [(size, HD), (16, HD)],
        )
        gain_terms = jnp.stack([jnp.sum(in_sums, axis=1), jnp.sum(mid_sums, axis=1), head_ends[0]])
        gain_terms = gain_terms + lax.ppermute(gain_terms, "tp", [(0, 1), (1, 0)])

        def finish(part):
            low = part.astype(BF16)
            sibling = core_swap(low)
            full = jnp.where(
                core == 0,
                jnp.concatenate([low, sibling], axis=0),
                jnp.concatenate([sibling, low], axis=0),
            )
            return jnp.where(native, full, lax.ppermute(full, PLANE, across_perm)).astype(F32)

        return (
            finish(layer_own),
            finish(input_own),
            gain_terms[0],
            grad_query,
            grad_key,
            grad_value,
            grad_gate_attn,
            grad_out,
            gain_terms[2, :head_rows],
            gain_terms[2, head_rows : 2 * head_rows],
            gain_terms[1],
            grad_gate,
            grad_up,
            grad_down,
        )

    return shards


def solution(mesh):
    return jax.shard_map(
        make_shards(mesh),
        mesh=mesh,
        in_specs=(
            P(("shard", "ctx"), None),
            P("shard", None),
            P("shard", None),
            P("shard"),
            P("shard", "tp"),
            P("shard", "tp"),
            P("shard", "tp"),
            P("shard", "tp"),
            P("tp", "shard"),
            P("shard"),
            P("shard"),
            P("shard"),
            P("shard", "tp"),
            P("shard", "tp"),
            P("tp", "shard"),
            P(("shard", "ctx"), None),
        ),
        out_specs=(
            P(("shard", "ctx"), None),
            P(("shard", "ctx"), None),
            P("shard"),
            P("shard", "tp"),
            P("shard", "tp"),
            P("shard", "tp"),
            P("shard", "tp"),
            P("tp", "shard"),
            P("shard"),
            P("shard"),
            P("shard"),
            P("shard", "tp"),
            P("shard", "tp"),
            P("tp", "shard"),
        ),
        check_vma=False,
    )
```

```python
import math

import jax
import jax.numpy as jnp
from jax import lax
from jax.experimental import pallas as pl
from jax.experimental.pallas import tpu as pltpu
from jax.sharding import PartitionSpec as P

HD = 128
EPS = 1e-06
BASE = 1000000.0
NEG = -1e30
F32 = jnp.float32
BF16 = jnp.bfloat16
PLANE = ("shard", "tp")
SCALE = 1.0 / math.sqrt(HD)
VMEM = 48 << 20


def lookup(onehot, table):
    return jnp.sum(onehot * table[None, :], axis=1)


def tree_layout(lengths, parents, places):
    labels = jnp.arange(lengths.shape[0], dtype=jnp.int32)
    ends = jnp.cumsum(lengths)
    starts = ends - lengths
    parent_hot = (parents[:, None] == labels[None, :]).astype(jnp.int32)
    grand = lookup(parent_hot, parents)
    parent_len = lookup(parent_hot, lengths)
    grand_hot = (grand[:, None] == labels[None, :]).astype(jnp.int32)
    grand_len = lookup(grand_hot, lengths)
    before = jnp.where(labels == 0, 0, parent_len + jnp.where(parents == 0, 0, grand_len))
    segment = jnp.sum((places[:, None] >= ends[None, :]).astype(jnp.int32), axis=1)
    token_hot = (segment[:, None] == labels[None, :]).astype(jnp.int32)
    position = places - lookup(token_hot, starts) + lookup(token_hot, before)
    return (segment, lookup(token_hot, parents), lookup(token_hot, grand), position)


def rope_tables(position, columns):
    halfway = columns // 2
    frequency = jnp.exp(jnp.arange(halfway, dtype=F32) * (-2.0 * math.log(BASE) / columns))
    angles = position.astype(F32)[:, None] * frequency[None, :]
    angles = jnp.concatenate([angles, angles], axis=1)
    return (jnp.cos(angles), jnp.sin(angles))


def rms_scale(inputs):
    return lax.rsqrt(jnp.mean(inputs * inputs, axis=-1, keepdims=True) + EPS)


def dot(left, right):
    return jnp.dot(left, right, preferred_element_type=F32)


def dot_rows(left, right):
    return lax.dot_general(left, right, (((0,), (0,)), ((), ())), preferred_element_type=F32)


def dot_back(left, right):
    return lax.dot_general(left, right, (((1,), (1,)), ((), ())), preferred_element_type=F32)


def turn(inputs):
    halfway = inputs.shape[-1] // 2
    return jnp.concatenate([-inputs[:, halfway:], inputs[:, :halfway]], axis=-1)


def unturn(inputs):
    halfway = inputs.shape[-1] // 2
    return jnp.concatenate([inputs[:, halfway:], -inputs[:, :halfway]], axis=-1)


def head(number):
    return slice(number * HD, (number + 1) * HD)


def call(kernel, grid, in_specs, out_specs, out_shape, flops, scratch=(), moved=8 << 20, behind=()):
    count = len(in_specs)

    def body(*refs):
        kernel(*refs[:count], *refs[count + len(behind) :])

    built = pl.pallas_call(
        body,
        grid=grid,
        in_specs=list(in_specs) + [pl.BlockSpec(memory_space=pl.ANY)] * len(behind),
        out_specs=out_specs,
        out_shape=out_shape,
        scratch_shapes=scratch,
        compiler_params=pltpu.CompilerParams(
            dimension_semantics=("arbitrary",) * len(grid), vmem_limit_bytes=VMEM
        ),
        cost_estimate=pl.CostEstimate(flops=flops, bytes_accessed=moved, transcendentals=0),
    )
    return lambda *operands: built(*operands, *behind)


def struct(shape, dtype):
    return jax.ShapeDtypeStruct(shape, dtype)


def fixed(shape):
    return pl.BlockSpec(shape, lambda i: (0,) * len(shape))


def rowed(rows, columns):
    return pl.BlockSpec((rows, columns), lambda i: (i, 0))


def piled(shape, which):
    return pl.BlockSpec((shape[0], shape[1] // 2, shape[2]), lambda i: (0, which, 0))


def flat(value):
    return value.reshape((-1,) + value.shape[2:])


def project_kernel(xa, xb, w, ends, cosine, sine, xn, pre, low, gate, gains):
    x = flat(jnp.where(pl.program_id(0) == 0, xa[...], xb[...])).astype(F32)
    normed = (x * rms_scale(x)).astype(BF16)
    xn[...] = normed
    out = dot(normed, w[...])
    found = jnp.zeros((16, HD), F32)
    for start in range(0, ends.shape[0], HD):
        found = found + ends[start : start + 16, :].astype(F32)
    gains[...] = found
    for place in range(3):
        raw = out[:, head(place)]
        pre[:, head(place)] = raw
        unit = raw * rms_scale(raw) * found[place // 2 : place // 2 + 1, :]
        low[:, head(place)] = (unit * cosine[...] + turn(unit) * sine[...]).astype(BF16)
    low[:, head(3)] = out[:, head(3)].astype(BF16)
    gate[...] = out[:, 4 * HD :]


def project(xa, xb, w, cosine, sine):
    half, width = xa.shape[0] * xa.shape[1] // 2, xa.shape[2]
    return call(
        project_kernel,
        (2,),
        [
            piled(xa.shape, 0),
            piled(xb.shape, 0),
            fixed((width, 6 * HD)),
            pl.BlockSpec((width, HD), lambda i: (0, 8)),
            rowed(half, HD),
            rowed(half, HD),
        ],
        [
            rowed(half, width),
            rowed(half, 3 * HD),
            rowed(half, 4 * HD),
            rowed(half, 2 * HD),
            fixed((16, HD)),
        ],
        [
            struct((2 * half, width), BF16),
            struct((2 * half, 3 * HD), F32),
            struct((2 * half, 4 * HD), BF16),
            struct((2 * half, 2 * HD), F32),
            struct((16, HD), F32),
        ],
        2 * 2 * half * width * 6 * HD,
    )(xa, xb, w, w, cosine, sine)


def attend_kernel(low, gate, w_out, of_row, of_column, probs, attended, gated, mine, other):
    step = pl.program_id(0)
    half = probs.shape[1]
    rows = pl.ds(step * half, half)
    key, value = low[:, head(2)], low[:, head(3)]
    seg, par, grand, place = (of_row[rows, n : n + 1] for n in range(4))
    key_seg, key_place = of_column[0:1, :], of_column[1:2, :]
    allowed = ((key_seg == seg) | (key_seg == par) | (key_seg == grand)) & (key_place <= place)
    for number in range(2):
        scores = dot_back(low[rows, head(number)], key) * SCALE
        scores = jnp.where(allowed, scores, NEG)
        raised = jnp.exp(scores - jnp.max(scores, axis=-1, keepdims=True))
        share = raised / jnp.sum(raised, axis=-1, keepdims=True)
        probs[number] = share
        seen = dot(share.astype(BF16), value)
        attended[:, head(number)] = seen
        gated[:, head(number)] = (seen * jax.nn.sigmoid(gate[:, head(number)])).astype(BF16)
    out = dot_back(gated[...], w_out[...])

    @pl.when(step == 0)
    def _():
        mine[...] = out

    @pl.when(step == 1)
    def _():
        other[...] = out.astype(BF16)


def attend(low, gate, w, of_row, of_column):
    length = low.shape[0]
    half, width = length // 2, w.shape[0]
    return call(
        attend_kernel,
        (2,),
        [
            fixed((length, 4 * HD)),
            rowed(half, 2 * HD),
            pl.BlockSpec((width, 2 * HD), lambda i: (0, 3)),
            fixed((length, 4)),
            fixed((2, length)),
        ],
        [
            pl.BlockSpec((2, half, length), lambda i: (0, i, 0)),
            rowed(half, 2 * HD),
            rowed(half, 2 * HD),
            fixed((half, width)),
            fixed((half, width)),
        ],
        [
            struct((2, length, length), F32),
            struct((length, 2 * HD), F32),
            struct((length, 2 * HD), BF16),
            struct((half, width), F32),
            struct((half, width), BF16),
        ],
        2 * length * width * 2 * HD + 8 * length * length * HD,
    )(low, gate, w, of_row, of_column)


def flip_kernel(pieces, out):
    at = 0
    for piece in pieces:
        out[:, at : at + piece.shape[0]] = piece[...].T
        at += piece.shape[0]


def flip(*pieces):
    length, width = sum(piece.shape[0] for piece in pieces), pieces[0].shape[1]
    chunk = 2 * HD
    return call(
        lambda *refs: flip_kernel(refs[:-1], refs[-1]),
        (width // chunk,),
        [pl.BlockSpec((piece.shape[0], chunk), lambda i: (0, i)) for piece in pieces],
        rowed(chunk, length),
        struct((width, length), BF16),
        1 << 20,
    )(*pieces)


def feed_kernel(ua, ub, ca, cb, wg, wu, wd, hidden, d_gate, d_up):
    half = ua.shape[0]
    for number, (u, cot) in enumerate(((ua, ca), (ub, cb))):
        rows = slice(number * half, (number + 1) * half)
        gate, up = dot(u[...], wg[...]), dot(u[...], wu[...])
        d_hidden = dot(flat(cot[...]), wd[...])
        sig = jax.nn.sigmoid(gate)
        silu = gate * sig
        hidden[rows, :] = (silu * up).astype(BF16)
        d_gate[rows, :] = (d_hidden * up * sig * (1.0 + gate * (1.0 - sig))).astype(BF16)
        d_up[rows, :] = (d_hidden * silu).astype(BF16)


def feed(ua, ub, ca, cb, w, behind):
    half, width = ua.shape
    chunk = 3 * HD
    parts = w.shape[1] // 3 // chunk
    column = lambda shift: pl.BlockSpec((width, chunk), lambda i: (0, shift * parts + i))
    unit = pl.BlockSpec((2 * half, chunk), lambda i: (0, i))
    units = parts * chunk
    return call(
        feed_kernel,
        (parts,),
        [fixed((half, width))] * 2
        + [piled(ca.shape, 1)] * 2
        + [column(0), column(1), column(2)],
        [unit, unit, unit],
        [struct((2 * half, units), BF16)] * 3,
        2 * 2 * half * width * units * 3,
        behind=behind,
    )(ua, ub, ca, cb, w, w, w)


def feed_back_kernel(d_gate, d_up, wg, wu, mine, other):
    half = mine.shape[0]
    out = dot_back(d_gate[...], wg[...]) + dot_back(d_up[...], wu[...])
    mine[...] = out[:half, :]
    other[...] = out[half:, :].astype(BF16)


def feed_back(d_gate, d_up, w):
    length, units = d_gate.shape
    half, width = length // 2, w.shape[0]
    chunk = 4 * HD
    slab = pl.BlockSpec((half, chunk), lambda i: (0, i))
    return call(
        feed_back_kernel,
        (width // chunk,),
        [fixed((length, units))] * 2
        + [
            pl.BlockSpec((chunk, units), lambda i: (i, 0)),
            pl.BlockSpec((chunk, units), lambda i: (i, 1)),
        ],
        [slab, slab],
        [struct((half, width), F32), struct((half, width), BF16)],
        2 * length * width * units * 2,
    )(d_gate, d_up, w, w)


def down_kernel(hidden, w, mine, other):
    out = dot_back(hidden[...], w[...])

    @pl.when(pl.program_id(0) == 0)
    def _():
        mine[...] = out

    @pl.when(pl.program_id(0) == 1)
    def _():
        other[...] = out.astype(BF16)


def down_product(left, w, place, behind):
    length, units = left.shape
    half, width = length // 2, w.shape[0]
    return call(
        down_kernel,
        (2,),
        [rowed(half, units), pl.BlockSpec((width, units), lambda i: (0, place))],
        [fixed((half, width)), fixed((half, width))],
        [struct((half, width), F32), struct((half, width), BF16)],
        2 * length * width * units,
        behind=behind,
    )(left, w)


def spread_blocks(left, right, out, start):
    for place in range(left.shape[1] // HD):
        term = dot_rows(left[:, head(place)], right)
        for owner in range(right.shape[1] // HD):
            at = start + place * HD
            out[owner * HD : (owner + 1) * HD, at : at + HD] = term[:, head(owner)].astype(BF16)


def feed_grads_kernel(u_flip, ca, cb, d_gate, d_up, hidden, out):
    units = hidden.shape[1]
    out[:, :units] = dot(u_flip[...], d_gate[...]).astype(BF16)
    out[:, units : 2 * units] = dot(u_flip[...], d_up[...]).astype(BF16)
    cot = jnp.concatenate([flat(ca[...]), flat(cb[...])], axis=0)
    spread_blocks(hidden, cot, out, 2 * units)


def feed_grads(u_flip, ca, cb, d_gate, d_up, hidden, behind):
    width, length = u_flip.shape
    units = hidden.shape[1]
    chunk = 4 * HD
    return call(
        feed_grads_kernel,
        (width // chunk,),
        [rowed(chunk, length)]
        + [pl.BlockSpec((ca.shape[0], ca.shape[1] // 2, chunk), lambda i: (0, 1, i))] * 2
        + [fixed((length, units))] * 3,
        rowed(chunk, 3 * units),
        struct((width, 3 * units), BF16),
        2 * length * width * units * 3,
        behind=behind,
    )(u_flip, ca, cb, d_gate, d_up, hidden)


def gate_back_kernel(da, db, w_out, gate, attended, d_attended, d_gate):
    half = da.shape[0]
    for number, low in enumerate((da, db)):
        rows = slice(number * half, (number + 1) * half)
        d_gated = dot(low[...], w_out[...])
        sig = jax.nn.sigmoid(gate[rows, :])
        d_attended[rows, :] = (d_gated * sig).astype(BF16)
        d_gate[rows, :] = (d_gated * attended[rows, :] * sig * (1.0 - sig)).astype(BF16)


def gate_back(da, db, w, gate, attended):
    half, width = da.shape
    wide = (2 * half, 2 * HD)
    return call(
        gate_back_kernel,
        (1,),
        [fixed((half, width))] * 2
        + [pl.BlockSpec((width, 2 * HD), lambda i: (0, 3)), fixed(wide), fixed(wide)],
        [fixed(wide), fixed(wide)],
        [struct(wide, BF16), struct(wide, BF16)],
        2 * 2 * half * width * 2 * HD,
    )(da, db, w, gate, attended)


def head_back(grads, inputs, gain):
    factor = rms_scale(inputs)
    scaled = gain * grads
    back = factor * scaled - inputs * factor**3 * jnp.mean(scaled * inputs, axis=-1, keepdims=True)
    return back.astype(BF16), jnp.sum(grads * inputs * factor, axis=0, keepdims=True)


def attend_back_kernel(
    probs, low, d_attended, pre, gains, cosine, sine, out, terms, d_key, d_value
):
    step = pl.program_id(0)
    half = probs.shape[1]
    start = pl.multiple_of(step * half, half)
    rows = pl.ds(start, half)
    key, value = low[:, head(2)], low[:, head(3)]
    cos_rows, sin_rows = cosine[rows, :], sine[rows, :]

    @pl.when(step == 0)
    def _():
        d_key[...] = jnp.zeros_like(d_key)
        d_value[...] = jnp.zeros_like(d_value)
        terms[...] = jnp.zeros_like(terms)

    for number in range(2):
        share = probs[number]
        d_seen = d_attended[:, head(number)]
        d_share = dot_back(d_seen, value)
        d_scores = share * (d_share - jnp.sum(share * d_share, axis=-1, keepdims=True))
        d_scores = d_scores.astype(BF16)
        d_query = dot(d_scores, key) * SCALE
        d_key[...] += dot_rows(d_scores, low[rows, head(number)])
        d_value[...] += dot_rows(share.astype(BF16), d_seen)
        grads = d_query * cos_rows + unturn(d_query * sin_rows)
        back, term = head_back(grads, pre[rows, head(number)], gains[0:1, :])
        out[rows, head(number)] = back
        terms[0:1, :] += term

    @pl.when(step == 1)
    def _():
        grads = d_key[...] * SCALE
        grads = grads * cosine[...] + unturn(grads * sine[...])
        back, term = head_back(grads, pre[:, head(2)], gains[1:2, :])
        out[:, head(2)] = back
        terms[1:2, :] = term
        out[:, head(3)] = d_value[...].astype(BF16)


def attend_back(probs, low, d_attended, pre, gains, cosine, sine, behind):
    length = low.shape[0]
    half = length // 2
    return call(
        attend_back_kernel,
        (2,),
        [
            pl.BlockSpec((2, half, length), lambda i: (0, i, 0)),
            fixed((length, 4 * HD)),
            rowed(half, 2 * HD),
            fixed((length, 3 * HD)),
            fixed((16, HD)),
            fixed((length, HD)),
            fixed((length, HD)),
        ],
        [fixed((length, 4 * HD)), fixed((8, HD))],
        [struct((length, 4 * HD), BF16), struct((8, HD), F32)],
        20 * length * length * HD,
        scratch=[pltpu.VMEM((length, HD), F32), pltpu.VMEM((length, HD), F32)],
        behind=behind,
    )(probs, low, d_attended, pre, gains, cosine, sine)


def input_back_kernel(d_qkv, d_gate, w, mine, other):
    out = dot_back(d_qkv[...], w[:, : 4 * HD]) + dot_back(d_gate[...], w[:, 4 * HD :])

    @pl.when(pl.program_id(0) == 0)
    def _():
        mine[...] = out

    @pl.when(pl.program_id(0) == 1)
    def _():
        other[...] = out.astype(BF16)


def input_back(d_qkv, d_gate, w):
    length = d_qkv.shape[0]
    half, width = length // 2, w.shape[0]
    return call(
        input_back_kernel,
        (2,),
        [rowed(half, 4 * HD), rowed(half, 2 * HD), fixed((width, 6 * HD))],
        [fixed((half, width)), fixed((half, width))],
        [struct((half, width), F32), struct((half, width), BF16)],
        2 * length * width * 6 * HD,
    )(d_qkv, d_gate, w)


def outer_grads_kernel(x_flip, da, db, d_gate, gated, out):
    split = d_gate.shape[1]
    out[:, :split] = dot(x_flip[...], d_gate[...]).astype(BF16)
    spread_blocks(gated, jnp.concatenate([da[...], db[...]], axis=0), out, split)


def outer_grads(x_flip, da, db, d_gate, gated):
    half, width = da.shape
    chunk = 4 * HD
    slab = pl.BlockSpec((half, chunk), lambda i: (0, i))
    return call(
        outer_grads_kernel,
        (width // chunk,),
        [rowed(chunk, 2 * half), slab, slab] + [fixed((2 * half, 2 * HD))] * 2,
        rowed(chunk, 4 * HD),
        struct((width, 4 * HD), BF16),
        2 * 2 * half * width * 4 * HD,
    )(x_flip, da, db, d_gate, gated)


def inner_grads_kernel(x_flip, d_qkv, terms, out):
    term = dot(x_flip[...], d_qkv[...]).astype(BF16)
    count, block = out.shape[0], out.shape[1] - terms.shape[1]
    for number in range(count):
        out[number, :block] = term[number * block : (number + 1) * block]
        out[number, block:] = terms[number].astype(BF16)


def inner_grads(x_flip, d_qkv, terms, behind):
    width, length = x_flip.shape
    columns, extra = d_qkv.shape[1], terms.shape[1]
    owners = terms.shape[0]
    block = width // owners
    return call(
        inner_grads_kernel,
        (owners // 4,),
        [
            rowed(4 * block, length),
            fixed((length, columns)),
            pl.BlockSpec((4, extra, columns), lambda i: (i, 0, 0)),
        ],
        pl.BlockSpec((4, block + extra, columns), lambda i: (i, 0, 0)),
        struct((owners, block + extra, columns), BF16),
        2 * length * width * columns,
        behind=behind,
    )(x_flip, d_qkv, terms)


def middle_kernel(parts, x, middle, spread):
    total = x[...].astype(F32) + jnp.sum(parts[...].astype(F32), axis=0)
    middle[...] = total
    low = (total * rms_scale(total)).astype(BF16)
    for number in range(spread.shape[0]):
        spread[number] = low


def middle_step(parts, x, behind):
    shape = x.shape
    return call(
        middle_kernel,
        (1,),
        [fixed(parts.shape), fixed(shape)],
        [fixed(shape), fixed(parts.shape)],
        [struct(shape, F32), struct(parts.shape, BF16)],
        1 << 20,
        behind=behind,
    )(parts, x)


def norm_back(grads, inputs):
    factor = rms_scale(inputs)
    return factor * grads - inputs * factor**3 * jnp.mean(grads * inputs, axis=-1, keepdims=True)


def d_middle_kernel(parts, middle, cot, d_middle, spread):
    grads = jnp.sum(parts[...].astype(F32), axis=0)
    total = cot[...].astype(F32) + norm_back(grads, middle[...])
    d_middle[...] = total
    for number in range(spread.shape[0]):
        spread[number] = total.astype(BF16)


def d_middle_step(parts, middle, cot):
    shape = cot.shape
    return call(
        d_middle_kernel,
        (1,),
        [fixed(parts.shape), fixed(shape), fixed(shape)],
        [fixed(shape), fixed(parts.shape)],
        [struct(shape, F32), struct(parts.shape, BF16)],
        1 << 20,
    )(parts, middle, cot)


def ends_kernel(parts, middle, d_middle, x, out):
    rows = x.shape[0]
    total = sum(part[...].astype(F32) for part in parts)
    out[:rows, :] = (middle[...] + total[:rows, :]).astype(BF16)
    back = norm_back(total[rows:, :], x[...].astype(F32))
    out[rows:, :] = (d_middle[...] + back).astype(BF16)


def ends_step(parts, middle, d_middle, x):
    shape, wide = x.shape, parts[0].shape
    count = len(parts)
    return call(
        lambda *refs: ends_kernel(refs[:count], *refs[count:]),
        (1,),
        [fixed(wide)] * count + [fixed(shape)] * 3,
        fixed(wide),
        struct(wide, BF16),
        1 << 20,
    )(*parts, middle, d_middle, x)


def sum_kernel(parts, out):
    out[...] = jnp.sum(parts[...].astype(F32), axis=0).astype(BF16)


def sum_step(parts, behind):
    return call(
        sum_kernel,
        (1,),
        [fixed(parts.shape)],
        fixed(parts.shape[1:]),
        struct(parts.shape[1:], BF16),
        1 << 20,
        behind=behind,
    )(parts)


def lanes(value):
    return sum(value[:, start : start + HD] for start in range(0, value.shape[1], HD))


def pick(blocks):
    step = pl.program_id(0)
    value = blocks[0][...]
    for number in range(1, len(blocks)):
        value = jnp.where(step == number, blocks[number][...], value)
    return value.astype(F32)


def close_feed_kernel(turn_at, b0, b1, b2, b3, w_gate, w_up, gain, g_gate, g_up, g_down, sums):
    raw = pick((b0, b1, b2, b3))
    units = w_gate.shape[1]
    raw_gate, raw_up = raw[:, :units], raw[:, units : 2 * units]
    g_gate[...] = raw_gate * gain[...]
    g_up[...] = raw_up * gain[...]
    for place in range(units // HD):
        g_down[head(place), :] = raw[:, 2 * units + place * HD : 2 * units + (place + 1) * HD]
    term = lanes(raw_gate * w_gate[...].astype(F32)) + lanes(raw_up * w_up[...].astype(F32))

    @pl.when(pl.program_id(0) == 0)
    def _():
        sums[...] = term

    @pl.when(pl.program_id(0) > 0)
    def _():
        sums[...] += term


def close_attend_kernel(
    turn_at, i0, i1, i2, i3, o0, o1, o2, o3, wq, wk, wv, wg, gain, gq, gk, gv, gg, go, sums, ends
):
    inner, outer = pick((i0, i1, i2, i3)), pick((o0, o1, o2, o3))
    block = outer.shape[0]
    scale = gain[...]
    raw_q, raw_k, raw_v = inner[:block, : 2 * HD], inner[:block, head(2)], inner[:block, head(3)]
    raw_g = outer[:, : 2 * HD]
    gq[...], gk[...], gv[...], gg[...] = raw_q * scale, raw_k * scale, raw_v * scale, raw_g * scale
    go[head(0), :], go[head(1), :] = outer[:, head(2)], outer[:, head(3)]
    pairs = ((raw_q, wq), (raw_k, wk), (raw_v, wv), (raw_g, wg))
    term = sum(lanes(raw * w[...].astype(F32)) for raw, w in pairs)
    last = inner[block:, :HD]

    @pl.when(pl.program_id(0) == 0)
    def _():
        sums[...] = term
        ends[...] = last

    @pl.when(pl.program_id(0) > 0)
    def _():
        sums[...] += term
        ends[...] += last


def close(kernel, turn_at, blocks, weights, gain, out_rows, extra):
    quarters = 4
    place = lambda i, at: (at[0] + quarters - i) % quarters
    whole = lambda value: pl.BlockSpec(value.shape, lambda i, at: (0, 0))
    columns = lambda w: pl.BlockSpec(
        (w.shape[0], w.shape[1] // quarters), lambda i, at: (0, place(i, at))
    )
    rows, width = out_rows
    in_specs = [whole(b) for b in blocks] + [columns(w) for w in weights] + [whole(gain)]
    out_specs = [columns(w) for w in weights]
    out_specs += [pl.BlockSpec((rows // quarters, width), lambda i, at: (place(i, at), 0))]
    out_specs += [pl.BlockSpec(shape, lambda i, at: (0, 0)) for shape in extra]
    out_shape = [struct(w.shape, F32) for w in weights] + [struct(out_rows, F32)]
    out_shape += [struct(shape, F32) for shape in extra]
    return pl.pallas_call(
        kernel,
        grid_spec=pltpu.PrefetchScalarGridSpec(
            num_scalar_prefetch=1, grid=(quarters,), in_specs=in_specs, out_specs=out_specs
        ),
        out_shape=out_shape,
        compiler_params=pltpu.CompilerParams(
            dimension_semantics=("arbitrary",), vmem_limit_bytes=VMEM
        ),
        cost_estimate=pl.CostEstimate(flops=1 << 20, bytes_accessed=8 << 20, transcendentals=0),
    )(turn_at, *blocks, *weights, gain)


def make_shards(mesh):
    n_shard, n_ctx, n_tp = mesh.shape["shard"], mesh.shape["ctx"], mesh.shape["tp"]
    pairs = n_shard // 2

    def joint(pair, core, tp):
        return (pair * 2 + core) * n_tp + tp

    core_perm = [(i, i ^ 1) for i in range(n_shard)]
    planes = [
        [joint(pair, core, tp) for pair in range(pairs) for tp in range(n_tp)] for core in range(2)
    ]
    swap_perm = [
        edge
        for pair in range(pairs)
        for edge in (
            (joint(pair, 1, 0), joint(pair, 0, 1)),
            (joint(pair, 0, 1), joint(pair, 1, 0)),
        )
    ]
    across_perm = [(joint(pair, t, t), joint(pair, t, 1 - t)) for pair in range(pairs) for t in range(2)]

    def spot(pair, core, ctx, tp):
        return ((pair * 2 + core) * n_ctx + ctx) * n_tp + tp

    owner_perms = [
        [
            (spot(pair, core, ctx, tp), spot(pair, tp, (ctx + by) % n_ctx, core))
            for pair in range(pairs)
            for core in range(2)
            for ctx in range(n_ctx)
            for tp in range(n_tp)
            if by > 0 or core != tp
        ]
        for by in range(n_ctx)
    ]

    def core_swap(value):
        return lax.ppermute(value, "shard", core_perm)

    def ctx_exchange(value):
        return lax.all_to_all(value, "ctx", 0, 0)

    def ctx_turn(value, by):
        return lax.ppermute(value, "ctx", [(i, (i + by) % n_ctx) for i in range(n_ctx)])

    def tree_rows(spread):
        mine = ctx_exchange(spread)
        return mine, core_swap(mine)

    def tree_half(mine, other):
        half = (mine + core_swap(other).astype(F32)).astype(BF16)
        return half.reshape((n_ctx, -1) + half.shape[1:])

    def plane_gather(value):
        return lax.all_gather(value, PLANE, axis=0, tiled=True, axis_index_groups=planes)

    def plane_scatter(value):
        return lax.psum_scatter(
            value, PLANE, scatter_dimension=0, tiled=True, axis_index_groups=planes
        )

    def plane_exchange(value):
        return lax.all_to_all(value, PLANE, 0, 0, axis_index_groups=planes)

    def shards(
        tokens,
        seg_lengths,
        seg_parents,
        gain_in,
        w_query,
        w_key,
        w_value,
        w_gate_attn,
        w_out,
        gain_query,
        gain_key,
        gain_mid,
        w_gate,
        w_up,
        w_down,
        cotangent,
    ):
        core = lax.axis_index("shard") % 2
        tp = lax.axis_index("tp")
        ctx = lax.axis_index("ctx")
        native = core == tp
        rows = tokens.shape[0] // 2

        def swapped(value):
            return jnp.where(native, value, lax.ppermute(value, PLANE, swap_perm))

        def quarter(weight, axis):
            size = weight.shape[axis] // n_ctx
            return lax.dynamic_slice_in_dim(weight, ctx * size, size, axis)

        gain_one = gain_in.astype(F32)[:, None]
        gain_two = gain_mid.astype(F32)[:, None]
        first = jnp.concatenate(
            [quarter(w, 1) for w in (w_query, w_key, w_value, w_gate_attn)], axis=1
        )
        first = (first.astype(F32) * gain_one).astype(BF16)
        head_rows = gain_query.shape[0]
        ends = lax.dynamic_update_slice(
            jnp.zeros((gain_in.shape[0], HD), BF16),
            jnp.stack([gain_query, gain_key]),
            (0, lax.axis_index("shard") * head_rows),
        )
        first = jnp.concatenate([first, quarter(w_out, 0).T, ends], axis=1)
        found = plane_gather(first)

        def half_rows(place):
            pieces = [lax.dynamic_slice_in_dim(v, place * rows, rows, 0) for v in (tokens, cotangent)]
            return jnp.concatenate(pieces, axis=0)

        own = jnp.where(native, half_rows(core), core_swap(half_rows(1 - core)))
        tree = jnp.concatenate([seg_lengths, seg_parents], axis=0)
        tree = jnp.where(native, tree, core_swap(tree))
        own_x, own_cot = own[:rows], own[rows:]
        xa, xb = tree_rows(jnp.broadcast_to(own[None], (n_ctx,) + own.shape))

        second = jnp.concatenate([quarter(w_gate, 1), quarter(w_up, 1)], axis=1)
        second = (second.astype(F32) * gain_two).astype(BF16)
        second = jnp.concatenate([second, quarter(w_down, 0).T], axis=1)
        w2 = plane_gather(swapped(second))

        half_at = jnp.where(jnp.arange(2) == 0, core, 1 - core) * rows
        places = (
            half_at[:, None, None]
            + jnp.arange(n_ctx, dtype=jnp.int32)[None, :, None] * (2 * rows)
            + jnp.arange(rows, dtype=jnp.int32)[None, None, :]
        ).reshape(-1)
        segment, parent_seg, grand_seg, position = tree_layout(tree[0], tree[1], places)
        of_row = jnp.stack([segment, parent_seg, grand_seg, places], axis=1)
        of_column = jnp.stack([segment, places], axis=0)
        cosine, sine = rope_tables(position, HD)

        found, xa, xb, of_row, of_column, cosine, sine = lax.optimization_barrier(
            (found, xa, xb, of_row, of_column, cosine, sine)
        )
        found = found.reshape(pairs, n_tp, gain_in.shape[0], -1)
        mine = lax.dynamic_index_in_dim(found, core, 1, False)
        other = core_swap(lax.dynamic_index_in_dim(found, 1 - core, 1, False))
        w1 = jnp.where(
            core == 0, jnp.stack([mine, other], axis=1), jnp.stack([other, mine], axis=1)
        ).reshape(-1, first.shape[1])

        xn, pre, low, gate, gains = project(xa, xb, w1, cosine, sine)
        probs, attended, gated, mine, other = attend(low, gate, w1, of_row, of_column)
        x_flip = flip(xn)
        middle, spread = middle_step(ctx_exchange(tree_half(mine, other)), own_x, (x_flip,))
        ua, ub = (flat(v) for v in tree_rows(spread))
        u_flip = flip(ua, ub)

        hidden, d_gate, d_up = feed(ua, ub, xa, xb, w2, (u_flip,))
        half = tree_half(*feed_back(d_gate, d_up, w2))
        ffn = feed_grads(u_flip, xa, xb, d_gate, d_up, hidden, (half,))
        d_middle, spread = d_middle_step(ctx_exchange(half), middle, own_cot)
        da, db = (flat(v) for v in tree_rows(spread))
        grad_ffn = plane_scatter(ffn)
        layer_mine, layer_other = down_product(hidden, w2, 2, (half,))

        d_attended, d_gate_pre = gate_back(da, db, w1, gate, attended)
        outer = outer_grads(x_flip, da, db, d_gate_pre, gated)
        outer_parts = plane_exchange(outer.reshape(n_shard, -1, 4 * HD))
        d_qkv, terms = attend_back(probs, low, d_attended, pre, gains, cosine, sine, (outer,))
        in_mine, in_other = input_back(d_qkv, d_gate_pre, w1)

        def spread_terms(vector):
            return jnp.pad(vector.reshape(n_shard, 1, -1), ((0, 0), (0, 15), (0, 0)))

        wide_terms = jnp.concatenate([spread_terms(terms[0]), spread_terms(terms[1])], axis=2)
        wide_terms = jnp.pad(wide_terms, ((0, 0), (0, 0), (0, 4 * HD - 2 * head_rows)))
        inner_parts = plane_exchange(inner_grads(x_flip, d_qkv, wide_terms, (in_other, outer_parts)))

        both = jnp.concatenate(
            [tree_half(layer_mine, layer_other), tree_half(in_mine, in_other)], axis=1
        )
        parts = [lax.dynamic_index_in_dim(both, ctx, 0, False)] + [
            ctx_turn(lax.dynamic_index_in_dim(both, (ctx + by) % n_ctx, 0, False), by)
            for by in range(1, n_ctx)
        ]
        ends = ends_step(parts, middle, d_middle, own_x)
        sibling = core_swap(ends)

        def whole(start):
            mine, other = ends[start : start + rows], sibling[start : start + rows]
            return jnp.where(
                core == 0,
                jnp.concatenate([mine, other], axis=0),
                jnp.concatenate([other, mine], axis=0),
            )

        full = jnp.stack([whole(0), whole(rows)])
        full = jnp.where(native, full, lax.ppermute(full, PLANE, across_perm))

        def owners(block):
            block = swapped(block)
            return [block] + [ctx_turn(block, by) for by in range(1, n_ctx)]

        def owners_at_once(block):
            moved = [lax.ppermute(block, ("shard", "ctx", "tp"), perm) for perm in owner_perms]
            return [jnp.where(native, block, moved[0])] + moved[1:]

        turn_at = ctx.astype(jnp.int32).reshape(1)
        size = gain_in.shape[0]
        outer_blocks = owners(sum_step(outer_parts, ()))
        ffn_blocks = owners(grad_ffn)
        inner_blocks = owners_at_once(
            sum_step(inner_parts, (full, *ffn_blocks[1:], *outer_blocks[1:]))
        )
        grad_gate, grad_up, grad_down, mid_sums = close(
            close_feed_kernel,
            turn_at,
            ffn_blocks,
            (w_gate, w_up),
            gain_two,
            w_down.shape,
            [(size, HD)],
        )
        grad_query, grad_key, grad_value, grad_gate_attn, grad_out, in_sums, head_ends = close(
            close_attend_kernel,
            turn_at,
            inner_blocks + outer_blocks,
            (w_query, w_key, w_value, w_gate_attn),
            gain_one,
            w_out.shape,
            [(size, HD), (16, HD)],
        )
        gain_terms = jnp.stack([jnp.sum(in_sums, axis=1), jnp.sum(mid_sums, axis=1), head_ends[0]])
        gain_terms = gain_terms + lax.ppermute(gain_terms, "tp", [(0, 1), (1, 0)])

        return (
            full[0].astype(F32),
            full[1].astype(F32),
            gain_terms[0],
            grad_query,
            grad_key,
            grad_value,
            grad_gate_attn,
            grad_out,
            gain_terms[2, :head_rows],
            gain_terms[2, head_rows : 2 * head_rows],
            gain_terms[1],
            grad_gate,
            grad_up,
            grad_down,
        )

    return shards


def solution(mesh):
    return jax.shard_map(
        make_shards(mesh),
        mesh=mesh,
        in_specs=(
            P(("shard", "ctx"), None),
            P("shard", None),
            P("shard", None),
            P("shard"),
            P("shard", "tp"),
            P("shard", "tp"),
            P("shard", "tp"),
            P("shard", "tp"),
            P("tp", "shard"),
            P("shard"),
            P("shard"),
            P("shard"),
            P("shard", "tp"),
            P("shard", "tp"),
            P("tp", "shard"),
            P(("shard", "ctx"), None),
        ),
        out_specs=(
            P(("shard", "ctx"), None),
            P(("shard", "ctx"), None),
            P("shard"),
            P("shard", "tp"),
            P("shard", "tp"),
            P("shard", "tp"),
            P("shard", "tp"),
            P("tp", "shard"),
            P("shard"),
            P("shard"),
            P("shard"),
            P("shard", "tp"),
            P("shard", "tp"),
            P("tp", "shard"),
        ),
        check_vma=False,
    )
```

```python
import math

import jax
import jax.numpy as jnp
from jax import lax
from jax.experimental import pallas as pl
from jax.experimental.pallas import tpu as pltpu
from jax.sharding import PartitionSpec as P

HD = 128
EPS = 1e-06
BASE = 1000000.0
NEG = -1e30
F32 = jnp.float32
BF16 = jnp.bfloat16
PLANE = ("shard", "tp")
SCALE = 1.0 / math.sqrt(HD)
VMEM = 48 << 20


def lookup(onehot, table):
    return jnp.sum(onehot * table[None, :], axis=1)


def tree_layout(lengths, parents, places):
    labels = jnp.arange(lengths.shape[0], dtype=jnp.int32)
    ends = jnp.cumsum(lengths)
    starts = ends - lengths
    parent_hot = (parents[:, None] == labels[None, :]).astype(jnp.int32)
    grand = lookup(parent_hot, parents)
    parent_len = lookup(parent_hot, lengths)
    grand_hot = (grand[:, None] == labels[None, :]).astype(jnp.int32)
    grand_len = lookup(grand_hot, lengths)
    before = jnp.where(labels == 0, 0, parent_len + jnp.where(parents == 0, 0, grand_len))
    segment = jnp.sum((places[:, None] >= ends[None, :]).astype(jnp.int32), axis=1)
    token_hot = (segment[:, None] == labels[None, :]).astype(jnp.int32)
    position = places - lookup(token_hot, starts) + lookup(token_hot, before)
    return (segment, lookup(token_hot, parents), lookup(token_hot, grand), position)


def rope_tables(position, columns):
    halfway = columns // 2
    frequency = jnp.exp(jnp.arange(halfway, dtype=F32) * (-2.0 * math.log(BASE) / columns))
    angles = position.astype(F32)[:, None] * frequency[None, :]
    angles = jnp.concatenate([angles, angles], axis=1)
    return (jnp.cos(angles), jnp.sin(angles))


def rms_scale(inputs):
    return lax.rsqrt(jnp.mean(inputs * inputs, axis=-1, keepdims=True) + EPS)


def dot(left, right):
    return jnp.dot(left, right, preferred_element_type=F32)


def dot_rows(left, right):
    return lax.dot_general(left, right, (((0,), (0,)), ((), ())), preferred_element_type=F32)


def dot_back(left, right):
    return lax.dot_general(left, right, (((1,), (1,)), ((), ())), preferred_element_type=F32)


def turn(inputs):
    halfway = inputs.shape[-1] // 2
    return jnp.concatenate([-inputs[:, halfway:], inputs[:, :halfway]], axis=-1)


def unturn(inputs):
    halfway = inputs.shape[-1] // 2
    return jnp.concatenate([inputs[:, halfway:], -inputs[:, :halfway]], axis=-1)


def head(number):
    return slice(number * HD, (number + 1) * HD)


def call(kernel, grid, in_specs, out_specs, out_shape, flops, scratch=(), moved=8 << 20, behind=()):
    count = len(in_specs)

    def body(*refs):
        kernel(*refs[:count], *refs[count + len(behind) :])

    built = pl.pallas_call(
        body,
        grid=grid,
        in_specs=list(in_specs) + [pl.BlockSpec(memory_space=pl.ANY)] * len(behind),
        out_specs=out_specs,
        out_shape=out_shape,
        scratch_shapes=scratch,
        compiler_params=pltpu.CompilerParams(
            dimension_semantics=("arbitrary",) * len(grid), vmem_limit_bytes=VMEM
        ),
        cost_estimate=pl.CostEstimate(flops=flops, bytes_accessed=moved, transcendentals=0),
    )
    return lambda *operands: built(*operands, *behind)


def struct(shape, dtype):
    return jax.ShapeDtypeStruct(shape, dtype)


def fixed(shape):
    return pl.BlockSpec(shape, lambda i: (0,) * len(shape))


def rowed(rows, columns):
    return pl.BlockSpec((rows, columns), lambda i: (i, 0))


def piled(shape, which):
    return pl.BlockSpec((shape[0], shape[1] // 2, shape[2]), lambda i: (0, which, 0))


def flat(value):
    return value.reshape((-1,) + value.shape[2:])


def project_kernel(xa, xb, w, ends, cosine, sine, xn, pre, low, gate, gains):
    x = flat(jnp.where(pl.program_id(0) == 0, xa[...], xb[...])).astype(F32)
    normed = (x * rms_scale(x)).astype(BF16)
    xn[...] = normed
    out = dot(normed, w[...])
    found = jnp.zeros((16, HD), F32)
    for start in range(0, ends.shape[0], HD):
        found = found + ends[start : start + 16, :].astype(F32)
    gains[...] = found
    for place in range(3):
        raw = out[:, head(place)]
        pre[:, head(place)] = raw
        unit = raw * rms_scale(raw) * found[place // 2 : place // 2 + 1, :]
        low[:, head(place)] = (unit * cosine[...] + turn(unit) * sine[...]).astype(BF16)
    low[:, head(3)] = out[:, head(3)].astype(BF16)
    gate[...] = out[:, 4 * HD :]


def project(xa, xb, w, cosine, sine):
    half, width = xa.shape[0] * xa.shape[1] // 2, xa.shape[2]
    return call(
        project_kernel,
        (2,),
        [
            piled(xa.shape, 0),
            piled(xb.shape, 0),
            fixed((width, 6 * HD)),
            pl.BlockSpec((width, HD), lambda i: (0, 8)),
            rowed(half, HD),
            rowed(half, HD),
        ],
        [
            rowed(half, width),
            rowed(half, 3 * HD),
            rowed(half, 4 * HD),
            rowed(half, 2 * HD),
            fixed((16, HD)),
        ],
        [
            struct((2 * half, width), BF16),
            struct((2 * half, 3 * HD), F32),
            struct((2 * half, 4 * HD), BF16),
            struct((2 * half, 2 * HD), F32),
            struct((16, HD), F32),
        ],
        2 * 2 * half * width * 6 * HD,
    )(xa, xb, w, w, cosine, sine)


def attend_kernel(low, gate, w_out, of_row, of_column, probs, attended, gated, mine, other):
    step = pl.program_id(0)
    half = probs.shape[1]
    rows = pl.ds(step * half, half)
    key, value = low[:, head(2)], low[:, head(3)]
    seg, par, grand, place = (of_row[rows, n : n + 1] for n in range(4))
    key_seg, key_place = of_column[0:1, :], of_column[1:2, :]
    allowed = ((key_seg == seg) | (key_seg == par) | (key_seg == grand)) & (key_place <= place)
    for number in range(2):
        scores = dot_back(low[rows, head(number)], key) * SCALE
        scores = jnp.where(allowed, scores, NEG)
        raised = jnp.exp(scores - jnp.max(scores, axis=-1, keepdims=True))
        share = raised / jnp.sum(raised, axis=-1, keepdims=True)
        probs[number] = share
        seen = dot(share.astype(BF16), value)
        attended[:, head(number)] = seen
        gated[:, head(number)] = (seen * jax.nn.sigmoid(gate[:, head(number)])).astype(BF16)
    out = dot_back(gated[...], w_out[...])

    @pl.when(step == 0)
    def _():
        mine[...] = out

    @pl.when(step == 1)
    def _():
        other[...] = out.astype(BF16)


def attend(low, gate, w, of_row, of_column):
    length = low.shape[0]
    half, width = length // 2, w.shape[0]
    return call(
        attend_kernel,
        (2,),
        [
            fixed((length, 4 * HD)),
            rowed(half, 2 * HD),
            pl.BlockSpec((width, 2 * HD), lambda i: (0, 3)),
            fixed((length, 4)),
            fixed((2, length)),
        ],
        [
            pl.BlockSpec((2, half, length), lambda i: (0, i, 0)),
            rowed(half, 2 * HD),
            rowed(half, 2 * HD),
            fixed((half, width)),
            fixed((half, width)),
        ],
        [
            struct((2, length, length), F32),
            struct((length, 2 * HD), F32),
            struct((length, 2 * HD), BF16),
            struct((half, width), F32),
            struct((half, width), BF16),
        ],
        2 * length * width * 2 * HD + 8 * length * length * HD,
    )(low, gate, w, of_row, of_column)


def flip_kernel(pieces, out):
    at = 0
    for piece in pieces:
        out[:, at : at + piece.shape[0]] = piece[...].T
        at += piece.shape[0]


def flip(*pieces):
    length, width = sum(piece.shape[0] for piece in pieces), pieces[0].shape[1]
    chunk = 2 * HD
    return call(
        lambda *refs: flip_kernel(refs[:-1], refs[-1]),
        (width // chunk,),
        [pl.BlockSpec((piece.shape[0], chunk), lambda i: (0, i)) for piece in pieces],
        rowed(chunk, length),
        struct((width, length), BF16),
        1 << 20,
    )(*pieces)


def feed_kernel(ua, ub, ca, cb, wg, wu, wd, hidden, d_gate, d_up):
    half = ua.shape[0]
    for number, (u, cot) in enumerate(((ua, ca), (ub, cb))):
        rows = slice(number * half, (number + 1) * half)
        gate, up = dot(u[...], wg[...]), dot(u[...], wu[...])
        d_hidden = dot(flat(cot[...]), wd[...])
        sig = jax.nn.sigmoid(gate)
        silu = gate * sig
        hidden[rows, :] = (silu * up).astype(BF16)
        d_gate[rows, :] = (d_hidden * up * sig * (1.0 + gate * (1.0 - sig))).astype(BF16)
        d_up[rows, :] = (d_hidden * silu).astype(BF16)


def feed(ua, ub, ca, cb, w, behind):
    half, width = ua.shape
    chunk = 3 * HD
    parts = w.shape[1] // 3 // chunk
    column = lambda shift: pl.BlockSpec((width, chunk), lambda i: (0, shift * parts + i))
    unit = pl.BlockSpec((2 * half, chunk), lambda i: (0, i))
    units = parts * chunk
    return call(
        feed_kernel,
        (parts,),
        [fixed((half, width))] * 2
        + [piled(ca.shape, 1)] * 2
        + [column(0), column(1), column(2)],
        [unit, unit, unit],
        [struct((2 * half, units), BF16)] * 3,
        2 * 2 * half * width * units * 3,
        behind=behind,
    )(ua, ub, ca, cb, w, w, w)


def feed_back_kernel(d_gate, d_up, wg, wu, mine, other):
    half = mine.shape[0]
    out = dot_back(d_gate[...], wg[...]) + dot_back(d_up[...], wu[...])
    mine[...] = out[:half, :]
    other[...] = out[half:, :].astype(BF16)


def feed_back(d_gate, d_up, w, behind):
    length, units = d_gate.shape
    half, width = length // 2, w.shape[0]
    chunk = 4 * HD
    slab = pl.BlockSpec((half, chunk), lambda i: (0, i))
    return call(
        feed_back_kernel,
        (width // chunk,),
        [fixed((length, units))] * 2
        + [
            pl.BlockSpec((chunk, units), lambda i: (i, 0)),
            pl.BlockSpec((chunk, units), lambda i: (i, 1)),
        ],
        [slab, slab],
        [struct((half, width), F32), struct((half, width), BF16)],
        2 * length * width * units * 2,
        behind=behind,
    )(d_gate, d_up, w, w)


def down_kernel(hidden, w, mine, other):
    out = dot_back(hidden[...], w[...])

    @pl.when(pl.program_id(0) == 0)
    def _():
        mine[...] = out

    @pl.when(pl.program_id(0) == 1)
    def _():
        other[...] = out.astype(BF16)


def down_product(left, w, place, behind):
    length, units = left.shape
    half, width = length // 2, w.shape[0]
    return call(
        down_kernel,
        (2,),
        [rowed(half, units), pl.BlockSpec((width, units), lambda i: (0, place))],
        [fixed((half, width)), fixed((half, width))],
        [struct((half, width), F32), struct((half, width), BF16)],
        2 * length * width * units,
        behind=behind,
    )(left, w)


def spread_blocks(left, right, out, start):
    for place in range(left.shape[1] // HD):
        term = dot_rows(left[:, head(place)], right)
        for owner in range(right.shape[1] // HD):
            at = start + place * HD
            out[owner * HD : (owner + 1) * HD, at : at + HD] = term[:, head(owner)].astype(BF16)


def feed_grads_kernel(u_flip, ca, cb, d_gate, d_up, hidden, out):
    units = hidden.shape[1]
    out[:, :units] = dot(u_flip[...], d_gate[...]).astype(BF16)
    out[:, units : 2 * units] = dot(u_flip[...], d_up[...]).astype(BF16)
    cot = jnp.concatenate([flat(ca[...]), flat(cb[...])], axis=0)
    spread_blocks(hidden, cot, out, 2 * units)


def feed_grads(u_flip, ca, cb, d_gate, d_up, hidden, behind):
    width, length = u_flip.shape
    units = hidden.shape[1]
    chunk = 4 * HD
    return call(
        feed_grads_kernel,
        (width // chunk,),
        [rowed(chunk, length)]
        + [pl.BlockSpec((ca.shape[0], ca.shape[1] // 2, chunk), lambda i: (0, 1, i))] * 2
        + [fixed((length, units))] * 3,
        rowed(chunk, 3 * units),
        struct((width, 3 * units), BF16),
        2 * length * width * units * 3,
        behind=behind,
    )(u_flip, ca, cb, d_gate, d_up, hidden)


def gate_back_kernel(da, db, w_out, gate, attended, d_attended, d_gate):
    half = da.shape[0]
    for number, low in enumerate((da, db)):
        rows = slice(number * half, (number + 1) * half)
        d_gated = dot(low[...], w_out[...])
        sig = jax.nn.sigmoid(gate[rows, :])
        d_attended[rows, :] = (d_gated * sig).astype(BF16)
        d_gate[rows, :] = (d_gated * attended[rows, :] * sig * (1.0 - sig)).astype(BF16)


def gate_back(da, db, w, gate, attended):
    half, width = da.shape
    wide = (2 * half, 2 * HD)
    return call(
        gate_back_kernel,
        (1,),
        [fixed((half, width))] * 2
        + [pl.BlockSpec((width, 2 * HD), lambda i: (0, 3)), fixed(wide), fixed(wide)],
        [fixed(wide), fixed(wide)],
        [struct(wide, BF16), struct(wide, BF16)],
        2 * 2 * half * width * 2 * HD,
    )(da, db, w, gate, attended)


def head_back(grads, inputs, gain):
    factor = rms_scale(inputs)
    scaled = gain * grads
    back = factor * scaled - inputs * factor**3 * jnp.mean(scaled * inputs, axis=-1, keepdims=True)
    return back.astype(BF16), jnp.sum(grads * inputs * factor, axis=0, keepdims=True)


def attend_back_kernel(
    probs, low, d_attended, pre, gains, cosine, sine, out, terms, d_key, d_value
):
    step = pl.program_id(0)
    half = probs.shape[1]
    start = pl.multiple_of(step * half, half)
    rows = pl.ds(start, half)
    key, value = low[:, head(2)], low[:, head(3)]
    cos_rows, sin_rows = cosine[rows, :], sine[rows, :]

    @pl.when(step == 0)
    def _():
        d_key[...] = jnp.zeros_like(d_key)
        d_value[...] = jnp.zeros_like(d_value)
        terms[...] = jnp.zeros_like(terms)

    for number in range(2):
        share = probs[number]
        d_seen = d_attended[:, head(number)]
        d_share = dot_back(d_seen, value)
        d_scores = share * (d_share - jnp.sum(share * d_share, axis=-1, keepdims=True))
        d_scores = d_scores.astype(BF16)
        d_query = dot(d_scores, key) * SCALE
        d_key[...] += dot_rows(d_scores, low[rows, head(number)])
        d_value[...] += dot_rows(share.astype(BF16), d_seen)
        grads = d_query * cos_rows + unturn(d_query * sin_rows)
        back, term = head_back(grads, pre[rows, head(number)], gains[0:1, :])
        out[rows, head(number)] = back
        terms[0:1, :] += term

    @pl.when(step == 1)
    def _():
        grads = d_key[...] * SCALE
        grads = grads * cosine[...] + unturn(grads * sine[...])
        back, term = head_back(grads, pre[:, head(2)], gains[1:2, :])
        out[:, head(2)] = back
        terms[1:2, :] = term
        out[:, head(3)] = d_value[...].astype(BF16)


def attend_back(probs, low, d_attended, pre, gains, cosine, sine, behind):
    length = low.shape[0]
    half = length // 2
    return call(
        attend_back_kernel,
        (2,),
        [
            pl.BlockSpec((2, half, length), lambda i: (0, i, 0)),
            fixed((length, 4 * HD)),
            rowed(half, 2 * HD),
            fixed((length, 3 * HD)),
            fixed((16, HD)),
            fixed((length, HD)),
            fixed((length, HD)),
        ],
        [fixed((length, 4 * HD)), fixed((8, HD))],
        [struct((length, 4 * HD), BF16), struct((8, HD), F32)],
        20 * length * length * HD,
        scratch=[pltpu.VMEM((length, HD), F32), pltpu.VMEM((length, HD), F32)],
        behind=behind,
    )(probs, low, d_attended, pre, gains, cosine, sine)


def input_back_kernel(d_qkv, d_gate, w, mine, other):
    out = dot_back(d_qkv[...], w[:, : 4 * HD]) + dot_back(d_gate[...], w[:, 4 * HD :])

    @pl.when(pl.program_id(0) == 0)
    def _():
        mine[...] = out

    @pl.when(pl.program_id(0) == 1)
    def _():
        other[...] = out.astype(BF16)


def input_back(d_qkv, d_gate, w, behind):
    length = d_qkv.shape[0]
    half, width = length // 2, w.shape[0]
    return call(
        input_back_kernel,
        (2,),
        [rowed(half, 4 * HD), rowed(half, 2 * HD), fixed((width, 6 * HD))],
        [fixed((half, width)), fixed((half, width))],
        [struct((half, width), F32), struct((half, width), BF16)],
        2 * length * width * 6 * HD,
        behind=behind,
    )(d_qkv, d_gate, w)


def attend_grads_kernel(x_flip, da, db, d_qkv, d_gate, gated, terms, out, outer):
    inner, split = d_qkv.shape[1], d_gate.shape[1]
    block = out.shape[1] - terms.shape[1]
    for number in range(out.shape[0]):
        out[number, block:, :] = terms[number].astype(BF16)
    term = dot(x_flip[...], d_qkv[...]).astype(BF16)
    gates = dot(x_flip[...], d_gate[...]).astype(BF16)
    spread_blocks(gated, jnp.concatenate([da[...], db[...]], axis=0), outer, 0)
    for number in range(out.shape[0]):
        rows = slice(number * block, (number + 1) * block)
        out[number, :block, :inner] = term[rows]
        out[number, :block, inner : inner + split] = gates[rows]
        out[number, :block, inner + split :] = outer[rows, :]


def attend_grads(x_flip, da, db, d_qkv, d_gate, gated, terms, behind):
    width, length = x_flip.shape
    owners, extra, columns = terms.shape
    block = width // owners
    many = 4
    slab = pl.BlockSpec((length // 2, many * block), lambda i: (0, i))
    return call(
        attend_grads_kernel,
        (owners // many,),
        [
            rowed(many * block, length),
            slab,
            slab,
            fixed(d_qkv.shape),
            fixed(d_gate.shape),
            fixed(gated.shape),
            pl.BlockSpec((many, extra, columns), lambda i: (i, 0, 0)),
        ],
        pl.BlockSpec((many, block + extra, columns), lambda i: (i, 0, 0)),
        struct((owners, block + extra, columns), BF16),
        2 * length * width * columns,
        scratch=[pltpu.VMEM((many * block, gated.shape[1]), BF16)],
        behind=behind,
    )(x_flip, da, db, d_qkv, d_gate, gated, terms)


def middle_kernel(parts, x, middle, spread):
    total = x[...].astype(F32) + jnp.sum(parts[...].astype(F32), axis=0)
    middle[...] = total
    low = (total * rms_scale(total)).astype(BF16)
    for number in range(spread.shape[0]):
        spread[number] = low


def middle_step(parts, x, behind):
    shape = x.shape
    return call(
        middle_kernel,
        (1,),
        [fixed(parts.shape), fixed(shape)],
        [fixed(shape), fixed(parts.shape)],
        [struct(shape, F32), struct(parts.shape, BF16)],
        1 << 20,
        behind=behind,
    )(parts, x)


def norm_back(grads, inputs):
    factor = rms_scale(inputs)
    return factor * grads - inputs * factor**3 * jnp.mean(grads * inputs, axis=-1, keepdims=True)


def d_middle_kernel(parts, middle, cot, d_middle, spread):
    grads = jnp.sum(parts[...].astype(F32), axis=0)
    total = cot[...].astype(F32) + norm_back(grads, middle[...])
    d_middle[...] = total
    for number in range(spread.shape[0]):
        spread[number] = total.astype(BF16)


def d_middle_step(parts, middle, cot):
    shape = cot.shape
    return call(
        d_middle_kernel,
        (1,),
        [fixed(parts.shape), fixed(shape), fixed(shape)],
        [fixed(shape), fixed(parts.shape)],
        [struct(shape, F32), struct(parts.shape, BF16)],
        1 << 20,
    )(parts, middle, cot)


def ends_kernel(parts, middle, d_middle, x, out):
    rows = x.shape[0]
    total = sum(part[...].astype(F32) for part in parts)
    out[:rows, :] = (middle[...] + total[:rows, :]).astype(BF16)
    back = norm_back(total[rows:, :], x[...].astype(F32))
    out[rows:, :] = (d_middle[...] + back).astype(BF16)


def ends_step(parts, middle, d_middle, x):
    shape, wide = x.shape, parts[0].shape
    count = len(parts)
    return call(
        lambda *refs: ends_kernel(refs[:count], *refs[count:]),
        (1,),
        [fixed(wide)] * count + [fixed(shape)] * 3,
        fixed(wide),
        struct(wide, BF16),
        1 << 20,
    )(*parts, middle, d_middle, x)


def sum_kernel(parts, out):
    out[...] = jnp.sum(parts[...].astype(F32), axis=0).astype(BF16)


def sum_step(parts, behind):
    return call(
        sum_kernel,
        (1,),
        [fixed(parts.shape)],
        fixed(parts.shape[1:]),
        struct(parts.shape[1:], BF16),
        1 << 20,
        behind=behind,
    )(parts)


def prefetched(kernel, grid, in_specs, out_specs, out_shape):
    return pl.pallas_call(
        kernel,
        grid_spec=pltpu.PrefetchScalarGridSpec(
            num_scalar_prefetch=1, grid=grid, in_specs=in_specs, out_specs=out_specs
        ),
        out_shape=out_shape,
        compiler_params=pltpu.CompilerParams(
            dimension_semantics=("arbitrary",) * len(grid), vmem_limit_bytes=VMEM
        ),
        cost_estimate=pl.CostEstimate(flops=1 << 20, bytes_accessed=8 << 20, transcendentals=0),
    )


def copy_kernel(core, source, out):
    out[...] = source[...]


def sibling_part(core, found):
    pairs, _, rows, columns = found.shape
    return prefetched(
        copy_kernel,
        (pairs // 2,),
        [pl.BlockSpec((2, None, rows, columns), lambda i, at: (i, 1 - at[0], 0, 0))],
        pl.BlockSpec((2, rows, columns), lambda i, at: (i, 0, 0)),
        struct((pairs, rows, columns), found.dtype),
    )(core, found)


def join_kernel(core, mine, other, out):
    out[:, core[0]] = mine[...]
    out[:, 1 - core[0]] = other[...]


def join_cores(core, found, other):
    pairs, _, rows, columns = found.shape
    return prefetched(
        join_kernel,
        (pairs // 2,),
        [
            pl.BlockSpec((2, None, rows, columns), lambda i, at: (i, at[0], 0, 0)),
            pl.BlockSpec((2, rows, columns), lambda i, at: (i, 0, 0)),
        ],
        pl.BlockSpec((2, 2, rows, columns), lambda i, at: (i, 0, 0, 0)),
        struct(found.shape, found.dtype),
    )(core, found, other)


def lanes(value):
    return sum(value[:, start : start + HD] for start in range(0, value.shape[1], HD))


def pick(blocks):
    step = pl.program_id(0)
    value = blocks[0][...]
    for number in range(1, len(blocks)):
        value = jnp.where(step == number, blocks[number][...], value)
    return value.astype(F32)


def close_feed_kernel(turn_at, b0, b1, b2, b3, w_gate, w_up, gain, g_gate, g_up, g_down, sums):
    raw = pick((b0, b1, b2, b3))
    units = w_gate.shape[1]
    raw_gate, raw_up = raw[:, :units], raw[:, units : 2 * units]
    g_gate[...] = raw_gate * gain[...]
    g_up[...] = raw_up * gain[...]
    for place in range(units // HD):
        g_down[head(place), :] = raw[:, 2 * units + place * HD : 2 * units + (place + 1) * HD]
    term = lanes(raw_gate * w_gate[...].astype(F32)) + lanes(raw_up * w_up[...].astype(F32))

    @pl.when(pl.program_id(0) == 0)
    def _():
        sums[...] = term

    @pl.when(pl.program_id(0) > 0)
    def _():
        sums[...] += term


def close_attend_kernel(
    turn_at, b0, b1, b2, b3, wq, wk, wv, wg, gain, gq, gk, gv, gg, go, sums, ends
):
    found = pick((b0, b1, b2, b3))
    inner, scale = found[:, : 4 * HD], gain[...]
    block = scale.shape[0]
    outer = found[:block, 4 * HD :]
    raw_q, raw_k, raw_v = inner[:block, : 2 * HD], inner[:block, head(2)], inner[:block, head(3)]
    raw_g = outer[:, : 2 * HD]
    gq[...], gk[...], gv[...], gg[...] = raw_q * scale, raw_k * scale, raw_v * scale, raw_g * scale
    go[head(0), :], go[head(1), :] = outer[:, head(2)], outer[:, head(3)]
    pairs = ((raw_q, wq), (raw_k, wk), (raw_v, wv), (raw_g, wg))
    term = sum(lanes(raw * w[...].astype(F32)) for raw, w in pairs)
    last = inner[block:, :HD]

    @pl.when(pl.program_id(0) == 0)
    def _():
        sums[...] = term
        ends[...] = last

    @pl.when(pl.program_id(0) > 0)
    def _():
        sums[...] += term
        ends[...] += last


def close(kernel, turn_at, blocks, weights, gain, out_rows, extra):
    quarters = 4
    place = lambda i, at: (at[0] + quarters - i) % quarters
    whole = lambda value: pl.BlockSpec(value.shape, lambda i, at: (0, 0))
    columns = lambda w: pl.BlockSpec(
        (w.shape[0], w.shape[1] // quarters), lambda i, at: (0, place(i, at))
    )
    rows, width = out_rows
    in_specs = [whole(b) for b in blocks] + [columns(w) for w in weights] + [whole(gain)]
    out_specs = [columns(w) for w in weights]
    out_specs += [pl.BlockSpec((rows // quarters, width), lambda i, at: (place(i, at), 0))]
    out_specs += [pl.BlockSpec(shape, lambda i, at: (0, 0)) for shape in extra]
    out_shape = [struct(w.shape, F32) for w in weights] + [struct(out_rows, F32)]
    out_shape += [struct(shape, F32) for shape in extra]
    return prefetched(kernel, (quarters,), in_specs, out_specs, out_shape)(
        turn_at, *blocks, *weights, gain
    )


def make_shards(mesh):
    n_shard, n_ctx, n_tp = mesh.shape["shard"], mesh.shape["ctx"], mesh.shape["tp"]
    pairs = n_shard // 2

    def joint(pair, core, tp):
        return (pair * 2 + core) * n_tp + tp

    core_perm = [(i, i ^ 1) for i in range(n_shard)]
    planes = [
        [joint(pair, core, tp) for pair in range(pairs) for tp in range(n_tp)] for core in range(2)
    ]
    swap_perm = [
        edge
        for pair in range(pairs)
        for edge in (
            (joint(pair, 1, 0), joint(pair, 0, 1)),
            (joint(pair, 0, 1), joint(pair, 1, 0)),
        )
    ]
    across_perm = [(joint(pair, t, t), joint(pair, t, 1 - t)) for pair in range(pairs) for t in range(2)]

    def spot(pair, core, ctx, tp):
        return ((pair * 2 + core) * n_ctx + ctx) * n_tp + tp

    owner_perms = [
        [
            (spot(pair, core, ctx, tp), spot(pair, tp, (ctx + by) % n_ctx, core))
            for pair in range(pairs)
            for core in range(2)
            for ctx in range(n_ctx)
            for tp in range(n_tp)
            if by > 0 or core != tp
        ]
        for by in range(n_ctx)
    ]

    def core_swap(value):
        return lax.ppermute(value, "shard", core_perm)

    def ctx_exchange(value):
        return lax.all_to_all(value, "ctx", 0, 0)

    def ctx_turn(value, by):
        return lax.ppermute(value, "ctx", [(i, (i + by) % n_ctx) for i in range(n_ctx)])

    def tree_rows(spread):
        mine = ctx_exchange(spread)
        return mine, core_swap(mine)

    def tree_half(mine, other):
        half = (mine + core_swap(other).astype(F32)).astype(BF16)
        return half.reshape((n_ctx, -1) + half.shape[1:])

    def plane_gather(value):
        return lax.all_gather(value, PLANE, axis=0, tiled=True, axis_index_groups=planes)

    def plane_scatter(value):
        return lax.psum_scatter(
            value, PLANE, scatter_dimension=0, tiled=True, axis_index_groups=planes
        )

    def plane_exchange(value):
        return lax.all_to_all(value, PLANE, 0, 0, axis_index_groups=planes)

    def shards(
        tokens,
        seg_lengths,
        seg_parents,
        gain_in,
        w_query,
        w_key,
        w_value,
        w_gate_attn,
        w_out,
        gain_query,
        gain_key,
        gain_mid,
        w_gate,
        w_up,
        w_down,
        cotangent,
    ):
        core = lax.axis_index("shard") % 2
        tp = lax.axis_index("tp")
        ctx = lax.axis_index("ctx")
        native = core == tp
        rows = tokens.shape[0] // 2

        def swapped(value):
            return jnp.where(native, value, lax.ppermute(value, PLANE, swap_perm))

        def quarter(weight, axis):
            size = weight.shape[axis] // n_ctx
            return lax.dynamic_slice_in_dim(weight, ctx * size, size, axis)

        gain_one = gain_in.astype(F32)[:, None]
        gain_two = gain_mid.astype(F32)[:, None]
        first = jnp.concatenate(
            [quarter(w, 1) for w in (w_query, w_key, w_value, w_gate_attn)], axis=1
        )
        first = (first.astype(F32) * gain_one).astype(BF16)
        head_rows = gain_query.shape[0]
        ends = lax.dynamic_update_slice(
            jnp.zeros((gain_in.shape[0], HD), BF16),
            jnp.stack([gain_query, gain_key]),
            (0, lax.axis_index("shard") * head_rows),
        )
        first = jnp.concatenate([first, quarter(w_out, 0).T, ends], axis=1)
        found = plane_gather(first)

        def half_rows(place):
            pieces = [lax.dynamic_slice_in_dim(v, place * rows, rows, 0) for v in (tokens, cotangent)]
            return jnp.concatenate(pieces, axis=0)

        own = jnp.where(native, half_rows(core), core_swap(half_rows(1 - core)))
        tree = jnp.concatenate([seg_lengths, seg_parents], axis=0)
        tree = jnp.where(native, tree, core_swap(tree))
        own_x, own_cot = own[:rows], own[rows:]
        xa, xb = tree_rows(jnp.broadcast_to(own[None], (n_ctx,) + own.shape))

        second = jnp.concatenate([quarter(w_gate, 1), quarter(w_up, 1)], axis=1)
        second = (second.astype(F32) * gain_two).astype(BF16)
        second = jnp.concatenate([second, quarter(w_down, 0).T], axis=1)
        w2 = plane_gather(swapped(second))

        half_at = jnp.where(jnp.arange(2) == 0, core, 1 - core) * rows
        places = (
            half_at[:, None, None]
            + jnp.arange(n_ctx, dtype=jnp.int32)[None, :, None] * (2 * rows)
            + jnp.arange(rows, dtype=jnp.int32)[None, None, :]
        ).reshape(-1)
        segment, parent_seg, grand_seg, position = tree_layout(tree[0], tree[1], places)
        of_row = jnp.stack([segment, parent_seg, grand_seg, places], axis=1)
        of_column = jnp.stack([segment, places], axis=0)
        cosine, sine = rope_tables(position, HD)

        found, xa, xb, of_row, of_column, cosine, sine = lax.optimization_barrier(
            (found, xa, xb, of_row, of_column, cosine, sine)
        )
        found = found.reshape(pairs, n_tp, gain_in.shape[0], -1)
        core_at = core.astype(jnp.int32).reshape(1)
        other = core_swap(sibling_part(core_at, found))
        w1 = join_cores(core_at, found, other).reshape(-1, first.shape[1])

        xn, pre, low, gate, gains = project(xa, xb, w1, cosine, sine)
        probs, attended, gated, mine, other = attend(low, gate, w1, of_row, of_column)
        x_flip = flip(xn)
        middle, spread = middle_step(ctx_exchange(tree_half(mine, other)), own_x, (x_flip,))
        ua, ub = (flat(v) for v in tree_rows(spread))
        u_flip = flip(ua, ub)

        hidden, d_gate, d_up = feed(ua, ub, xa, xb, w2, (u_flip,))
        ffn = feed_grads(u_flip, xa, xb, d_gate, d_up, hidden, ())
        half = tree_half(*feed_back(d_gate, d_up, w2, (ffn,)))
        d_middle, spread = d_middle_step(ctx_exchange(half), middle, own_cot)
        da, db = (flat(v) for v in tree_rows(spread))
        grad_ffn = plane_scatter(ffn)
        layer_mine, layer_other = down_product(hidden, w2, 2, (half,))

        d_attended, d_gate_pre = gate_back(da, db, w1, gate, attended)
        d_qkv, terms = attend_back(probs, low, d_attended, pre, gains, cosine, sine, ())

        def spread_terms(vector):
            return jnp.pad(vector.reshape(n_shard, 1, -1), ((0, 0), (0, 15), (0, 0)))

        wide_terms = jnp.concatenate([spread_terms(terms[0]), spread_terms(terms[1])], axis=2)
        wide_terms = jnp.pad(wide_terms, ((0, 0), (0, 0), (0, 8 * HD - 2 * head_rows)))
        attn = attend_grads(x_flip, da, db, d_qkv, d_gate_pre, gated, wide_terms, ())
        attn_parts = plane_exchange(attn)
        in_mine, in_other = input_back(d_qkv, d_gate_pre, w1, (attn,))

        both = jnp.concatenate(
            [tree_half(layer_mine, layer_other), tree_half(in_mine, in_other)], axis=1
        )
        parts = [lax.dynamic_index_in_dim(both, ctx, 0, False)] + [
            ctx_turn(lax.dynamic_index_in_dim(both, (ctx + by) % n_ctx, 0, False), by)
            for by in range(1, n_ctx)
        ]
        ends = ends_step(parts, middle, d_middle, own_x)
        sibling = core_swap(ends)

        def whole(start):
            mine, other = ends[start : start + rows], sibling[start : start + rows]
            return jnp.where(
                core == 0,
                jnp.concatenate([mine, other], axis=0),
                jnp.concatenate([other, mine], axis=0),
            )

        full = jnp.stack([whole(0), whole(rows)])
        full = jnp.where(native, full, lax.ppermute(full, PLANE, across_perm))

        def owners(block):
            block = swapped(block)
            return [block] + [ctx_turn(block, by) for by in range(1, n_ctx)]

        def owners_at_once(block):
            moved = [lax.ppermute(block, ("shard", "ctx", "tp"), perm) for perm in owner_perms]
            return [jnp.where(native, block, moved[0])] + moved[1:]

        turn_at = ctx.astype(jnp.int32).reshape(1)
        size = gain_in.shape[0]
        ffn_blocks = owners(grad_ffn)
        grad_gate, grad_up, grad_down, mid_sums = close(
            close_feed_kernel,
            turn_at,
            ffn_blocks,
            (w_gate, w_up),
            gain_two,
            w_down.shape,
            [(size, HD)],
        )
        attn_blocks = owners_at_once(sum_step(attn_parts, (full, mid_sums)))
        grad_query, grad_key, grad_value, grad_gate_attn, grad_out, in_sums, head_ends = close(
            close_attend_kernel,
            turn_at,
            attn_blocks,
            (w_query, w_key, w_value, w_gate_attn),
            gain_one,
            w_out.shape,
            [(size, HD), (16, HD)],
        )
        gain_terms = jnp.stack([jnp.sum(in_sums, axis=1), jnp.sum(mid_sums, axis=1), head_ends[0]])
        gain_terms = gain_terms + lax.ppermute(gain_terms, "tp", [(0, 1), (1, 0)])

        return (
            full[0].astype(F32),
            full[1].astype(F32),
            gain_terms[0],
            grad_query,
            grad_key,
            grad_value,
            grad_gate_attn,
            grad_out,
            gain_terms[2, :head_rows],
            gain_terms[2, head_rows : 2 * head_rows],
            gain_terms[1],
            grad_gate,
            grad_up,
            grad_down,
        )

    return shards


def solution(mesh):
    return jax.shard_map(
        make_shards(mesh),
        mesh=mesh,
        in_specs=(
            P(("shard", "ctx"), None),
            P("shard", None),
            P("shard", None),
            P("shard"),
            P("shard", "tp"),
            P("shard", "tp"),
            P("shard", "tp"),
            P("shard", "tp"),
            P("tp", "shard"),
            P("shard"),
            P("shard"),
            P("shard"),
            P("shard", "tp"),
            P("shard", "tp"),
            P("tp", "shard"),
            P(("shard", "ctx"), None),
        ),
        out_specs=(
            P(("shard", "ctx"), None),
            P(("shard", "ctx"), None),
            P("shard"),
            P("shard", "tp"),
            P("shard", "tp"),
            P("shard", "tp"),
            P("shard", "tp"),
            P("tp", "shard"),
            P("shard"),
            P("shard"),
            P("shard"),
            P("shard", "tp"),
            P("shard", "tp"),
            P("tp", "shard"),
        ),
        check_vma=False,
    )
```

```python
import math

import jax
import jax.numpy as jnp
from jax import lax
from jax.experimental import pallas as pl
from jax.experimental.pallas import tpu as pltpu
from jax.sharding import PartitionSpec as P

HD = 128
EPS = 1e-06
BASE = 1000000.0
NEG = -1e30
F32 = jnp.float32
BF16 = jnp.bfloat16
PLANE = ("shard", "tp")
SCALE = 1.0 / math.sqrt(HD)
VMEM = 48 << 20


def lookup(onehot, table):
    return jnp.sum(onehot * table[None, :], axis=1)


def tree_layout(lengths, parents, places):
    labels = jnp.arange(lengths.shape[0], dtype=jnp.int32)
    ends = jnp.cumsum(lengths)
    starts = ends - lengths
    parent_hot = (parents[:, None] == labels[None, :]).astype(jnp.int32)
    grand = lookup(parent_hot, parents)
    parent_len = lookup(parent_hot, lengths)
    grand_hot = (grand[:, None] == labels[None, :]).astype(jnp.int32)
    grand_len = lookup(grand_hot, lengths)
    before = jnp.where(labels == 0, 0, parent_len + jnp.where(parents == 0, 0, grand_len))
    segment = jnp.sum((places[:, None] >= ends[None, :]).astype(jnp.int32), axis=1)
    token_hot = (segment[:, None] == labels[None, :]).astype(jnp.int32)
    position = places - lookup(token_hot, starts) + lookup(token_hot, before)
    return (segment, lookup(token_hot, parents), lookup(token_hot, grand), position)


def rope_tables(position, columns):
    halfway = columns // 2
    frequency = jnp.exp(jnp.arange(halfway, dtype=F32) * (-2.0 * math.log(BASE) / columns))
    angles = position.astype(F32)[:, None] * frequency[None, :]
    angles = jnp.concatenate([angles, angles], axis=1)
    return (jnp.cos(angles), jnp.sin(angles))


def rms_scale(inputs):
    return lax.rsqrt(jnp.mean(inputs * inputs, axis=-1, keepdims=True) + EPS)


def dot(left, right):
    return jnp.dot(left, right, preferred_element_type=F32)


def dot_rows(left, right):
    return lax.dot_general(left, right, (((0,), (0,)), ((), ())), preferred_element_type=F32)


def dot_back(left, right):
    return lax.dot_general(left, right, (((1,), (1,)), ((), ())), preferred_element_type=F32)


def turn(inputs):
    halfway = inputs.shape[-1] // 2
    return jnp.concatenate([-inputs[:, halfway:], inputs[:, :halfway]], axis=-1)


def unturn(inputs):
    halfway = inputs.shape[-1] // 2
    return jnp.concatenate([inputs[:, halfway:], -inputs[:, :halfway]], axis=-1)


def head(number):
    return slice(number * HD, (number + 1) * HD)


def call(kernel, grid, in_specs, out_specs, out_shape, flops, scratch=(), moved=8 << 20, behind=()):
    count = len(in_specs)

    def body(*refs):
        kernel(*refs[:count], *refs[count + len(behind) :])

    built = pl.pallas_call(
        body,
        grid=grid,
        in_specs=list(in_specs) + [pl.BlockSpec(memory_space=pl.ANY)] * len(behind),
        out_specs=out_specs,
        out_shape=out_shape,
        scratch_shapes=scratch,
        compiler_params=pltpu.CompilerParams(
            dimension_semantics=("arbitrary",) * len(grid), vmem_limit_bytes=VMEM
        ),
        cost_estimate=pl.CostEstimate(flops=flops, bytes_accessed=moved, transcendentals=0),
    )
    return lambda *operands: built(*operands, *behind)


def struct(shape, dtype):
    return jax.ShapeDtypeStruct(shape, dtype)


def fixed(shape):
    return pl.BlockSpec(shape, lambda i: (0,) * len(shape))


def rowed(rows, columns):
    return pl.BlockSpec((rows, columns), lambda i: (i, 0))


def piled(shape, which):
    return pl.BlockSpec((shape[0], shape[1] // 2, shape[2]), lambda i: (0, which, 0))


def flat(value):
    return value.reshape((-1,) + value.shape[2:])


def project_kernel(xa, xb, w, ends, cosine, sine, xn, pre, low, gate, gains):
    x = flat(jnp.where(pl.program_id(0) == 0, xa[...], xb[...])).astype(F32)
    normed = (x * rms_scale(x)).astype(BF16)
    xn[...] = normed
    out = dot(normed, w[...])
    found = jnp.zeros((16, HD), F32)
    for start in range(0, ends.shape[0], HD):
        found = found + ends[start : start + 16, :].astype(F32)
    gains[...] = found
    for place in range(3):
        raw = out[:, head(place)]
        pre[:, head(place)] = raw
        unit = raw * rms_scale(raw) * found[place // 2 : place // 2 + 1, :]
        low[:, head(place)] = (unit * cosine[...] + turn(unit) * sine[...]).astype(BF16)
    low[:, head(3)] = out[:, head(3)].astype(BF16)
    gate[...] = out[:, 4 * HD :]


def project(xa, xb, w, cosine, sine):
    half, width = xa.shape[0] * xa.shape[1] // 2, xa.shape[2]
    return call(
        project_kernel,
        (2,),
        [
            piled(xa.shape, 0),
            piled(xb.shape, 0),
            fixed((width, 6 * HD)),
            pl.BlockSpec((width, HD), lambda i: (0, 8)),
            rowed(half, HD),
            rowed(half, HD),
        ],
        [
            rowed(half, width),
            rowed(half, 3 * HD),
            rowed(half, 4 * HD),
            rowed(half, 2 * HD),
            fixed((16, HD)),
        ],
        [
            struct((2 * half, width), BF16),
            struct((2 * half, 3 * HD), F32),
            struct((2 * half, 4 * HD), BF16),
            struct((2 * half, 2 * HD), F32),
            struct((16, HD), F32),
        ],
        2 * 2 * half * width * 6 * HD,
    )(xa, xb, w, w, cosine, sine)


def attend_kernel(low, gate, w_out, of_row, of_column, probs, attended, gated, mine, other):
    step = pl.program_id(0)
    half = probs.shape[1]
    rows = pl.ds(step * half, half)
    key, value = low[:, head(2)], low[:, head(3)]
    seg, par, grand, place = (of_row[rows, n : n + 1] for n in range(4))
    key_seg, key_place = of_column[0:1, :], of_column[1:2, :]
    allowed = ((key_seg == seg) | (key_seg == par) | (key_seg == grand)) & (key_place <= place)
    for number in range(2):
        scores = dot_back(low[rows, head(number)], key) * SCALE
        scores = jnp.where(allowed, scores, NEG)
        raised = jnp.exp(scores - jnp.max(scores, axis=-1, keepdims=True))
        share = raised / jnp.sum(raised, axis=-1, keepdims=True)
        probs[number] = share
        seen = dot(share.astype(BF16), value)
        attended[:, head(number)] = seen
        gated[:, head(number)] = (seen * jax.nn.sigmoid(gate[:, head(number)])).astype(BF16)
    out = dot_back(gated[...], w_out[...])

    @pl.when(step == 0)
    def _():
        mine[...] = out.astype(BF16)

    @pl.when(step == 1)
    def _():
        other[...] = out.astype(BF16)


def attend(low, gate, w, of_row, of_column):
    length = low.shape[0]
    half, width = length // 2, w.shape[0]
    return call(
        attend_kernel,
        (2,),
        [
            fixed((length, 4 * HD)),
            rowed(half, 2 * HD),
            pl.BlockSpec((width, 2 * HD), lambda i: (0, 3)),
            fixed((length, 4)),
            fixed((2, length)),
        ],
        [
            pl.BlockSpec((2, half, length), lambda i: (0, i, 0)),
            rowed(half, 2 * HD),
            rowed(half, 2 * HD),
            fixed((half, width)),
            fixed((half, width)),
        ],
        [
            struct((2, length, length), F32),
            struct((length, 2 * HD), F32),
            struct((length, 2 * HD), BF16),
            struct((half, width), BF16),
            struct((half, width), BF16),
        ],
        2 * length * width * 2 * HD + 8 * length * length * HD,
    )(low, gate, w, of_row, of_column)


def flip_kernel(pieces, out):
    at = 0
    for piece in pieces:
        out[:, at : at + piece.shape[0]] = piece[...].T
        at += piece.shape[0]


def flip(*pieces):
    length, width = sum(piece.shape[0] for piece in pieces), pieces[0].shape[1]
    chunk = 2 * HD
    return call(
        lambda *refs: flip_kernel(refs[:-1], refs[-1]),
        (width // chunk,),
        [pl.BlockSpec((piece.shape[0], chunk), lambda i: (0, i)) for piece in pieces],
        rowed(chunk, length),
        struct((width, length), BF16),
        1 << 20,
    )(*pieces)


def feed_kernel(ua, ub, ca, cb, wg, wu, wd, hidden, d_gate, d_up):
    half = ua.shape[0]
    for number, (u, cot) in enumerate(((ua, ca), (ub, cb))):
        rows = slice(number * half, (number + 1) * half)
        gate, up = dot(u[...], wg[...]), dot(u[...], wu[...])
        d_hidden = dot(flat(cot[...]), wd[...])
        sig = jax.nn.sigmoid(gate)
        silu = gate * sig
        hidden[rows, :] = (silu * up).astype(BF16)
        d_gate[rows, :] = (d_hidden * up * sig * (1.0 + gate * (1.0 - sig))).astype(BF16)
        d_up[rows, :] = (d_hidden * silu).astype(BF16)


def feed(ua, ub, ca, cb, w, behind):
    half, width = ua.shape
    chunk = 3 * HD
    parts = w.shape[1] // 3 // chunk
    column = lambda shift: pl.BlockSpec((width, chunk), lambda i: (0, shift * parts + i))
    unit = pl.BlockSpec((2 * half, chunk), lambda i: (0, i))
    units = parts * chunk
    return call(
        feed_kernel,
        (parts,),
        [fixed((half, width))] * 2
        + [piled(ca.shape, 1)] * 2
        + [column(0), column(1), column(2)],
        [unit, unit, unit],
        [struct((2 * half, units), BF16)] * 3,
        2 * 2 * half * width * units * 3,
        behind=behind,
    )(ua, ub, ca, cb, w, w, w)


def feed_back_kernel(d_gate, d_up, wg, wu, mine, other):
    half = mine.shape[0]
    out = dot_back(d_gate[...], wg[...]) + dot_back(d_up[...], wu[...])
    mine[...] = out[:half, :].astype(BF16)
    other[...] = out[half:, :].astype(BF16)


def feed_back(d_gate, d_up, w, behind):
    length, units = d_gate.shape
    half, width = length // 2, w.shape[0]
    chunk = 4 * HD
    slab = pl.BlockSpec((half, chunk), lambda i: (0, i))
    return call(
        feed_back_kernel,
        (width // chunk,),
        [fixed((length, units))] * 2
        + [
            pl.BlockSpec((chunk, units), lambda i: (i, 0)),
            pl.BlockSpec((chunk, units), lambda i: (i, 1)),
        ],
        [slab, slab],
        [struct((half, width), BF16), struct((half, width), BF16)],
        2 * length * width * units * 2,
        behind=behind,
    )(d_gate, d_up, w, w)


def down_kernel(hidden, w, mine, other):
    out = dot_back(hidden[...], w[...])

    @pl.when(pl.program_id(0) == 0)
    def _():
        mine[...] = out.astype(BF16)

    @pl.when(pl.program_id(0) == 1)
    def _():
        other[...] = out.astype(BF16)


def down_product(left, w, place, behind):
    length, units = left.shape
    half, width = length // 2, w.shape[0]
    return call(
        down_kernel,
        (2,),
        [rowed(half, units), pl.BlockSpec((width, units), lambda i: (0, place))],
        [fixed((half, width)), fixed((half, width))],
        [struct((half, width), BF16), struct((half, width), BF16)],
        2 * length * width * units,
        behind=behind,
    )(left, w)


def spread_blocks(left, right, out, start):
    for place in range(left.shape[1] // HD):
        term = dot_rows(left[:, head(place)], right)
        for owner in range(right.shape[1] // HD):
            at = start + place * HD
            out[owner * HD : (owner + 1) * HD, at : at + HD] = term[:, head(owner)].astype(BF16)


def feed_grads_kernel(u_flip, ca, cb, d_gate, d_up, hidden, out):
    units = hidden.shape[1]
    out[:, :units] = dot(u_flip[...], d_gate[...]).astype(BF16)
    out[:, units : 2 * units] = dot(u_flip[...], d_up[...]).astype(BF16)
    cot = jnp.concatenate([flat(ca[...]), flat(cb[...])], axis=0)
    spread_blocks(hidden, cot, out, 2 * units)


def feed_grads(u_flip, ca, cb, d_gate, d_up, hidden, behind):
    width, length = u_flip.shape
    units = hidden.shape[1]
    chunk = 4 * HD
    return call(
        feed_grads_kernel,
        (width // chunk,),
        [rowed(chunk, length)]
        + [pl.BlockSpec((ca.shape[0], ca.shape[1] // 2, chunk), lambda i: (0, 1, i))] * 2
        + [fixed((length, units))] * 3,
        rowed(chunk, 3 * units),
        struct((width, 3 * units), BF16),
        2 * length * width * units * 3,
        behind=behind,
    )(u_flip, ca, cb, d_gate, d_up, hidden)


def gate_back_kernel(da, db, w_out, gate, attended, d_attended, d_gate):
    half = da.shape[0]
    for number, low in enumerate((da, db)):
        rows = slice(number * half, (number + 1) * half)
        d_gated = dot(low[...], w_out[...])
        sig = jax.nn.sigmoid(gate[rows, :])
        d_attended[rows, :] = (d_gated * sig).astype(BF16)
        d_gate[rows, :] = (d_gated * attended[rows, :] * sig * (1.0 - sig)).astype(BF16)


def gate_back(da, db, w, gate, attended):
    half, width = da.shape
    wide = (2 * half, 2 * HD)
    return call(
        gate_back_kernel,
        (1,),
        [fixed((half, width))] * 2
        + [pl.BlockSpec((width, 2 * HD), lambda i: (0, 3)), fixed(wide), fixed(wide)],
        [fixed(wide), fixed(wide)],
        [struct(wide, BF16), struct(wide, BF16)],
        2 * 2 * half * width * 2 * HD,
    )(da, db, w, gate, attended)


def head_back(grads, inputs, gain):
    factor = rms_scale(inputs)
    scaled = gain * grads
    back = factor * scaled - inputs * factor**3 * jnp.mean(scaled * inputs, axis=-1, keepdims=True)
    return back.astype(BF16), jnp.sum(grads * inputs * factor, axis=0, keepdims=True)


def attend_back_kernel(
    probs, low, d_attended, pre, gains, cosine, sine, out, terms, d_key, d_value
):
    step = pl.program_id(0)
    half = probs.shape[1]
    start = pl.multiple_of(step * half, half)
    rows = pl.ds(start, half)
    key, value = low[:, head(2)], low[:, head(3)]
    cos_rows, sin_rows = cosine[rows, :], sine[rows, :]

    @pl.when(step == 0)
    def _():
        d_key[...] = jnp.zeros_like(d_key)
        d_value[...] = jnp.zeros_like(d_value)
        terms[...] = jnp.zeros_like(terms)

    for number in range(2):
        share = probs[number]
        d_seen = d_attended[:, head(number)]
        d_share = dot_back(d_seen, value)
        d_scores = share * (d_share - jnp.sum(share * d_share, axis=-1, keepdims=True))
        d_scores = d_scores.astype(BF16)
        d_query = dot(d_scores, key) * SCALE
        d_key[...] += dot_rows(d_scores, low[rows, head(number)])
        d_value[...] += dot_rows(share.astype(BF16), d_seen)
        grads = d_query * cos_rows + unturn(d_query * sin_rows)
        back, term = head_back(grads, pre[rows, head(number)], gains[0:1, :])
        out[rows, head(number)] = back
        terms[0:1, :] += term

    @pl.when(step == 1)
    def _():
        grads = d_key[...] * SCALE
        grads = grads * cosine[...] + unturn(grads * sine[...])
        back, term = head_back(grads, pre[:, head(2)], gains[1:2, :])
        out[:, head(2)] = back
        terms[1:2, :] = term
        out[:, head(3)] = d_value[...].astype(BF16)


def attend_back(probs, low, d_attended, pre, gains, cosine, sine, behind):
    length = low.shape[0]
    half = length // 2
    return call(
        attend_back_kernel,
        (2,),
        [
            pl.BlockSpec((2, half, length), lambda i: (0, i, 0)),
            fixed((length, 4 * HD)),
            rowed(half, 2 * HD),
            fixed((length, 3 * HD)),
            fixed((16, HD)),
            fixed((length, HD)),
            fixed((length, HD)),
        ],
        [fixed((length, 4 * HD)), fixed((8, HD))],
        [struct((length, 4 * HD), BF16), struct((8, HD), F32)],
        20 * length * length * HD,
        scratch=[pltpu.VMEM((length, HD), F32), pltpu.VMEM((length, HD), F32)],
        behind=behind,
    )(probs, low, d_attended, pre, gains, cosine, sine)


def input_back_kernel(d_qkv, d_gate, w, mine, other):
    out = dot_back(d_qkv[...], w[:, : 4 * HD]) + dot_back(d_gate[...], w[:, 4 * HD :])

    @pl.when(pl.program_id(0) == 0)
    def _():
        mine[...] = out.astype(BF16)

    @pl.when(pl.program_id(0) == 1)
    def _():
        other[...] = out.astype(BF16)


def input_back(d_qkv, d_gate, w, behind):
    length = d_qkv.shape[0]
    half, width = length // 2, w.shape[0]
    return call(
        input_back_kernel,
        (2,),
        [rowed(half, 4 * HD), rowed(half, 2 * HD), fixed((width, 6 * HD))],
        [fixed((half, width)), fixed((half, width))],
        [struct((half, width), BF16), struct((half, width), BF16)],
        2 * length * width * 6 * HD,
        behind=behind,
    )(d_qkv, d_gate, w)


def attend_grads_kernel(x_flip, da, db, d_qkv, d_gate, gated, terms, out, outer):
    inner, split = d_qkv.shape[1], d_gate.shape[1]
    block = out.shape[1] - terms.shape[1]
    for number in range(out.shape[0]):
        out[number, block:, :] = terms[number].astype(BF16)
    term = dot(x_flip[...], d_qkv[...]).astype(BF16)
    gates = dot(x_flip[...], d_gate[...]).astype(BF16)
    spread_blocks(gated, jnp.concatenate([da[...], db[...]], axis=0), outer, 0)
    for number in range(out.shape[0]):
        rows = slice(number * block, (number + 1) * block)
        out[number, :block, :inner] = term[rows]
        out[number, :block, inner : inner + split] = gates[rows]
        out[number, :block, inner + split :] = outer[rows, :]


def attend_grads(x_flip, da, db, d_qkv, d_gate, gated, terms, behind):
    width, length = x_flip.shape
    owners, extra, columns = terms.shape
    block = width // owners
    many = 4
    slab = pl.BlockSpec((length // 2, many * block), lambda i: (0, i))
    return call(
        attend_grads_kernel,
        (owners // many,),
        [
            rowed(many * block, length),
            slab,
            slab,
            fixed(d_qkv.shape),
            fixed(d_gate.shape),
            fixed(gated.shape),
            pl.BlockSpec((many, extra, columns), lambda i: (i, 0, 0)),
        ],
        pl.BlockSpec((many, block + extra, columns), lambda i: (i, 0, 0)),
        struct((owners, block + extra, columns), BF16),
        2 * length * width * columns,
        scratch=[pltpu.VMEM((many * block, gated.shape[1]), BF16)],
        behind=behind,
    )(x_flip, da, db, d_qkv, d_gate, gated, terms)


def middle_kernel(parts, x, middle, spread):
    total = x[...].astype(F32) + jnp.sum(parts[...].astype(F32), axis=0)
    middle[...] = total
    low = (total * rms_scale(total)).astype(BF16)
    for number in range(spread.shape[0]):
        spread[number] = low


def middle_step(parts, x, behind):
    shape = x.shape
    return call(
        middle_kernel,
        (1,),
        [fixed(parts.shape), fixed(shape)],
        [fixed(shape), fixed(parts.shape)],
        [struct(shape, F32), struct(parts.shape, BF16)],
        1 << 20,
        behind=behind,
    )(parts, x)


def norm_back(grads, inputs):
    factor = rms_scale(inputs)
    return factor * grads - inputs * factor**3 * jnp.mean(grads * inputs, axis=-1, keepdims=True)


def d_middle_kernel(parts, middle, cot, d_middle, spread):
    grads = jnp.sum(parts[...].astype(F32), axis=0)
    total = cot[...].astype(F32) + norm_back(grads, middle[...])
    d_middle[...] = total
    for number in range(spread.shape[0]):
        spread[number] = total.astype(BF16)


def d_middle_step(parts, middle, cot):
    shape = cot.shape
    return call(
        d_middle_kernel,
        (1,),
        [fixed(parts.shape), fixed(shape), fixed(shape)],
        [fixed(shape), fixed(parts.shape)],
        [struct(shape, F32), struct(parts.shape, BF16)],
        1 << 20,
    )(parts, middle, cot)


def ends_kernel(parts, middle, d_middle, x, out):
    rows = x.shape[0]
    total = sum(part[...].astype(F32) for part in parts)
    out[:rows, :] = (middle[...] + total[:rows, :]).astype(BF16)
    back = norm_back(total[rows:, :], x[...].astype(F32))
    out[rows:, :] = (d_middle[...] + back).astype(BF16)


def ends_step(parts, middle, d_middle, x):
    shape, wide = x.shape, parts[0].shape
    count = len(parts)
    return call(
        lambda *refs: ends_kernel(refs[:count], *refs[count:]),
        (1,),
        [fixed(wide)] * count + [fixed(shape)] * 3,
        fixed(wide),
        struct(wide, BF16),
        1 << 20,
    )(*parts, middle, d_middle, x)


def sum_kernel(parts, out):
    out[...] = jnp.sum(parts[...].astype(F32), axis=0).astype(BF16)


def sum_step(parts, behind):
    return call(
        sum_kernel,
        (1,),
        [fixed(parts.shape)],
        fixed(parts.shape[1:]),
        struct(parts.shape[1:], BF16),
        1 << 20,
        behind=behind,
    )(parts)


def prefetched(kernel, grid, in_specs, out_specs, out_shape):
    return pl.pallas_call(
        kernel,
        grid_spec=pltpu.PrefetchScalarGridSpec(
            num_scalar_prefetch=1, grid=grid, in_specs=in_specs, out_specs=out_specs
        ),
        out_shape=out_shape,
        compiler_params=pltpu.CompilerParams(
            dimension_semantics=("arbitrary",) * len(grid), vmem_limit_bytes=VMEM
        ),
        cost_estimate=pl.CostEstimate(flops=1 << 20, bytes_accessed=8 << 20, transcendentals=0),
    )


def copy_kernel(core, source, out):
    out[...] = source[...]


def sibling_part(core, found):
    pairs, _, rows, columns = found.shape
    return prefetched(
        copy_kernel,
        (pairs // 2,),
        [pl.BlockSpec((2, None, rows, columns), lambda i, at: (i, 1 - at[0], 0, 0))],
        pl.BlockSpec((2, rows, columns), lambda i, at: (i, 0, 0)),
        struct((pairs, rows, columns), found.dtype),
    )(core, found)


def join_kernel(core, mine, other, out):
    out[:, core[0]] = mine[...]
    out[:, 1 - core[0]] = other[...]


def join_cores(core, found, other):
    pairs, _, rows, columns = found.shape
    return prefetched(
        join_kernel,
        (pairs // 2,),
        [
            pl.BlockSpec((2, None, rows, columns), lambda i, at: (i, at[0], 0, 0)),
            pl.BlockSpec((2, rows, columns), lambda i, at: (i, 0, 0)),
        ],
        pl.BlockSpec((2, 2, rows, columns), lambda i, at: (i, 0, 0, 0)),
        struct(found.shape, found.dtype),
    )(core, found, other)


def lanes(value):
    return sum(value[:, start : start + HD] for start in range(0, value.shape[1], HD))


def pick(blocks):
    step = pl.program_id(0)
    value = blocks[0][...]
    for number in range(1, len(blocks)):
        value = jnp.where(step == number, blocks[number][...], value)
    return value.astype(F32)


def close_feed_kernel(turn_at, b0, b1, b2, b3, w_gate, w_up, gain, g_gate, g_up, g_down, sums):
    raw = pick((b0, b1, b2, b3))
    units = w_gate.shape[1]
    raw_gate, raw_up = raw[:, :units], raw[:, units : 2 * units]
    g_gate[...] = raw_gate * gain[...]
    g_up[...] = raw_up * gain[...]
    for place in range(units // HD):
        g_down[head(place), :] = raw[:, 2 * units + place * HD : 2 * units + (place + 1) * HD]
    term = lanes(raw_gate * w_gate[...].astype(F32)) + lanes(raw_up * w_up[...].astype(F32))

    @pl.when(pl.program_id(0) == 0)
    def _():
        sums[...] = term

    @pl.when(pl.program_id(0) > 0)
    def _():
        sums[...] += term


def close_attend_kernel(
    turn_at, b0, b1, b2, b3, wq, wk, wv, wg, gain, gq, gk, gv, gg, go, sums, ends
):
    found = pick((b0, b1, b2, b3))
    inner, scale = found[:, : 4 * HD], gain[...]
    block = scale.shape[0]
    outer = found[:block, 4 * HD :]
    raw_q, raw_k, raw_v = inner[:block, : 2 * HD], inner[:block, head(2)], inner[:block, head(3)]
    raw_g = outer[:, : 2 * HD]
    gq[...], gk[...], gv[...], gg[...] = raw_q * scale, raw_k * scale, raw_v * scale, raw_g * scale
    go[head(0), :], go[head(1), :] = outer[:, head(2)], outer[:, head(3)]
    pairs = ((raw_q, wq), (raw_k, wk), (raw_v, wv), (raw_g, wg))
    term = sum(lanes(raw * w[...].astype(F32)) for raw, w in pairs)
    last = inner[block:, :HD]

    @pl.when(pl.program_id(0) == 0)
    def _():
        sums[...] = term
        ends[...] = last

    @pl.when(pl.program_id(0) > 0)
    def _():
        sums[...] += term
        ends[...] += last


def close(kernel, turn_at, blocks, weights, gain, out_rows, extra):
    quarters = 4
    place = lambda i, at: (at[0] + quarters - i) % quarters
    whole = lambda value: pl.BlockSpec(value.shape, lambda i, at: (0, 0))
    columns = lambda w: pl.BlockSpec(
        (w.shape[0], w.shape[1] // quarters), lambda i, at: (0, place(i, at))
    )
    rows, width = out_rows
    in_specs = [whole(b) for b in blocks] + [columns(w) for w in weights] + [whole(gain)]
    out_specs = [columns(w) for w in weights]
    out_specs += [pl.BlockSpec((rows // quarters, width), lambda i, at: (place(i, at), 0))]
    out_specs += [pl.BlockSpec(shape, lambda i, at: (0, 0)) for shape in extra]
    out_shape = [struct(w.shape, F32) for w in weights] + [struct(out_rows, F32)]
    out_shape += [struct(shape, F32) for shape in extra]
    return prefetched(kernel, (quarters,), in_specs, out_specs, out_shape)(
        turn_at, *blocks, *weights, gain
    )


def make_shards(mesh):
    n_shard, n_ctx, n_tp = mesh.shape["shard"], mesh.shape["ctx"], mesh.shape["tp"]
    pairs = n_shard // 2

    def joint(pair, core, tp):
        return (pair * 2 + core) * n_tp + tp

    core_perm = [(i, i ^ 1) for i in range(n_shard)]
    planes = [
        [joint(pair, core, tp) for pair in range(pairs) for tp in range(n_tp)] for core in range(2)
    ]
    swap_perm = [
        edge
        for pair in range(pairs)
        for edge in (
            (joint(pair, 1, 0), joint(pair, 0, 1)),
            (joint(pair, 0, 1), joint(pair, 1, 0)),
        )
    ]
    across_perm = [(joint(pair, t, t), joint(pair, t, 1 - t)) for pair in range(pairs) for t in range(2)]

    def spot(pair, core, ctx, tp):
        return ((pair * 2 + core) * n_ctx + ctx) * n_tp + tp

    owner_perms = [
        [
            (spot(pair, core, ctx, tp), spot(pair, tp, (ctx + by) % n_ctx, core))
            for pair in range(pairs)
            for core in range(2)
            for ctx in range(n_ctx)
            for tp in range(n_tp)
            if by > 0 or core != tp
        ]
        for by in range(n_ctx)
    ]

    def core_swap(value):
        return lax.ppermute(value, "shard", core_perm)

    def ctx_exchange(value):
        return lax.all_to_all(value, "ctx", 0, 0)

    def ctx_turn(value, by):
        return lax.ppermute(value, "ctx", [(i, (i + by) % n_ctx) for i in range(n_ctx)])

    def tree_rows(spread, *before):
        mine = ctx_exchange(spread)
        if before:
            mine, *before = lax.optimization_barrier((mine, *before))
        return mine, core_swap(mine), *before

    def tree_half(mine, other):
        half = (mine.astype(F32) + core_swap(other).astype(F32)).astype(BF16)
        return half.reshape((n_ctx, -1) + half.shape[1:])

    def plane_gather(value):
        return lax.all_gather(value, PLANE, axis=0, tiled=True, axis_index_groups=planes)

    def plane_scatter(value):
        return lax.psum_scatter(
            value, PLANE, scatter_dimension=0, tiled=True, axis_index_groups=planes
        )

    def plane_exchange(value):
        return lax.all_to_all(value, PLANE, 0, 0, axis_index_groups=planes)

    def shards(
        tokens,
        seg_lengths,
        seg_parents,
        gain_in,
        w_query,
        w_key,
        w_value,
        w_gate_attn,
        w_out,
        gain_query,
        gain_key,
        gain_mid,
        w_gate,
        w_up,
        w_down,
        cotangent,
    ):
        core = lax.axis_index("shard") % 2
        tp = lax.axis_index("tp")
        ctx = lax.axis_index("ctx")
        native = core == tp
        rows = tokens.shape[0] // 2

        def swapped(value):
            return jnp.where(native, value, lax.ppermute(value, PLANE, swap_perm))

        def quarter(weight, axis):
            size = weight.shape[axis] // n_ctx
            return lax.dynamic_slice_in_dim(weight, ctx * size, size, axis)

        gain_one = gain_in.astype(F32)[:, None]
        gain_two = gain_mid.astype(F32)[:, None]
        first = jnp.concatenate(
            [quarter(w, 1) for w in (w_query, w_key, w_value, w_gate_attn)], axis=1
        )
        first = (first.astype(F32) * gain_one).astype(BF16)
        head_rows = gain_query.shape[0]
        ends = lax.dynamic_update_slice(
            jnp.zeros((gain_in.shape[0], HD), BF16),
            jnp.stack([gain_query, gain_key]),
            (0, lax.axis_index("shard") * head_rows),
        )
        first = jnp.concatenate([first, quarter(w_out, 0).T, ends], axis=1)
        found = plane_gather(first)

        def half_rows(place):
            pieces = [lax.dynamic_slice_in_dim(v, place * rows, rows, 0) for v in (tokens, cotangent)]
            return jnp.concatenate(pieces, axis=0)

        own = jnp.where(native, half_rows(core), core_swap(half_rows(1 - core)))
        tree = jnp.concatenate([seg_lengths, seg_parents], axis=0)
        tree = jnp.where(native, tree, core_swap(tree))
        own_x, own_cot = own[:rows], own[rows:]
        xa, xb = tree_rows(jnp.broadcast_to(own[None], (n_ctx,) + own.shape))

        second = jnp.concatenate([quarter(w_gate, 1), quarter(w_up, 1)], axis=1)
        second = (second.astype(F32) * gain_two).astype(BF16)
        second = jnp.concatenate([second, quarter(w_down, 0).T], axis=1)
        w2 = plane_gather(swapped(second))

        half_at = jnp.where(jnp.arange(2) == 0, core, 1 - core) * rows
        places = (
            half_at[:, None, None]
            + jnp.arange(n_ctx, dtype=jnp.int32)[None, :, None] * (2 * rows)
            + jnp.arange(rows, dtype=jnp.int32)[None, None, :]
        ).reshape(-1)
        segment, parent_seg, grand_seg, position = tree_layout(tree[0], tree[1], places)
        of_row = jnp.stack([segment, parent_seg, grand_seg, places], axis=1)
        of_column = jnp.stack([segment, places], axis=0)
        cosine, sine = rope_tables(position, HD)

        found, xa, xb, of_row, of_column, cosine, sine = lax.optimization_barrier(
            (found, xa, xb, of_row, of_column, cosine, sine)
        )
        found = found.reshape(pairs, n_tp, gain_in.shape[0], -1)
        core_at = core.astype(jnp.int32).reshape(1)
        other = core_swap(sibling_part(core_at, found))
        w1 = join_cores(core_at, found, other).reshape(-1, first.shape[1])

        xn, pre, low, gate, gains = project(xa, xb, w1, cosine, sine)
        probs, attended, gated, mine, other = attend(low, gate, w1, of_row, of_column)
        x_flip = flip(xn)
        middle, spread = middle_step(ctx_exchange(tree_half(mine, other)), own_x, (x_flip,))
        ua, ub = (flat(v) for v in tree_rows(spread))
        u_flip = flip(ua, ub)

        hidden, d_gate, d_up = feed(ua, ub, xa, xb, w2, (u_flip,))
        ffn = feed_grads(u_flip, xa, xb, d_gate, d_up, hidden, ())
        half = tree_half(*feed_back(d_gate, d_up, w2, (ffn,)))
        d_middle, spread = d_middle_step(ctx_exchange(half), middle, own_cot)
        layer_mine, layer_other = down_product(hidden, w2, 2, (half,))
        da, db, layer_mine, layer_other = tree_rows(spread, layer_mine, layer_other)
        da, db = flat(da), flat(db)
        grad_ffn = plane_scatter(ffn)

        d_attended, d_gate_pre = gate_back(da, db, w1, gate, attended)
        d_qkv, terms = attend_back(probs, low, d_attended, pre, gains, cosine, sine, ())

        def spread_terms(vector):
            return jnp.pad(vector.reshape(n_shard, 1, -1), ((0, 0), (0, 15), (0, 0)))

        wide_terms = jnp.concatenate([spread_terms(terms[0]), spread_terms(terms[1])], axis=2)
        wide_terms = jnp.pad(wide_terms, ((0, 0), (0, 0), (0, 8 * HD - 2 * head_rows)))
        attn = attend_grads(x_flip, da, db, d_qkv, d_gate_pre, gated, wide_terms, ())
        in_mine, in_other = input_back(d_qkv, d_gate_pre, w1, (attn,))
        layer_half, in_half = tree_half(layer_mine, layer_other), tree_half(in_mine, in_other)
        attn, layer_half, in_half, grad_ffn = lax.optimization_barrier(
            (attn, layer_half, in_half, grad_ffn)
        )
        attn_parts = plane_exchange(attn)

        def owners(block):
            block = swapped(block)
            return [block] + [ctx_turn(block, by) for by in range(1, n_ctx)]

        def owners_at_once(block):
            moved = [lax.ppermute(block, ("shard", "ctx", "tp"), perm) for perm in owner_perms]
            return [jnp.where(native, block, moved[0])] + moved[1:]

        both = jnp.concatenate(
            [layer_half, in_half], axis=1
        )
        parts = [lax.dynamic_index_in_dim(both, ctx, 0, False)] + [
            ctx_turn(lax.dynamic_index_in_dim(both, (ctx + by) % n_ctx, 0, False), by)
            for by in range(1, n_ctx)
        ]
        ends = ends_step(parts, middle, d_middle, own_x)
        ffn_blocks = owners(grad_ffn)
        attn_sum = sum_step(attn_parts, (ends, ffn_blocks[0]))
        ends, attn_sum = lax.optimization_barrier((ends, attn_sum))
        sibling = core_swap(ends)

        def whole(start):
            mine, other = ends[start : start + rows], sibling[start : start + rows]
            return jnp.where(
                core == 0,
                jnp.concatenate([mine, other], axis=0),
                jnp.concatenate([other, mine], axis=0),
            )

        full = jnp.stack([whole(0), whole(rows)])
        full = jnp.where(native, full, lax.ppermute(full, PLANE, across_perm))

        turn_at = ctx.astype(jnp.int32).reshape(1)
        size = gain_in.shape[0]
        grad_gate, grad_up, grad_down, mid_sums = close(
            close_feed_kernel,
            turn_at,
            ffn_blocks,
            (w_gate, w_up),
            gain_two,
            w_down.shape,
            [(size, HD)],
        )
        attn_blocks = owners(attn_sum)
        grad_query, grad_key, grad_value, grad_gate_attn, grad_out, in_sums, head_ends = close(
            close_attend_kernel,
            turn_at,
            attn_blocks,
            (w_query, w_key, w_value, w_gate_attn),
            gain_one,
            w_out.shape,
            [(size, HD), (16, HD)],
        )
        gain_terms = jnp.stack([jnp.sum(in_sums, axis=1), jnp.sum(mid_sums, axis=1), head_ends[0]])
        gain_terms = gain_terms + lax.ppermute(gain_terms, "tp", [(0, 1), (1, 0)])

        return (
            full[0].astype(F32),
            full[1].astype(F32),
            gain_terms[0],
            grad_query,
            grad_key,
            grad_value,
            grad_gate_attn,
            grad_out,
            gain_terms[2, :head_rows],
            gain_terms[2, head_rows : 2 * head_rows],
            gain_terms[1],
            grad_gate,
            grad_up,
            grad_down,
        )

    return shards


def solution(mesh):
    return jax.shard_map(
        make_shards(mesh),
        mesh=mesh,
        in_specs=(
            P(("shard", "ctx"), None),
            P("shard", None),
            P("shard", None),
            P("shard"),
            P("shard", "tp"),
            P("shard", "tp"),
            P("shard", "tp"),
            P("shard", "tp"),
            P("tp", "shard"),
            P("shard"),
            P("shard"),
            P("shard"),
            P("shard", "tp"),
            P("shard", "tp"),
            P("tp", "shard"),
            P(("shard", "ctx"), None),
        ),
        out_specs=(
            P(("shard", "ctx"), None),
            P(("shard", "ctx"), None),
            P("shard"),
            P("shard", "tp"),
            P("shard", "tp"),
            P("shard", "tp"),
            P("shard", "tp"),
            P("tp", "shard"),
            P("shard"),
            P("shard"),
            P("shard"),
            P("shard", "tp"),
            P("shard", "tp"),
            P("tp", "shard"),
        ),
        check_vma=False,
    )
```

```python
import math

import jax
import jax.numpy as jnp
from jax import lax
from jax.experimental import pallas as pl
from jax.experimental.pallas import tpu as pltpu
from jax.sharding import PartitionSpec as P

HD = 128
EPS = 1e-06
BASE = 1000000.0
NEG = -1e30
F32 = jnp.float32
BF16 = jnp.bfloat16
PLANE = ("shard", "tp")
SCALE = 1.0 / math.sqrt(HD)
VMEM = 48 << 20


def lookup(onehot, table):
    return jnp.sum(onehot * table[None, :], axis=1)


def tree_layout(lengths, parents, places):
    labels = jnp.arange(lengths.shape[0], dtype=jnp.int32)
    ends = jnp.cumsum(lengths)
    starts = ends - lengths
    parent_hot = (parents[:, None] == labels[None, :]).astype(jnp.int32)
    grand = lookup(parent_hot, parents)
    parent_len = lookup(parent_hot, lengths)
    grand_hot = (grand[:, None] == labels[None, :]).astype(jnp.int32)
    grand_len = lookup(grand_hot, lengths)
    before = jnp.where(labels == 0, 0, parent_len + jnp.where(parents == 0, 0, grand_len))
    segment = jnp.sum((places[:, None] >= ends[None, :]).astype(jnp.int32), axis=1)
    token_hot = (segment[:, None] == labels[None, :]).astype(jnp.int32)
    position = places - lookup(token_hot, starts) + lookup(token_hot, before)
    return (segment, lookup(token_hot, parents), lookup(token_hot, grand), position)


def rope_tables(position, columns):
    halfway = columns // 2
    frequency = jnp.exp(jnp.arange(halfway, dtype=F32) * (-2.0 * math.log(BASE) / columns))
    angles = position.astype(F32)[:, None] * frequency[None, :]
    angles = jnp.concatenate([angles, angles], axis=1)
    return (jnp.cos(angles), jnp.sin(angles))


def rms_scale(inputs):
    return lax.rsqrt(jnp.mean(inputs * inputs, axis=-1, keepdims=True) + EPS)


def dot(left, right):
    return jnp.dot(left, right, preferred_element_type=F32)


def dot_rows(left, right):
    return lax.dot_general(left, right, (((0,), (0,)), ((), ())), preferred_element_type=F32)


def dot_back(left, right):
    return lax.dot_general(left, right, (((1,), (1,)), ((), ())), preferred_element_type=F32)


def turn(inputs):
    halfway = inputs.shape[-1] // 2
    return jnp.concatenate([-inputs[:, halfway:], inputs[:, :halfway]], axis=-1)


def unturn(inputs):
    halfway = inputs.shape[-1] // 2
    return jnp.concatenate([inputs[:, halfway:], -inputs[:, :halfway]], axis=-1)


def head(number):
    return slice(number * HD, (number + 1) * HD)


def call(kernel, grid, in_specs, out_specs, out_shape, flops, scratch=(), moved=8 << 20, behind=()):
    count = len(in_specs)

    def body(*refs):
        kernel(*refs[:count], *refs[count + len(behind) :])

    built = pl.pallas_call(
        body,
        grid=grid,
        in_specs=list(in_specs) + [pl.BlockSpec(memory_space=pl.ANY)] * len(behind),
        out_specs=out_specs,
        out_shape=out_shape,
        scratch_shapes=scratch,
        compiler_params=pltpu.CompilerParams(
            dimension_semantics=("arbitrary",) * len(grid), vmem_limit_bytes=VMEM
        ),
        cost_estimate=pl.CostEstimate(flops=flops, bytes_accessed=moved, transcendentals=0),
    )
    return lambda *operands: built(*operands, *behind)


def prefetched(
    kernel, grid, in_specs, out_specs, out_shape, flops=1 << 20, scratch=(), behind=()
):
    count = len(in_specs) + 1

    def body(*refs):
        kernel(*refs[:count], *refs[count + len(behind) :])

    built = pl.pallas_call(
        body,
        grid_spec=pltpu.PrefetchScalarGridSpec(
            num_scalar_prefetch=1,
            grid=grid,
            in_specs=list(in_specs) + [pl.BlockSpec(memory_space=pl.ANY)] * len(behind),
            out_specs=out_specs,
            scratch_shapes=scratch,
        ),
        out_shape=out_shape,
        compiler_params=pltpu.CompilerParams(
            dimension_semantics=("arbitrary",) * len(grid), vmem_limit_bytes=VMEM
        ),
        cost_estimate=pl.CostEstimate(flops=flops, bytes_accessed=8 << 20, transcendentals=0),
    )
    return lambda *operands: built(*operands, *behind)


def struct(shape, dtype):
    return jax.ShapeDtypeStruct(shape, dtype)


def fixed(shape):
    return pl.BlockSpec(shape, lambda i: (0,) * len(shape))


def rowed(rows, columns):
    return pl.BlockSpec((rows, columns), lambda i: (i, 0))


def piled(shape, which):
    return pl.BlockSpec((shape[0], shape[1] // 2, shape[2]), lambda i: (0, which, 0))


def flat(value):
    return value.reshape((-1,) + value.shape[2:])


def project_kernel(xa, xb, w, ends, cosine, sine, xn, pre, low, gate, gains):
    x = flat(jnp.where(pl.program_id(0) == 0, xa[...], xb[...])).astype(F32)
    normed = (x * rms_scale(x)).astype(BF16)
    xn[...] = normed
    out = dot(normed, w[...])
    found = jnp.zeros((16, HD), F32)
    for start in range(0, ends.shape[0], HD):
        found = found + ends[start : start + 16, :].astype(F32)
    gains[...] = found
    for place in range(3):
        raw = out[:, head(place)]
        pre[:, head(place)] = raw
        unit = raw * rms_scale(raw) * found[place // 2 : place // 2 + 1, :]
        low[:, head(place)] = (unit * cosine[...] + turn(unit) * sine[...]).astype(BF16)
    low[:, head(3)] = out[:, head(3)].astype(BF16)
    gate[...] = out[:, 4 * HD :]


def project(xa, xb, w, cosine, sine):
    half, width = xa.shape[0] * xa.shape[1] // 2, xa.shape[2]
    return call(
        project_kernel,
        (2,),
        [
            piled(xa.shape, 0),
            piled(xb.shape, 0),
            fixed((width, 6 * HD)),
            pl.BlockSpec((width, HD), lambda i: (0, 8)),
            rowed(half, HD),
            rowed(half, HD),
        ],
        [
            rowed(half, width),
            rowed(half, 3 * HD),
            rowed(half, 4 * HD),
            rowed(half, 2 * HD),
            fixed((16, HD)),
        ],
        [
            struct((2 * half, width), BF16),
            struct((2 * half, 3 * HD), F32),
            struct((2 * half, 4 * HD), BF16),
            struct((2 * half, 2 * HD), F32),
            struct((16, HD), F32),
        ],
        2 * 2 * half * width * 6 * HD,
    )(xa, xb, w, w, cosine, sine)


def attend_kernel(low, gate, w_out, of_row, of_column, probs, attended, gated, mine, other):
    step = pl.program_id(0)
    half = probs.shape[1]
    rows = pl.ds(step * half, half)
    key, value = low[:, head(2)], low[:, head(3)]
    seg, par, grand, place = (of_row[rows, n : n + 1] for n in range(4))
    key_seg, key_place = of_column[0:1, :], of_column[1:2, :]
    allowed = ((key_seg == seg) | (key_seg == par) | (key_seg == grand)) & (key_place <= place)
    for number in range(2):
        scores = dot_back(low[rows, head(number)], key) * SCALE
        scores = jnp.where(allowed, scores, NEG)
        raised = jnp.exp(scores - jnp.max(scores, axis=-1, keepdims=True))
        share = raised / jnp.sum(raised, axis=-1, keepdims=True)
        probs[number] = share
        seen = dot(share.astype(BF16), value)
        attended[:, head(number)] = seen
        gated[:, head(number)] = (seen * jax.nn.sigmoid(gate[:, head(number)])).astype(BF16)
    out = dot_back(gated[...], w_out[...])

    @pl.when(step == 0)
    def _():
        mine[...] = out.astype(BF16)

    @pl.when(step == 1)
    def _():
        other[...] = out.astype(BF16)


def attend(low, gate, w, of_row, of_column):
    length = low.shape[0]
    half, width = length // 2, w.shape[0]
    return call(
        attend_kernel,
        (2,),
        [
            fixed((length, 4 * HD)),
            rowed(half, 2 * HD),
            pl.BlockSpec((width, 2 * HD), lambda i: (0, 3)),
            fixed((length, 4)),
            fixed((2, length)),
        ],
        [
            pl.BlockSpec((2, half, length), lambda i: (0, i, 0)),
            rowed(half, 2 * HD),
            rowed(half, 2 * HD),
            fixed((half, width)),
            fixed((half, width)),
        ],
        [
            struct((2, length, length), F32),
            struct((length, 2 * HD), F32),
            struct((length, 2 * HD), BF16),
            struct((half, width), BF16),
            struct((half, width), BF16),
        ],
        2 * length * width * 2 * HD + 8 * length * length * HD,
    )(low, gate, w, of_row, of_column)


def flip_kernel(pieces, out):
    at = 0
    for piece in pieces:
        out[:, at : at + piece.shape[0]] = piece[...].T
        at += piece.shape[0]


def flip(*pieces):
    length, width = sum(piece.shape[0] for piece in pieces), pieces[0].shape[1]
    chunk = 2 * HD
    return call(
        lambda *refs: flip_kernel(refs[:-1], refs[-1]),
        (width // chunk,),
        [pl.BlockSpec((piece.shape[0], chunk), lambda i: (0, i)) for piece in pieces],
        rowed(chunk, length),
        struct((width, length), BF16),
        1 << 20,
    )(*pieces)


def feed_kernel(ua, ub, ca, cb, wg, wu, wd, hidden, d_gate, d_up):
    half = ua.shape[0]
    for number, (u, cot) in enumerate(((ua, ca), (ub, cb))):
        rows = slice(number * half, (number + 1) * half)
        gate, up = dot(u[...], wg[...]), dot(u[...], wu[...])
        d_hidden = dot(flat(cot[...]), wd[...])
        sig = jax.nn.sigmoid(gate)
        silu = gate * sig
        hidden[rows, :] = (silu * up).astype(BF16)
        d_gate[rows, :] = (d_hidden * up * sig * (1.0 + gate * (1.0 - sig))).astype(BF16)
        d_up[rows, :] = (d_hidden * silu).astype(BF16)


def feed(ua, ub, ca, cb, w, behind):
    half, width = ua.shape
    chunk = 3 * HD
    parts = w.shape[1] // 3 // chunk
    column = lambda shift: pl.BlockSpec((width, chunk), lambda i: (0, shift * parts + i))
    unit = pl.BlockSpec((2 * half, chunk), lambda i: (0, i))
    units = parts * chunk
    return call(
        feed_kernel,
        (parts,),
        [fixed((half, width))] * 2
        + [piled(ca.shape, 1)] * 2
        + [column(0), column(1), column(2)],
        [unit, unit, unit],
        [struct((2 * half, units), BF16)] * 3,
        2 * 2 * half * width * units * 3,
        behind=behind,
    )(ua, ub, ca, cb, w, w, w)


def feed_back_kernel(d_gate, d_up, wg, wu, mine, other):
    half = mine.shape[0]
    out = dot_back(d_gate[...], wg[...]) + dot_back(d_up[...], wu[...])
    mine[...] = out[:half, :].astype(BF16)
    other[...] = out[half:, :].astype(BF16)


def feed_back(d_gate, d_up, w, behind):
    length, units = d_gate.shape
    half, width = length // 2, w.shape[0]
    chunk = 4 * HD
    slab = pl.BlockSpec((half, chunk), lambda i: (0, i))
    return call(
        feed_back_kernel,
        (width // chunk,),
        [fixed((length, units))] * 2
        + [
            pl.BlockSpec((chunk, units), lambda i: (i, 0)),
            pl.BlockSpec((chunk, units), lambda i: (i, 1)),
        ],
        [slab, slab],
        [struct((half, width), BF16), struct((half, width), BF16)],
        2 * length * width * units * 2,
        behind=behind,
    )(d_gate, d_up, w, w)


def down_kernel(hidden, w, mine, other):
    out = dot_back(hidden[...], w[...])

    @pl.when(pl.program_id(0) == 0)
    def _():
        mine[...] = out.astype(BF16)

    @pl.when(pl.program_id(0) == 1)
    def _():
        other[...] = out.astype(BF16)


def down_product(left, w, place, behind):
    length, units = left.shape
    half, width = length // 2, w.shape[0]
    return call(
        down_kernel,
        (2,),
        [rowed(half, units), pl.BlockSpec((width, units), lambda i: (0, place))],
        [fixed((half, width)), fixed((half, width))],
        [struct((half, width), BF16), struct((half, width), BF16)],
        2 * length * width * units,
        behind=behind,
    )(left, w)


def spread_blocks(left, right, out, start):
    for place in range(left.shape[1] // HD):
        term = dot_rows(left[:, head(place)], right)
        for owner in range(right.shape[1] // HD):
            at = start + place * HD
            out[owner * HD : (owner + 1) * HD, at : at + HD] = term[:, head(owner)].astype(BF16)


def feed_grads_kernel(u_flip, ca, cb, d_gate, d_up, hidden, out):
    units = hidden.shape[1]
    out[:, :units] = dot(u_flip[...], d_gate[...]).astype(BF16)
    out[:, units : 2 * units] = dot(u_flip[...], d_up[...]).astype(BF16)
    cot = jnp.concatenate([flat(ca[...]), flat(cb[...])], axis=0)
    spread_blocks(hidden, cot, out, 2 * units)


def feed_grads(u_flip, ca, cb, d_gate, d_up, hidden, behind):
    width, length = u_flip.shape
    units = hidden.shape[1]
    chunk = 4 * HD
    return call(
        feed_grads_kernel,
        (width // chunk,),
        [rowed(chunk, length)]
        + [pl.BlockSpec((ca.shape[0], ca.shape[1] // 2, chunk), lambda i: (0, 1, i))] * 2
        + [fixed((length, units))] * 3,
        rowed(chunk, 3 * units),
        struct((width, 3 * units), BF16),
        2 * length * width * units * 3,
        behind=behind,
    )(u_flip, ca, cb, d_gate, d_up, hidden)


def gate_back_kernel(da, db, w_out, gate, attended, d_attended, d_gate):
    half = da.shape[0]
    for number, low in enumerate((da, db)):
        rows = slice(number * half, (number + 1) * half)
        d_gated = dot(low[...], w_out[...])
        sig = jax.nn.sigmoid(gate[rows, :])
        d_attended[rows, :] = (d_gated * sig).astype(BF16)
        d_gate[rows, :] = (d_gated * attended[rows, :] * sig * (1.0 - sig)).astype(BF16)


def gate_back(da, db, w, gate, attended):
    half, width = da.shape
    wide = (2 * half, 2 * HD)
    return call(
        gate_back_kernel,
        (1,),
        [fixed((half, width))] * 2
        + [pl.BlockSpec((width, 2 * HD), lambda i: (0, 3)), fixed(wide), fixed(wide)],
        [fixed(wide), fixed(wide)],
        [struct(wide, BF16), struct(wide, BF16)],
        2 * 2 * half * width * 2 * HD,
    )(da, db, w, gate, attended)


def head_back(grads, inputs, gain):
    factor = rms_scale(inputs)
    scaled = gain * grads
    back = factor * scaled - inputs * factor**3 * jnp.mean(scaled * inputs, axis=-1, keepdims=True)
    return back.astype(BF16), jnp.sum(grads * inputs * factor, axis=0, keepdims=True)


def attend_back_kernel(
    probs, low, d_attended, pre, gains, cosine, sine, out, terms, d_key, d_value
):
    step = pl.program_id(0)
    half = probs.shape[1]
    start = pl.multiple_of(step * half, half)
    rows = pl.ds(start, half)
    key, value = low[:, head(2)], low[:, head(3)]
    cos_rows, sin_rows = cosine[rows, :], sine[rows, :]

    @pl.when(step == 0)
    def _():
        d_key[...] = jnp.zeros_like(d_key)
        d_value[...] = jnp.zeros_like(d_value)
        terms[...] = jnp.zeros_like(terms)

    for number in range(2):
        share = probs[number]
        d_seen = d_attended[:, head(number)]
        d_share = dot_back(d_seen, value)
        d_scores = share * (d_share - jnp.sum(share * d_share, axis=-1, keepdims=True))
        d_scores = d_scores.astype(BF16)
        d_query = dot(d_scores, key) * SCALE
        d_key[...] += dot_rows(d_scores, low[rows, head(number)])
        d_value[...] += dot_rows(share.astype(BF16), d_seen)
        grads = d_query * cos_rows + unturn(d_query * sin_rows)
        back, term = head_back(grads, pre[rows, head(number)], gains[0:1, :])
        out[rows, head(number)] = back
        terms[0:1, :] += term

    @pl.when(step == 1)
    def _():
        grads = d_key[...] * SCALE
        grads = grads * cosine[...] + unturn(grads * sine[...])
        back, term = head_back(grads, pre[:, head(2)], gains[1:2, :])
        out[:, head(2)] = back
        terms[1:2, :] = term
        out[:, head(3)] = d_value[...].astype(BF16)


def attend_back(probs, low, d_attended, pre, gains, cosine, sine, behind):
    length = low.shape[0]
    half = length // 2
    return call(
        attend_back_kernel,
        (2,),
        [
            pl.BlockSpec((2, half, length), lambda i: (0, i, 0)),
            fixed((length, 4 * HD)),
            rowed(half, 2 * HD),
            fixed((length, 3 * HD)),
            fixed((16, HD)),
            fixed((length, HD)),
            fixed((length, HD)),
        ],
        [fixed((length, 4 * HD)), fixed((8, HD))],
        [struct((length, 4 * HD), BF16), struct((8, HD), F32)],
        20 * length * length * HD,
        scratch=[pltpu.VMEM((length, HD), F32), pltpu.VMEM((length, HD), F32)],
        behind=behind,
    )(probs, low, d_attended, pre, gains, cosine, sine)


def input_back_kernel(d_qkv, d_gate, w, mine, other):
    out = dot_back(d_qkv[...], w[:, : 4 * HD]) + dot_back(d_gate[...], w[:, 4 * HD :])

    @pl.when(pl.program_id(0) == 0)
    def _():
        mine[...] = out.astype(BF16)

    @pl.when(pl.program_id(0) == 1)
    def _():
        other[...] = out.astype(BF16)


def input_back(d_qkv, d_gate, w, behind):
    length = d_qkv.shape[0]
    half, width = length // 2, w.shape[0]
    return call(
        input_back_kernel,
        (2,),
        [rowed(half, 4 * HD), rowed(half, 2 * HD), fixed((width, 6 * HD))],
        [fixed((half, width)), fixed((half, width))],
        [struct((half, width), BF16), struct((half, width), BF16)],
        2 * length * width * 6 * HD,
        behind=behind,
    )(d_qkv, d_gate, w)


SIDE = 4


def attend_grads_kernel(at, x_flip, da, db, d_qkv, d_gate, gated, terms, *refs):
    first, second, (whole, outer) = refs[:SIDE], refs[SIDE : 2 * SIDE], refs[2 * SIDE :]
    step = pl.program_id(0)
    x = (at[0] + step) % SIDE
    inner, split = d_qkv.shape[1], d_gate.shape[1]
    block = second[0].shape[1]
    term = dot(x_flip[...], d_qkv[...]).astype(BF16)
    for owner in range(SIDE):
        whole[owner, :block, :inner] = term[owner * block : (owner + 1) * block]
        whole[owner, block:, :inner] = terms[owner].astype(BF16)
    gates = dot(x_flip[...], d_gate[...]).astype(BF16)
    spread_blocks(gated, jnp.concatenate([da[...], db[...]], axis=0), outer, 0)
    for owner in range(SIDE):
        rows = slice(owner * block, (owner + 1) * block)
        whole[owner, :block, inner : inner + split] = gates[rows]
        whole[owner, :block, inner + split :] = outer[rows, :]
    for turn_by in range(SIDE):

        @pl.when(step == turn_by)
        def _():
            first[turn_by][...] = whole[:, :, :inner]

        second[turn_by][x] = whole[(at[1] + turn_by) % SIDE, :block, inner:]


def attend_grads(at, x_flip, da, db, d_qkv, d_gate, gated, terms):
    width, length = x_flip.shape
    owners, extra, inner = terms.shape
    block, outer = width // owners, d_gate.shape[1] + gated.shape[1]
    place = lambda i, at: (at[0] + i) % SIDE
    slab = pl.BlockSpec((length // 2, SIDE * block), lambda i, at: (0, place(i, at)))
    whole = lambda value: pl.BlockSpec(value.shape, lambda i, at: (0, 0))
    piece = lambda shape: pl.BlockSpec(shape, lambda i, at: (0, 0, 0))
    shapes = [(SIDE, block + extra, inner)] * SIDE + [(SIDE, block, outer)] * SIDE
    found = prefetched(
        attend_grads_kernel,
        (SIDE,),
        [
            pl.BlockSpec((SIDE * block, length), lambda i, at: (place(i, at), 0)),
            slab,
            slab,
            whole(d_qkv),
            whole(d_gate),
            whole(gated),
            pl.BlockSpec((SIDE, extra, inner), lambda i, at: (place(i, at), 0, 0)),
        ],
        [piece(shape) for shape in shapes],
        [struct(shape, BF16) for shape in shapes],
        2 * length * width * (inner + outer),
        scratch=[
            pltpu.VMEM((SIDE, block + extra, inner + outer), BF16),
            pltpu.VMEM((SIDE * block, gated.shape[1]), BF16),
        ],
    )(at, x_flip, da, db, d_qkv, d_gate, gated, terms)
    return found[:SIDE], found[SIDE:]


def turn_sums_kernel(at, *refs):
    parts, outs = refs[:SIDE], refs[SIDE:]
    for turn_by in range(SIDE):
        place = (at[0] + turn_by) % SIDE
        total = sum(part[place].astype(F32) for part in parts)
        outs[turn_by][...] = total.astype(BF16)


def turn_sums(at, parts):
    shape = parts[0].shape
    return prefetched(
        turn_sums_kernel,
        (1,),
        [pl.BlockSpec(shape, lambda i, at: (0, 0, 0))] * SIDE,
        [pl.BlockSpec(shape[1:], lambda i, at: (0, 0))] * SIDE,
        [struct(shape[1:], BF16)] * SIDE,
    )(at, *parts)


def both_sums_kernel(first, second, out):
    columns, rows = first[0].shape[1], second[0].shape[0]
    out[:, :columns] = sum(part[...].astype(F32) for part in first).astype(BF16)
    out[:rows, columns:] = sum(part[...].astype(F32) for part in second).astype(BF16)
    out[rows:, columns:] = jnp.zeros((out.shape[0] - rows, out.shape[1] - columns), BF16)


def both_sums(first, second, behind):
    rows, columns = first[0].shape
    wide = (rows, columns + second[0].shape[1])
    return call(
        lambda *refs: both_sums_kernel(refs[:SIDE], refs[SIDE : 2 * SIDE], refs[-1]),
        (1,),
        [fixed(part.shape) for part in (*first, *second)],
        fixed(wide),
        struct(wide, BF16),
        1 << 20,
        behind=behind,
    )(*first, *second)


def middle_kernel(parts, x, middle, spread):
    total = x[...].astype(F32) + jnp.sum(parts[...].astype(F32), axis=0)
    middle[...] = total
    low = (total * rms_scale(total)).astype(BF16)
    for number in range(spread.shape[0]):
        spread[number] = low


def middle_step(parts, x, behind):
    shape = x.shape
    return call(
        middle_kernel,
        (1,),
        [fixed(parts.shape), fixed(shape)],
        [fixed(shape), fixed(parts.shape)],
        [struct(shape, F32), struct(parts.shape, BF16)],
        1 << 20,
        behind=behind,
    )(parts, x)


def norm_back(grads, inputs):
    factor = rms_scale(inputs)
    return factor * grads - inputs * factor**3 * jnp.mean(grads * inputs, axis=-1, keepdims=True)


def d_middle_kernel(parts, middle, cot, d_middle, spread):
    grads = jnp.sum(parts[...].astype(F32), axis=0)
    total = cot[...].astype(F32) + norm_back(grads, middle[...])
    d_middle[...] = total
    for number in range(spread.shape[0]):
        spread[number] = total.astype(BF16)


def d_middle_step(parts, middle, cot):
    shape = cot.shape
    return call(
        d_middle_kernel,
        (1,),
        [fixed(parts.shape), fixed(shape), fixed(shape)],
        [fixed(shape), fixed(parts.shape)],
        [struct(shape, F32), struct(parts.shape, BF16)],
        1 << 20,
    )(parts, middle, cot)


def ends_kernel(parts, middle, d_middle, x, out):
    rows = x.shape[0]
    total = sum(part[...].astype(F32) for part in parts)
    out[:rows, :] = (middle[...] + total[:rows, :]).astype(BF16)
    back = norm_back(total[rows:, :], x[...].astype(F32))
    out[rows:, :] = (d_middle[...] + back).astype(BF16)


def ends_step(parts, middle, d_middle, x):
    shape, wide = x.shape, parts[0].shape
    count = len(parts)
    return call(
        lambda *refs: ends_kernel(refs[:count], *refs[count:]),
        (1,),
        [fixed(wide)] * count + [fixed(shape)] * 3,
        fixed(wide),
        struct(wide, BF16),
        1 << 20,
    )(*parts, middle, d_middle, x)


def copy_kernel(core, source, out):
    out[...] = source[...]


def sibling_part(core, found):
    pairs, _, rows, columns = found.shape
    return prefetched(
        copy_kernel,
        (pairs // 2,),
        [pl.BlockSpec((2, None, rows, columns), lambda i, at: (i, 1 - at[0], 0, 0))],
        pl.BlockSpec((2, rows, columns), lambda i, at: (i, 0, 0)),
        struct((pairs, rows, columns), found.dtype),
    )(core, found)


def join_kernel(core, mine, other, out):
    out[:, core[0]] = mine[...]
    out[:, 1 - core[0]] = other[...]


def join_cores(core, found, other):
    pairs, _, rows, columns = found.shape
    return prefetched(
        join_kernel,
        (pairs // 2,),
        [
            pl.BlockSpec((2, None, rows, columns), lambda i, at: (i, at[0], 0, 0)),
            pl.BlockSpec((2, rows, columns), lambda i, at: (i, 0, 0)),
        ],
        pl.BlockSpec((2, 2, rows, columns), lambda i, at: (i, 0, 0, 0)),
        struct(found.shape, found.dtype),
    )(core, found, other)


def lanes(value):
    return sum(value[:, start : start + HD] for start in range(0, value.shape[1], HD))


def pick(blocks):
    step = pl.program_id(0)
    value = blocks[0][...]
    for number in range(1, len(blocks)):
        value = jnp.where(step == number, blocks[number][...], value)
    return value.astype(F32)


def close_feed_kernel(turn_at, b0, b1, b2, b3, w_gate, w_up, gain, g_gate, g_up, g_down, sums):
    raw = pick((b0, b1, b2, b3))
    units = w_gate.shape[1]
    raw_gate, raw_up = raw[:, :units], raw[:, units : 2 * units]
    g_gate[...] = raw_gate * gain[...]
    g_up[...] = raw_up * gain[...]
    for place in range(units // HD):
        g_down[head(place), :] = raw[:, 2 * units + place * HD : 2 * units + (place + 1) * HD]
    term = lanes(raw_gate * w_gate[...].astype(F32)) + lanes(raw_up * w_up[...].astype(F32))

    @pl.when(pl.program_id(0) == 0)
    def _():
        sums[...] = term

    @pl.when(pl.program_id(0) > 0)
    def _():
        sums[...] += term


def close_attend_kernel(
    turn_at, b0, b1, b2, b3, wq, wk, wv, wg, gain, gq, gk, gv, gg, go, sums, ends
):
    found = pick((b0, b1, b2, b3))
    inner, scale = found[:, : 4 * HD], gain[...]
    block = scale.shape[0]
    outer = found[:block, 4 * HD :]
    raw_q, raw_k, raw_v = inner[:block, : 2 * HD], inner[:block, head(2)], inner[:block, head(3)]
    raw_g = outer[:, : 2 * HD]
    gq[...], gk[...], gv[...], gg[...] = raw_q * scale, raw_k * scale, raw_v * scale, raw_g * scale
    go[head(0), :], go[head(1), :] = outer[:, head(2)], outer[:, head(3)]
    pairs = ((raw_q, wq), (raw_k, wk), (raw_v, wv), (raw_g, wg))
    term = sum(lanes(raw * w[...].astype(F32)) for raw, w in pairs)
    last = inner[block:, :HD]

    @pl.when(pl.program_id(0) == 0)
    def _():
        sums[...] = term
        ends[...] = last

    @pl.when(pl.program_id(0) > 0)
    def _():
        sums[...] += term
        ends[...] += last


def close(kernel, turn_at, blocks, weights, gain, out_rows, extra):
    quarters = 4
    place = lambda i, at: (at[0] + quarters - i) % quarters
    whole = lambda value: pl.BlockSpec(value.shape, lambda i, at: (0, 0))
    columns = lambda w: pl.BlockSpec(
        (w.shape[0], w.shape[1] // quarters), lambda i, at: (0, place(i, at))
    )
    rows, width = out_rows
    in_specs = [whole(b) for b in blocks] + [columns(w) for w in weights] + [whole(gain)]
    out_specs = [columns(w) for w in weights]
    out_specs += [pl.BlockSpec((rows // quarters, width), lambda i, at: (place(i, at), 0))]
    out_specs += [pl.BlockSpec(shape, lambda i, at: (0, 0)) for shape in extra]
    out_shape = [struct(w.shape, F32) for w in weights] + [struct(out_rows, F32)]
    out_shape += [struct(shape, F32) for shape in extra]
    return prefetched(kernel, (quarters,), in_specs, out_specs, out_shape)(
        turn_at, *blocks, *weights, gain
    )


def make_shards(mesh):
    n_shard, n_ctx, n_tp = mesh.shape["shard"], mesh.shape["ctx"], mesh.shape["tp"]
    pairs = n_shard // 2

    def joint(pair, core, tp):
        return (pair * 2 + core) * n_tp + tp

    core_perm = [(i, i ^ 1) for i in range(n_shard)]
    planes = [
        [joint(pair, core, tp) for pair in range(pairs) for tp in range(n_tp)] for core in range(2)
    ]
    swap_perm = [
        edge
        for pair in range(pairs)
        for edge in (
            (joint(pair, 1, 0), joint(pair, 0, 1)),
            (joint(pair, 0, 1), joint(pair, 1, 0)),
        )
    ]
    across_perm = [(joint(pair, t, t), joint(pair, t, 1 - t)) for pair in range(pairs) for t in range(2)]

    def spot(pair, core, ctx, tp):
        return ((pair * 2 + core) * n_ctx + ctx) * n_tp + tp

    owner_perms = [
        [
            (spot(pair, core, ctx, tp), spot(pair, tp, (ctx + by) % n_ctx, core))
            for pair in range(pairs)
            for core in range(2)
            for ctx in range(n_ctx)
            for tp in range(n_tp)
            if by > 0 or core != tp
        ]
        for by in range(n_ctx)
    ]

    def core_swap(value):
        return lax.ppermute(value, "shard", core_perm)

    def ctx_exchange(value):
        return lax.all_to_all(value, "ctx", 0, 0)

    def ctx_turn(value, by):
        return lax.ppermute(value, "ctx", [(i, (i + by) % n_ctx) for i in range(n_ctx)])

    def tree_rows(spread, *before):
        mine = ctx_exchange(spread)
        if before:
            mine, *before = lax.optimization_barrier((mine, *before))
        return mine, core_swap(mine), *before

    def tree_half(mine, other):
        half = (mine.astype(F32) + core_swap(other).astype(F32)).astype(BF16)
        return half.reshape((n_ctx, -1) + half.shape[1:])

    def plane_gather(value):
        return lax.all_gather(value, PLANE, axis=0, tiled=True, axis_index_groups=planes)

    def plane_scatter(value):
        return lax.psum_scatter(
            value, PLANE, scatter_dimension=0, tiled=True, axis_index_groups=planes
        )

    def x_turn(value, by):
        perm = [(s, (s + by * SIDE) % n_shard) for s in range(n_shard)]
        return lax.ppermute(value, "shard", perm)

    def y_turn(value, by):
        perm = []
        for s in range(n_shard):
            for tp in range(n_tp):
                y = (s // 2 % 2) * n_tp + tp
                to = (y + by) % SIDE
                perm.append((s * n_tp + tp, (s // 4 * 4 + to // n_tp * 2 + s % 2) * n_tp + to % n_tp))
        return lax.ppermute(value, PLANE, perm)

    def turned(turn_along, pieces):
        return [pieces[0]] + [turn_along(pieces[by], by) for by in range(1, SIDE)]

    def shards(
        tokens,
        seg_lengths,
        seg_parents,
        gain_in,
        w_query,
        w_key,
        w_value,
        w_gate_attn,
        w_out,
        gain_query,
        gain_key,
        gain_mid,
        w_gate,
        w_up,
        w_down,
        cotangent,
    ):
        core = lax.axis_index("shard") % 2
        tp = lax.axis_index("tp")
        ctx = lax.axis_index("ctx")
        native = core == tp
        rows = tokens.shape[0] // 2

        def swapped(value):
            return jnp.where(native, value, lax.ppermute(value, PLANE, swap_perm))

        def quarter(weight, axis):
            size = weight.shape[axis] // n_ctx
            return lax.dynamic_slice_in_dim(weight, ctx * size, size, axis)

        gain_one = gain_in.astype(F32)[:, None]
        gain_two = gain_mid.astype(F32)[:, None]
        first = jnp.concatenate(
            [quarter(w, 1) for w in (w_query, w_key, w_value, w_gate_attn)], axis=1
        )
        first = (first.astype(F32) * gain_one).astype(BF16)
        head_rows = gain_query.shape[0]
        ends = lax.dynamic_update_slice(
            jnp.zeros((gain_in.shape[0], HD), BF16),
            jnp.stack([gain_query, gain_key]),
            (0, lax.axis_index("shard") * head_rows),
        )
        first = jnp.concatenate([first, quarter(w_out, 0).T, ends], axis=1)
        found = plane_gather(first)

        def half_rows(place):
            pieces = [lax.dynamic_slice_in_dim(v, place * rows, rows, 0) for v in (tokens, cotangent)]
            return jnp.concatenate(pieces, axis=0)

        own = jnp.where(native, half_rows(core), core_swap(half_rows(1 - core)))
        tree = jnp.concatenate([seg_lengths, seg_parents], axis=0)
        tree = jnp.where(native, tree, core_swap(tree))
        own_x, own_cot = own[:rows], own[rows:]
        xa, xb = tree_rows(jnp.broadcast_to(own[None], (n_ctx,) + own.shape))

        second = jnp.concatenate([quarter(w_gate, 1), quarter(w_up, 1)], axis=1)
        second = (second.astype(F32) * gain_two).astype(BF16)
        second = jnp.concatenate([second, quarter(w_down, 0).T], axis=1)
        w2 = plane_gather(swapped(second))

        half_at = jnp.where(jnp.arange(2) == 0, core, 1 - core) * rows
        places = (
            half_at[:, None, None]
            + jnp.arange(n_ctx, dtype=jnp.int32)[None, :, None] * (2 * rows)
            + jnp.arange(rows, dtype=jnp.int32)[None, None, :]
        ).reshape(-1)
        segment, parent_seg, grand_seg, position = tree_layout(tree[0], tree[1], places)
        of_row = jnp.stack([segment, parent_seg, grand_seg, places], axis=1)
        of_column = jnp.stack([segment, places], axis=0)
        cosine, sine = rope_tables(position, HD)

        found, xa, xb, of_row, of_column, cosine, sine = lax.optimization_barrier(
            (found, xa, xb, of_row, of_column, cosine, sine)
        )
        found = found.reshape(pairs, n_tp, gain_in.shape[0], -1)
        core_at = core.astype(jnp.int32).reshape(1)
        other = core_swap(sibling_part(core_at, found))
        w1 = join_cores(core_at, found, other).reshape(-1, first.shape[1])

        xn, pre, low, gate, gains = project(xa, xb, w1, cosine, sine)
        probs, attended, gated, mine, other = attend(low, gate, w1, of_row, of_column)
        x_flip = flip(xn)
        middle, spread = middle_step(ctx_exchange(tree_half(mine, other)), own_x, (x_flip,))
        ua, ub = (flat(v) for v in tree_rows(spread))
        u_flip = flip(ua, ub)

        hidden, d_gate, d_up = feed(ua, ub, xa, xb, w2, (u_flip,))
        ffn = feed_grads(u_flip, xa, xb, d_gate, d_up, hidden, ())
        half = tree_half(*feed_back(d_gate, d_up, w2, (ffn,)))
        d_middle, spread = d_middle_step(ctx_exchange(half), middle, own_cot)
        layer_mine, layer_other = down_product(hidden, w2, 2, (half,))
        da, db, layer_mine, layer_other = tree_rows(spread, layer_mine, layer_other)
        da, db = flat(da), flat(db)
        grad_ffn = plane_scatter(ffn)

        d_attended, d_gate_pre = gate_back(da, db, w1, gate, attended)
        d_qkv, terms = attend_back(probs, low, d_attended, pre, gains, cosine, sine, ())

        def spread_terms(vector):
            return jnp.pad(vector.reshape(n_shard, 1, -1), ((0, 0), (0, 15), (0, 0)))

        wide_terms = jnp.concatenate([spread_terms(terms[0]), spread_terms(terms[1])], axis=2)
        wide_terms = jnp.pad(wide_terms, ((0, 0), (0, 0), (0, 4 * HD - 2 * head_rows)))
        x_at = (lax.axis_index("shard") // SIDE).astype(jnp.int32)
        y_at = (lax.axis_index("shard") // 2 % 2 * n_tp + tp).astype(jnp.int32)
        first, second = attend_grads(
            jnp.stack([x_at, y_at]), x_flip, da, db, d_qkv, d_gate_pre, gated, wide_terms
        )
        in_mine, in_other = input_back(d_qkv, d_gate_pre, w1, (first[0],))
        layer_half, in_half = tree_half(layer_mine, layer_other), tree_half(in_mine, in_other)
        first = turn_sums(y_at.reshape(1), turned(x_turn, first))
        second = turn_sums(x_at.reshape(1), turned(y_turn, second))
        first, second, grad_ffn = lax.optimization_barrier((first, second, grad_ffn))
        first, second = turned(y_turn, first), turned(x_turn, second)

        def owners(block):
            block = swapped(block)
            return [block] + [ctx_turn(block, by) for by in range(1, n_ctx)]

        def owners_at_once(block):
            moved = [lax.ppermute(block, ("shard", "ctx", "tp"), perm) for perm in owner_perms]
            return [jnp.where(native, block, moved[0])] + moved[1:]

        both = jnp.concatenate(
            [layer_half, in_half], axis=1
        )
        parts = [lax.dynamic_index_in_dim(both, ctx, 0, False)] + [
            ctx_turn(lax.dynamic_index_in_dim(both, (ctx + by) % n_ctx, 0, False), by)
            for by in range(1, n_ctx)
        ]
        ends = ends_step(parts, middle, d_middle, own_x)
        ffn_blocks = owners(grad_ffn)
        attn_sum = both_sums(first, second, (ends, ffn_blocks[0]))
        ends, attn_sum = lax.optimization_barrier((ends, attn_sum))
        sibling = core_swap(ends)

        def whole(start):
            mine, other = ends[start : start + rows], sibling[start : start + rows]
            return jnp.where(
                core == 0,
                jnp.concatenate([mine, other], axis=0),
                jnp.concatenate([other, mine], axis=0),
            )

        full = jnp.stack([whole(0), whole(rows)])
        full = jnp.where(native, full, lax.ppermute(full, PLANE, across_perm))

        turn_at = ctx.astype(jnp.int32).reshape(1)
        size = gain_in.shape[0]
        grad_gate, grad_up, grad_down, mid_sums = close(
            close_feed_kernel,
            turn_at,
            ffn_blocks,
            (w_gate, w_up),
            gain_two,
            w_down.shape,
            [(size, HD)],
        )
        attn_blocks = owners(attn_sum)
        grad_query, grad_key, grad_value, grad_gate_attn, grad_out, in_sums, head_ends = close(
            close_attend_kernel,
            turn_at,
            attn_blocks,
            (w_query, w_key, w_value, w_gate_attn),
            gain_one,
            w_out.shape,
            [(size, HD), (16, HD)],
        )
        gain_terms = jnp.stack([jnp.sum(in_sums, axis=1), jnp.sum(mid_sums, axis=1), head_ends[0]])
        gain_terms = gain_terms + lax.ppermute(gain_terms, "tp", [(0, 1), (1, 0)])

        return (
            full[0].astype(F32),
            full[1].astype(F32),
            gain_terms[0],
            grad_query,
            grad_key,
            grad_value,
            grad_gate_attn,
            grad_out,
            gain_terms[2, :head_rows],
            gain_terms[2, head_rows : 2 * head_rows],
            gain_terms[1],
            grad_gate,
            grad_up,
            grad_down,
        )

    return shards


def solution(mesh):
    return jax.shard_map(
        make_shards(mesh),
        mesh=mesh,
        in_specs=(
            P(("shard", "ctx"), None),
            P("shard", None),
            P("shard", None),
            P("shard"),
            P("shard", "tp"),
            P("shard", "tp"),
            P("shard", "tp"),
            P("shard", "tp"),
            P("tp", "shard"),
            P("shard"),
            P("shard"),
            P("shard"),
            P("shard", "tp"),
            P("shard", "tp"),
            P("tp", "shard"),
            P(("shard", "ctx"), None),
        ),
        out_specs=(
            P(("shard", "ctx"), None),
            P(("shard", "ctx"), None),
            P("shard"),
            P("shard", "tp"),
            P("shard", "tp"),
            P("shard", "tp"),
            P("shard", "tp"),
            P("tp", "shard"),
            P("shard"),
            P("shard"),
            P("shard"),
            P("shard", "tp"),
            P("shard", "tp"),
            P("tp", "shard"),
        ),
        check_vma=False,
    )
```

```python
import math

import jax
import jax.numpy as jnp
from jax import lax
from jax.experimental import pallas as pl
from jax.experimental.pallas import tpu as pltpu
from jax.sharding import PartitionSpec as P

HD = 128
EPS = 1e-06
BASE = 1000000.0
NEG = -1e30
F32 = jnp.float32
BF16 = jnp.bfloat16
PLANE = ("shard", "tp")
SCALE = 1.0 / math.sqrt(HD)
VMEM = 48 << 20


def lookup(onehot, table):
    return jnp.sum(onehot * table[None, :], axis=1)


def tree_layout(lengths, parents, places):
    labels = jnp.arange(lengths.shape[0], dtype=jnp.int32)
    ends = jnp.cumsum(lengths)
    starts = ends - lengths
    parent_hot = (parents[:, None] == labels[None, :]).astype(jnp.int32)
    grand = lookup(parent_hot, parents)
    parent_len = lookup(parent_hot, lengths)
    grand_hot = (grand[:, None] == labels[None, :]).astype(jnp.int32)
    grand_len = lookup(grand_hot, lengths)
    before = jnp.where(labels == 0, 0, parent_len + jnp.where(parents == 0, 0, grand_len))
    segment = jnp.sum((places[:, None] >= ends[None, :]).astype(jnp.int32), axis=1)
    token_hot = (segment[:, None] == labels[None, :]).astype(jnp.int32)
    position = places - lookup(token_hot, starts) + lookup(token_hot, before)
    return (segment, lookup(token_hot, parents), lookup(token_hot, grand), position)


def rope_tables(position, columns):
    halfway = columns // 2
    frequency = jnp.exp(jnp.arange(halfway, dtype=F32) * (-2.0 * math.log(BASE) / columns))
    angles = position.astype(F32)[:, None] * frequency[None, :]
    angles = jnp.concatenate([angles, angles], axis=1)
    return (jnp.cos(angles), jnp.sin(angles))


def rms_scale(inputs):
    return lax.rsqrt(jnp.mean(inputs * inputs, axis=-1, keepdims=True) + EPS)


def dot(left, right):
    return jnp.dot(left, right, preferred_element_type=F32)


def dot_rows(left, right):
    return lax.dot_general(left, right, (((0,), (0,)), ((), ())), preferred_element_type=F32)


def dot_back(left, right):
    return lax.dot_general(left, right, (((1,), (1,)), ((), ())), preferred_element_type=F32)


def turn(inputs):
    halfway = inputs.shape[-1] // 2
    return jnp.concatenate([-inputs[:, halfway:], inputs[:, :halfway]], axis=-1)


def unturn(inputs):
    halfway = inputs.shape[-1] // 2
    return jnp.concatenate([inputs[:, halfway:], -inputs[:, :halfway]], axis=-1)


def head(number):
    return slice(number * HD, (number + 1) * HD)


def call(kernel, grid, in_specs, out_specs, out_shape, flops, scratch=(), moved=8 << 20, behind=()):
    count = len(in_specs)

    def body(*refs):
        kernel(*refs[:count], *refs[count + len(behind) :])

    built = pl.pallas_call(
        body,
        grid=grid,
        in_specs=list(in_specs) + [pl.BlockSpec(memory_space=pl.ANY)] * len(behind),
        out_specs=out_specs,
        out_shape=out_shape,
        scratch_shapes=scratch,
        compiler_params=pltpu.CompilerParams(
            dimension_semantics=("arbitrary",) * len(grid), vmem_limit_bytes=VMEM
        ),
        cost_estimate=pl.CostEstimate(flops=flops, bytes_accessed=moved, transcendentals=0),
    )
    return lambda *operands: built(*operands, *behind)


def struct(shape, dtype):
    return jax.ShapeDtypeStruct(shape, dtype)


def fixed(shape):
    return pl.BlockSpec(shape, lambda i: (0,) * len(shape))


def rowed(rows, columns):
    return pl.BlockSpec((rows, columns), lambda i: (i, 0))


def piled(shape, which):
    return pl.BlockSpec((shape[0], shape[1] // 2, shape[2]), lambda i: (0, which, 0))


def flat(value):
    return value.reshape((-1,) + value.shape[2:])


def project_kernel(xa, xb, w, ends, cosine, sine, xn, pre, low, gate, gains):
    x = flat(jnp.where(pl.program_id(0) == 0, xa[...], xb[...])).astype(F32)
    normed = (x * rms_scale(x)).astype(BF16)
    xn[...] = normed
    out = dot(normed, w[...])
    found = jnp.zeros((16, HD), F32)
    for start in range(0, ends.shape[0], HD):
        found = found + ends[start : start + 16, :].astype(F32)
    gains[...] = found
    for place in range(3):
        raw = out[:, head(place)]
        pre[:, head(place)] = raw
        unit = raw * rms_scale(raw) * found[place // 2 : place // 2 + 1, :]
        low[:, head(place)] = (unit * cosine[...] + turn(unit) * sine[...]).astype(BF16)
    low[:, head(3)] = out[:, head(3)].astype(BF16)
    gate[...] = out[:, 4 * HD :]


def project(xa, xb, w, cosine, sine):
    half, width = xa.shape[0] * xa.shape[1] // 2, xa.shape[2]
    return call(
        project_kernel,
        (2,),
        [
            piled(xa.shape, 0),
            piled(xb.shape, 0),
            fixed((width, 6 * HD)),
            pl.BlockSpec((width, HD), lambda i: (0, 8)),
            rowed(half, HD),
            rowed(half, HD),
        ],
        [
            rowed(half, width),
            rowed(half, 3 * HD),
            rowed(half, 4 * HD),
            rowed(half, 2 * HD),
            fixed((16, HD)),
        ],
        [
            struct((2 * half, width), BF16),
            struct((2 * half, 3 * HD), F32),
            struct((2 * half, 4 * HD), BF16),
            struct((2 * half, 2 * HD), F32),
            struct((16, HD), F32),
        ],
        2 * 2 * half * width * 6 * HD,
    )(xa, xb, w, w, cosine, sine)


def attend_kernel(low, gate, w_out, of_row, of_column, probs, attended, gated, mine, other):
    step = pl.program_id(0)
    half = probs.shape[1]
    rows = pl.ds(step * half, half)
    key, value = low[:, head(2)], low[:, head(3)]
    seg, par, grand, place = (of_row[rows, n : n + 1] for n in range(4))
    key_seg, key_place = of_column[0:1, :], of_column[1:2, :]
    allowed = ((key_seg == seg) | (key_seg == par) | (key_seg == grand)) & (key_place <= place)
    for number in range(2):
        scores = dot_back(low[rows, head(number)], key) * SCALE
        scores = jnp.where(allowed, scores, NEG)
        raised = jnp.exp(scores - jnp.max(scores, axis=-1, keepdims=True))
        share = raised / jnp.sum(raised, axis=-1, keepdims=True)
        probs[number] = share
        seen = dot(share.astype(BF16), value)
        attended[:, head(number)] = seen
        gated[:, head(number)] = (seen * jax.nn.sigmoid(gate[:, head(number)])).astype(BF16)
    out = dot_back(gated[...], w_out[...])

    @pl.when(step == 0)
    def _():
        mine[...] = out.astype(BF16)

    @pl.when(step == 1)
    def _():
        other[...] = out.astype(BF16)


def attend(low, gate, w, of_row, of_column):
    length = low.shape[0]
    half, width = length // 2, w.shape[0]
    return call(
        attend_kernel,
        (2,),
        [
            fixed((length, 4 * HD)),
            rowed(half, 2 * HD),
            pl.BlockSpec((width, 2 * HD), lambda i: (0, 3)),
            fixed((length, 4)),
            fixed((2, length)),
        ],
        [
            pl.BlockSpec((2, half, length), lambda i: (0, i, 0)),
            rowed(half, 2 * HD),
            rowed(half, 2 * HD),
            fixed((half, width)),
            fixed((half, width)),
        ],
        [
            struct((2, length, length), F32),
            struct((length, 2 * HD), F32),
            struct((length, 2 * HD), BF16),
            struct((half, width), BF16),
            struct((half, width), BF16),
        ],
        2 * length * width * 2 * HD + 8 * length * length * HD,
    )(low, gate, w, of_row, of_column)


def flip_kernel(pieces, out):
    at = 0
    for piece in pieces:
        out[:, at : at + piece.shape[0]] = piece[...].T
        at += piece.shape[0]


def flip(*pieces):
    length, width = sum(piece.shape[0] for piece in pieces), pieces[0].shape[1]
    chunk = 2 * HD
    return call(
        lambda *refs: flip_kernel(refs[:-1], refs[-1]),
        (width // chunk,),
        [pl.BlockSpec((piece.shape[0], chunk), lambda i: (0, i)) for piece in pieces],
        rowed(chunk, length),
        struct((width, length), BF16),
        1 << 20,
    )(*pieces)


def feed_kernel(ua, ub, ca, cb, wg, wu, wd, hidden, d_gate, d_up):
    half = ua.shape[0]
    for number, (u, cot) in enumerate(((ua, ca), (ub, cb))):
        rows = slice(number * half, (number + 1) * half)
        gate, up = dot(u[...], wg[...]), dot(u[...], wu[...])
        d_hidden = dot(flat(cot[...]), wd[...])
        sig = jax.nn.sigmoid(gate)
        silu = gate * sig
        hidden[rows, :] = (silu * up).astype(BF16)
        d_gate[rows, :] = (d_hidden * up * sig * (1.0 + gate * (1.0 - sig))).astype(BF16)
        d_up[rows, :] = (d_hidden * silu).astype(BF16)


def feed(ua, ub, ca, cb, w, behind):
    half, width = ua.shape
    chunk = 2 * HD
    parts = w.shape[1] // 3 // chunk
    column = lambda shift: pl.BlockSpec((width, chunk), lambda i: (0, shift * parts + i))
    unit = pl.BlockSpec((2 * half, chunk), lambda i: (0, i))
    units = parts * chunk
    return call(
        feed_kernel,
        (parts,),
        [fixed((half, width))] * 2
        + [piled(ca.shape, 1)] * 2
        + [column(0), column(1), column(2)],
        [unit, unit, unit],
        [struct((2 * half, units), BF16)] * 3,
        2 * 2 * half * width * units * 3,
        behind=behind,
    )(ua, ub, ca, cb, w, w, w)


def feed_back_kernel(d_gate, d_up, wg, wu, mine, other):
    half = mine.shape[0]
    out = dot_back(d_gate[...], wg[...]) + dot_back(d_up[...], wu[...])
    mine[...] = out[:half, :].astype(BF16)
    other[...] = out[half:, :].astype(BF16)


def feed_back(d_gate, d_up, w, behind):
    length, units = d_gate.shape
    half, width = length // 2, w.shape[0]
    chunk = 4 * HD
    slab = pl.BlockSpec((half, chunk), lambda i: (0, i))
    return call(
        feed_back_kernel,
        (width // chunk,),
        [fixed((length, units))] * 2
        + [
            pl.BlockSpec((chunk, units), lambda i: (i, 0)),
            pl.BlockSpec((chunk, units), lambda i: (i, 1)),
        ],
        [slab, slab],
        [struct((half, width), BF16), struct((half, width), BF16)],
        2 * length * width * units * 2,
        behind=behind,
    )(d_gate, d_up, w, w)


def down_kernel(hidden, w, mine, other):
    out = dot_back(hidden[...], w[...])

    @pl.when(pl.program_id(0) == 0)
    def _():
        mine[...] = out.astype(BF16)

    @pl.when(pl.program_id(0) == 1)
    def _():
        other[...] = out.astype(BF16)


def down_product(left, w, place, behind):
    length, units = left.shape
    half, width = length // 2, w.shape[0]
    return call(
        down_kernel,
        (2,),
        [rowed(half, units), pl.BlockSpec((width, units), lambda i: (0, place))],
        [fixed((half, width)), fixed((half, width))],
        [struct((half, width), BF16), struct((half, width), BF16)],
        2 * length * width * units,
        behind=behind,
    )(left, w)


def spread_blocks(flipped, right, out, start):
    term = dot(flipped, right).astype(BF16)
    for place in range(flipped.shape[0] // HD):
        for owner in range(right.shape[1] // HD):
            at = start + place * HD
            out[owner * HD : (owner + 1) * HD, at : at + HD] = term[head(place), head(owner)]


def feed_grads_kernel(u_flip, ca, cb, d_gate, d_up, hidden, out, flipped):
    @pl.when(pl.program_id(0) == 0)
    def _():
        flipped[...] = hidden[...].T

    units = hidden.shape[1]
    out[:, :units] = dot(u_flip[...], d_gate[...]).astype(BF16)
    out[:, units : 2 * units] = dot(u_flip[...], d_up[...]).astype(BF16)
    cot = jnp.concatenate([flat(ca[...]), flat(cb[...])], axis=0)
    spread_blocks(flipped[...], cot, out, 2 * units)


def feed_grads(u_flip, ca, cb, d_gate, d_up, hidden, behind):
    width, length = u_flip.shape
    units = hidden.shape[1]
    chunk = 4 * HD
    return call(
        feed_grads_kernel,
        (width // chunk,),
        [rowed(chunk, length)]
        + [pl.BlockSpec((ca.shape[0], ca.shape[1] // 2, chunk), lambda i: (0, 1, i))] * 2
        + [fixed((length, units))] * 3,
        rowed(chunk, 3 * units),
        struct((width, 3 * units), BF16),
        2 * length * width * units * 3,
        scratch=[pltpu.VMEM((units, length), BF16)],
        behind=behind,
    )(u_flip, ca, cb, d_gate, d_up, hidden)


def gate_back_kernel(da, db, w_out, gate, attended, d_attended, d_gate):
    half = da.shape[0]
    for number, low in enumerate((da, db)):
        rows = slice(number * half, (number + 1) * half)
        d_gated = dot(low[...], w_out[...])
        sig = jax.nn.sigmoid(gate[rows, :])
        d_attended[rows, :] = (d_gated * sig).astype(BF16)
        d_gate[rows, :] = (d_gated * attended[rows, :] * sig * (1.0 - sig)).astype(BF16)


def gate_back(da, db, w, gate, attended):
    half, width = da.shape
    wide = (2 * half, 2 * HD)
    return call(
        gate_back_kernel,
        (1,),
        [fixed((half, width))] * 2
        + [pl.BlockSpec((width, 2 * HD), lambda i: (0, 3)), fixed(wide), fixed(wide)],
        [fixed(wide), fixed(wide)],
        [struct(wide, BF16), struct(wide, BF16)],
        2 * 2 * half * width * 2 * HD,
    )(da, db, w, gate, attended)


def head_back(grads, inputs, gain):
    factor = rms_scale(inputs)
    scaled = gain * grads
    back = factor * scaled - inputs * factor**3 * jnp.mean(scaled * inputs, axis=-1, keepdims=True)
    return back.astype(BF16), jnp.sum(grads * inputs * factor, axis=0, keepdims=True)


def attend_back_kernel(
    probs, low, d_attended, pre, gains, cosine, sine, out, terms, d_key, d_value
):
    step = pl.program_id(0)
    half = probs.shape[1]
    start = pl.multiple_of(step * half, half)
    rows = pl.ds(start, half)
    key, value = low[:, head(2)], low[:, head(3)]
    cos_rows, sin_rows = cosine[rows, :], sine[rows, :]

    @pl.when(step == 0)
    def _():
        d_key[...] = jnp.zeros_like(d_key)
        d_value[...] = jnp.zeros_like(d_value)
        terms[...] = jnp.zeros_like(terms)

    for number in range(2):
        share = probs[number]
        d_seen = d_attended[:, head(number)]
        d_share = dot_back(d_seen, value)
        d_scores = share * (d_share - jnp.sum(share * d_share, axis=-1, keepdims=True))
        d_scores = d_scores.astype(BF16)
        d_query = dot(d_scores, key) * SCALE
        d_key[...] += dot_rows(d_scores, low[rows, head(number)])
        d_value[...] += dot_rows(share.astype(BF16), d_seen)
        grads = d_query * cos_rows + unturn(d_query * sin_rows)
        back, term = head_back(grads, pre[rows, head(number)], gains[0:1, :])
        out[rows, head(number)] = back
        terms[0:1, :] += term

    @pl.when(step == 1)
    def _():
        grads = d_key[...] * SCALE
        grads = grads * cosine[...] + unturn(grads * sine[...])
        back, term = head_back(grads, pre[:, head(2)], gains[1:2, :])
        out[:, head(2)] = back
        terms[1:2, :] = term
        out[:, head(3)] = d_value[...].astype(BF16)


def attend_back(probs, low, d_attended, pre, gains, cosine, sine, behind):
    length = low.shape[0]
    half = length // 2
    return call(
        attend_back_kernel,
        (2,),
        [
            pl.BlockSpec((2, half, length), lambda i: (0, i, 0)),
            fixed((length, 4 * HD)),
            rowed(half, 2 * HD),
            fixed((length, 3 * HD)),
            fixed((16, HD)),
            fixed((length, HD)),
            fixed((length, HD)),
        ],
        [fixed((length, 4 * HD)), fixed((8, HD))],
        [struct((length, 4 * HD), BF16), struct((8, HD), F32)],
        20 * length * length * HD,
        scratch=[pltpu.VMEM((length, HD), F32), pltpu.VMEM((length, HD), F32)],
        behind=behind,
    )(probs, low, d_attended, pre, gains, cosine, sine)


def input_back_kernel(d_qkv, d_gate, w, mine, other):
    out = dot_back(d_qkv[...], w[:, : 4 * HD]) + dot_back(d_gate[...], w[:, 4 * HD :])

    @pl.when(pl.program_id(0) == 0)
    def _():
        mine[...] = out.astype(BF16)

    @pl.when(pl.program_id(0) == 1)
    def _():
        other[...] = out.astype(BF16)


def input_back(d_qkv, d_gate, w, behind):
    length = d_qkv.shape[0]
    half, width = length // 2, w.shape[0]
    return call(
        input_back_kernel,
        (2,),
        [rowed(half, 4 * HD), rowed(half, 2 * HD), fixed((width, 6 * HD))],
        [fixed((half, width)), fixed((half, width))],
        [struct((half, width), BF16), struct((half, width), BF16)],
        2 * length * width * 6 * HD,
        behind=behind,
    )(d_qkv, d_gate, w)


def attend_grads_kernel(x_flip, da, db, d_qkv, d_gate, gated, out, flipped):
    @pl.when(pl.program_id(0) == 0)
    def _():
        flipped[...] = gated[...].T

    inner, split = d_qkv.shape[1], d_gate.shape[1]
    out[:, :inner] = dot(x_flip[...], d_qkv[...]).astype(BF16)
    out[:, inner : inner + split] = dot(x_flip[...], d_gate[...]).astype(BF16)
    spread_blocks(
        flipped[...], jnp.concatenate([da[...], db[...]], axis=0), out, inner + split
    )


def attend_grads(x_flip, da, db, d_qkv, d_gate, gated, behind):
    width, length = x_flip.shape
    columns = d_qkv.shape[1] + d_gate.shape[1] + gated.shape[1]
    chunk = 4 * HD
    slab = pl.BlockSpec((length // 2, chunk), lambda i: (0, i))
    return call(
        attend_grads_kernel,
        (width // chunk,),
        [
            rowed(chunk, length),
            slab,
            slab,
            fixed(d_qkv.shape),
            fixed(d_gate.shape),
            fixed(gated.shape),
        ],
        rowed(chunk, columns),
        struct((width, columns), BF16),
        2 * length * width * columns,
        scratch=[pltpu.VMEM(gated.shape[::-1], BF16)],
        behind=behind,
    )(x_flip, da, db, d_qkv, d_gate, gated)


def middle_kernel(parts, x, middle, spread):
    total = x[...].astype(F32) + jnp.sum(parts[...].astype(F32), axis=0)
    middle[...] = total
    low = (total * rms_scale(total)).astype(BF16)
    for number in range(spread.shape[0]):
        spread[number] = low


def middle_step(parts, x, behind):
    shape = x.shape
    return call(
        middle_kernel,
        (1,),
        [fixed(parts.shape), fixed(shape)],
        [fixed(shape), fixed(parts.shape)],
        [struct(shape, F32), struct(parts.shape, BF16)],
        1 << 20,
        behind=behind,
    )(parts, x)


def norm_back(grads, inputs):
    factor = rms_scale(inputs)
    return factor * grads - inputs * factor**3 * jnp.mean(grads * inputs, axis=-1, keepdims=True)


def d_middle_kernel(parts, middle, cot, d_middle, spread):
    grads = jnp.sum(parts[...].astype(F32), axis=0)
    total = cot[...].astype(F32) + norm_back(grads, middle[...])
    d_middle[...] = total
    for number in range(spread.shape[0]):
        spread[number] = total.astype(BF16)


def d_middle_step(parts, middle, cot):
    shape = cot.shape
    return call(
        d_middle_kernel,
        (1,),
        [fixed(parts.shape), fixed(shape), fixed(shape)],
        [fixed(shape), fixed(parts.shape)],
        [struct(shape, F32), struct(parts.shape, BF16)],
        1 << 20,
    )(parts, middle, cot)


def ends_kernel(parts, middle, d_middle, x, out):
    rows = x.shape[0]
    total = sum(part[...].astype(F32) for part in parts)
    out[:rows, :] = (middle[...] + total[:rows, :]).astype(BF16)
    back = norm_back(total[rows:, :], x[...].astype(F32))
    out[rows:, :] = (d_middle[...] + back).astype(BF16)


def ends_step(parts, middle, d_middle, x):
    shape, wide = x.shape, parts[0].shape
    count = len(parts)
    return call(
        lambda *refs: ends_kernel(refs[:count], *refs[count:]),
        (1,),
        [fixed(wide)] * count + [fixed(shape)] * 3,
        fixed(wide),
        struct(wide, BF16),
        1 << 20,
    )(*parts, middle, d_middle, x)


def sum_kernel(parts, out):
    out[...] = jnp.sum(parts[...].astype(F32), axis=0).astype(BF16)


def sum_step(parts, behind):
    return call(
        sum_kernel,
        (1,),
        [fixed(parts.shape)],
        fixed(parts.shape[1:]),
        struct(parts.shape[1:], BF16),
        1 << 20,
        behind=behind,
    )(parts)


def prefetched(kernel, grid, in_specs, out_specs, out_shape):
    return pl.pallas_call(
        kernel,
        grid_spec=pltpu.PrefetchScalarGridSpec(
            num_scalar_prefetch=1, grid=grid, in_specs=in_specs, out_specs=out_specs
        ),
        out_shape=out_shape,
        compiler_params=pltpu.CompilerParams(
            dimension_semantics=("arbitrary",) * len(grid), vmem_limit_bytes=VMEM
        ),
        cost_estimate=pl.CostEstimate(flops=1 << 20, bytes_accessed=8 << 20, transcendentals=0),
    )


def copy_kernel(core, source, out):
    out[...] = source[...]


def sibling_part(core, found):
    pairs, _, rows, columns = found.shape
    return prefetched(
        copy_kernel,
        (pairs // 2,),
        [pl.BlockSpec((2, None, rows, columns), lambda i, at: (i, 1 - at[0], 0, 0))],
        pl.BlockSpec((2, rows, columns), lambda i, at: (i, 0, 0)),
        struct((pairs, rows, columns), found.dtype),
    )(core, found)


def join_kernel(core, mine, other, out):
    out[:, core[0]] = mine[...]
    out[:, 1 - core[0]] = other[...]


def join_cores(core, found, other):
    pairs, _, rows, columns = found.shape
    return prefetched(
        join_kernel,
        (pairs // 2,),
        [
            pl.BlockSpec((2, None, rows, columns), lambda i, at: (i, at[0], 0, 0)),
            pl.BlockSpec((2, rows, columns), lambda i, at: (i, 0, 0)),
        ],
        pl.BlockSpec((2, 2, rows, columns), lambda i, at: (i, 0, 0, 0)),
        struct(found.shape, found.dtype),
    )(core, found, other)


def lanes(value):
    return sum(value[:, start : start + HD] for start in range(0, value.shape[1], HD))


def pick(blocks):
    step = pl.program_id(0)
    value = blocks[0][...]
    for number in range(1, len(blocks)):
        value = jnp.where(step == number, blocks[number][...], value)
    return value.astype(F32)


def close_feed_kernel(turn_at, b0, b1, b2, b3, w_gate, w_up, gain, g_gate, g_up, g_down, sums):
    raw = pick((b0, b1, b2, b3))
    units = w_gate.shape[1]
    raw_gate, raw_up = raw[:, :units], raw[:, units : 2 * units]
    g_gate[...] = raw_gate * gain[...]
    g_up[...] = raw_up * gain[...]
    for place in range(units // HD):
        g_down[head(place), :] = raw[:, 2 * units + place * HD : 2 * units + (place + 1) * HD]
    term = lanes(raw_gate * w_gate[...].astype(F32)) + lanes(raw_up * w_up[...].astype(F32))

    @pl.when(pl.program_id(0) == 0)
    def _():
        sums[...] = term

    @pl.when(pl.program_id(0) > 0)
    def _():
        sums[...] += term


def close_attend_kernel(
    turn_at, b0, b1, b2, b3, wq, wk, wv, wg, gain, gq, gk, gv, gg, go, sums
):
    found = pick((b0, b1, b2, b3))
    inner, outer, scale = found[:, : 4 * HD], found[:, 4 * HD :], gain[...]
    raw_q, raw_k, raw_v = inner[:, : 2 * HD], inner[:, head(2)], inner[:, head(3)]
    raw_g = outer[:, : 2 * HD]
    gq[...], gk[...], gv[...], gg[...] = raw_q * scale, raw_k * scale, raw_v * scale, raw_g * scale
    go[head(0), :], go[head(1), :] = outer[:, head(2)], outer[:, head(3)]
    pairs = ((raw_q, wq), (raw_k, wk), (raw_v, wv), (raw_g, wg))
    term = sum(lanes(raw * w[...].astype(F32)) for raw, w in pairs)

    @pl.when(pl.program_id(0) == 0)
    def _():
        sums[...] = term

    @pl.when(pl.program_id(0) > 0)
    def _():
        sums[...] += term


def close(kernel, turn_at, blocks, weights, gain, out_rows, extra):
    quarters = 4
    place = lambda i, at: (at[0] + quarters - i) % quarters
    whole = lambda value: pl.BlockSpec(value.shape, lambda i, at: (0, 0))
    columns = lambda w: pl.BlockSpec(
        (w.shape[0], w.shape[1] // quarters), lambda i, at: (0, place(i, at))
    )
    rows, width = out_rows
    in_specs = [whole(b) for b in blocks] + [columns(w) for w in weights] + [whole(gain)]
    out_specs = [columns(w) for w in weights]
    out_specs += [pl.BlockSpec((rows // quarters, width), lambda i, at: (place(i, at), 0))]
    out_specs += [pl.BlockSpec(shape, lambda i, at: (0, 0)) for shape in extra]
    out_shape = [struct(w.shape, F32) for w in weights] + [struct(out_rows, F32)]
    out_shape += [struct(shape, F32) for shape in extra]
    return prefetched(kernel, (quarters,), in_specs, out_specs, out_shape)(
        turn_at, *blocks, *weights, gain
    )


def make_shards(mesh):
    n_shard, n_ctx, n_tp = mesh.shape["shard"], mesh.shape["ctx"], mesh.shape["tp"]
    pairs = n_shard // 2

    def joint(pair, core, tp):
        return (pair * 2 + core) * n_tp + tp

    core_perm = [(i, i ^ 1) for i in range(n_shard)]
    planes = [
        [joint(pair, core, tp) for pair in range(pairs) for tp in range(n_tp)] for core in range(2)
    ]
    swap_perm = [
        edge
        for pair in range(pairs)
        for edge in (
            (joint(pair, 1, 0), joint(pair, 0, 1)),
            (joint(pair, 0, 1), joint(pair, 1, 0)),
        )
    ]
    across_perm = [(joint(pair, t, t), joint(pair, t, 1 - t)) for pair in range(pairs) for t in range(2)]

    def spot(pair, core, ctx, tp):
        return ((pair * 2 + core) * n_ctx + ctx) * n_tp + tp

    owner_perms = [
        [
            (spot(pair, core, ctx, tp), spot(pair, tp, (ctx + by) % n_ctx, core))
            for pair in range(pairs)
            for core in range(2)
            for ctx in range(n_ctx)
            for tp in range(n_tp)
            if by > 0 or core != tp
        ]
        for by in range(n_ctx)
    ]

    def core_swap(value):
        return lax.ppermute(value, "shard", core_perm)

    def ctx_exchange(value):
        return lax.all_to_all(value, "ctx", 0, 0)

    def ctx_turn(value, by):
        return lax.ppermute(value, "ctx", [(i, (i + by) % n_ctx) for i in range(n_ctx)])

    def tree_rows(spread, *before):
        mine = ctx_exchange(spread)
        if before:
            mine, *before = lax.optimization_barrier((mine, *before))
        return mine, core_swap(mine), *before

    def tree_half(mine, other):
        half = (mine.astype(F32) + core_swap(other).astype(F32)).astype(BF16)
        return half.reshape((n_ctx, -1) + half.shape[1:])

    def plane_gather(value):
        return lax.all_gather(value, PLANE, axis=0, tiled=True, axis_index_groups=planes)

    def plane_scatter(value):
        return lax.psum_scatter(
            value, PLANE, scatter_dimension=0, tiled=True, axis_index_groups=planes
        )

    def plane_exchange(value):
        return lax.all_to_all(value, PLANE, 0, 0, axis_index_groups=planes)

    def shards(
        tokens,
        seg_lengths,
        seg_parents,
        gain_in,
        w_query,
        w_key,
        w_value,
        w_gate_attn,
        w_out,
        gain_query,
        gain_key,
        gain_mid,
        w_gate,
        w_up,
        w_down,
        cotangent,
    ):
        core = lax.axis_index("shard") % 2
        tp = lax.axis_index("tp")
        ctx = lax.axis_index("ctx")
        native = core == tp
        rows = tokens.shape[0] // 2

        def swapped(value):
            return jnp.where(native, value, lax.ppermute(value, PLANE, swap_perm))

        def quarter(weight, axis):
            size = weight.shape[axis] // n_ctx
            return lax.dynamic_slice_in_dim(weight, ctx * size, size, axis)

        gain_one = gain_in.astype(F32)[:, None]
        gain_two = gain_mid.astype(F32)[:, None]
        first = jnp.concatenate(
            [quarter(w, 1) for w in (w_query, w_key, w_value, w_gate_attn)], axis=1
        )
        first = (first.astype(F32) * gain_one).astype(BF16)
        head_rows = gain_query.shape[0]
        ends = lax.dynamic_update_slice(
            jnp.zeros((gain_in.shape[0], HD), BF16),
            jnp.stack([gain_query, gain_key]),
            (0, lax.axis_index("shard") * head_rows),
        )
        first = jnp.concatenate([first, quarter(w_out, 0).T, ends], axis=1)
        found = plane_gather(first)

        def half_rows(place):
            pieces = [lax.dynamic_slice_in_dim(v, place * rows, rows, 0) for v in (tokens, cotangent)]
            return jnp.concatenate(pieces, axis=0)

        own = jnp.where(native, half_rows(core), core_swap(half_rows(1 - core)))
        tree = jnp.concatenate([seg_lengths, seg_parents], axis=0)
        tree = jnp.where(native, tree, core_swap(tree))
        own_x, own_cot = own[:rows], own[rows:]
        xa, xb = tree_rows(jnp.broadcast_to(own[None], (n_ctx,) + own.shape))

        second = jnp.concatenate([quarter(w_gate, 1), quarter(w_up, 1)], axis=1)
        second = (second.astype(F32) * gain_two).astype(BF16)
        second = jnp.concatenate([second, quarter(w_down, 0).T], axis=1)
        w2 = plane_gather(swapped(second))

        half_at = jnp.where(jnp.arange(2) == 0, core, 1 - core) * rows
        places = (
            half_at[:, None, None]
            + jnp.arange(n_ctx, dtype=jnp.int32)[None, :, None] * (2 * rows)
            + jnp.arange(rows, dtype=jnp.int32)[None, None, :]
        ).reshape(-1)
        segment, parent_seg, grand_seg, position = tree_layout(tree[0], tree[1], places)
        of_row = jnp.stack([segment, parent_seg, grand_seg, places], axis=1)
        of_column = jnp.stack([segment, places], axis=0)
        cosine, sine = rope_tables(position, HD)

        found, xa, xb, of_row, of_column, cosine, sine = lax.optimization_barrier(
            (found, xa, xb, of_row, of_column, cosine, sine)
        )
        found = found.reshape(pairs, n_tp, gain_in.shape[0], -1)
        core_at = core.astype(jnp.int32).reshape(1)
        other = core_swap(sibling_part(core_at, found))
        w1 = join_cores(core_at, found, other).reshape(-1, first.shape[1])

        xn, pre, low, gate, gains = project(xa, xb, w1, cosine, sine)
        probs, attended, gated, mine, other = attend(low, gate, w1, of_row, of_column)
        x_flip = flip(xn)
        middle, spread = middle_step(ctx_exchange(tree_half(mine, other)), own_x, (x_flip,))
        ua, ub = (flat(v) for v in tree_rows(spread))
        u_flip = flip(ua, ub)

        hidden, d_gate, d_up = feed(ua, ub, xa, xb, w2, (u_flip,))
        ffn = feed_grads(u_flip, xa, xb, d_gate, d_up, hidden, ())
        half = tree_half(*feed_back(d_gate, d_up, w2, (ffn,)))
        d_middle, spread = d_middle_step(ctx_exchange(half), middle, own_cot)
        layer_mine, layer_other = down_product(hidden, w2, 2, (half,))
        da, db, layer_mine, layer_other = tree_rows(spread, layer_mine, layer_other)
        da, db = flat(da), flat(db)
        grad_ffn = plane_scatter(ffn)

        d_attended, d_gate_pre = gate_back(da, db, w1, gate, attended)
        d_qkv, terms = attend_back(probs, low, d_attended, pre, gains, cosine, sine, ())

        pieces = jnp.concatenate(
            [terms[0].reshape(n_shard, -1), terms[1].reshape(n_shard, -1)], axis=1
        )
        copies = n_ctx * n_tp
        pieces = jnp.pad(pieces, ((0, 0), (0, HD - pieces.shape[1]))).astype(BF16)
        pieces = jnp.broadcast_to(pieces[:, None, None], (n_shard, copies, 8, HD))
        pieces = lax.all_to_all(
            pieces.reshape(n_shard * copies, 8, HD), ("shard", "ctx", "tp"), 0, 0
        )
        head_ends = jnp.sum(pieces.astype(F32), axis=0)
        attn = attend_grads(x_flip, da, db, d_qkv, d_gate_pre, gated, ())
        in_mine, in_other = input_back(d_qkv, d_gate_pre, w1, (attn,))
        layer_half, in_half = tree_half(layer_mine, layer_other), tree_half(in_mine, in_other)
        attn, layer_half, in_half, grad_ffn, head_ends = lax.optimization_barrier(
            (attn, layer_half, in_half, grad_ffn, head_ends)
        )
        attn_parts = plane_exchange(attn.reshape(n_shard, -1, attn.shape[1]))

        def owners(block):
            block = swapped(block)
            return [block] + [ctx_turn(block, by) for by in range(1, n_ctx)]

        def owners_at_once(block):
            moved = [lax.ppermute(block, ("shard", "ctx", "tp"), perm) for perm in owner_perms]
            return [jnp.where(native, block, moved[0])] + moved[1:]

        both = jnp.concatenate(
            [layer_half, in_half], axis=1
        )
        parts = [lax.dynamic_index_in_dim(both, ctx, 0, False)] + [
            ctx_turn(lax.dynamic_index_in_dim(both, (ctx + by) % n_ctx, 0, False), by)
            for by in range(1, n_ctx)
        ]
        ends = ends_step(parts, middle, d_middle, own_x)
        ffn_blocks = owners(grad_ffn)
        sibling = core_swap(ends)

        def whole(start):
            mine, other = ends[start : start + rows], sibling[start : start + rows]
            return jnp.where(
                core == 0,
                jnp.concatenate([mine, other], axis=0),
                jnp.concatenate([other, mine], axis=0),
            )

        full = jnp.stack([whole(0), whole(rows)])
        attn_sum = sum_step(attn_parts, (full, ffn_blocks[0]))
        full, attn_sum = lax.optimization_barrier((full, attn_sum))
        full = jnp.where(native, full, lax.ppermute(full, PLANE, across_perm))

        turn_at = ctx.astype(jnp.int32).reshape(1)
        size = gain_in.shape[0]
        grad_gate, grad_up, grad_down, mid_sums = close(
            close_feed_kernel,
            turn_at,
            ffn_blocks,
            (w_gate, w_up),
            gain_two,
            w_down.shape,
            [(size, HD)],
        )
        attn_blocks = owners(attn_sum)
        grad_query, grad_key, grad_value, grad_gate_attn, grad_out, in_sums = close(
            close_attend_kernel,
            turn_at,
            attn_blocks,
            (w_query, w_key, w_value, w_gate_attn),
            gain_one,
            w_out.shape,
            [(size, HD)],
        )
        gain_terms = jnp.stack([jnp.sum(in_sums, axis=1), jnp.sum(mid_sums, axis=1)])
        gain_terms = gain_terms + lax.ppermute(gain_terms, "tp", [(0, 1), (1, 0)])

        return (
            full[0].astype(F32),
            full[1].astype(F32),
            gain_terms[0],
            grad_query,
            grad_key,
            grad_value,
            grad_gate_attn,
            grad_out,
            head_ends[0, :head_rows],
            head_ends[0, head_rows : 2 * head_rows],
            gain_terms[1],
            grad_gate,
            grad_up,
            grad_down,
        )

    return shards


def solution(mesh):
    return jax.shard_map(
        make_shards(mesh),
        mesh=mesh,
        in_specs=(
            P(("shard", "ctx"), None),
            P("shard", None),
            P("shard", None),
            P("shard"),
            P("shard", "tp"),
            P("shard", "tp"),
            P("shard", "tp"),
            P("shard", "tp"),
            P("tp", "shard"),
            P("shard"),
            P("shard"),
            P("shard"),
            P("shard", "tp"),
            P("shard", "tp"),
            P("tp", "shard"),
            P(("shard", "ctx"), None),
        ),
        out_specs=(
            P(("shard", "ctx"), None),
            P(("shard", "ctx"), None),
            P("shard"),
            P("shard", "tp"),
            P("shard", "tp"),
            P("shard", "tp"),
            P("shard", "tp"),
            P("tp", "shard"),
            P("shard"),
            P("shard"),
            P("shard"),
            P("shard", "tp"),
            P("shard", "tp"),
            P("tp", "shard"),
        ),
        check_vma=False,
    )
```

```python
import math

import jax
import jax.numpy as jnp
from jax import lax
from jax.experimental import pallas as pl
from jax.experimental.pallas import tpu as pltpu
from jax.sharding import PartitionSpec as P

HD = 128
EPS = 1e-06
BASE = 1000000.0
NEG = -1e30
F32 = jnp.float32
BF16 = jnp.bfloat16
PLANE = ("shard", "tp")
SCALE = 1.0 / math.sqrt(HD)
VMEM = 48 << 20


def lookup(onehot, table):
    return jnp.sum(onehot * table[None, :], axis=1)


def tree_layout(lengths, parents, places):
    labels = jnp.arange(lengths.shape[0], dtype=jnp.int32)
    ends = jnp.cumsum(lengths)
    starts = ends - lengths
    parent_hot = (parents[:, None] == labels[None, :]).astype(jnp.int32)
    grand = lookup(parent_hot, parents)
    parent_len = lookup(parent_hot, lengths)
    grand_hot = (grand[:, None] == labels[None, :]).astype(jnp.int32)
    grand_len = lookup(grand_hot, lengths)
    before = jnp.where(labels == 0, 0, parent_len + jnp.where(parents == 0, 0, grand_len))
    segment = jnp.sum((places[:, None] >= ends[None, :]).astype(jnp.int32), axis=1)
    token_hot = (segment[:, None] == labels[None, :]).astype(jnp.int32)
    position = places - lookup(token_hot, starts) + lookup(token_hot, before)
    return (segment, lookup(token_hot, parents), lookup(token_hot, grand), position)


def rope_tables(position, columns):
    halfway = columns // 2
    frequency = jnp.exp(jnp.arange(halfway, dtype=F32) * (-2.0 * math.log(BASE) / columns))
    angles = position.astype(F32)[:, None] * frequency[None, :]
    angles = jnp.concatenate([angles, angles], axis=1)
    return (jnp.cos(angles), jnp.sin(angles))


def rms_scale(inputs):
    return lax.rsqrt(jnp.mean(inputs * inputs, axis=-1, keepdims=True) + EPS)


def dot(left, right):
    return jnp.dot(left, right, preferred_element_type=F32)


def dot_rows(left, right):
    return lax.dot_general(left, right, (((0,), (0,)), ((), ())), preferred_element_type=F32)


def dot_back(left, right):
    return lax.dot_general(left, right, (((1,), (1,)), ((), ())), preferred_element_type=F32)


def turn(inputs):
    halfway = inputs.shape[-1] // 2
    return jnp.concatenate([-inputs[:, halfway:], inputs[:, :halfway]], axis=-1)


def unturn(inputs):
    halfway = inputs.shape[-1] // 2
    return jnp.concatenate([inputs[:, halfway:], -inputs[:, :halfway]], axis=-1)


def head(number):
    return slice(number * HD, (number + 1) * HD)


def call(kernel, grid, in_specs, out_specs, out_shape, flops, scratch=(), moved=8 << 20, behind=()):
    count = len(in_specs)

    def body(*refs):
        kernel(*refs[:count], *refs[count + len(behind) :])

    built = pl.pallas_call(
        body,
        grid=grid,
        in_specs=list(in_specs) + [pl.BlockSpec(memory_space=pl.ANY)] * len(behind),
        out_specs=out_specs,
        out_shape=out_shape,
        scratch_shapes=scratch,
        compiler_params=pltpu.CompilerParams(
            dimension_semantics=("arbitrary",) * len(grid), vmem_limit_bytes=VMEM
        ),
        cost_estimate=pl.CostEstimate(flops=flops, bytes_accessed=moved, transcendentals=0),
    )
    return lambda *operands: built(*operands, *behind)


def struct(shape, dtype):
    return jax.ShapeDtypeStruct(shape, dtype)


def fixed(shape):
    return pl.BlockSpec(shape, lambda i: (0,) * len(shape))


def rowed(rows, columns):
    return pl.BlockSpec((rows, columns), lambda i: (i, 0))


def piled(shape, which):
    return pl.BlockSpec((shape[0], shape[1] // 2, shape[2]), lambda i: (0, which, 0))


def flat(value):
    return value.reshape((-1,) + value.shape[2:])


def project_kernel(xa, xb, w, ends, cosine, sine, xn, pre, low, gate, gains):
    x = flat(jnp.where(pl.program_id(0) == 0, xa[...], xb[...])).astype(F32)
    normed = (x * rms_scale(x)).astype(BF16)
    xn[...] = normed
    out = dot(normed, w[...])
    found = jnp.zeros((16, HD), F32)
    for start in range(0, ends.shape[0], HD):
        found = found + ends[start : start + 16, :].astype(F32)
    gains[...] = found
    for place in range(3):
        raw = out[:, head(place)]
        pre[:, head(place)] = raw
        unit = raw * rms_scale(raw) * found[place // 2 : place // 2 + 1, :]
        low[:, head(place)] = (unit * cosine[...] + turn(unit) * sine[...]).astype(BF16)
    low[:, head(3)] = out[:, head(3)].astype(BF16)
    gate[...] = out[:, 4 * HD :]


def project(xa, xb, w, cosine, sine):
    half, width = xa.shape[0] * xa.shape[1] // 2, xa.shape[2]
    return call(
        project_kernel,
        (2,),
        [
            piled(xa.shape, 0),
            piled(xb.shape, 0),
            fixed((width, 6 * HD)),
            pl.BlockSpec((width, HD), lambda i: (0, 8)),
            rowed(half, HD),
            rowed(half, HD),
        ],
        [
            rowed(half, width),
            rowed(half, 3 * HD),
            rowed(half, 4 * HD),
            rowed(half, 2 * HD),
            fixed((16, HD)),
        ],
        [
            struct((2 * half, width), BF16),
            struct((2 * half, 3 * HD), F32),
            struct((2 * half, 4 * HD), BF16),
            struct((2 * half, 2 * HD), F32),
            struct((16, HD), F32),
        ],
        2 * 2 * half * width * 6 * HD,
    )(xa, xb, w, w, cosine, sine)


def attend_kernel(low, gate, w_out, of_row, of_column, probs, attended, gated, mine, other):
    step = pl.program_id(0)
    half = probs.shape[1]
    rows = pl.ds(step * half, half)
    key, value = low[:, head(2)], low[:, head(3)]
    seg, par, grand, place = (of_row[rows, n : n + 1] for n in range(4))
    key_seg, key_place = of_column[0:1, :], of_column[1:2, :]
    allowed = ((key_seg == seg) | (key_seg == par) | (key_seg == grand)) & (key_place <= place)
    for number in range(2):
        scores = dot_back(low[rows, head(number)], key) * SCALE
        scores = jnp.where(allowed, scores, NEG)
        raised = jnp.exp(scores - jnp.max(scores, axis=-1, keepdims=True))
        share = raised / jnp.sum(raised, axis=-1, keepdims=True)
        probs[number] = share
        seen = dot(share.astype(BF16), value)
        attended[:, head(number)] = seen
        gated[:, head(number)] = (seen * jax.nn.sigmoid(gate[:, head(number)])).astype(BF16)
    out = dot_back(gated[...], w_out[...])

    @pl.when(step == 0)
    def _():
        mine[...] = out.astype(BF16)

    @pl.when(step == 1)
    def _():
        other[...] = out.astype(BF16)


def attend(low, gate, w, of_row, of_column):
    length = low.shape[0]
    half, width = length // 2, w.shape[0]
    return call(
        attend_kernel,
        (2,),
        [
            fixed((length, 4 * HD)),
            rowed(half, 2 * HD),
            pl.BlockSpec((width, 2 * HD), lambda i: (0, 3)),
            fixed((length, 4)),
            fixed((2, length)),
        ],
        [
            pl.BlockSpec((2, half, length), lambda i: (0, i, 0)),
            rowed(half, 2 * HD),
            rowed(half, 2 * HD),
            fixed((half, width)),
            fixed((half, width)),
        ],
        [
            struct((2, length, length), F32),
            struct((length, 2 * HD), F32),
            struct((length, 2 * HD), BF16),
            struct((half, width), BF16),
            struct((half, width), BF16),
        ],
        2 * length * width * 2 * HD + 8 * length * length * HD,
    )(low, gate, w, of_row, of_column)


def flip_kernel(pieces, out):
    at = 0
    for piece in pieces:
        out[:, at : at + piece.shape[0]] = piece[...].T
        at += piece.shape[0]


def flip(*pieces):
    length, width = sum(piece.shape[0] for piece in pieces), pieces[0].shape[1]
    chunk = 2 * HD
    return call(
        lambda *refs: flip_kernel(refs[:-1], refs[-1]),
        (width // chunk,),
        [pl.BlockSpec((piece.shape[0], chunk), lambda i: (0, i)) for piece in pieces],
        rowed(chunk, length),
        struct((width, length), BF16),
        1 << 20,
    )(*pieces)


def feed_kernel(ua, ub, ca, cb, wg, wu, wd, hidden, d_gate, d_up):
    half = ua.shape[0]
    for number, (u, cot) in enumerate(((ua, ca), (ub, cb))):
        rows = slice(number * half, (number + 1) * half)
        gate, up = dot(u[...], wg[...]), dot(u[...], wu[...])
        d_hidden = dot(flat(cot[...]), wd[...])
        sig = jax.nn.sigmoid(gate)
        silu = gate * sig
        hidden[rows, :] = (silu * up).astype(BF16)
        d_gate[rows, :] = (d_hidden * up * sig * (1.0 + gate * (1.0 - sig))).astype(BF16)
        d_up[rows, :] = (d_hidden * silu).astype(BF16)


def feed(ua, ub, ca, cb, w, behind):
    half, width = ua.shape
    chunk = 2 * HD
    parts = w.shape[1] // 3 // chunk
    column = lambda shift: pl.BlockSpec((width, chunk), lambda i: (0, shift * parts + i))
    unit = pl.BlockSpec((2 * half, chunk), lambda i: (0, i))
    units = parts * chunk
    return call(
        feed_kernel,
        (parts,),
        [fixed((half, width))] * 2
        + [piled(ca.shape, 1)] * 2
        + [column(0), column(1), column(2)],
        [unit, unit, unit],
        [struct((2 * half, units), BF16)] * 3,
        2 * 2 * half * width * units * 3,
        behind=behind,
    )(ua, ub, ca, cb, w, w, w)


def feed_back_kernel(d_gate, d_up, wg, wu, mine, other):
    half = mine.shape[0]
    out = dot_back(d_gate[...], wg[...]) + dot_back(d_up[...], wu[...])
    mine[...] = out[:half, :].astype(BF16)
    other[...] = out[half:, :].astype(BF16)


def feed_back(d_gate, d_up, w, behind):
    length, units = d_gate.shape
    half, width = length // 2, w.shape[0]
    chunk = 4 * HD
    slab = pl.BlockSpec((half, chunk), lambda i: (0, i))
    return call(
        feed_back_kernel,
        (width // chunk,),
        [fixed((length, units))] * 2
        + [
            pl.BlockSpec((chunk, units), lambda i: (i, 0)),
            pl.BlockSpec((chunk, units), lambda i: (i, 1)),
        ],
        [slab, slab],
        [struct((half, width), BF16), struct((half, width), BF16)],
        2 * length * width * units * 2,
        behind=behind,
    )(d_gate, d_up, w, w)


def down_kernel(hidden, w, mine, other):
    out = dot_back(hidden[...], w[...])

    @pl.when(pl.program_id(0) == 0)
    def _():
        mine[...] = out.astype(BF16)

    @pl.when(pl.program_id(0) == 1)
    def _():
        other[...] = out.astype(BF16)


def down_product(left, w, place, behind):
    length, units = left.shape
    half, width = length // 2, w.shape[0]
    return call(
        down_kernel,
        (2,),
        [rowed(half, units), pl.BlockSpec((width, units), lambda i: (0, place))],
        [fixed((half, width)), fixed((half, width))],
        [struct((half, width), BF16), struct((half, width), BF16)],
        2 * length * width * units,
        behind=behind,
    )(left, w)


def spread_blocks(flipped, right, out, start):
    term = dot(flipped, right).astype(BF16)
    for place in range(flipped.shape[0] // HD):
        for owner in range(right.shape[1] // HD):
            at = start + place * HD
            out[owner * HD : (owner + 1) * HD, at : at + HD] = term[head(place), head(owner)]


def feed_grads_kernel(u_flip, ca, cb, d_gate, d_up, hidden, out, flipped):
    @pl.when(pl.program_id(0) == 0)
    def _():
        flipped[...] = hidden[...].T

    units = hidden.shape[1]
    out[:, :units] = dot(u_flip[...], d_gate[...]).astype(BF16)
    out[:, units : 2 * units] = dot(u_flip[...], d_up[...]).astype(BF16)
    cot = jnp.concatenate([flat(ca[...]), flat(cb[...])], axis=0)
    spread_blocks(flipped[...], cot, out, 2 * units)


def feed_grads(u_flip, ca, cb, d_gate, d_up, hidden, behind):
    width, length = u_flip.shape
    units = hidden.shape[1]
    chunk = 4 * HD
    return call(
        feed_grads_kernel,
        (width // chunk,),
        [rowed(chunk, length)]
        + [pl.BlockSpec((ca.shape[0], ca.shape[1] // 2, chunk), lambda i: (0, 1, i))] * 2
        + [fixed((length, units))] * 3,
        rowed(chunk, 3 * units),
        struct((width, 3 * units), BF16),
        2 * length * width * units * 3,
        scratch=[pltpu.VMEM((units, length), BF16)],
        behind=behind,
    )(u_flip, ca, cb, d_gate, d_up, hidden)


def gate_back_kernel(da, db, w_out, gate, attended, d_attended, d_gate):
    half = da.shape[0]
    for number, low in enumerate((da, db)):
        rows = slice(number * half, (number + 1) * half)
        d_gated = dot(low[...], w_out[...])
        sig = jax.nn.sigmoid(gate[rows, :])
        d_attended[rows, :] = (d_gated * sig).astype(BF16)
        d_gate[rows, :] = (d_gated * attended[rows, :] * sig * (1.0 - sig)).astype(BF16)


def gate_back(da, db, w, gate, attended):
    half, width = da.shape
    wide = (2 * half, 2 * HD)
    return call(
        gate_back_kernel,
        (1,),
        [fixed((half, width))] * 2
        + [pl.BlockSpec((width, 2 * HD), lambda i: (0, 3)), fixed(wide), fixed(wide)],
        [fixed(wide), fixed(wide)],
        [struct(wide, BF16), struct(wide, BF16)],
        2 * 2 * half * width * 2 * HD,
    )(da, db, w, gate, attended)


def head_back(grads, inputs, gain):
    factor = rms_scale(inputs)
    scaled = gain * grads
    back = factor * scaled - inputs * factor**3 * jnp.mean(scaled * inputs, axis=-1, keepdims=True)
    return back.astype(BF16), jnp.sum(grads * inputs * factor, axis=0, keepdims=True)


def attend_back_kernel(
    probs, low, d_attended, pre, gains, cosine, sine, out, terms, d_key, d_value
):
    step = pl.program_id(0)
    half = probs.shape[1]
    start = pl.multiple_of(step * half, half)
    rows = pl.ds(start, half)
    key, value = low[:, head(2)], low[:, head(3)]
    cos_rows, sin_rows = cosine[rows, :], sine[rows, :]

    @pl.when(step == 0)
    def _():
        d_key[...] = jnp.zeros_like(d_key)
        d_value[...] = jnp.zeros_like(d_value)
        terms[...] = jnp.zeros_like(terms)

    for number in range(2):
        share = probs[number]
        d_seen = d_attended[:, head(number)]
        d_share = dot_back(d_seen, value)
        d_scores = share * (d_share - jnp.sum(share * d_share, axis=-1, keepdims=True))
        d_scores = d_scores.astype(BF16)
        d_query = dot(d_scores, key) * SCALE
        d_key[...] += dot_rows(d_scores, low[rows, head(number)])
        d_value[...] += dot_rows(share.astype(BF16), d_seen)
        grads = d_query * cos_rows + unturn(d_query * sin_rows)
        back, term = head_back(grads, pre[rows, head(number)], gains[0:1, :])
        out[rows, head(number)] = back
        terms[0:1, :] += term

    @pl.when(step == 1)
    def _():
        grads = d_key[...] * SCALE
        grads = grads * cosine[...] + unturn(grads * sine[...])
        back, term = head_back(grads, pre[:, head(2)], gains[1:2, :])
        out[:, head(2)] = back
        terms[1:2, :] = term
        out[:, head(3)] = d_value[...].astype(BF16)


def attend_back(probs, low, d_attended, pre, gains, cosine, sine, behind):
    length = low.shape[0]
    half = length // 2
    return call(
        attend_back_kernel,
        (2,),
        [
            pl.BlockSpec((2, half, length), lambda i: (0, i, 0)),
            fixed((length, 4 * HD)),
            rowed(half, 2 * HD),
            fixed((length, 3 * HD)),
            fixed((16, HD)),
            fixed((length, HD)),
            fixed((length, HD)),
        ],
        [fixed((length, 4 * HD)), fixed((8, HD))],
        [struct((length, 4 * HD), BF16), struct((8, HD), F32)],
        20 * length * length * HD,
        scratch=[pltpu.VMEM((length, HD), F32), pltpu.VMEM((length, HD), F32)],
        behind=behind,
    )(probs, low, d_attended, pre, gains, cosine, sine)


def input_back_kernel(d_qkv, d_gate, w, mine, other):
    out = dot_back(d_qkv[...], w[:, : 4 * HD]) + dot_back(d_gate[...], w[:, 4 * HD :])

    @pl.when(pl.program_id(0) == 0)
    def _():
        mine[...] = out.astype(BF16)

    @pl.when(pl.program_id(0) == 1)
    def _():
        other[...] = out.astype(BF16)


def input_back(d_qkv, d_gate, w, behind):
    length = d_qkv.shape[0]
    half, width = length // 2, w.shape[0]
    return call(
        input_back_kernel,
        (2,),
        [rowed(half, 4 * HD), rowed(half, 2 * HD), fixed((width, 6 * HD))],
        [fixed((half, width)), fixed((half, width))],
        [struct((half, width), BF16), struct((half, width), BF16)],
        2 * length * width * 6 * HD,
        behind=behind,
    )(d_qkv, d_gate, w)


def attend_grads_kernel(x_flip, da, db, d_qkv, d_gate, gated, out, flipped):
    @pl.when(pl.program_id(0) == 0)
    def _():
        flipped[...] = gated[...].T

    inner, split = d_qkv.shape[1], d_gate.shape[1]
    out[:, :inner] = dot(x_flip[...], d_qkv[...]).astype(BF16)
    out[:, inner : inner + split] = dot(x_flip[...], d_gate[...]).astype(BF16)
    spread_blocks(
        flipped[...], jnp.concatenate([da[...], db[...]], axis=0), out, inner + split
    )


def attend_grads(x_flip, da, db, d_qkv, d_gate, gated, behind):
    width, length = x_flip.shape
    columns = d_qkv.shape[1] + d_gate.shape[1] + gated.shape[1]
    chunk = 4 * HD
    slab = pl.BlockSpec((length // 2, chunk), lambda i: (0, i))
    return call(
        attend_grads_kernel,
        (width // chunk,),
        [
            rowed(chunk, length),
            slab,
            slab,
            fixed(d_qkv.shape),
            fixed(d_gate.shape),
            fixed(gated.shape),
        ],
        rowed(chunk, columns),
        struct((width, columns), BF16),
        2 * length * width * columns,
        scratch=[pltpu.VMEM(gated.shape[::-1], BF16)],
        behind=behind,
    )(x_flip, da, db, d_qkv, d_gate, gated)


def middle_kernel(parts, x, middle, spread):
    total = x[...].astype(F32) + jnp.sum(parts[...].astype(F32), axis=0)
    middle[...] = total
    low = (total * rms_scale(total)).astype(BF16)
    for number in range(spread.shape[0]):
        spread[number] = low


def middle_step(parts, x, behind):
    shape = x.shape
    return call(
        middle_kernel,
        (1,),
        [fixed(parts.shape), fixed(shape)],
        [fixed(shape), fixed(parts.shape)],
        [struct(shape, F32), struct(parts.shape, BF16)],
        1 << 20,
        behind=behind,
    )(parts, x)


def norm_back(grads, inputs):
    factor = rms_scale(inputs)
    return factor * grads - inputs * factor**3 * jnp.mean(grads * inputs, axis=-1, keepdims=True)


def d_middle_kernel(parts, middle, cot, d_middle, spread):
    grads = jnp.sum(parts[...].astype(F32), axis=0)
    total = cot[...].astype(F32) + norm_back(grads, middle[...])
    d_middle[...] = total
    for number in range(spread.shape[0]):
        spread[number] = total.astype(BF16)


def d_middle_step(parts, middle, cot):
    shape = cot.shape
    return call(
        d_middle_kernel,
        (1,),
        [fixed(parts.shape), fixed(shape), fixed(shape)],
        [fixed(shape), fixed(parts.shape)],
        [struct(shape, F32), struct(parts.shape, BF16)],
        1 << 20,
    )(parts, middle, cot)


def ends_kernel(parts, middle, d_middle, x, out):
    rows = x.shape[0]
    total = sum(part[...].astype(F32) for part in parts)
    out[:rows, :] = (middle[...] + total[:rows, :]).astype(BF16)
    back = norm_back(total[rows:, :], x[...].astype(F32))
    out[rows:, :] = (d_middle[...] + back).astype(BF16)


def ends_step(parts, middle, d_middle, x):
    shape, wide = x.shape, parts[0].shape
    count = len(parts)
    return call(
        lambda *refs: ends_kernel(refs[:count], *refs[count:]),
        (1,),
        [fixed(wide)] * count + [fixed(shape)] * 3,
        fixed(wide),
        struct(wide, BF16),
        1 << 20,
    )(*parts, middle, d_middle, x)


def sum_kernel(parts, out):
    out[...] = jnp.sum(parts[...].astype(F32), axis=0).astype(BF16)


def sum_step(parts, behind):
    return call(
        sum_kernel,
        (1,),
        [fixed(parts.shape)],
        fixed(parts.shape[1:]),
        struct(parts.shape[1:], BF16),
        1 << 20,
        behind=behind,
    )(parts)


def prefetched(kernel, grid, in_specs, out_specs, out_shape):
    return pl.pallas_call(
        kernel,
        grid_spec=pltpu.PrefetchScalarGridSpec(
            num_scalar_prefetch=1, grid=grid, in_specs=in_specs, out_specs=out_specs
        ),
        out_shape=out_shape,
        compiler_params=pltpu.CompilerParams(
            dimension_semantics=("arbitrary",) * len(grid), vmem_limit_bytes=VMEM
        ),
        cost_estimate=pl.CostEstimate(flops=1 << 20, bytes_accessed=8 << 20, transcendentals=0),
    )


def copy_kernel(core, source, out):
    out[...] = source[...]


def sibling_part(core, found):
    pairs, _, rows, columns = found.shape
    return prefetched(
        copy_kernel,
        (pairs // 2,),
        [pl.BlockSpec((2, None, rows, columns), lambda i, at: (i, 1 - at[0], 0, 0))],
        pl.BlockSpec((2, rows, columns), lambda i, at: (i, 0, 0)),
        struct((pairs, rows, columns), found.dtype),
    )(core, found)


def join_kernel(core, mine, other, out):
    out[:, core[0]] = mine[...]
    out[:, 1 - core[0]] = other[...]


def join_cores(core, found, other):
    pairs, _, rows, columns = found.shape
    return prefetched(
        join_kernel,
        (pairs // 2,),
        [
            pl.BlockSpec((2, None, rows, columns), lambda i, at: (i, at[0], 0, 0)),
            pl.BlockSpec((2, rows, columns), lambda i, at: (i, 0, 0)),
        ],
        pl.BlockSpec((2, 2, rows, columns), lambda i, at: (i, 0, 0, 0)),
        struct(found.shape, found.dtype),
    )(core, found, other)


def lanes(value):
    return sum(value[:, start : start + HD] for start in range(0, value.shape[1], HD))


def pick(blocks):
    step = pl.program_id(0)
    value = blocks[0][...]
    for number in range(1, len(blocks)):
        value = jnp.where(step == number, blocks[number][...], value)
    return value.astype(F32)


def close_feed_kernel(turn_at, b0, b1, b2, b3, w_gate, w_up, gain, g_gate, g_up, g_down, sums):
    raw = pick((b0, b1, b2, b3))
    units = w_gate.shape[1]
    raw_gate, raw_up = raw[:, :units], raw[:, units : 2 * units]
    g_gate[...] = raw_gate * gain[...]
    g_up[...] = raw_up * gain[...]
    for place in range(units // HD):
        g_down[head(place), :] = raw[:, 2 * units + place * HD : 2 * units + (place + 1) * HD]
    term = lanes(raw_gate * w_gate[...].astype(F32)) + lanes(raw_up * w_up[...].astype(F32))

    @pl.when(pl.program_id(0) == 0)
    def _():
        sums[...] = term

    @pl.when(pl.program_id(0) > 0)
    def _():
        sums[...] += term


def close_attend_kernel(
    turn_at, b0, b1, b2, b3, wq, wk, wv, wg, gain, gq, gk, gv, gg, go, sums
):
    found = pick((b0, b1, b2, b3))
    inner, outer, scale = found[:, : 4 * HD], found[:, 4 * HD :], gain[...]
    raw_q, raw_k, raw_v = inner[:, : 2 * HD], inner[:, head(2)], inner[:, head(3)]
    raw_g = outer[:, : 2 * HD]
    gq[...], gk[...], gv[...], gg[...] = raw_q * scale, raw_k * scale, raw_v * scale, raw_g * scale
    go[head(0), :], go[head(1), :] = outer[:, head(2)], outer[:, head(3)]
    pairs = ((raw_q, wq), (raw_k, wk), (raw_v, wv), (raw_g, wg))
    term = sum(lanes(raw * w[...].astype(F32)) for raw, w in pairs)

    @pl.when(pl.program_id(0) == 0)
    def _():
        sums[...] = term

    @pl.when(pl.program_id(0) > 0)
    def _():
        sums[...] += term


def close(kernel, turn_at, blocks, weights, gain, out_rows, extra):
    quarters = 4
    place = lambda i, at: (at[0] + quarters - i) % quarters
    whole = lambda value: pl.BlockSpec(value.shape, lambda i, at: (0, 0))
    columns = lambda w: pl.BlockSpec(
        (w.shape[0], w.shape[1] // quarters), lambda i, at: (0, place(i, at))
    )
    rows, width = out_rows
    in_specs = [whole(b) for b in blocks] + [columns(w) for w in weights] + [whole(gain)]
    out_specs = [columns(w) for w in weights]
    out_specs += [pl.BlockSpec((rows // quarters, width), lambda i, at: (place(i, at), 0))]
    out_specs += [pl.BlockSpec(shape, lambda i, at: (0, 0)) for shape in extra]
    out_shape = [struct(w.shape, F32) for w in weights] + [struct(out_rows, F32)]
    out_shape += [struct(shape, F32) for shape in extra]
    return prefetched(kernel, (quarters,), in_specs, out_specs, out_shape)(
        turn_at, *blocks, *weights, gain
    )


def column(row):
    shape = (HD, HD)
    there = lax.broadcasted_iota(jnp.int32, shape, 0) == lax.broadcasted_iota(jnp.int32, shape, 1)
    return jnp.sum(jnp.where(there, jnp.broadcast_to(row, shape), 0.0), axis=1, keepdims=True)


def first_kernel(at, wq, wk, wv, wg, wo, gain, gain_q, gain_k, out):
    scale = column(gain[...].astype(F32))
    start = 0
    for w in (wq, wk, wv, wg):
        stop = start + w.shape[1]
        out[:, start:stop] = (w[...].astype(F32) * scale).astype(BF16)
        start = stop
    out[:, start : start + wo.shape[0]] = wo[...].T
    start += wo.shape[0]
    count = gain_q.shape[1]
    lane = lax.broadcasted_iota(jnp.int32, (count, HD), 1)
    spot = lax.broadcasted_iota(jnp.int32, (count, HD), 0) + at[1] * count
    there = jnp.where(lane == spot, 1.0, 0.0)
    ends = [dot(g[...].astype(F32), there) for g in (gain_q, gain_k)]
    ends = jnp.concatenate(ends + [jnp.zeros((14, HD), F32)], axis=0)
    out[:16, start:] = ends.astype(BF16)
    out[16:, start:] = jnp.zeros((HD - 16, HD), BF16)


def first_columns(at, wq, wk, wv, wg, wo, gain, gain_q, gain_k):
    quarter = lambda w: pl.BlockSpec((w.shape[0], w.shape[1] // 4), lambda i, at: (0, at[0]))
    row = lambda g: pl.BlockSpec(g.shape, lambda i, at: (0, 0))
    rows = wq.shape[0]
    heads = wo.shape[0] // 4
    columns = sum(w.shape[1] // 4 for w in (wq, wk, wv, wg)) + heads + HD
    return prefetched(
        first_kernel,
        (1,),
        [quarter(w) for w in (wq, wk, wv, wg)]
        + [pl.BlockSpec((heads, rows), lambda i, at: (at[0], 0))]
        + [row(g) for g in (gain, gain_q, gain_k)],
        pl.BlockSpec((rows, columns), lambda i, at: (0, 0)),
        struct((rows, columns), BF16),
    )(at, wq, wk, wv, wg, wo, gain, gain_q, gain_k)


def make_shards(mesh):
    n_shard, n_ctx, n_tp = mesh.shape["shard"], mesh.shape["ctx"], mesh.shape["tp"]
    pairs = n_shard // 2

    def joint(pair, core, tp):
        return (pair * 2 + core) * n_tp + tp

    core_perm = [(i, i ^ 1) for i in range(n_shard)]
    planes = [
        [joint(pair, core, tp) for pair in range(pairs) for tp in range(n_tp)] for core in range(2)
    ]
    swap_perm = [
        edge
        for pair in range(pairs)
        for edge in (
            (joint(pair, 1, 0), joint(pair, 0, 1)),
            (joint(pair, 0, 1), joint(pair, 1, 0)),
        )
    ]
    across_perm = [(joint(pair, t, t), joint(pair, t, 1 - t)) for pair in range(pairs) for t in range(2)]

    def core_swap(value):
        return lax.ppermute(value, "shard", core_perm)

    def ctx_exchange(value):
        return lax.all_to_all(value, "ctx", 0, 0)

    def ctx_turn(value, by):
        return lax.ppermute(value, "ctx", [(i, (i + by) % n_ctx) for i in range(n_ctx)])

    def tree_rows(spread, *before):
        mine = ctx_exchange(spread)
        if before:
            mine, *before = lax.optimization_barrier((mine, *before))
        return mine, core_swap(mine), *before

    def tree_half(mine, other):
        half = (mine.astype(F32) + core_swap(other).astype(F32)).astype(BF16)
        return half.reshape((n_ctx, -1) + half.shape[1:])

    def plane_gather(value):
        return lax.all_gather(value, PLANE, axis=0, tiled=True, axis_index_groups=planes)

    def plane_scatter(value):
        return lax.psum_scatter(
            value, PLANE, scatter_dimension=0, tiled=True, axis_index_groups=planes
        )

    def plane_exchange(value):
        return lax.all_to_all(value, PLANE, 0, 0, axis_index_groups=planes)

    def shards(
        tokens,
        seg_lengths,
        seg_parents,
        gain_in,
        w_query,
        w_key,
        w_value,
        w_gate_attn,
        w_out,
        gain_query,
        gain_key,
        gain_mid,
        w_gate,
        w_up,
        w_down,
        cotangent,
    ):
        core = lax.axis_index("shard") % 2
        tp = lax.axis_index("tp")
        ctx = lax.axis_index("ctx")
        native = core == tp
        rows = tokens.shape[0] // 2

        def swapped(value):
            return jnp.where(native, value, lax.ppermute(value, PLANE, swap_perm))

        def quarter(weight, axis):
            size = weight.shape[axis] // n_ctx
            return lax.dynamic_slice_in_dim(weight, ctx * size, size, axis)

        gain_one = gain_in.astype(F32)[:, None]
        gain_two = gain_mid.astype(F32)[:, None]
        head_rows = gain_query.shape[0]
        first = first_columns(
            jnp.stack([ctx, lax.axis_index("shard")]).astype(jnp.int32),
            w_query,
            w_key,
            w_value,
            w_gate_attn,
            w_out,
            gain_in[None],
            gain_query[None],
            gain_key[None],
        )
        found = plane_gather(first)

        def half_rows(place):
            pieces = [lax.dynamic_slice_in_dim(v, place * rows, rows, 0) for v in (tokens, cotangent)]
            return jnp.concatenate(pieces, axis=0)

        own = jnp.where(native, half_rows(core), core_swap(half_rows(1 - core)))
        tree = jnp.concatenate([seg_lengths, seg_parents], axis=0)
        tree = jnp.where(native, tree, core_swap(tree))
        own_x, own_cot = own[:rows], own[rows:]
        xa, xb = tree_rows(jnp.broadcast_to(own[None], (n_ctx,) + own.shape))

        second = jnp.concatenate([quarter(w_gate, 1), quarter(w_up, 1)], axis=1)
        second = (second.astype(F32) * gain_two).astype(BF16)
        second = jnp.concatenate([second, quarter(w_down, 0).T], axis=1)
        w2 = plane_gather(swapped(second))

        half_at = jnp.where(jnp.arange(2) == 0, core, 1 - core) * rows
        places = (
            half_at[:, None, None]
            + jnp.arange(n_ctx, dtype=jnp.int32)[None, :, None] * (2 * rows)
            + jnp.arange(rows, dtype=jnp.int32)[None, None, :]
        ).reshape(-1)
        segment, parent_seg, grand_seg, position = tree_layout(tree[0], tree[1], places)
        of_row = jnp.stack([segment, parent_seg, grand_seg, places], axis=1)
        of_column = jnp.stack([segment, places], axis=0)
        cosine, sine = rope_tables(position, HD)

        found, xa, xb, of_row, of_column, cosine, sine = lax.optimization_barrier(
            (found, xa, xb, of_row, of_column, cosine, sine)
        )
        found = found.reshape(pairs, n_tp, gain_in.shape[0], -1)
        core_at = core.astype(jnp.int32).reshape(1)
        other = core_swap(sibling_part(core_at, found))
        w1 = join_cores(core_at, found, other).reshape(-1, first.shape[1])

        xn, pre, low, gate, gains = project(xa, xb, w1, cosine, sine)
        probs, attended, gated, mine, other = attend(low, gate, w1, of_row, of_column)
        x_flip = flip(xn)
        middle, spread = middle_step(ctx_exchange(tree_half(mine, other)), own_x, (x_flip,))
        ua, ub = (flat(v) for v in tree_rows(spread))
        u_flip = flip(ua, ub)

        hidden, d_gate, d_up = feed(ua, ub, xa, xb, w2, (u_flip,))
        ffn = feed_grads(u_flip, xa, xb, d_gate, d_up, hidden, ())
        half = tree_half(*feed_back(d_gate, d_up, w2, (ffn,)))
        d_middle, spread = d_middle_step(ctx_exchange(half), middle, own_cot)
        layer_mine, layer_other = down_product(hidden, w2, 2, (half,))
        da, db, layer_mine, layer_other = tree_rows(spread, layer_mine, layer_other)
        da, db = flat(da), flat(db)
        grad_ffn = plane_scatter(ffn)

        d_attended, d_gate_pre = gate_back(da, db, w1, gate, attended)
        d_qkv, terms = attend_back(probs, low, d_attended, pre, gains, cosine, sine, ())

        pieces = jnp.concatenate(
            [terms[0].reshape(n_shard, -1), terms[1].reshape(n_shard, -1)], axis=1
        )
        copies = n_ctx * n_tp
        pieces = jnp.pad(pieces, ((0, 0), (0, HD - pieces.shape[1]))).astype(BF16)
        pieces = jnp.broadcast_to(pieces[:, None, None], (n_shard, copies, 8, HD))
        pieces = lax.all_to_all(
            pieces.reshape(n_shard * copies, 8, HD), ("shard", "ctx", "tp"), 0, 0
        )
        head_ends = jnp.sum(pieces.astype(F32), axis=0)
        attn = attend_grads(x_flip, da, db, d_qkv, d_gate_pre, gated, ())
        in_mine, in_other = input_back(d_qkv, d_gate_pre, w1, (attn,))
        layer_half, in_half = tree_half(layer_mine, layer_other), tree_half(in_mine, in_other)
        own_ffn = swapped(grad_ffn)
        attn, layer_half, in_half, own_ffn, head_ends = lax.optimization_barrier(
            (attn, layer_half, in_half, own_ffn, head_ends)
        )
        attn_parts = plane_exchange(attn.reshape(n_shard, -1, attn.shape[1]))

        def owners(block):
            return [block] + [ctx_turn(block, by) for by in range(1, n_ctx)]


        both = jnp.concatenate(
            [layer_half, in_half], axis=1
        )
        parts = [lax.dynamic_index_in_dim(both, ctx, 0, False)] + [
            ctx_turn(lax.dynamic_index_in_dim(both, (ctx + by) % n_ctx, 0, False), by)
            for by in range(1, n_ctx)
        ]
        ends = ends_step(parts, middle, d_middle, own_x)
        ffn_blocks = owners(own_ffn)
        sibling = core_swap(ends)

        def whole(start):
            mine, other = ends[start : start + rows], sibling[start : start + rows]
            return jnp.where(
                core == 0,
                jnp.concatenate([mine, other], axis=0),
                jnp.concatenate([other, mine], axis=0),
            )

        full = jnp.stack([whole(0), whole(rows)])
        turn_at = ctx.astype(jnp.int32).reshape(1)
        size = gain_in.shape[0]
        grad_gate, grad_up, grad_down, mid_sums = close(
            close_feed_kernel,
            turn_at,
            ffn_blocks,
            (w_gate, w_up),
            gain_two,
            w_down.shape,
            [(size, HD)],
        )
        attn_sum = sum_step(attn_parts, (full, mid_sums))
        full, attn_sum = lax.optimization_barrier((full, attn_sum))
        full = jnp.where(native, full, lax.ppermute(full, PLANE, across_perm))

        attn_blocks = owners(swapped(attn_sum))
        grad_query, grad_key, grad_value, grad_gate_attn, grad_out, in_sums = close(
            close_attend_kernel,
            turn_at,
            attn_blocks,
            (w_query, w_key, w_value, w_gate_attn),
            gain_one,
            w_out.shape,
            [(size, HD)],
        )
        gain_terms = jnp.stack([jnp.sum(in_sums, axis=1), jnp.sum(mid_sums, axis=1)])
        gain_terms = gain_terms + lax.ppermute(gain_terms, "tp", [(0, 1), (1, 0)])

        return (
            full[0].astype(F32),
            full[1].astype(F32),
            gain_terms[0],
            grad_query,
            grad_key,
            grad_value,
            grad_gate_attn,
            grad_out,
            head_ends[0, :head_rows],
            head_ends[0, head_rows : 2 * head_rows],
            gain_terms[1],
            grad_gate,
            grad_up,
            grad_down,
        )

    return shards


def solution(mesh):
    return jax.shard_map(
        make_shards(mesh),
        mesh=mesh,
        in_specs=(
            P(("shard", "ctx"), None),
            P("shard", None),
            P("shard", None),
            P("shard"),
            P("shard", "tp"),
            P("shard", "tp"),
            P("shard", "tp"),
            P("shard", "tp"),
            P("tp", "shard"),
            P("shard"),
            P("shard"),
            P("shard"),
            P("shard", "tp"),
            P("shard", "tp"),
            P("tp", "shard"),
            P(("shard", "ctx"), None),
        ),
        out_specs=(
            P(("shard", "ctx"), None),
            P(("shard", "ctx"), None),
            P("shard"),
            P("shard", "tp"),
            P("shard", "tp"),
            P("shard", "tp"),
            P("shard", "tp"),
            P("tp", "shard"),
            P("shard"),
            P("shard"),
            P("shard"),
            P("shard", "tp"),
            P("shard", "tp"),
            P("tp", "shard"),
        ),
        check_vma=False,
    )
```

```python
import math

import jax
import jax.numpy as jnp
from jax import lax
from jax.experimental import pallas as pl
from jax.experimental.pallas import tpu as pltpu
from jax.sharding import PartitionSpec as P

HD = 128
EPS = 1e-06
BASE = 1000000.0
NEG = -1e30
F32 = jnp.float32
BF16 = jnp.bfloat16
PLANE = ("shard", "tp")
SCALE = 1.0 / math.sqrt(HD)
VMEM = 48 << 20
ALL_VMEM = 60 << 20


def lookup(onehot, table):
    return jnp.sum(onehot * table[None, :], axis=1)


def tree_layout(lengths, parents, places):
    labels = jnp.arange(lengths.shape[0], dtype=jnp.int32)
    ends = jnp.cumsum(lengths)
    starts = ends - lengths
    parent_hot = (parents[:, None] == labels[None, :]).astype(jnp.int32)
    grand = lookup(parent_hot, parents)
    parent_len = lookup(parent_hot, lengths)
    grand_hot = (grand[:, None] == labels[None, :]).astype(jnp.int32)
    grand_len = lookup(grand_hot, lengths)
    before = jnp.where(labels == 0, 0, parent_len + jnp.where(parents == 0, 0, grand_len))
    segment = jnp.sum((places[:, None] >= ends[None, :]).astype(jnp.int32), axis=1)
    token_hot = (segment[:, None] == labels[None, :]).astype(jnp.int32)
    position = places - lookup(token_hot, starts) + lookup(token_hot, before)
    return (segment, lookup(token_hot, parents), lookup(token_hot, grand), position)


def rope_tables(position, columns):
    halfway = columns // 2
    frequency = jnp.exp(jnp.arange(halfway, dtype=F32) * (-2.0 * math.log(BASE) / columns))
    angles = position.astype(F32)[:, None] * frequency[None, :]
    angles = jnp.concatenate([angles, angles], axis=1)
    return (jnp.cos(angles), jnp.sin(angles))


def rms_scale(inputs):
    return lax.rsqrt(jnp.mean(inputs * inputs, axis=-1, keepdims=True) + EPS)


def dot(left, right):
    return jnp.dot(left, right, preferred_element_type=F32)


def dot_rows(left, right):
    return lax.dot_general(left, right, (((0,), (0,)), ((), ())), preferred_element_type=F32)


def dot_back(left, right):
    return lax.dot_general(left, right, (((1,), (1,)), ((), ())), preferred_element_type=F32)


def turn(inputs):
    halfway = inputs.shape[-1] // 2
    return jnp.concatenate([-inputs[:, halfway:], inputs[:, :halfway]], axis=-1)


def unturn(inputs):
    halfway = inputs.shape[-1] // 2
    return jnp.concatenate([inputs[:, halfway:], -inputs[:, :halfway]], axis=-1)


def head(number):
    return slice(number * HD, (number + 1) * HD)


def call(kernel, grid, in_specs, out_specs, out_shape, flops, scratch=(), moved=8 << 20, behind=()):
    count = len(in_specs)

    def body(*refs):
        kernel(*refs[:count], *refs[count + len(behind) :])

    built = pl.pallas_call(
        body,
        grid=grid,
        in_specs=list(in_specs) + [pl.BlockSpec(memory_space=pl.ANY)] * len(behind),
        out_specs=out_specs,
        out_shape=out_shape,
        scratch_shapes=scratch,
        compiler_params=pltpu.CompilerParams(
            dimension_semantics=("arbitrary",) * len(grid), vmem_limit_bytes=VMEM
        ),
        cost_estimate=pl.CostEstimate(flops=flops, bytes_accessed=moved, transcendentals=0),
    )
    return lambda *operands: built(*operands, *behind)


def struct(shape, dtype):
    return jax.ShapeDtypeStruct(shape, dtype)


def fixed(shape):
    return pl.BlockSpec(shape, lambda i: (0,) * len(shape))


def rowed(rows, columns):
    return pl.BlockSpec((rows, columns), lambda i: (i, 0))


def piled(shape, which):
    return pl.BlockSpec((shape[0], shape[1] // 2, shape[2]), lambda i: (0, which, 0))


def flat(value):
    return value.reshape((-1,) + value.shape[2:])


def project_kernel(xa, xb, w, gains, cosine, sine, xn, pre, low, gate):
    x = flat(jnp.where(pl.program_id(0) == 0, xa[...], xb[...])).astype(F32)
    normed = (x * rms_scale(x)).astype(BF16)
    xn[...] = normed
    out = dot(normed, w[...])
    for place in range(3):
        raw = out[:, head(place)]
        pre[:, head(place)] = raw
        unit = raw * rms_scale(raw) * gains[place // 2 : place // 2 + 1, :]
        low[:, head(place)] = (unit * cosine[...] + turn(unit) * sine[...]).astype(BF16)
    low[:, head(3)] = out[:, head(3)].astype(BF16)
    gate[...] = out[:, 4 * HD :]


def project(xa, xb, w, gains, cosine, sine):
    half, width = xa.shape[0] * xa.shape[1] // 2, xa.shape[2]
    return call(
        project_kernel,
        (2,),
        [
            piled(xa.shape, 0),
            piled(xb.shape, 0),
            fixed((width, 6 * HD)),
            fixed(gains.shape),
            rowed(half, HD),
            rowed(half, HD),
        ],
        [
            rowed(half, width),
            rowed(half, 3 * HD),
            rowed(half, 4 * HD),
            rowed(half, 2 * HD),
        ],
        [
            struct((2 * half, width), BF16),
            struct((2 * half, 3 * HD), F32),
            struct((2 * half, 4 * HD), BF16),
            struct((2 * half, 2 * HD), F32),
        ],
        2 * 2 * half * width * 6 * HD,
    )(xa, xb, w, gains, cosine, sine)


def attend_kernel(low, gate, w_out, of_row, of_column, probs, attended, gated, mine, other):
    step = pl.program_id(0)
    half = probs.shape[1]
    rows = pl.ds(step * half, half)
    key, value = low[:, head(2)], low[:, head(3)]
    seg, par, grand, place = (of_row[rows, n : n + 1] for n in range(4))
    key_seg, key_place = of_column[0:1, :], of_column[1:2, :]
    allowed = ((key_seg == seg) | (key_seg == par) | (key_seg == grand)) & (key_place <= place)
    for number in range(2):
        scores = dot_back(low[rows, head(number)], key) * SCALE
        scores = jnp.where(allowed, scores, NEG)
        raised = jnp.exp(scores - jnp.max(scores, axis=-1, keepdims=True))
        share = raised / jnp.sum(raised, axis=-1, keepdims=True)
        probs[number] = share
        seen = dot(share.astype(BF16), value)
        attended[:, head(number)] = seen
        gated[:, head(number)] = (seen * jax.nn.sigmoid(gate[:, head(number)])).astype(BF16)
    out = dot_back(gated[...], w_out[...])

    @pl.when(step == 0)
    def _():
        mine[...] = out.astype(BF16)

    @pl.when(step == 1)
    def _():
        other[...] = out.astype(BF16)


def attend(low, gate, w, of_row, of_column):
    length = low.shape[0]
    half, width = length // 2, w.shape[0]
    return call(
        attend_kernel,
        (2,),
        [
            fixed((length, 4 * HD)),
            rowed(half, 2 * HD),
            pl.BlockSpec((width, 2 * HD), lambda i: (0, 3)),
            fixed((length, 4)),
            fixed((2, length)),
        ],
        [
            pl.BlockSpec((2, half, length), lambda i: (0, i, 0)),
            rowed(half, 2 * HD),
            rowed(half, 2 * HD),
            fixed((half, width)),
            fixed((half, width)),
        ],
        [
            struct((2, length, length), F32),
            struct((length, 2 * HD), F32),
            struct((length, 2 * HD), BF16),
            struct((half, width), BF16),
            struct((half, width), BF16),
        ],
        2 * length * width * 2 * HD + 8 * length * length * HD,
    )(low, gate, w, of_row, of_column)


def flip_kernel(pieces, out):
    at = 0
    for piece in pieces:
        out[:, at : at + piece.shape[0]] = piece[...].T
        at += piece.shape[0]


def flip(*pieces):
    length, width = sum(piece.shape[0] for piece in pieces), pieces[0].shape[1]
    chunk = 2 * HD
    return call(
        lambda *refs: flip_kernel(refs[:-1], refs[-1]),
        (width // chunk,),
        [pl.BlockSpec((piece.shape[0], chunk), lambda i: (0, i)) for piece in pieces],
        rowed(chunk, length),
        struct((width, length), BF16),
        1 << 20,
    )(*pieces)


def feed_kernel(ua, ub, ca, cb, wg, wu, wd, hidden, d_gate, d_up):
    half = ua.shape[0]
    for number, (u, cot) in enumerate(((ua, ca), (ub, cb))):
        rows = slice(number * half, (number + 1) * half)
        gate, up = dot(u[...], wg[...]), dot(u[...], wu[...])
        d_hidden = dot(flat(cot[...]), wd[...])
        sig = jax.nn.sigmoid(gate)
        silu = gate * sig
        hidden[rows, :] = (silu * up).astype(BF16)
        d_gate[rows, :] = (d_hidden * up * sig * (1.0 + gate * (1.0 - sig))).astype(BF16)
        d_up[rows, :] = (d_hidden * silu).astype(BF16)


def feed(ua, ub, ca, cb, w, behind):
    half, width = ua.shape
    chunk = 2 * HD
    parts = w.shape[1] // 3 // chunk
    column = lambda shift: pl.BlockSpec((width, chunk), lambda i: (0, shift * parts + i))
    unit = pl.BlockSpec((2 * half, chunk), lambda i: (0, i))
    units = parts * chunk
    return call(
        feed_kernel,
        (parts,),
        [fixed((half, width))] * 2
        + [piled(ca.shape, 1)] * 2
        + [column(0), column(1), column(2)],
        [unit, unit, unit],
        [struct((2 * half, units), BF16)] * 3,
        2 * 2 * half * width * units * 3,
        behind=behind,
    )(ua, ub, ca, cb, w, w, w)


def feed_back_kernel(d_gate, d_up, wg, wu, mine, other):
    half = mine.shape[0]
    out = dot_back(d_gate[...], wg[...]) + dot_back(d_up[...], wu[...])
    mine[...] = out[:half, :].astype(BF16)
    other[...] = out[half:, :].astype(BF16)


def feed_back(d_gate, d_up, w, behind):
    length, units = d_gate.shape
    half, width = length // 2, w.shape[0]
    chunk = 4 * HD
    slab = pl.BlockSpec((half, chunk), lambda i: (0, i))
    return call(
        feed_back_kernel,
        (width // chunk,),
        [fixed((length, units))] * 2
        + [
            pl.BlockSpec((chunk, units), lambda i: (i, 0)),
            pl.BlockSpec((chunk, units), lambda i: (i, 1)),
        ],
        [slab, slab],
        [struct((half, width), BF16), struct((half, width), BF16)],
        2 * length * width * units * 2,
        behind=behind,
    )(d_gate, d_up, w, w)


def down_kernel(hidden, w, mine, other):
    out = dot_back(hidden[...], w[...])

    @pl.when(pl.program_id(0) == 0)
    def _():
        mine[...] = out.astype(BF16)

    @pl.when(pl.program_id(0) == 1)
    def _():
        other[...] = out.astype(BF16)


def down_product(left, w, place, behind):
    length, units = left.shape
    half, width = length // 2, w.shape[0]
    return call(
        down_kernel,
        (2,),
        [rowed(half, units), pl.BlockSpec((width, units), lambda i: (0, place))],
        [fixed((half, width)), fixed((half, width))],
        [struct((half, width), BF16), struct((half, width), BF16)],
        2 * length * width * units,
        behind=behind,
    )(left, w)


def spread_blocks(flipped, right, out, start):
    term = dot(flipped, right).astype(BF16)
    for place in range(flipped.shape[0] // HD):
        for owner in range(right.shape[1] // HD):
            at = start + place * HD
            out[owner * HD : (owner + 1) * HD, at : at + HD] = term[head(place), head(owner)]


def feed_grads_kernel(u_flip, ca, cb, d_gate, d_up, hidden, out, flipped):
    @pl.when(pl.program_id(0) == 0)
    def _():
        flipped[...] = hidden[...].T

    units = hidden.shape[1]
    out[:, :units] = dot(u_flip[...], d_gate[...]).astype(BF16)
    out[:, units : 2 * units] = dot(u_flip[...], d_up[...]).astype(BF16)
    cot = jnp.concatenate([flat(ca[...]), flat(cb[...])], axis=0)
    spread_blocks(flipped[...], cot, out, 2 * units)


def feed_grads(u_flip, ca, cb, d_gate, d_up, hidden, behind):
    width, length = u_flip.shape
    units = hidden.shape[1]
    chunk = 4 * HD
    return call(
        feed_grads_kernel,
        (width // chunk,),
        [rowed(chunk, length)]
        + [pl.BlockSpec((ca.shape[0], ca.shape[1] // 2, chunk), lambda i: (0, 1, i))] * 2
        + [fixed((length, units))] * 3,
        rowed(chunk, 3 * units),
        struct((width, 3 * units), BF16),
        2 * length * width * units * 3,
        scratch=[pltpu.VMEM((units, length), BF16)],
        behind=behind,
    )(u_flip, ca, cb, d_gate, d_up, hidden)


def gate_back_kernel(da, db, w_out, gate, attended, d_attended, d_gate):
    half = da.shape[0]
    for number, low in enumerate((da, db)):
        rows = slice(number * half, (number + 1) * half)
        d_gated = dot(low[...], w_out[...])
        sig = jax.nn.sigmoid(gate[rows, :])
        d_attended[rows, :] = (d_gated * sig).astype(BF16)
        d_gate[rows, :] = (d_gated * attended[rows, :] * sig * (1.0 - sig)).astype(BF16)


def gate_back(da, db, w, gate, attended):
    half, width = da.shape
    wide = (2 * half, 2 * HD)
    return call(
        gate_back_kernel,
        (1,),
        [fixed((half, width))] * 2
        + [pl.BlockSpec((width, 2 * HD), lambda i: (0, 3)), fixed(wide), fixed(wide)],
        [fixed(wide), fixed(wide)],
        [struct(wide, BF16), struct(wide, BF16)],
        2 * 2 * half * width * 2 * HD,
    )(da, db, w, gate, attended)


def head_back(grads, inputs, gain):
    factor = rms_scale(inputs)
    scaled = gain * grads
    back = factor * scaled - inputs * factor**3 * jnp.mean(scaled * inputs, axis=-1, keepdims=True)
    return back.astype(BF16), jnp.sum(grads * inputs * factor, axis=0, keepdims=True)


def attend_back_kernel(
    probs, low, d_attended, pre, gains, cosine, sine, out, terms, d_key, d_value
):
    step = pl.program_id(0)
    half = probs.shape[1]
    start = pl.multiple_of(step * half, half)
    rows = pl.ds(start, half)
    key, value = low[:, head(2)], low[:, head(3)]
    cos_rows, sin_rows = cosine[rows, :], sine[rows, :]

    @pl.when(step == 0)
    def _():
        d_key[...] = jnp.zeros_like(d_key)
        d_value[...] = jnp.zeros_like(d_value)
        terms[...] = jnp.zeros_like(terms)

    for number in range(2):
        share = probs[number]
        d_seen = d_attended[:, head(number)]
        d_share = dot_back(d_seen, value)
        d_scores = share * (d_share - jnp.sum(share * d_share, axis=-1, keepdims=True))
        d_scores = d_scores.astype(BF16)
        d_query = dot(d_scores, key) * SCALE
        d_key[...] += dot_rows(d_scores, low[rows, head(number)])
        d_value[...] += dot_rows(share.astype(BF16), d_seen)
        grads = d_query * cos_rows + unturn(d_query * sin_rows)
        back, term = head_back(grads, pre[rows, head(number)], gains[0:1, :])
        out[rows, head(number)] = back
        terms[0:1, :] += term

    @pl.when(step == 1)
    def _():
        grads = d_key[...] * SCALE
        grads = grads * cosine[...] + unturn(grads * sine[...])
        back, term = head_back(grads, pre[:, head(2)], gains[1:2, :])
        out[:, head(2)] = back
        terms[1:2, :] = term
        out[:, head(3)] = d_value[...].astype(BF16)


def attend_back(probs, low, d_attended, pre, gains, cosine, sine, behind):
    length = low.shape[0]
    half = length // 2
    return call(
        attend_back_kernel,
        (2,),
        [
            pl.BlockSpec((2, half, length), lambda i: (0, i, 0)),
            fixed((length, 4 * HD)),
            rowed(half, 2 * HD),
            fixed((length, 3 * HD)),
            fixed((8, HD)),
            fixed((length, HD)),
            fixed((length, HD)),
        ],
        [fixed((length, 4 * HD)), fixed((8, HD))],
        [struct((length, 4 * HD), BF16), struct((8, HD), F32)],
        20 * length * length * HD,
        scratch=[pltpu.VMEM((length, HD), F32), pltpu.VMEM((length, HD), F32)],
        behind=behind,
    )(probs, low, d_attended, pre, gains, cosine, sine)


def input_back_kernel(d_qkv, d_gate, w, mine, other):
    out = dot_back(d_qkv[...], w[:, : 4 * HD]) + dot_back(d_gate[...], w[:, 4 * HD :])

    @pl.when(pl.program_id(0) == 0)
    def _():
        mine[...] = out.astype(BF16)

    @pl.when(pl.program_id(0) == 1)
    def _():
        other[...] = out.astype(BF16)


def input_back(d_qkv, d_gate, w, behind):
    length = d_qkv.shape[0]
    half, width = length // 2, w.shape[0]
    return call(
        input_back_kernel,
        (2,),
        [rowed(half, 4 * HD), rowed(half, 2 * HD), fixed((width, 6 * HD))],
        [fixed((half, width)), fixed((half, width))],
        [struct((half, width), BF16), struct((half, width), BF16)],
        2 * length * width * 6 * HD,
        behind=behind,
    )(d_qkv, d_gate, w)


def attend_grads_kernel(x_flip, da, db, d_qkv, d_gate, gated, out, flipped):
    @pl.when(pl.program_id(0) == 0)
    def _():
        flipped[...] = gated[...].T

    inner, split = d_qkv.shape[1], d_gate.shape[1]
    out[:, :inner] = dot(x_flip[...], d_qkv[...]).astype(BF16)
    out[:, inner : inner + split] = dot(x_flip[...], d_gate[...]).astype(BF16)
    spread_blocks(
        flipped[...], jnp.concatenate([da[...], db[...]], axis=0), out, inner + split
    )


def attend_grads(x_flip, da, db, d_qkv, d_gate, gated, behind):
    width, length = x_flip.shape
    columns = d_qkv.shape[1] + d_gate.shape[1] + gated.shape[1]
    chunk = 4 * HD
    slab = pl.BlockSpec((length // 2, chunk), lambda i: (0, i))
    return call(
        attend_grads_kernel,
        (width // chunk,),
        [
            rowed(chunk, length),
            slab,
            slab,
            fixed(d_qkv.shape),
            fixed(d_gate.shape),
            fixed(gated.shape),
        ],
        rowed(chunk, columns),
        struct((width, columns), BF16),
        2 * length * width * columns,
        scratch=[pltpu.VMEM(gated.shape[::-1], BF16)],
        behind=behind,
    )(x_flip, da, db, d_qkv, d_gate, gated)


def middle_kernel(parts, x, middle, spread):
    total = x[...].astype(F32) + jnp.sum(parts[...].astype(F32), axis=0)
    middle[...] = total
    low = (total * rms_scale(total)).astype(BF16)
    for number in range(spread.shape[0]):
        spread[number] = low


def middle_step(parts, x, behind):
    shape = x.shape
    return call(
        middle_kernel,
        (1,),
        [fixed(parts.shape), fixed(shape)],
        [fixed(shape), fixed(parts.shape)],
        [struct(shape, F32), struct(parts.shape, BF16)],
        1 << 20,
        behind=behind,
    )(parts, x)


def norm_back(grads, inputs):
    factor = rms_scale(inputs)
    return factor * grads - inputs * factor**3 * jnp.mean(grads * inputs, axis=-1, keepdims=True)


def d_middle_kernel(parts, middle, cot, d_middle, spread):
    grads = jnp.sum(parts[...].astype(F32), axis=0)
    total = cot[...].astype(F32) + norm_back(grads, middle[...])
    d_middle[...] = total
    for number in range(spread.shape[0]):
        spread[number] = total.astype(BF16)


def d_middle_step(parts, middle, cot):
    shape = cot.shape
    return call(
        d_middle_kernel,
        (1,),
        [fixed(parts.shape), fixed(shape), fixed(shape)],
        [fixed(shape), fixed(parts.shape)],
        [struct(shape, F32), struct(parts.shape, BF16)],
        1 << 20,
    )(parts, middle, cot)


def ends_kernel(parts, middle, d_middle, x, out, terms):
    rows = x.shape[0]
    total = sum(part[...].astype(F32) for part in parts)
    out[:rows, :] = (middle[...] + total[:rows, :]).astype(BF16)
    inputs = x[...].astype(F32)
    grads = total[rows:, :]
    out[rows:, :] = (d_middle[...] + norm_back(grads, inputs)).astype(BF16)
    found = jnp.sum(grads * inputs * rms_scale(inputs), axis=0, keepdims=True)
    terms[...] = jnp.broadcast_to(found, terms.shape)


def ends_step(parts, middle, d_middle, x):
    shape, wide = x.shape, parts[0].shape
    count = len(parts)
    return call(
        lambda *refs: ends_kernel(refs[:count], *refs[count:]),
        (1,),
        [fixed(wide)] * count + [fixed(shape)] * 3,
        [fixed(wide), fixed((8, shape[1]))],
        [struct(wide, BF16), struct((8, shape[1]), F32)],
        1 << 20,
    )(*parts, middle, d_middle, x)


def prefetched(kernel, grid, in_specs, out_specs, out_shape, vmem=VMEM):
    return pl.pallas_call(
        kernel,
        grid_spec=pltpu.PrefetchScalarGridSpec(
            num_scalar_prefetch=1, grid=grid, in_specs=in_specs, out_specs=out_specs
        ),
        out_shape=out_shape,
        compiler_params=pltpu.CompilerParams(
            dimension_semantics=("arbitrary",) * len(grid), vmem_limit_bytes=vmem
        ),
        cost_estimate=pl.CostEstimate(flops=1 << 20, bytes_accessed=8 << 20, transcendentals=0),
    )


def copy_kernel(core, source, out):
    out[...] = source[...]


def sibling_part(core, found):
    pairs, _, rows, columns = found.shape
    return prefetched(
        copy_kernel,
        (pairs // 2,),
        [pl.BlockSpec((2, None, rows, columns), lambda i, at: (i, 1 - at[0], 0, 0))],
        pl.BlockSpec((2, rows, columns), lambda i, at: (i, 0, 0)),
        struct((pairs, rows, columns), found.dtype),
    )(core, found)


def join_kernel(core, mine, other, out):
    out[:, core[0]] = mine[...]
    out[:, 1 - core[0]] = other[...]


def join_cores(core, found, other):
    pairs, _, rows, columns = found.shape
    return prefetched(
        join_kernel,
        (pairs // 2,),
        [
            pl.BlockSpec((2, None, rows, columns), lambda i, at: (i, at[0], 0, 0)),
            pl.BlockSpec((2, rows, columns), lambda i, at: (i, 0, 0)),
        ],
        pl.BlockSpec((2, 2, rows, columns), lambda i, at: (i, 0, 0, 0)),
        struct(found.shape, found.dtype),
    )(core, found, other)


def lanes(value):
    return sum(value[:, start : start + HD] for start in range(0, value.shape[1], HD))


def pick(blocks):
    step = pl.program_id(0)
    value = blocks[0][...]
    for number in range(1, len(blocks)):
        value = jnp.where(step == number, blocks[number][...], value)
    return value.astype(F32)


def close_feed_kernel(turn_at, b0, b1, b2, b3, w_gate, w_up, gain, g_gate, g_up, g_down, sums):
    raw = pick((b0, b1, b2, b3))
    units = w_gate.shape[1]
    raw_gate, raw_up = raw[:, :units], raw[:, units : 2 * units]
    g_gate[...] = raw_gate * gain[...]
    g_up[...] = raw_up * gain[...]
    for place in range(units // HD):
        g_down[head(place), :] = raw[:, 2 * units + place * HD : 2 * units + (place + 1) * HD]
    term = lanes(raw_gate * w_gate[...].astype(F32)) + lanes(raw_up * w_up[...].astype(F32))

    @pl.when(pl.program_id(0) == 0)
    def _():
        sums[...] = term

    @pl.when(pl.program_id(0) > 0)
    def _():
        sums[...] += term


def close_attend_kernel(turn_at, b0, b1, b2, b3, gain, gq, gk, gv, gg, go):
    found, scale = pick((b0, b1, b2, b3)), gain[...]
    gq[...], gk[...] = found[:, : 2 * HD] * scale, found[:, head(2)] * scale
    gv[...], gg[...] = found[:, head(3)] * scale, found[:, 4 * HD : 6 * HD] * scale
    go[...] = jnp.concatenate([found[:, head(6)], found[:, head(7)]], axis=0)


def close(kernel, turn_at, blocks, weights, gain, out_rows, extra, read):
    quarters = 4
    place = lambda i, at: (at[0] + quarters - i) % quarters
    whole = lambda value: pl.BlockSpec(value.shape, lambda i, at: (0, 0))
    columns = lambda w: pl.BlockSpec(
        (w.shape[0], w.shape[1] // quarters), lambda i, at: (0, place(i, at))
    )
    rows, width = out_rows
    operands = weights if read else ()
    in_specs = [whole(b) for b in blocks] + [columns(w) for w in operands] + [whole(gain)]
    out_specs = [columns(w) for w in weights]
    out_specs += [pl.BlockSpec((rows // quarters, width), lambda i, at: (place(i, at), 0))]
    out_specs += [pl.BlockSpec(shape, lambda i, at: (0, 0)) for shape in extra]
    out_shape = [struct(w.shape, F32) for w in weights] + [struct(out_rows, F32)]
    out_shape += [struct(shape, F32) for shape in extra]
    return prefetched(kernel, (quarters,), in_specs, out_specs, out_shape, vmem=ALL_VMEM)(
        turn_at, *blocks, *operands, gain
    )


def column(row):
    shape = (HD, HD)
    there = lax.broadcasted_iota(jnp.int32, shape, 0) == lax.broadcasted_iota(jnp.int32, shape, 1)
    return jnp.sum(jnp.where(there, jnp.broadcast_to(row, shape), 0.0), axis=1, keepdims=True)


def first_kernel(at, wq, wk, wv, wg, wo, gain, out):
    scale = column(gain[...].astype(F32))
    start = 0
    for w in (wq, wk, wv, wg):
        stop = start + w.shape[1]
        out[:, start:stop] = (w[...].astype(F32) * scale).astype(BF16)
        start = stop
    out[:, start:] = wo[...].T


def first_columns(at, wq, wk, wv, wg, wo, gain):
    quarter = lambda w: pl.BlockSpec((w.shape[0], w.shape[1] // 4), lambda i, at: (0, at[0]))
    rows = wq.shape[0]
    heads = wo.shape[0] // 4
    columns = sum(w.shape[1] // 4 for w in (wq, wk, wv, wg)) + heads
    return prefetched(
        first_kernel,
        (1,),
        [quarter(w) for w in (wq, wk, wv, wg)]
        + [pl.BlockSpec((heads, rows), lambda i, at: (at[0], 0))]
        + [pl.BlockSpec(gain.shape, lambda i, at: (0, 0))],
        pl.BlockSpec((rows, columns), lambda i, at: (0, 0)),
        struct((rows, columns), BF16),
        vmem=ALL_VMEM,
    )(at, wq, wk, wv, wg, wo, gain)


def make_shards(mesh):
    n_shard, n_ctx, n_tp = mesh.shape["shard"], mesh.shape["ctx"], mesh.shape["tp"]
    pairs = n_shard // 2

    def joint(pair, core, tp):
        return (pair * 2 + core) * n_tp + tp

    core_perm = [(i, i ^ 1) for i in range(n_shard)]
    planes = [
        [joint(pair, core, tp) for pair in range(pairs) for tp in range(n_tp)] for core in range(2)
    ]
    swap_perm = [
        edge
        for pair in range(pairs)
        for edge in (
            (joint(pair, 1, 0), joint(pair, 0, 1)),
            (joint(pair, 0, 1), joint(pair, 1, 0)),
        )
    ]
    across_perm = [(joint(pair, t, t), joint(pair, t, 1 - t)) for pair in range(pairs) for t in range(2)]

    def spot(pair, core, ctx, tp):
        return ((pair * 2 + core) * n_ctx + ctx) * n_tp + tp

    owner_perms = [
        [
            (spot(pair, core, ctx, tp), spot(pair, tp, (ctx + by) % n_ctx, core))
            for pair in range(pairs)
            for core in range(2)
            for ctx in range(n_ctx)
            for tp in range(n_tp)
            if by > 0 or core != tp
        ]
        for by in range(n_ctx)
    ]

    def core_swap(value):
        return lax.ppermute(value, "shard", core_perm)

    def ctx_exchange(value):
        return lax.all_to_all(value, "ctx", 0, 0)

    def ctx_turn(value, by):
        return lax.ppermute(value, "ctx", [(i, (i + by) % n_ctx) for i in range(n_ctx)])

    def tree_rows(spread, *before):
        mine = ctx_exchange(spread)
        if before:
            mine, *before = lax.optimization_barrier((mine, *before))
        return mine, core_swap(mine), *before

    def tree_half(mine, other):
        half = (mine.astype(F32) + core_swap(other).astype(F32)).astype(BF16)
        return half.reshape((n_ctx, -1) + half.shape[1:])

    def plane_gather(value):
        return lax.all_gather(value, PLANE, axis=0, tiled=True, axis_index_groups=planes)

    def plane_scatter(value):
        return lax.psum_scatter(
            value, PLANE, scatter_dimension=0, tiled=True, axis_index_groups=planes
        )

    def shards(
        tokens,
        seg_lengths,
        seg_parents,
        gain_in,
        w_query,
        w_key,
        w_value,
        w_gate_attn,
        w_out,
        gain_query,
        gain_key,
        gain_mid,
        w_gate,
        w_up,
        w_down,
        cotangent,
    ):
        core = lax.axis_index("shard") % 2
        tp = lax.axis_index("tp")
        ctx = lax.axis_index("ctx")
        native = core == tp
        rows = tokens.shape[0] // 2

        def swapped(value):
            return jnp.where(native, value, lax.ppermute(value, PLANE, swap_perm))

        def quarter(weight, axis):
            size = weight.shape[axis] // n_ctx
            return lax.dynamic_slice_in_dim(weight, ctx * size, size, axis)

        gain_one = gain_in.astype(F32)[:, None]
        gain_two = gain_mid.astype(F32)[:, None]
        head_rows = gain_query.shape[0]
        first = first_columns(
            ctx.astype(jnp.int32).reshape(1), w_query, w_key, w_value, w_gate_attn, w_out, gain_in[None]
        )
        found = plane_gather(first)
        both_gains = jnp.pad(jnp.stack([gain_query, gain_key]), ((0, 6), (0, HD - head_rows)))
        both_gains = lax.all_to_all(
            jnp.broadcast_to(both_gains[None], (n_shard, 8, HD)), "shard", 0, 0
        )
        gains = both_gains[:, :, :head_rows].astype(F32).transpose(1, 0, 2).reshape(8, HD)

        def half_rows(place):
            pieces = [lax.dynamic_slice_in_dim(v, place * rows, rows, 0) for v in (tokens, cotangent)]
            return jnp.concatenate(pieces, axis=0)

        own = jnp.where(native, half_rows(core), core_swap(half_rows(1 - core)))
        tree = jnp.concatenate([seg_lengths, seg_parents], axis=0)
        tree = jnp.where(native, tree, core_swap(tree))
        own_x, own_cot = own[:rows], own[rows:]
        xa, xb = tree_rows(jnp.broadcast_to(own[None], (n_ctx,) + own.shape))

        second = jnp.concatenate([quarter(w_gate, 1), quarter(w_up, 1)], axis=1)
        second = (second.astype(F32) * gain_two).astype(BF16)
        second = jnp.concatenate([second, quarter(w_down, 0).T], axis=1)
        w2 = plane_gather(swapped(second))

        half_at = jnp.where(jnp.arange(2) == 0, core, 1 - core) * rows
        places = (
            half_at[:, None, None]
            + jnp.arange(n_ctx, dtype=jnp.int32)[None, :, None] * (2 * rows)
            + jnp.arange(rows, dtype=jnp.int32)[None, None, :]
        ).reshape(-1)
        segment, parent_seg, grand_seg, position = tree_layout(tree[0], tree[1], places)
        of_row = jnp.stack([segment, parent_seg, grand_seg, places], axis=1)
        of_column = jnp.stack([segment, places], axis=0)
        cosine, sine = rope_tables(position, HD)

        found, xa, xb, of_row, of_column, cosine, sine = lax.optimization_barrier(
            (found, xa, xb, of_row, of_column, cosine, sine)
        )
        found = found.reshape(pairs, n_tp, gain_in.shape[0], -1)
        core_at = core.astype(jnp.int32).reshape(1)
        other = core_swap(sibling_part(core_at, found))
        w1 = join_cores(core_at, found, other).reshape(-1, first.shape[1])

        xn, pre, low, gate = project(xa, xb, w1, gains, cosine, sine)
        probs, attended, gated, mine, other = attend(low, gate, w1, of_row, of_column)
        x_flip = flip(xn)
        middle, spread = middle_step(ctx_exchange(tree_half(mine, other)), own_x, (x_flip,))
        ua, ub = (flat(v) for v in tree_rows(spread))
        u_flip = flip(ua, ub)

        hidden, d_gate, d_up = feed(ua, ub, xa, xb, w2, (u_flip,))
        ffn = feed_grads(u_flip, xa, xb, d_gate, d_up, hidden, ())
        half = tree_half(*feed_back(d_gate, d_up, w2, (ffn,)))
        d_middle, spread = d_middle_step(ctx_exchange(half), middle, own_cot)
        layer_mine, layer_other = down_product(hidden, w2, 2, (half,))
        da, db, layer_mine, layer_other = tree_rows(spread, layer_mine, layer_other)
        da, db = flat(da), flat(db)
        grad_ffn = plane_scatter(ffn)

        d_attended, d_gate_pre = gate_back(da, db, w1, gate, attended)
        d_qkv, terms = attend_back(probs, low, d_attended, pre, gains, cosine, sine, ())

        attn = attend_grads(x_flip, da, db, d_qkv, d_gate_pre, gated, ())
        in_mine, in_other = input_back(d_qkv, d_gate_pre, w1, (attn,))
        layer_half, in_half = tree_half(layer_mine, layer_other), tree_half(in_mine, in_other)
        grad_attn = plane_scatter(attn)

        def owners(block):
            block = swapped(block)
            return [block] + [ctx_turn(block, by) for by in range(1, n_ctx)]

        def owners_at_once(block):
            moved = [lax.ppermute(block, ("shard", "ctx", "tp"), perm) for perm in owner_perms]
            return [jnp.where(native, block, moved[0])] + moved[1:]


        both = jnp.concatenate(
            [layer_half, in_half], axis=1
        )
        parts = [lax.dynamic_index_in_dim(both, ctx, 0, False)] + [
            ctx_turn(lax.dynamic_index_in_dim(both, (ctx + by) % n_ctx, 0, False), by)
            for by in range(1, n_ctx)
        ]
        ends, in_terms = ends_step(parts, middle, d_middle, own_x)
        pieces = jnp.concatenate(
            [terms[0].reshape(n_shard, -1), terms[1].reshape(n_shard, -1)], axis=1
        )
        pieces = jnp.pad(pieces, ((0, 0), (0, HD - pieces.shape[1])))
        pieces = jnp.stack([in_terms[0].reshape(n_shard, HD), pieces], axis=1).astype(BF16)
        copies = n_ctx * n_tp
        pieces = jnp.broadcast_to(
            jnp.pad(pieces, ((0, 0), (0, 6), (0, 0)))[:, None], (n_shard, copies, 8, HD)
        )
        pieces = lax.all_to_all(
            pieces.reshape(n_shard * copies, 8, HD), ("shard", "ctx", "tp"), 0, 0
        )
        end_sums = jnp.sum(pieces.astype(F32), axis=0)
        ffn_blocks = owners(grad_ffn)
        sibling = core_swap(ends)

        def whole(start):
            mine, other = ends[start : start + rows], sibling[start : start + rows]
            return jnp.where(
                core == 0,
                jnp.concatenate([mine, other], axis=0),
                jnp.concatenate([other, mine], axis=0),
            )

        full = jnp.stack([whole(0), whole(rows)])
        turn_at = ctx.astype(jnp.int32).reshape(1)
        size = gain_in.shape[0]
        grad_gate, grad_up, grad_down, mid_sums = close(
            close_feed_kernel,
            turn_at,
            ffn_blocks,
            (w_gate, w_up),
            gain_two,
            w_down.shape,
            [(size, HD)],
            True,
        )
        mid_terms = jnp.sum(mid_sums, axis=1)
        mid_terms = mid_terms + lax.ppermute(mid_terms, "tp", [(0, 1), (1, 0)])
        full = jnp.where(native, full, lax.ppermute(full, PLANE, across_perm))
        full = full.astype(F32)
        grad_attn, mid_terms, full = lax.optimization_barrier((grad_attn, mid_terms, full))
        grad_query, grad_key, grad_value, grad_gate_attn, grad_out = close(
            close_attend_kernel,
            turn_at,
            owners_at_once(grad_attn),
            (w_query, w_key, w_value, w_gate_attn),
            gain_one,
            w_out.shape,
            [],
            False,
        )

        return (
            full[0],
            full[1],
            end_sums[0] / gain_one[:, 0],
            grad_query,
            grad_key,
            grad_value,
            grad_gate_attn,
            grad_out,
            end_sums[1, :head_rows],
            end_sums[1, head_rows : 2 * head_rows],
            mid_terms,
            grad_gate,
            grad_up,
            grad_down,
        )

    return shards


def solution(mesh):
    return jax.shard_map(
        make_shards(mesh),
        mesh=mesh,
        in_specs=(
            P(("shard", "ctx"), None),
            P("shard", None),
            P("shard", None),
            P("shard"),
            P("shard", "tp"),
            P("shard", "tp"),
            P("shard", "tp"),
            P("shard", "tp"),
            P("tp", "shard"),
            P("shard"),
            P("shard"),
            P("shard"),
            P("shard", "tp"),
            P("shard", "tp"),
            P("tp", "shard"),
            P(("shard", "ctx"), None),
        ),
        out_specs=(
            P(("shard", "ctx"), None),
            P(("shard", "ctx"), None),
            P("shard"),
            P("shard", "tp"),
            P("shard", "tp"),
            P("shard", "tp"),
            P("shard", "tp"),
            P("tp", "shard"),
            P("shard"),
            P("shard"),
            P("shard"),
            P("shard", "tp"),
            P("shard", "tp"),
            P("tp", "shard"),
        ),
        check_vma=False,
    )
```

```python
import math

import jax
import jax.numpy as jnp
from jax import lax
from jax.experimental import pallas as pl
from jax.experimental.pallas import tpu as pltpu
from jax.sharding import PartitionSpec as P

HD = 128
EPS = 1e-06
BASE = 1000000.0
NEG = -1e30
F32 = jnp.float32
BF16 = jnp.bfloat16
PLANE = ("shard", "tp")
SCALE = 1.0 / math.sqrt(HD)
VMEM = 48 << 20
ALL_VMEM = 60 << 20


def lookup(onehot, table):
    return jnp.sum(onehot * table[None, :], axis=1)


def tree_layout(lengths, parents, places):
    labels = jnp.arange(lengths.shape[0], dtype=jnp.int32)
    ends = jnp.cumsum(lengths)
    starts = ends - lengths
    parent_hot = (parents[:, None] == labels[None, :]).astype(jnp.int32)
    grand = lookup(parent_hot, parents)
    parent_len = lookup(parent_hot, lengths)
    grand_hot = (grand[:, None] == labels[None, :]).astype(jnp.int32)
    grand_len = lookup(grand_hot, lengths)
    before = jnp.where(labels == 0, 0, parent_len + jnp.where(parents == 0, 0, grand_len))
    segment = jnp.sum((places[:, None] >= ends[None, :]).astype(jnp.int32), axis=1)
    token_hot = (segment[:, None] == labels[None, :]).astype(jnp.int32)
    position = places - lookup(token_hot, starts) + lookup(token_hot, before)
    return (segment, lookup(token_hot, parents), lookup(token_hot, grand), position)


def rope_tables(position, columns):
    halfway = columns // 2
    frequency = jnp.exp(jnp.arange(halfway, dtype=F32) * (-2.0 * math.log(BASE) / columns))
    angles = position.astype(F32)[:, None] * frequency[None, :]
    angles = jnp.concatenate([angles, angles], axis=1)
    return (jnp.cos(angles), jnp.sin(angles))


def rms_scale(inputs):
    return lax.rsqrt(jnp.mean(inputs * inputs, axis=-1, keepdims=True) + EPS)


def dot(left, right):
    return jnp.dot(left, right, preferred_element_type=F32)


def dot_rows(left, right):
    return lax.dot_general(left, right, (((0,), (0,)), ((), ())), preferred_element_type=F32)


def dot_back(left, right):
    return lax.dot_general(left, right, (((1,), (1,)), ((), ())), preferred_element_type=F32)


def turn(inputs):
    halfway = inputs.shape[-1] // 2
    return jnp.concatenate([-inputs[:, halfway:], inputs[:, :halfway]], axis=-1)


def unturn(inputs):
    halfway = inputs.shape[-1] // 2
    return jnp.concatenate([inputs[:, halfway:], -inputs[:, :halfway]], axis=-1)


def head(number):
    return slice(number * HD, (number + 1) * HD)


def call(
    kernel, grid, in_specs, out_specs, out_shape, flops, scratch=(), moved=8 << 20, behind=(), vmem=VMEM
):
    count = len(in_specs)

    def body(*refs):
        kernel(*refs[:count], *refs[count + len(behind) :])

    built = pl.pallas_call(
        body,
        grid=grid,
        in_specs=list(in_specs) + [pl.BlockSpec(memory_space=pl.ANY)] * len(behind),
        out_specs=out_specs,
        out_shape=out_shape,
        scratch_shapes=scratch,
        compiler_params=pltpu.CompilerParams(
            dimension_semantics=("arbitrary",) * len(grid), vmem_limit_bytes=vmem
        ),
        cost_estimate=pl.CostEstimate(flops=flops, bytes_accessed=moved, transcendentals=0),
    )
    return lambda *operands: built(*operands, *behind)


def struct(shape, dtype):
    return jax.ShapeDtypeStruct(shape, dtype)


def fixed(shape):
    return pl.BlockSpec(shape, lambda i: (0,) * len(shape))


def rowed(rows, columns):
    return pl.BlockSpec((rows, columns), lambda i: (i, 0))


def piled(shape, which):
    return pl.BlockSpec((shape[0], shape[1] // 2, shape[2]), lambda i: (0, which, 0))


def flat(value):
    return value.reshape((-1,) + value.shape[2:])


def project_kernel(xa, xb, w, gains, cosine, sine, xn, pre, low, gate):
    x = flat(jnp.where(pl.program_id(0) == 0, xa[...], xb[...])).astype(F32)
    normed = (x * rms_scale(x)).astype(BF16)
    xn[...] = normed
    out = dot(normed, w[...])
    for place in range(3):
        raw = out[:, head(place)]
        pre[:, head(place)] = raw
        unit = raw * rms_scale(raw) * gains[place // 2 : place // 2 + 1, :]
        low[:, head(place)] = (unit * cosine[...] + turn(unit) * sine[...]).astype(BF16)
    low[:, head(3)] = out[:, head(3)].astype(BF16)
    gate[...] = out[:, 4 * HD :]


def project(xa, xb, w, gains, cosine, sine):
    half, width = xa.shape[0] * xa.shape[1] // 2, xa.shape[2]
    return call(
        project_kernel,
        (2,),
        [
            piled(xa.shape, 0),
            piled(xb.shape, 0),
            fixed((width, 6 * HD)),
            fixed(gains.shape),
            rowed(half, HD),
            rowed(half, HD),
        ],
        [
            rowed(half, width),
            rowed(half, 3 * HD),
            rowed(half, 4 * HD),
            rowed(half, 2 * HD),
        ],
        [
            struct((2 * half, width), BF16),
            struct((2 * half, 3 * HD), F32),
            struct((2 * half, 4 * HD), BF16),
            struct((2 * half, 2 * HD), F32),
        ],
        2 * 2 * half * width * 6 * HD,
    )(xa, xb, w, gains, cosine, sine)


def attend_kernel(low, gate, w_out, of_row, of_column, probs, attended, gated, mine, other):
    step = pl.program_id(0)
    half = probs.shape[1]
    rows = pl.ds(step * half, half)
    key, value = low[:, head(2)], low[:, head(3)]
    seg, par, grand, place = (of_row[rows, n : n + 1] for n in range(4))
    key_seg, key_place = of_column[0:1, :], of_column[1:2, :]
    allowed = ((key_seg == seg) | (key_seg == par) | (key_seg == grand)) & (key_place <= place)
    for number in range(2):
        scores = dot_back(low[rows, head(number)], key) * SCALE
        scores = jnp.where(allowed, scores, NEG)
        raised = jnp.exp(scores - jnp.max(scores, axis=-1, keepdims=True))
        share = raised / jnp.sum(raised, axis=-1, keepdims=True)
        probs[number] = share
        seen = dot(share.astype(BF16), value)
        attended[:, head(number)] = seen
        gated[:, head(number)] = (seen * jax.nn.sigmoid(gate[:, head(number)])).astype(BF16)
    out = dot_back(gated[...], w_out[...])

    @pl.when(step == 0)
    def _():
        mine[...] = out.astype(BF16)

    @pl.when(step == 1)
    def _():
        other[...] = out.astype(BF16)


def attend(low, gate, w, of_row, of_column):
    length = low.shape[0]
    half, width = length // 2, w.shape[0]
    return call(
        attend_kernel,
        (2,),
        [
            fixed((length, 4 * HD)),
            rowed(half, 2 * HD),
            pl.BlockSpec((width, 2 * HD), lambda i: (0, 3)),
            fixed((length, 4)),
            fixed((2, length)),
        ],
        [
            pl.BlockSpec((2, half, length), lambda i: (0, i, 0)),
            rowed(half, 2 * HD),
            rowed(half, 2 * HD),
            fixed((half, width)),
            fixed((half, width)),
        ],
        [
            struct((2, length, length), F32),
            struct((length, 2 * HD), F32),
            struct((length, 2 * HD), BF16),
            struct((half, width), BF16),
            struct((half, width), BF16),
        ],
        2 * length * width * 2 * HD + 8 * length * length * HD,
    )(low, gate, w, of_row, of_column)


def flip_kernel(pieces, out):
    at = 0
    for piece in pieces:
        out[:, at : at + piece.shape[0]] = piece[...].T
        at += piece.shape[0]


def flip(*pieces):
    length, width = sum(piece.shape[0] for piece in pieces), pieces[0].shape[1]
    chunk = 2 * HD
    return call(
        lambda *refs: flip_kernel(refs[:-1], refs[-1]),
        (width // chunk,),
        [pl.BlockSpec((piece.shape[0], chunk), lambda i: (0, i)) for piece in pieces],
        rowed(chunk, length),
        struct((width, length), BF16),
        1 << 20,
    )(*pieces)


def feed_kernel(ua, ub, ca, cb, wg, wu, wd, hidden, d_gate, d_up):
    half = ua.shape[0]
    for number, (u, cot) in enumerate(((ua, ca), (ub, cb))):
        rows = slice(number * half, (number + 1) * half)
        gate, up = dot(u[...], wg[...]), dot(u[...], wu[...])
        d_hidden = dot(flat(cot[...]), wd[...])
        sig = jax.nn.sigmoid(gate)
        silu = gate * sig
        hidden[rows, :] = (silu * up).astype(BF16)
        d_gate[rows, :] = (d_hidden * up * sig * (1.0 + gate * (1.0 - sig))).astype(BF16)
        d_up[rows, :] = (d_hidden * silu).astype(BF16)


def feed(ua, ub, ca, cb, w, behind):
    half, width = ua.shape
    chunk = 2 * HD
    parts = w.shape[1] // 3 // chunk
    column = lambda shift: pl.BlockSpec((width, chunk), lambda i: (0, shift * parts + i))
    unit = pl.BlockSpec((2 * half, chunk), lambda i: (0, i))
    units = parts * chunk
    return call(
        feed_kernel,
        (parts,),
        [fixed((half, width))] * 2
        + [piled(ca.shape, 1)] * 2
        + [column(0), column(1), column(2)],
        [unit, unit, unit],
        [struct((2 * half, units), BF16)] * 3,
        2 * 2 * half * width * units * 3,
        behind=behind,
        vmem=60 << 20,
    )(ua, ub, ca, cb, w, w, w)


def feed_back_kernel(d_gate, d_up, wg, wu, mine, other):
    half = mine.shape[0]
    out = dot_back(d_gate[...], wg[...]) + dot_back(d_up[...], wu[...])
    mine[...] = out[:half, :].astype(BF16)
    other[...] = out[half:, :].astype(BF16)


def feed_back(d_gate, d_up, w, behind):
    length, units = d_gate.shape
    half, width = length // 2, w.shape[0]
    chunk = 4 * HD
    slab = pl.BlockSpec((half, chunk), lambda i: (0, i))
    return call(
        feed_back_kernel,
        (width // chunk,),
        [fixed((length, units))] * 2
        + [
            pl.BlockSpec((chunk, units), lambda i: (i, 0)),
            pl.BlockSpec((chunk, units), lambda i: (i, 1)),
        ],
        [slab, slab],
        [struct((half, width), BF16), struct((half, width), BF16)],
        2 * length * width * units * 2,
        behind=behind,
        vmem=48 << 20,
    )(d_gate, d_up, w, w)


def down_kernel(hidden, w, mine, other):
    out = dot_back(hidden[...], w[...])

    @pl.when(pl.program_id(0) == 0)
    def _():
        mine[...] = out.astype(BF16)

    @pl.when(pl.program_id(0) == 1)
    def _():
        other[...] = out.astype(BF16)


def down_product(left, w, place, behind):
    length, units = left.shape
    half, width = length // 2, w.shape[0]
    return call(
        down_kernel,
        (2,),
        [rowed(half, units), pl.BlockSpec((width, units), lambda i: (0, place))],
        [fixed((half, width)), fixed((half, width))],
        [struct((half, width), BF16), struct((half, width), BF16)],
        2 * length * width * units,
        behind=behind,
    )(left, w)


def spread_blocks(flipped, right, out, start):
    term = dot(flipped, right).astype(BF16)
    for place in range(flipped.shape[0] // HD):
        for owner in range(right.shape[1] // HD):
            at = start + place * HD
            out[owner * HD : (owner + 1) * HD, at : at + HD] = term[head(place), head(owner)]


def feed_grads_kernel(u_flip, ca, cb, d_gate, d_up, hidden, out, flipped):
    @pl.when(pl.program_id(0) == 0)
    def _():
        flipped[...] = hidden[...].T

    units = hidden.shape[1]
    out[:, :units] = dot(u_flip[...], d_gate[...]).astype(BF16)
    out[:, units : 2 * units] = dot(u_flip[...], d_up[...]).astype(BF16)
    cot = jnp.concatenate([flat(ca[...]), flat(cb[...])], axis=0)
    spread_blocks(flipped[...], cot, out, 2 * units)


def feed_grads(u_flip, ca, cb, d_gate, d_up, hidden, behind):
    width, length = u_flip.shape
    units = hidden.shape[1]
    chunk = 4 * HD
    return call(
        feed_grads_kernel,
        (width // chunk,),
        [rowed(chunk, length)]
        + [pl.BlockSpec((ca.shape[0], ca.shape[1] // 2, chunk), lambda i: (0, 1, i))] * 2
        + [fixed((length, units))] * 3,
        rowed(chunk, 3 * units),
        struct((width, 3 * units), BF16),
        2 * length * width * units * 3,
        scratch=[pltpu.VMEM((units, length), BF16)],
        vmem=56 << 20,
        behind=behind,
    )(u_flip, ca, cb, d_gate, d_up, hidden)


def gate_back_kernel(da, db, w_out, gate, attended, d_attended, d_gate):
    half = da.shape[0]
    for number, low in enumerate((da, db)):
        rows = slice(number * half, (number + 1) * half)
        d_gated = dot(low[...], w_out[...])
        sig = jax.nn.sigmoid(gate[rows, :])
        d_attended[rows, :] = (d_gated * sig).astype(BF16)
        d_gate[rows, :] = (d_gated * attended[rows, :] * sig * (1.0 - sig)).astype(BF16)


def gate_back(da, db, w, gate, attended):
    half, width = da.shape
    wide = (2 * half, 2 * HD)
    return call(
        gate_back_kernel,
        (1,),
        [fixed((half, width))] * 2
        + [pl.BlockSpec((width, 2 * HD), lambda i: (0, 3)), fixed(wide), fixed(wide)],
        [fixed(wide), fixed(wide)],
        [struct(wide, BF16), struct(wide, BF16)],
        2 * 2 * half * width * 2 * HD,
    )(da, db, w, gate, attended)


def head_back(grads, inputs, gain):
    factor = rms_scale(inputs)
    scaled = gain * grads
    back = factor * scaled - inputs * factor**3 * jnp.mean(scaled * inputs, axis=-1, keepdims=True)
    return back.astype(BF16), jnp.sum(grads * inputs * factor, axis=0, keepdims=True)


def attend_back_kernel(
    probs, low, d_attended, pre, gains, cosine, sine, out, terms, d_key, d_value
):
    step = pl.program_id(0)
    half = probs.shape[1]
    start = pl.multiple_of(step * half, half)
    rows = pl.ds(start, half)
    key, value = low[:, head(2)], low[:, head(3)]
    cos_rows, sin_rows = cosine[rows, :], sine[rows, :]

    @pl.when(step == 0)
    def _():
        d_key[...] = jnp.zeros_like(d_key)
        d_value[...] = jnp.zeros_like(d_value)
        terms[...] = jnp.zeros_like(terms)

    for number in range(2):
        share = probs[number]
        d_seen = d_attended[:, head(number)]
        d_share = dot_back(d_seen, value)
        d_scores = share * (d_share - jnp.sum(share * d_share, axis=-1, keepdims=True))
        d_scores = d_scores.astype(BF16)
        d_query = dot(d_scores, key) * SCALE
        d_key[...] += dot_rows(d_scores, low[rows, head(number)])
        d_value[...] += dot_rows(share.astype(BF16), d_seen)
        grads = d_query * cos_rows + unturn(d_query * sin_rows)
        back, term = head_back(grads, pre[rows, head(number)], gains[0:1, :])
        out[rows, head(number)] = back
        terms[0:1, :] += term

    @pl.when(step == 1)
    def _():
        grads = d_key[...] * SCALE
        grads = grads * cosine[...] + unturn(grads * sine[...])
        back, term = head_back(grads, pre[:, head(2)], gains[1:2, :])
        out[:, head(2)] = back
        terms[1:2, :] = term
        out[:, head(3)] = d_value[...].astype(BF16)


def attend_back(probs, low, d_attended, pre, gains, cosine, sine, behind):
    length = low.shape[0]
    half = length // 2
    return call(
        attend_back_kernel,
        (2,),
        [
            pl.BlockSpec((2, half, length), lambda i: (0, i, 0)),
            fixed((length, 4 * HD)),
            rowed(half, 2 * HD),
            fixed((length, 3 * HD)),
            fixed((8, HD)),
            fixed((length, HD)),
            fixed((length, HD)),
        ],
        [fixed((length, 4 * HD)), fixed((8, HD))],
        [struct((length, 4 * HD), BF16), struct((8, HD), F32)],
        20 * length * length * HD,
        scratch=[pltpu.VMEM((length, HD), F32), pltpu.VMEM((length, HD), F32)],
        behind=behind,
    )(probs, low, d_attended, pre, gains, cosine, sine)


def input_back_kernel(d_qkv, d_gate, w, mine, other):
    out = dot_back(d_qkv[...], w[:, : 4 * HD]) + dot_back(d_gate[...], w[:, 4 * HD :])

    @pl.when(pl.program_id(0) == 0)
    def _():
        mine[...] = out.astype(BF16)

    @pl.when(pl.program_id(0) == 1)
    def _():
        other[...] = out.astype(BF16)


def input_back(d_qkv, d_gate, w, behind):
    length = d_qkv.shape[0]
    half, width = length // 2, w.shape[0]
    return call(
        input_back_kernel,
        (2,),
        [rowed(half, 4 * HD), rowed(half, 2 * HD), fixed((width, 6 * HD))],
        [fixed((half, width)), fixed((half, width))],
        [struct((half, width), BF16), struct((half, width), BF16)],
        2 * length * width * 6 * HD,
        behind=behind,
    )(d_qkv, d_gate, w)


def attend_grads_kernel(x_flip, da, db, d_qkv, d_gate, gated, out, flipped):
    @pl.when(pl.program_id(0) == 0)
    def _():
        flipped[...] = gated[...].T

    inner, split = d_qkv.shape[1], d_gate.shape[1]
    out[:, :inner] = dot(x_flip[...], d_qkv[...]).astype(BF16)
    out[:, inner : inner + split] = dot(x_flip[...], d_gate[...]).astype(BF16)
    spread_blocks(
        flipped[...], jnp.concatenate([da[...], db[...]], axis=0), out, inner + split
    )


def attend_grads(x_flip, da, db, d_qkv, d_gate, gated, behind):
    width, length = x_flip.shape
    columns = d_qkv.shape[1] + d_gate.shape[1] + gated.shape[1]
    chunk = 4 * HD
    slab = pl.BlockSpec((length // 2, chunk), lambda i: (0, i))
    return call(
        attend_grads_kernel,
        (width // chunk,),
        [
            rowed(chunk, length),
            slab,
            slab,
            fixed(d_qkv.shape),
            fixed(d_gate.shape),
            fixed(gated.shape),
        ],
        rowed(chunk, columns),
        struct((width, columns), BF16),
        2 * length * width * columns,
        scratch=[pltpu.VMEM(gated.shape[::-1], BF16)],
        behind=behind,
    )(x_flip, da, db, d_qkv, d_gate, gated)


def middle_kernel(parts, x, middle, spread):
    total = x[...].astype(F32) + jnp.sum(parts[...].astype(F32), axis=0)
    middle[...] = total
    low = (total * rms_scale(total)).astype(BF16)
    for number in range(spread.shape[0]):
        spread[number] = low


def middle_step(parts, x, behind):
    shape = x.shape
    return call(
        middle_kernel,
        (1,),
        [fixed(parts.shape), fixed(shape)],
        [fixed(shape), fixed(parts.shape)],
        [struct(shape, F32), struct(parts.shape, BF16)],
        1 << 20,
        behind=behind,
    )(parts, x)


def norm_back(grads, inputs):
    factor = rms_scale(inputs)
    return factor * grads - inputs * factor**3 * jnp.mean(grads * inputs, axis=-1, keepdims=True)


def d_middle_kernel(parts, middle, cot, d_middle, spread):
    grads = jnp.sum(parts[...].astype(F32), axis=0)
    total = cot[...].astype(F32) + norm_back(grads, middle[...])
    d_middle[...] = total
    for number in range(spread.shape[0]):
        spread[number] = total.astype(BF16)


def d_middle_step(parts, middle, cot):
    shape = cot.shape
    return call(
        d_middle_kernel,
        (1,),
        [fixed(parts.shape), fixed(shape), fixed(shape)],
        [fixed(shape), fixed(parts.shape)],
        [struct(shape, F32), struct(parts.shape, BF16)],
        1 << 20,
    )(parts, middle, cot)


def ends_kernel(parts, middle, d_middle, x, out, terms):
    rows = x.shape[0]
    total = sum(part[...].astype(F32) for part in parts)
    out[:rows, :] = (middle[...] + total[:rows, :]).astype(BF16)
    inputs = x[...].astype(F32)
    grads = total[rows:, :]
    out[rows:, :] = (d_middle[...] + norm_back(grads, inputs)).astype(BF16)
    found = jnp.sum(grads * inputs * rms_scale(inputs), axis=0, keepdims=True)
    terms[...] = jnp.broadcast_to(found, terms.shape)


def ends_step(parts, middle, d_middle, x):
    shape, wide = x.shape, parts[0].shape
    count = len(parts)
    return call(
        lambda *refs: ends_kernel(refs[:count], *refs[count:]),
        (1,),
        [fixed(wide)] * count + [fixed(shape)] * 3,
        [fixed(wide), fixed((8, shape[1]))],
        [struct(wide, BF16), struct((8, shape[1]), F32)],
        1 << 20,
    )(*parts, middle, d_middle, x)


def prefetched(kernel, grid, in_specs, out_specs, out_shape, vmem=VMEM):
    return pl.pallas_call(
        kernel,
        grid_spec=pltpu.PrefetchScalarGridSpec(
            num_scalar_prefetch=1, grid=grid, in_specs=in_specs, out_specs=out_specs
        ),
        out_shape=out_shape,
        compiler_params=pltpu.CompilerParams(
            dimension_semantics=("arbitrary",) * len(grid), vmem_limit_bytes=vmem
        ),
        cost_estimate=pl.CostEstimate(flops=1 << 20, bytes_accessed=8 << 20, transcendentals=0),
    )


def copy_kernel(core, source, out):
    out[...] = source[...]


def sibling_part(core, found):
    pairs, _, rows, columns = found.shape
    return prefetched(
        copy_kernel,
        (pairs // 2,),
        [pl.BlockSpec((2, None, rows, columns), lambda i, at: (i, 1 - at[0], 0, 0))],
        pl.BlockSpec((2, rows, columns), lambda i, at: (i, 0, 0)),
        struct((pairs, rows, columns), found.dtype),
    )(core, found)


def join_kernel(core, mine, other, out):
    out[:, core[0]] = mine[...]
    out[:, 1 - core[0]] = other[...]


def join_cores(core, found, other):
    pairs, _, rows, columns = found.shape
    return prefetched(
        join_kernel,
        (pairs // 2,),
        [
            pl.BlockSpec((2, None, rows, columns), lambda i, at: (i, at[0], 0, 0)),
            pl.BlockSpec((2, rows, columns), lambda i, at: (i, 0, 0)),
        ],
        pl.BlockSpec((2, 2, rows, columns), lambda i, at: (i, 0, 0, 0)),
        struct(found.shape, found.dtype),
    )(core, found, other)


def lanes(value):
    return sum(value[:, start : start + HD] for start in range(0, value.shape[1], HD))


def pick(blocks):
    step = pl.program_id(0)
    value = blocks[0][...]
    for number in range(1, len(blocks)):
        value = jnp.where(step == number, blocks[number][...], value)
    return value.astype(F32)


def close_feed_kernel(turn_at, b0, b1, b2, b3, w_gate, w_up, gain, g_gate, g_up, g_down, sums):
    raw = pick((b0, b1, b2, b3))
    units = w_gate.shape[1]
    raw_gate, raw_up = raw[:, :units], raw[:, units : 2 * units]
    g_gate[...] = raw_gate * gain[...]
    g_up[...] = raw_up * gain[...]
    for place in range(units // HD):
        g_down[head(place), :] = raw[:, 2 * units + place * HD : 2 * units + (place + 1) * HD]
    term = lanes(raw_gate * w_gate[...].astype(F32)) + lanes(raw_up * w_up[...].astype(F32))

    @pl.when(pl.program_id(0) == 0)
    def _():
        sums[...] = term

    @pl.when(pl.program_id(0) > 0)
    def _():
        sums[...] += term


def close_attend_kernel(turn_at, b0, b1, b2, b3, gain, gq, gk, gv, gg, go):
    found, scale = pick((b0, b1, b2, b3)), gain[...]
    gq[...], gk[...] = found[:, : 2 * HD] * scale, found[:, head(2)] * scale
    gv[...], gg[...] = found[:, head(3)] * scale, found[:, 4 * HD : 6 * HD] * scale
    go[...] = jnp.concatenate([found[:, head(6)], found[:, head(7)]], axis=0)


def close(kernel, turn_at, blocks, weights, gain, out_rows, extra, read):
    quarters = 4
    place = lambda i, at: (at[0] + quarters - i) % quarters
    whole = lambda value: pl.BlockSpec(value.shape, lambda i, at: (0, 0))
    columns = lambda w: pl.BlockSpec(
        (w.shape[0], w.shape[1] // quarters), lambda i, at: (0, place(i, at))
    )
    rows, width = out_rows
    operands = weights if read else ()
    in_specs = [whole(b) for b in blocks] + [columns(w) for w in operands] + [whole(gain)]
    out_specs = [columns(w) for w in weights]
    out_specs += [pl.BlockSpec((rows // quarters, width), lambda i, at: (place(i, at), 0))]
    out_specs += [pl.BlockSpec(shape, lambda i, at: (0, 0)) for shape in extra]
    out_shape = [struct(w.shape, F32) for w in weights] + [struct(out_rows, F32)]
    out_shape += [struct(shape, F32) for shape in extra]
    return prefetched(kernel, (quarters,), in_specs, out_specs, out_shape, vmem=ALL_VMEM)(
        turn_at, *blocks, *operands, gain
    )


def column(row):
    shape = (HD, HD)
    there = lax.broadcasted_iota(jnp.int32, shape, 0) == lax.broadcasted_iota(jnp.int32, shape, 1)
    return jnp.sum(jnp.where(there, jnp.broadcast_to(row, shape), 0.0), axis=1, keepdims=True)


def first_kernel(at, wq, wk, wv, wg, wo, gain, out):
    scale = column(gain[...].astype(F32))
    start = 0
    for w in (wq, wk, wv, wg):
        stop = start + w.shape[1]
        out[:, start:stop] = (w[...].astype(F32) * scale).astype(BF16)
        start = stop
    out[:, start:] = wo[...].T


def first_columns(at, wq, wk, wv, wg, wo, gain):
    quarter = lambda w: pl.BlockSpec((w.shape[0], w.shape[1] // 4), lambda i, at: (0, at[0]))
    rows = wq.shape[0]
    heads = wo.shape[0] // 4
    columns = sum(w.shape[1] // 4 for w in (wq, wk, wv, wg)) + heads
    return prefetched(
        first_kernel,
        (1,),
        [quarter(w) for w in (wq, wk, wv, wg)]
        + [pl.BlockSpec((heads, rows), lambda i, at: (at[0], 0))]
        + [pl.BlockSpec(gain.shape, lambda i, at: (0, 0))],
        pl.BlockSpec((rows, columns), lambda i, at: (0, 0)),
        struct((rows, columns), BF16),
        vmem=ALL_VMEM,
    )(at, wq, wk, wv, wg, wo, gain)


def make_shards(mesh):
    n_shard, n_ctx, n_tp = mesh.shape["shard"], mesh.shape["ctx"], mesh.shape["tp"]
    pairs = n_shard // 2

    def joint(pair, core, tp):
        return (pair * 2 + core) * n_tp + tp

    core_perm = [(i, i ^ 1) for i in range(n_shard)]
    planes = [
        [joint(pair, core, tp) for pair in range(pairs) for tp in range(n_tp)] for core in range(2)
    ]
    swap_perm = [
        edge
        for pair in range(pairs)
        for edge in (
            (joint(pair, 1, 0), joint(pair, 0, 1)),
            (joint(pair, 0, 1), joint(pair, 1, 0)),
        )
    ]
    across_perm = [(joint(pair, t, t), joint(pair, t, 1 - t)) for pair in range(pairs) for t in range(2)]

    def spot(pair, core, ctx, tp):
        return ((pair * 2 + core) * n_ctx + ctx) * n_tp + tp

    owner_perms = [
        [
            (spot(pair, core, ctx, tp), spot(pair, tp, (ctx + by) % n_ctx, core))
            for pair in range(pairs)
            for core in range(2)
            for ctx in range(n_ctx)
            for tp in range(n_tp)
            if by > 0 or core != tp
        ]
        for by in range(n_ctx)
    ]

    def core_swap(value):
        return lax.ppermute(value, "shard", core_perm)

    def ctx_exchange(value):
        return lax.all_to_all(value, "ctx", 0, 0)

    def ctx_turn(value, by):
        return lax.ppermute(value, "ctx", [(i, (i + by) % n_ctx) for i in range(n_ctx)])

    def tree_rows(spread, *before):
        mine = ctx_exchange(spread)
        if before:
            mine, *before = lax.optimization_barrier((mine, *before))
        return mine, core_swap(mine), *before

    def tree_half(mine, other):
        half = (mine.astype(F32) + core_swap(other).astype(F32)).astype(BF16)
        return half.reshape((n_ctx, -1) + half.shape[1:])

    def plane_gather(value):
        return lax.all_gather(value, PLANE, axis=0, tiled=True, axis_index_groups=planes)

    def plane_scatter(value):
        return lax.psum_scatter(
            value, PLANE, scatter_dimension=0, tiled=True, axis_index_groups=planes
        )

    def shards(
        tokens,
        seg_lengths,
        seg_parents,
        gain_in,
        w_query,
        w_key,
        w_value,
        w_gate_attn,
        w_out,
        gain_query,
        gain_key,
        gain_mid,
        w_gate,
        w_up,
        w_down,
        cotangent,
    ):
        core = lax.axis_index("shard") % 2
        tp = lax.axis_index("tp")
        ctx = lax.axis_index("ctx")
        native = core == tp
        rows = tokens.shape[0] // 2

        def swapped(value):
            return jnp.where(native, value, lax.ppermute(value, PLANE, swap_perm))

        def quarter(weight, axis):
            size = weight.shape[axis] // n_ctx
            return lax.dynamic_slice_in_dim(weight, ctx * size, size, axis)

        gain_one = gain_in.astype(F32)[:, None]
        gain_two = gain_mid.astype(F32)[:, None]
        head_rows = gain_query.shape[0]
        first = first_columns(
            ctx.astype(jnp.int32).reshape(1), w_query, w_key, w_value, w_gate_attn, w_out, gain_in[None]
        )
        found = plane_gather(first)
        both_gains = jnp.pad(jnp.stack([gain_query, gain_key]), ((0, 6), (0, HD - head_rows)))
        both_gains = lax.all_to_all(
            jnp.broadcast_to(both_gains[None], (n_shard, 8, HD)), "shard", 0, 0
        )

        def half_rows(place):
            pieces = [lax.dynamic_slice_in_dim(v, place * rows, rows, 0) for v in (tokens, cotangent)]
            return jnp.concatenate(pieces, axis=0)

        own = jnp.where(native, half_rows(core), core_swap(half_rows(1 - core)))
        tree = jnp.concatenate([seg_lengths, seg_parents], axis=0)
        tree = jnp.where(native, tree, core_swap(tree))
        own, both_gains = lax.optimization_barrier((own, both_gains))
        own_x, own_cot = own[:rows], own[rows:]
        xa, xb = tree_rows(jnp.broadcast_to(own[None], (n_ctx,) + own.shape))

        second = jnp.concatenate([quarter(w_gate, 1), quarter(w_up, 1)], axis=1)
        second = (second.astype(F32) * gain_two).astype(BF16)
        second = jnp.concatenate([second, quarter(w_down, 0).T], axis=1)
        moved = lax.ppermute(second, PLANE, swap_perm)
        moved, xa = lax.optimization_barrier((moved, xa))
        w2 = plane_gather(jnp.where(native, second, moved))

        gains = both_gains[:, :, :head_rows].astype(F32).transpose(1, 0, 2).reshape(8, HD)
        half_at = jnp.where(jnp.arange(2) == 0, core, 1 - core) * rows
        places = (
            half_at[:, None, None]
            + jnp.arange(n_ctx, dtype=jnp.int32)[None, :, None] * (2 * rows)
            + jnp.arange(rows, dtype=jnp.int32)[None, None, :]
        ).reshape(-1)
        segment, parent_seg, grand_seg, position = tree_layout(tree[0], tree[1], places)
        of_row = jnp.stack([segment, parent_seg, grand_seg, places], axis=1)
        of_column = jnp.stack([segment, places], axis=0)
        cosine, sine = rope_tables(position, HD)

        found, xa, xb, of_row, of_column, cosine, sine = lax.optimization_barrier(
            (found, xa, xb, of_row, of_column, cosine, sine)
        )
        found = found.reshape(pairs, n_tp, gain_in.shape[0], -1)
        core_at = core.astype(jnp.int32).reshape(1)
        other = core_swap(sibling_part(core_at, found))
        w1 = join_cores(core_at, found, other).reshape(-1, first.shape[1])

        xn, pre, low, gate = project(xa, xb, w1, gains, cosine, sine)
        probs, attended, gated, mine, other = attend(low, gate, w1, of_row, of_column)
        x_flip = flip(xn)
        middle, spread = middle_step(ctx_exchange(tree_half(mine, other)), own_x, (x_flip,))
        ua, ub = (flat(v) for v in tree_rows(spread))
        u_flip = flip(ua, ub)

        hidden, d_gate, d_up = feed(ua, ub, xa, xb, w2, (u_flip,))
        ffn = feed_grads(u_flip, xa, xb, d_gate, d_up, hidden, ())
        half = tree_half(*feed_back(d_gate, d_up, w2, (ffn,)))
        d_middle, spread = d_middle_step(ctx_exchange(half), middle, own_cot)
        layer_mine, layer_other = down_product(hidden, w2, 2, (half,))
        da, db, layer_mine, layer_other = tree_rows(spread, layer_mine, layer_other)
        da, db = flat(da), flat(db)
        grad_ffn = plane_scatter(ffn)

        d_attended, d_gate_pre = gate_back(da, db, w1, gate, attended)
        d_qkv, terms = attend_back(probs, low, d_attended, pre, gains, cosine, sine, ())

        attn = attend_grads(x_flip, da, db, d_qkv, d_gate_pre, gated, ())
        in_mine, in_other = input_back(d_qkv, d_gate_pre, w1, (attn,))
        layer_half, in_half = tree_half(layer_mine, layer_other), tree_half(in_mine, in_other)
        grad_attn = plane_scatter(attn)
        layer_half, in_half, grad_ffn = lax.optimization_barrier((layer_half, in_half, grad_ffn))

        def owners(block):
            block = swapped(block)
            return [block] + [ctx_turn(block, by) for by in range(1, n_ctx)]

        def owners_at_once(block):
            moved = [lax.ppermute(block, ("shard", "ctx", "tp"), perm) for perm in owner_perms]
            return [jnp.where(native, block, moved[0])] + moved[1:]


        both = jnp.concatenate(
            [layer_half, in_half], axis=1
        )
        parts = [lax.dynamic_index_in_dim(both, ctx, 0, False)] + [
            ctx_turn(lax.dynamic_index_in_dim(both, (ctx + by) % n_ctx, 0, False), by)
            for by in range(1, n_ctx)
        ]
        ends, in_terms = ends_step(parts, middle, d_middle, own_x)
        pieces = jnp.concatenate(
            [terms[0].reshape(n_shard, -1), terms[1].reshape(n_shard, -1)], axis=1
        )
        pieces = jnp.pad(pieces, ((0, 0), (0, HD - pieces.shape[1])))
        pieces = jnp.stack([in_terms[0].reshape(n_shard, HD), pieces], axis=1).astype(BF16)
        copies = n_ctx * n_tp
        pieces = jnp.broadcast_to(
            jnp.pad(pieces, ((0, 0), (0, 6), (0, 0)))[:, None], (n_shard, copies, 8, HD)
        )
        pieces = lax.all_to_all(
            pieces.reshape(n_shard * copies, 8, HD), ("shard", "ctx", "tp"), 0, 0
        )
        end_sums = jnp.sum(pieces.astype(F32), axis=0)
        ffn_blocks = owners(grad_ffn)
        sibling = core_swap(ends)

        def whole(start):
            mine, other = ends[start : start + rows], sibling[start : start + rows]
            return jnp.where(
                core == 0,
                jnp.concatenate([mine, other], axis=0),
                jnp.concatenate([other, mine], axis=0),
            )

        full = jnp.stack([whole(0), whole(rows)])
        turn_at = ctx.astype(jnp.int32).reshape(1)
        size = gain_in.shape[0]
        grad_gate, grad_up, grad_down, mid_sums = close(
            close_feed_kernel,
            turn_at,
            ffn_blocks,
            (w_gate, w_up),
            gain_two,
            w_down.shape,
            [(size, HD)],
            True,
        )
        mid_terms = jnp.sum(mid_sums, axis=1)
        mid_terms = mid_terms + lax.ppermute(mid_terms, "tp", [(0, 1), (1, 0)])
        full = jnp.where(native, full, lax.ppermute(full, PLANE, across_perm))
        full = full.astype(F32)
        grad_attn, mid_terms, full = lax.optimization_barrier((grad_attn, mid_terms, full))
        grad_query, grad_key, grad_value, grad_gate_attn, grad_out = close(
            close_attend_kernel,
            turn_at,
            owners_at_once(grad_attn),
            (w_query, w_key, w_value, w_gate_attn),
            gain_one,
            w_out.shape,
            [],
            False,
        )

        return (
            full[0],
            full[1],
            end_sums[0] / gain_one[:, 0],
            grad_query,
            grad_key,
            grad_value,
            grad_gate_attn,
            grad_out,
            end_sums[1, :head_rows],
            end_sums[1, head_rows : 2 * head_rows],
            mid_terms,
            grad_gate,
            grad_up,
            grad_down,
        )

    return shards


def solution(mesh):
    return jax.shard_map(
        make_shards(mesh),
        mesh=mesh,
        in_specs=(
            P(("shard", "ctx"), None),
            P("shard", None),
            P("shard", None),
            P("shard"),
            P("shard", "tp"),
            P("shard", "tp"),
            P("shard", "tp"),
            P("shard", "tp"),
            P("tp", "shard"),
            P("shard"),
            P("shard"),
            P("shard"),
            P("shard", "tp"),
            P("shard", "tp"),
            P("tp", "shard"),
            P(("shard", "ctx"), None),
        ),
        out_specs=(
            P(("shard", "ctx"), None),
            P(("shard", "ctx"), None),
            P("shard"),
            P("shard", "tp"),
            P("shard", "tp"),
            P("shard", "tp"),
            P("shard", "tp"),
            P("tp", "shard"),
            P("shard"),
            P("shard"),
            P("shard"),
            P("shard", "tp"),
            P("shard", "tp"),
            P("tp", "shard"),
        ),
        check_vma=False,
    )
```

```python
import math

import jax
import jax.numpy as jnp
from jax import lax
from jax.experimental import pallas as pl
from jax.experimental.pallas import tpu as pltpu
from jax.sharding import PartitionSpec as P

HD = 128
EPS = 1e-06
BASE = 1000000.0
NEG = -1e30
F32 = jnp.float32
BF16 = jnp.bfloat16
PLANE = ("shard", "tp")
SCALE = 1.0 / math.sqrt(HD)
VMEM = 48 << 20
ALL_VMEM = 60 << 20


def lookup(onehot, table):
    return jnp.sum(onehot * table[None, :], axis=1)


def tree_layout(lengths, parents, places):
    labels = jnp.arange(lengths.shape[0], dtype=jnp.int32)
    ends = jnp.cumsum(lengths)
    starts = ends - lengths
    parent_hot = (parents[:, None] == labels[None, :]).astype(jnp.int32)
    grand = lookup(parent_hot, parents)
    parent_len = lookup(parent_hot, lengths)
    grand_hot = (grand[:, None] == labels[None, :]).astype(jnp.int32)
    grand_len = lookup(grand_hot, lengths)
    before = jnp.where(labels == 0, 0, parent_len + jnp.where(parents == 0, 0, grand_len))
    segment = jnp.sum((places[:, None] >= ends[None, :]).astype(jnp.int32), axis=1)
    token_hot = (segment[:, None] == labels[None, :]).astype(jnp.int32)
    position = places - lookup(token_hot, starts) + lookup(token_hot, before)
    return (segment, lookup(token_hot, parents), lookup(token_hot, grand), position)


def rope_tables(position, columns):
    halfway = columns // 2
    frequency = jnp.exp(jnp.arange(halfway, dtype=F32) * (-2.0 * math.log(BASE) / columns))
    angles = position.astype(F32)[:, None] * frequency[None, :]
    angles = jnp.concatenate([angles, angles], axis=1)
    return (jnp.cos(angles), jnp.sin(angles))


def rms_scale(inputs):
    return lax.rsqrt(jnp.mean(inputs * inputs, axis=-1, keepdims=True) + EPS)


def dot(left, right):
    return jnp.dot(left, right, preferred_element_type=F32)


def dot_rows(left, right):
    return lax.dot_general(left, right, (((0,), (0,)), ((), ())), preferred_element_type=F32)


def dot_back(left, right):
    return lax.dot_general(left, right, (((1,), (1,)), ((), ())), preferred_element_type=F32)


def turn(inputs):
    halfway = inputs.shape[-1] // 2
    return jnp.concatenate([-inputs[:, halfway:], inputs[:, :halfway]], axis=-1)


def unturn(inputs):
    halfway = inputs.shape[-1] // 2
    return jnp.concatenate([inputs[:, halfway:], -inputs[:, :halfway]], axis=-1)


def head(number):
    return slice(number * HD, (number + 1) * HD)


def call(
    kernel, grid, in_specs, out_specs, out_shape, flops, scratch=(), moved=8 << 20, behind=(), vmem=VMEM
):
    count = len(in_specs)

    def body(*refs):
        kernel(*refs[:count], *refs[count + len(behind) :])

    built = pl.pallas_call(
        body,
        grid=grid,
        in_specs=list(in_specs) + [pl.BlockSpec(memory_space=pl.ANY)] * len(behind),
        out_specs=out_specs,
        out_shape=out_shape,
        scratch_shapes=scratch,
        compiler_params=pltpu.CompilerParams(
            dimension_semantics=("arbitrary",) * len(grid), vmem_limit_bytes=vmem
        ),
        cost_estimate=pl.CostEstimate(flops=flops, bytes_accessed=moved, transcendentals=0),
    )
    return lambda *operands: built(*operands, *behind)


def struct(shape, dtype):
    return jax.ShapeDtypeStruct(shape, dtype)


def fixed(shape):
    return pl.BlockSpec(shape, lambda i: (0,) * len(shape))


def rowed(rows, columns):
    return pl.BlockSpec((rows, columns), lambda i: (i, 0))


def piled(shape, which):
    return pl.BlockSpec((shape[0], shape[1] // 2, shape[2]), lambda i: (0, which, 0))


def flat(value):
    return value.reshape((-1,) + value.shape[2:])


def project_kernel(xa, xb, w, gains, cosine, sine, xn, pre, low, gate):
    x = flat(jnp.where(pl.program_id(0) == 0, xa[...], xb[...])).astype(F32)
    normed = (x * rms_scale(x)).astype(BF16)
    xn[...] = normed
    out = dot(normed, w[...])
    for place in range(3):
        raw = out[:, head(place)]
        pre[:, head(place)] = raw
        unit = raw * rms_scale(raw) * gains[place // 2 : place // 2 + 1, :]
        low[:, head(place)] = (unit * cosine[...] + turn(unit) * sine[...]).astype(BF16)
    low[:, head(3)] = out[:, head(3)].astype(BF16)
    gate[...] = out[:, 4 * HD :]


def project(xa, xb, w, gains, cosine, sine):
    half, width = xa.shape[0] * xa.shape[1] // 2, xa.shape[2]
    return call(
        project_kernel,
        (2,),
        [
            piled(xa.shape, 0),
            piled(xb.shape, 0),
            fixed((width, 6 * HD)),
            fixed(gains.shape),
            rowed(half, HD),
            rowed(half, HD),
        ],
        [
            rowed(half, width),
            rowed(half, 3 * HD),
            rowed(half, 4 * HD),
            rowed(half, 2 * HD),
        ],
        [
            struct((2 * half, width), BF16),
            struct((2 * half, 3 * HD), F32),
            struct((2 * half, 4 * HD), BF16),
            struct((2 * half, 2 * HD), F32),
        ],
        2 * 2 * half * width * 6 * HD,
    )(xa, xb, w, gains, cosine, sine)


def attend_kernel(low, gate, w_out, of_row, of_column, probs, attended, gated, mine, other):
    step = pl.program_id(0)
    half = probs.shape[1]
    rows = pl.ds(step * half, half)
    key, value = low[:, head(2)], low[:, head(3)]
    seg, par, grand, place = (of_row[rows, n : n + 1] for n in range(4))
    key_seg, key_place = of_column[0:1, :], of_column[1:2, :]
    allowed = ((key_seg == seg) | (key_seg == par) | (key_seg == grand)) & (key_place <= place)
    for number in range(2):
        scores = dot_back(low[rows, head(number)], key) * SCALE
        scores = jnp.where(allowed, scores, NEG)
        raised = jnp.exp(scores - jnp.max(scores, axis=-1, keepdims=True))
        share = raised / jnp.sum(raised, axis=-1, keepdims=True)
        probs[number] = share
        seen = dot(share.astype(BF16), value)
        attended[:, head(number)] = seen
        gated[:, head(number)] = (seen * jax.nn.sigmoid(gate[:, head(number)])).astype(BF16)
    out = dot_back(gated[...], w_out[...])

    @pl.when(step == 0)
    def _():
        mine[...] = out.astype(BF16)

    @pl.when(step == 1)
    def _():
        other[...] = out.astype(BF16)


def attend(low, gate, w, of_row, of_column):
    length = low.shape[0]
    half, width = length // 2, w.shape[0]
    return call(
        attend_kernel,
        (2,),
        [
            fixed((length, 4 * HD)),
            rowed(half, 2 * HD),
            pl.BlockSpec((width, 2 * HD), lambda i: (0, 3)),
            fixed((length, 4)),
            fixed((2, length)),
        ],
        [
            pl.BlockSpec((2, half, length), lambda i: (0, i, 0)),
            rowed(half, 2 * HD),
            rowed(half, 2 * HD),
            fixed((half, width)),
            fixed((half, width)),
        ],
        [
            struct((2, length, length), F32),
            struct((length, 2 * HD), F32),
            struct((length, 2 * HD), BF16),
            struct((half, width), BF16),
            struct((half, width), BF16),
        ],
        2 * length * width * 2 * HD + 8 * length * length * HD,
    )(low, gate, w, of_row, of_column)


def flip_kernel(pieces, out):
    at = 0
    for piece in pieces:
        out[:, at : at + piece.shape[0]] = piece[...].T
        at += piece.shape[0]


def flip(*pieces):
    length, width = sum(piece.shape[0] for piece in pieces), pieces[0].shape[1]
    chunk = 2 * HD
    return call(
        lambda *refs: flip_kernel(refs[:-1], refs[-1]),
        (width // chunk,),
        [pl.BlockSpec((piece.shape[0], chunk), lambda i: (0, i)) for piece in pieces],
        rowed(chunk, length),
        struct((width, length), BF16),
        1 << 20,
    )(*pieces)


def feed_kernel(ua, ub, ca, cb, wg, wu, wd, hidden, d_gate, d_up):
    half = ua.shape[0]
    for number, (u, cot) in enumerate(((ua, ca), (ub, cb))):
        rows = slice(number * half, (number + 1) * half)
        gate, up = dot(u[...], wg[...]), dot(u[...], wu[...])
        d_hidden = dot(flat(cot[...]), wd[...])
        sig = jax.nn.sigmoid(gate)
        silu = gate * sig
        hidden[rows, :] = (silu * up).astype(BF16)
        d_gate[rows, :] = (d_hidden * up * sig * (1.0 + gate * (1.0 - sig))).astype(BF16)
        d_up[rows, :] = (d_hidden * silu).astype(BF16)


def feed(ua, ub, ca, cb, w, behind):
    half, width = ua.shape
    chunk = 2 * HD
    parts = w.shape[1] // 3 // chunk
    column = lambda shift: pl.BlockSpec((width, chunk), lambda i: (0, shift * parts + i))
    unit = pl.BlockSpec((2 * half, chunk), lambda i: (0, i))
    units = parts * chunk
    return call(
        feed_kernel,
        (parts,),
        [fixed((half, width))] * 2
        + [piled(ca.shape, 1)] * 2
        + [column(0), column(1), column(2)],
        [unit, unit, unit],
        [struct((2 * half, units), BF16)] * 3,
        2 * 2 * half * width * units * 3,
        behind=behind,
        vmem=60 << 20,
    )(ua, ub, ca, cb, w, w, w)


def feed_back_kernel(d_gate, d_up, wg, wu, mine, other):
    half = mine.shape[0]
    out = dot_back(d_gate[...], wg[...]) + dot_back(d_up[...], wu[...])
    mine[...] = out[:half, :].astype(BF16)
    other[...] = out[half:, :].astype(BF16)


def feed_back(d_gate, d_up, w, behind):
    length, units = d_gate.shape
    half, width = length // 2, w.shape[0]
    chunk = 4 * HD
    slab = pl.BlockSpec((half, chunk), lambda i: (0, i))
    return call(
        feed_back_kernel,
        (width // chunk,),
        [fixed((length, units))] * 2
        + [
            pl.BlockSpec((chunk, units), lambda i: (i, 0)),
            pl.BlockSpec((chunk, units), lambda i: (i, 1)),
        ],
        [slab, slab],
        [struct((half, width), BF16), struct((half, width), BF16)],
        2 * length * width * units * 2,
        behind=behind,
        vmem=48 << 20,
    )(d_gate, d_up, w, w)


def down_kernel(hidden, w, mine, other):
    out = dot_back(hidden[...], w[...])

    @pl.when(pl.program_id(0) == 0)
    def _():
        mine[...] = out.astype(BF16)

    @pl.when(pl.program_id(0) == 1)
    def _():
        other[...] = out.astype(BF16)


def down_product(left, w, place, behind):
    length, units = left.shape
    half, width = length // 2, w.shape[0]
    return call(
        down_kernel,
        (2,),
        [rowed(half, units), pl.BlockSpec((width, units), lambda i: (0, place))],
        [fixed((half, width)), fixed((half, width))],
        [struct((half, width), BF16), struct((half, width), BF16)],
        2 * length * width * units,
        behind=behind,
    )(left, w)


def spread_blocks(flipped, right, out, start):
    term = dot(flipped, right).astype(BF16)
    for place in range(flipped.shape[0] // HD):
        for owner in range(right.shape[1] // HD):
            at = start + place * HD
            out[owner * HD : (owner + 1) * HD, at : at + HD] = term[head(place), head(owner)]


def feed_grads_kernel(u_flip, ca, cb, d_gate, d_up, hidden, out, flipped):
    @pl.when(pl.program_id(0) == 0)
    def _():
        flipped[...] = hidden[...].T

    units = hidden.shape[1]
    out[:, :units] = dot(u_flip[...], d_gate[...]).astype(BF16)
    out[:, units : 2 * units] = dot(u_flip[...], d_up[...]).astype(BF16)
    cot = jnp.concatenate([flat(ca[...]), flat(cb[...])], axis=0)
    spread_blocks(flipped[...], cot, out, 2 * units)


def feed_grads(u_flip, ca, cb, d_gate, d_up, hidden, behind):
    width, length = u_flip.shape
    units = hidden.shape[1]
    chunk = 4 * HD
    return call(
        feed_grads_kernel,
        (width // chunk,),
        [rowed(chunk, length)]
        + [pl.BlockSpec((ca.shape[0], ca.shape[1] // 2, chunk), lambda i: (0, 1, i))] * 2
        + [fixed((length, units))] * 3,
        rowed(chunk, 3 * units),
        struct((width, 3 * units), BF16),
        2 * length * width * units * 3,
        scratch=[pltpu.VMEM((units, length), BF16)],
        vmem=56 << 20,
        behind=behind,
    )(u_flip, ca, cb, d_gate, d_up, hidden)


def gate_back_kernel(da, db, w_out, gate, attended, d_attended, d_gate):
    half = da.shape[0]
    for number, low in enumerate((da, db)):
        rows = slice(number * half, (number + 1) * half)
        d_gated = dot(low[...], w_out[...])
        sig = jax.nn.sigmoid(gate[rows, :])
        d_attended[rows, :] = (d_gated * sig).astype(BF16)
        d_gate[rows, :] = (d_gated * attended[rows, :] * sig * (1.0 - sig)).astype(BF16)


def gate_back(da, db, w, gate, attended):
    half, width = da.shape
    wide = (2 * half, 2 * HD)
    return call(
        gate_back_kernel,
        (1,),
        [fixed((half, width))] * 2
        + [pl.BlockSpec((width, 2 * HD), lambda i: (0, 3)), fixed(wide), fixed(wide)],
        [fixed(wide), fixed(wide)],
        [struct(wide, BF16), struct(wide, BF16)],
        2 * 2 * half * width * 2 * HD,
    )(da, db, w, gate, attended)


def head_back(grads, inputs, gain):
    factor = rms_scale(inputs)
    scaled = gain * grads
    back = factor * scaled - inputs * factor**3 * jnp.mean(scaled * inputs, axis=-1, keepdims=True)
    return back.astype(BF16), jnp.sum(grads * inputs * factor, axis=0, keepdims=True)


def attend_back_kernel(
    probs, low, d_attended, pre, gains, cosine, sine, out, terms, d_key, d_value
):
    step = pl.program_id(0)
    half = probs.shape[1]
    start = pl.multiple_of(step * half, half)
    rows = pl.ds(start, half)
    key, value = low[:, head(2)], low[:, head(3)]
    cos_rows, sin_rows = cosine[rows, :], sine[rows, :]

    @pl.when(step == 0)
    def _():
        d_key[...] = jnp.zeros_like(d_key)
        d_value[...] = jnp.zeros_like(d_value)
        terms[...] = jnp.zeros_like(terms)

    for number in range(2):
        share = probs[number]
        d_seen = d_attended[:, head(number)]
        d_share = dot_back(d_seen, value)
        d_scores = share * (d_share - jnp.sum(share * d_share, axis=-1, keepdims=True))
        d_scores = d_scores.astype(BF16)
        d_query = dot(d_scores, key) * SCALE
        d_key[...] += dot_rows(d_scores, low[rows, head(number)])
        d_value[...] += dot_rows(share.astype(BF16), d_seen)
        grads = d_query * cos_rows + unturn(d_query * sin_rows)
        back, term = head_back(grads, pre[rows, head(number)], gains[0:1, :])
        out[rows, head(number)] = back
        terms[0:1, :] += term

    @pl.when(step == 1)
    def _():
        grads = d_key[...] * SCALE
        grads = grads * cosine[...] + unturn(grads * sine[...])
        back, term = head_back(grads, pre[:, head(2)], gains[1:2, :])
        out[:, head(2)] = back
        terms[1:2, :] = term
        out[:, head(3)] = d_value[...].astype(BF16)


def attend_back(probs, low, d_attended, pre, gains, cosine, sine, behind):
    length = low.shape[0]
    half = length // 2
    return call(
        attend_back_kernel,
        (2,),
        [
            pl.BlockSpec((2, half, length), lambda i: (0, i, 0)),
            fixed((length, 4 * HD)),
            rowed(half, 2 * HD),
            fixed((length, 3 * HD)),
            fixed((8, HD)),
            fixed((length, HD)),
            fixed((length, HD)),
        ],
        [fixed((length, 4 * HD)), fixed((8, HD))],
        [struct((length, 4 * HD), BF16), struct((8, HD), F32)],
        20 * length * length * HD,
        scratch=[pltpu.VMEM((length, HD), F32), pltpu.VMEM((length, HD), F32)],
        behind=behind,
    )(probs, low, d_attended, pre, gains, cosine, sine)


def input_back_kernel(d_qkv, d_gate, w, mine, other):
    out = dot_back(d_qkv[...], w[:, : 4 * HD]) + dot_back(d_gate[...], w[:, 4 * HD :])

    @pl.when(pl.program_id(0) == 0)
    def _():
        mine[...] = out.astype(BF16)

    @pl.when(pl.program_id(0) == 1)
    def _():
        other[...] = out.astype(BF16)


def input_back(d_qkv, d_gate, w, behind):
    length = d_qkv.shape[0]
    half, width = length // 2, w.shape[0]
    return call(
        input_back_kernel,
        (2,),
        [rowed(half, 4 * HD), rowed(half, 2 * HD), fixed((width, 6 * HD))],
        [fixed((half, width)), fixed((half, width))],
        [struct((half, width), BF16), struct((half, width), BF16)],
        2 * length * width * 6 * HD,
        behind=behind,
    )(d_qkv, d_gate, w)


def attend_grads_kernel(x_flip, da, db, d_qkv, d_gate, gated, out, flipped):
    @pl.when(pl.program_id(0) == 0)
    def _():
        flipped[...] = gated[...].T

    inner, split = d_qkv.shape[1], d_gate.shape[1]
    out[:, :inner] = dot(x_flip[...], d_qkv[...]).astype(BF16)
    out[:, inner : inner + split] = dot(x_flip[...], d_gate[...]).astype(BF16)
    spread_blocks(
        flipped[...], jnp.concatenate([da[...], db[...]], axis=0), out, inner + split
    )


def attend_grads(x_flip, da, db, d_qkv, d_gate, gated, behind):
    width, length = x_flip.shape
    columns = d_qkv.shape[1] + d_gate.shape[1] + gated.shape[1]
    chunk = 4 * HD
    slab = pl.BlockSpec((length // 2, chunk), lambda i: (0, i))
    return call(
        attend_grads_kernel,
        (width // chunk,),
        [
            rowed(chunk, length),
            slab,
            slab,
            fixed(d_qkv.shape),
            fixed(d_gate.shape),
            fixed(gated.shape),
        ],
        rowed(chunk, columns),
        struct((width, columns), BF16),
        2 * length * width * columns,
        scratch=[pltpu.VMEM(gated.shape[::-1], BF16)],
        behind=behind,
    )(x_flip, da, db, d_qkv, d_gate, gated)


def middle_kernel(parts, x, middle, spread):
    total = x[...].astype(F32) + jnp.sum(parts[...].astype(F32), axis=0)
    middle[...] = total
    low = (total * rms_scale(total)).astype(BF16)
    for number in range(spread.shape[0]):
        spread[number] = low


def middle_step(parts, x, behind):
    shape = x.shape
    return call(
        middle_kernel,
        (1,),
        [fixed(parts.shape), fixed(shape)],
        [fixed(shape), fixed(parts.shape)],
        [struct(shape, F32), struct(parts.shape, BF16)],
        1 << 20,
        behind=behind,
    )(parts, x)


def norm_back(grads, inputs):
    factor = rms_scale(inputs)
    return factor * grads - inputs * factor**3 * jnp.mean(grads * inputs, axis=-1, keepdims=True)


def d_middle_kernel(parts, middle, cot, d_middle, spread):
    grads = jnp.sum(parts[...].astype(F32), axis=0)
    total = cot[...].astype(F32) + norm_back(grads, middle[...])
    d_middle[...] = total
    for number in range(spread.shape[0]):
        spread[number] = total.astype(BF16)


def d_middle_step(parts, middle, cot):
    shape = cot.shape
    return call(
        d_middle_kernel,
        (1,),
        [fixed(parts.shape), fixed(shape), fixed(shape)],
        [fixed(shape), fixed(parts.shape)],
        [struct(shape, F32), struct(parts.shape, BF16)],
        1 << 20,
    )(parts, middle, cot)


def ends_kernel(parts, middle, d_middle, x, out, terms):
    rows = x.shape[0]
    total = sum(part[...].astype(F32) for part in parts)
    out[:rows, :] = (middle[...] + total[:rows, :]).astype(BF16)
    inputs = x[...].astype(F32)
    grads = total[rows:, :]
    out[rows:, :] = (d_middle[...] + norm_back(grads, inputs)).astype(BF16)
    found = jnp.sum(grads * inputs * rms_scale(inputs), axis=0, keepdims=True)
    terms[...] = jnp.broadcast_to(found, terms.shape)


def ends_step(parts, middle, d_middle, x, behind):
    shape, wide = x.shape, parts[0].shape
    count = len(parts)
    return call(
        lambda *refs: ends_kernel(refs[:count], *refs[count:]),
        (1,),
        [fixed(wide)] * count + [fixed(shape)] * 3,
        [fixed(wide), fixed((8, shape[1]))],
        [struct(wide, BF16), struct((8, shape[1]), F32)],
        1 << 20,
        behind=behind,
    )(*parts, middle, d_middle, x)


def prefetched(kernel, grid, in_specs, out_specs, out_shape, vmem=VMEM):
    return pl.pallas_call(
        kernel,
        grid_spec=pltpu.PrefetchScalarGridSpec(
            num_scalar_prefetch=1, grid=grid, in_specs=in_specs, out_specs=out_specs
        ),
        out_shape=out_shape,
        compiler_params=pltpu.CompilerParams(
            dimension_semantics=("arbitrary",) * len(grid), vmem_limit_bytes=vmem
        ),
        cost_estimate=pl.CostEstimate(flops=1 << 20, bytes_accessed=8 << 20, transcendentals=0),
    )


def copy_kernel(core, source, out):
    out[...] = source[...]


def sibling_part(core, found):
    pairs, _, rows, columns = found.shape
    return prefetched(
        copy_kernel,
        (pairs // 2,),
        [pl.BlockSpec((2, None, rows, columns), lambda i, at: (i, 1 - at[0], 0, 0))],
        pl.BlockSpec((2, rows, columns), lambda i, at: (i, 0, 0)),
        struct((pairs, rows, columns), found.dtype),
    )(core, found)


def join_kernel(core, mine, other, out):
    out[:, core[0]] = mine[...]
    out[:, 1 - core[0]] = other[...]


def join_cores(core, found, other):
    pairs, _, rows, columns = found.shape
    return prefetched(
        join_kernel,
        (pairs // 2,),
        [
            pl.BlockSpec((2, None, rows, columns), lambda i, at: (i, at[0], 0, 0)),
            pl.BlockSpec((2, rows, columns), lambda i, at: (i, 0, 0)),
        ],
        pl.BlockSpec((2, 2, rows, columns), lambda i, at: (i, 0, 0, 0)),
        struct(found.shape, found.dtype),
    )(core, found, other)


def lanes(value):
    return sum(value[:, start : start + HD] for start in range(0, value.shape[1], HD))


def pick(blocks):
    step = pl.program_id(0)
    value = blocks[0][...]
    for number in range(1, len(blocks)):
        value = jnp.where(step == number, blocks[number][...], value)
    return value.astype(F32)


def close_feed_kernel(turn_at, b0, b1, b2, b3, w_gate, w_up, gain, g_gate, g_up, g_down, sums):
    raw = pick((b0, b1, b2, b3))
    units = w_gate.shape[1]
    raw_gate, raw_up = raw[:, :units], raw[:, units : 2 * units]
    g_gate[...] = raw_gate * gain[...]
    g_up[...] = raw_up * gain[...]
    for place in range(units // HD):
        g_down[head(place), :] = raw[:, 2 * units + place * HD : 2 * units + (place + 1) * HD]
    term = lanes(raw_gate * w_gate[...].astype(F32)) + lanes(raw_up * w_up[...].astype(F32))

    @pl.when(pl.program_id(0) == 0)
    def _():
        sums[...] = term

    @pl.when(pl.program_id(0) > 0)
    def _():
        sums[...] += term


def close_attend_kernel(turn_at, b0, b1, b2, b3, gain, gq, gk, gv, gg, go):
    found, scale = pick((b0, b1, b2, b3)), gain[...]
    gq[...], gk[...] = found[:, : 2 * HD] * scale, found[:, head(2)] * scale
    gv[...], gg[...] = found[:, head(3)] * scale, found[:, 4 * HD : 6 * HD] * scale
    go[...] = jnp.concatenate([found[:, head(6)], found[:, head(7)]], axis=0)


def close(kernel, turn_at, blocks, weights, gain, out_rows, extra, read):
    quarters = 4
    place = lambda i, at: (at[0] + quarters - i) % quarters
    whole = lambda value: pl.BlockSpec(value.shape, lambda i, at: (0, 0))
    columns = lambda w: pl.BlockSpec(
        (w.shape[0], w.shape[1] // quarters), lambda i, at: (0, place(i, at))
    )
    rows, width = out_rows
    operands = weights if read else ()
    in_specs = [whole(b) for b in blocks] + [columns(w) for w in operands] + [whole(gain)]
    out_specs = [columns(w) for w in weights]
    out_specs += [pl.BlockSpec((rows // quarters, width), lambda i, at: (place(i, at), 0))]
    out_specs += [pl.BlockSpec(shape, lambda i, at: (0, 0)) for shape in extra]
    out_shape = [struct(w.shape, F32) for w in weights] + [struct(out_rows, F32)]
    out_shape += [struct(shape, F32) for shape in extra]
    return prefetched(kernel, (quarters,), in_specs, out_specs, out_shape, vmem=ALL_VMEM)(
        turn_at, *blocks, *operands, gain
    )


def column(row):
    shape = (HD, HD)
    there = lax.broadcasted_iota(jnp.int32, shape, 0) == lax.broadcasted_iota(jnp.int32, shape, 1)
    return jnp.sum(jnp.where(there, jnp.broadcast_to(row, shape), 0.0), axis=1, keepdims=True)


def first_kernel(at, wq, wk, wv, wg, wo, gain, out):
    scale = column(gain[...].astype(F32))
    start = 0
    for w in (wq, wk, wv, wg):
        stop = start + w.shape[1]
        out[:, start:stop] = (w[...].astype(F32) * scale).astype(BF16)
        start = stop
    out[:, start:] = wo[...].T


def first_columns(at, wq, wk, wv, wg, wo, gain):
    quarter = lambda w: pl.BlockSpec((w.shape[0], w.shape[1] // 4), lambda i, at: (0, at[0]))
    rows = wq.shape[0]
    heads = wo.shape[0] // 4
    columns = sum(w.shape[1] // 4 for w in (wq, wk, wv, wg)) + heads
    return prefetched(
        first_kernel,
        (1,),
        [quarter(w) for w in (wq, wk, wv, wg)]
        + [pl.BlockSpec((heads, rows), lambda i, at: (at[0], 0))]
        + [pl.BlockSpec(gain.shape, lambda i, at: (0, 0))],
        pl.BlockSpec((rows, columns), lambda i, at: (0, 0)),
        struct((rows, columns), BF16),
        vmem=ALL_VMEM,
    )(at, wq, wk, wv, wg, wo, gain)


def make_shards(mesh):
    n_shard, n_ctx, n_tp = mesh.shape["shard"], mesh.shape["ctx"], mesh.shape["tp"]
    pairs = n_shard // 2

    def joint(pair, core, tp):
        return (pair * 2 + core) * n_tp + tp

    core_perm = [(i, i ^ 1) for i in range(n_shard)]
    planes = [
        [joint(pair, core, tp) for pair in range(pairs) for tp in range(n_tp)] for core in range(2)
    ]
    swap_perm = [
        edge
        for pair in range(pairs)
        for edge in (
            (joint(pair, 1, 0), joint(pair, 0, 1)),
            (joint(pair, 0, 1), joint(pair, 1, 0)),
        )
    ]
    across_perm = [(joint(pair, t, t), joint(pair, t, 1 - t)) for pair in range(pairs) for t in range(2)]

    def spot(pair, core, ctx, tp):
        return ((pair * 2 + core) * n_ctx + ctx) * n_tp + tp

    owner_perms = [
        [
            (spot(pair, core, ctx, tp), spot(pair, tp, (ctx + by) % n_ctx, core))
            for pair in range(pairs)
            for core in range(2)
            for ctx in range(n_ctx)
            for tp in range(n_tp)
            if by > 0 or core != tp
        ]
        for by in range(n_ctx)
    ]

    def core_swap(value):
        return lax.ppermute(value, "shard", core_perm)

    def ctx_exchange(value):
        return lax.all_to_all(value, "ctx", 0, 0)

    def ctx_turn(value, by):
        return lax.ppermute(value, "ctx", [(i, (i + by) % n_ctx) for i in range(n_ctx)])

    def tree_rows(spread, *before):
        mine = ctx_exchange(spread)
        if before:
            mine, *before = lax.optimization_barrier((mine, *before))
        return mine, core_swap(mine), *before

    def tree_half(mine, other):
        half = (mine.astype(F32) + core_swap(other).astype(F32)).astype(BF16)
        return half.reshape((n_ctx, -1) + half.shape[1:])

    def plane_gather(value):
        return lax.all_gather(value, PLANE, axis=0, tiled=True, axis_index_groups=planes)

    def plane_scatter(value):
        return lax.psum_scatter(
            value, PLANE, scatter_dimension=0, tiled=True, axis_index_groups=planes
        )

    def shards(
        tokens,
        seg_lengths,
        seg_parents,
        gain_in,
        w_query,
        w_key,
        w_value,
        w_gate_attn,
        w_out,
        gain_query,
        gain_key,
        gain_mid,
        w_gate,
        w_up,
        w_down,
        cotangent,
    ):
        core = lax.axis_index("shard") % 2
        tp = lax.axis_index("tp")
        ctx = lax.axis_index("ctx")
        native = core == tp
        rows = tokens.shape[0] // 2

        def swapped(value):
            return jnp.where(native, value, lax.ppermute(value, PLANE, swap_perm))

        def quarter(weight, axis):
            size = weight.shape[axis] // n_ctx
            return lax.dynamic_slice_in_dim(weight, ctx * size, size, axis)

        gain_one = gain_in.astype(F32)[:, None]
        gain_two = gain_mid.astype(F32)[:, None]
        head_rows = gain_query.shape[0]
        first = first_columns(
            ctx.astype(jnp.int32).reshape(1), w_query, w_key, w_value, w_gate_attn, w_out, gain_in[None]
        )
        found = plane_gather(first)
        both_gains = jnp.pad(jnp.stack([gain_query, gain_key]), ((0, 6), (0, HD - head_rows)))
        both_gains = lax.all_to_all(
            jnp.broadcast_to(both_gains[None], (n_shard, 8, HD)), "shard", 0, 0
        )

        def half_rows(place):
            pieces = [lax.dynamic_slice_in_dim(v, place * rows, rows, 0) for v in (tokens, cotangent)]
            return jnp.concatenate(pieces, axis=0)

        own = jnp.where(native, half_rows(core), core_swap(half_rows(1 - core)))
        tree = jnp.concatenate([seg_lengths, seg_parents], axis=0)
        tree = jnp.where(native, tree, core_swap(tree))
        own, both_gains = lax.optimization_barrier((own, both_gains))
        own_x, own_cot = own[:rows], own[rows:]
        xa, xb = tree_rows(jnp.broadcast_to(own[None], (n_ctx,) + own.shape))

        second = jnp.concatenate([quarter(w_gate, 1), quarter(w_up, 1)], axis=1)
        second = (second.astype(F32) * gain_two).astype(BF16)
        second = jnp.concatenate([second, quarter(w_down, 0).T], axis=1)
        moved = lax.ppermute(second, PLANE, swap_perm)
        moved, xa = lax.optimization_barrier((moved, xa))
        w2 = plane_gather(jnp.where(native, second, moved))

        gains = both_gains[:, :, :head_rows].astype(F32).transpose(1, 0, 2).reshape(8, HD)
        half_at = jnp.where(jnp.arange(2) == 0, core, 1 - core) * rows
        places = (
            half_at[:, None, None]
            + jnp.arange(n_ctx, dtype=jnp.int32)[None, :, None] * (2 * rows)
            + jnp.arange(rows, dtype=jnp.int32)[None, None, :]
        ).reshape(-1)
        segment, parent_seg, grand_seg, position = tree_layout(tree[0], tree[1], places)
        of_row = jnp.stack([segment, parent_seg, grand_seg, places], axis=1)
        of_column = jnp.stack([segment, places], axis=0)
        cosine, sine = rope_tables(position, HD)

        found, xa, xb, of_row, of_column, cosine, sine = lax.optimization_barrier(
            (found, xa, xb, of_row, of_column, cosine, sine)
        )
        found = found.reshape(pairs, n_tp, gain_in.shape[0], -1)
        core_at = core.astype(jnp.int32).reshape(1)
        other = core_swap(sibling_part(core_at, found))
        w1 = join_cores(core_at, found, other).reshape(-1, first.shape[1])

        xn, pre, low, gate = project(xa, xb, w1, gains, cosine, sine)
        probs, attended, gated, mine, other = attend(low, gate, w1, of_row, of_column)
        x_flip = flip(xn)
        middle, spread = middle_step(ctx_exchange(tree_half(mine, other)), own_x, (x_flip,))
        ua, ub = (flat(v) for v in tree_rows(spread))
        u_flip = flip(ua, ub)

        hidden, d_gate, d_up = feed(ua, ub, xa, xb, w2, (u_flip,))
        ffn = feed_grads(u_flip, xa, xb, d_gate, d_up, hidden, ())
        half = tree_half(*feed_back(d_gate, d_up, w2, (ffn,)))
        d_middle, spread = d_middle_step(ctx_exchange(half), middle, own_cot)
        layer_mine, layer_other = down_product(hidden, w2, 2, (half,))
        da, db, layer_mine, layer_other = tree_rows(spread, layer_mine, layer_other)
        da, db = flat(da), flat(db)
        grad_ffn = plane_scatter(ffn)

        d_attended, d_gate_pre = gate_back(da, db, w1, gate, attended)
        d_qkv, terms = attend_back(probs, low, d_attended, pre, gains, cosine, sine, ())

        attn = attend_grads(x_flip, da, db, d_qkv, d_gate_pre, gated, ())
        in_mine, in_other = input_back(d_qkv, d_gate_pre, w1, (attn,))
        layer_half, in_half = tree_half(layer_mine, layer_other), tree_half(in_mine, in_other)
        grad_attn = plane_scatter(attn)
        layer_half, in_half, grad_ffn = lax.optimization_barrier((layer_half, in_half, grad_ffn))

        def owners(block):
            block = swapped(block)
            return [block] + [ctx_turn(block, by) for by in range(1, n_ctx)]

        def owners_at_once(block):
            moved = [lax.ppermute(block, ("shard", "ctx", "tp"), perm) for perm in owner_perms]
            return [jnp.where(native, block, moved[0])] + moved[1:]


        both = jnp.concatenate(
            [layer_half, in_half], axis=1
        )
        parts = [lax.dynamic_index_in_dim(both, ctx, 0, False)] + [
            ctx_turn(lax.dynamic_index_in_dim(both, (ctx + by) % n_ctx, 0, False), by)
            for by in range(1, n_ctx)
        ]
        ffn_blocks = owners(grad_ffn)
        ends, in_terms = ends_step(parts, middle, d_middle, own_x, (ffn_blocks[0],))
        ends, in_terms, ffn_blocks[1] = lax.optimization_barrier((ends, in_terms, ffn_blocks[1]))
        pieces = jnp.concatenate(
            [terms[0].reshape(n_shard, -1), terms[1].reshape(n_shard, -1)], axis=1
        )
        pieces = jnp.pad(pieces, ((0, 0), (0, HD - pieces.shape[1])))
        pieces = jnp.stack([in_terms[0].reshape(n_shard, HD), pieces], axis=1).astype(BF16)
        copies = n_ctx * n_tp
        pieces = jnp.broadcast_to(
            jnp.pad(pieces, ((0, 0), (0, 6), (0, 0)))[:, None], (n_shard, copies, 8, HD)
        )
        pieces = lax.all_to_all(
            pieces.reshape(n_shard * copies, 8, HD), ("shard", "ctx", "tp"), 0, 0
        )
        end_sums = jnp.sum(pieces.astype(F32), axis=0)
        sibling = core_swap(ends)

        def whole(start):
            mine, other = ends[start : start + rows], sibling[start : start + rows]
            return jnp.where(
                core == 0,
                jnp.concatenate([mine, other], axis=0),
                jnp.concatenate([other, mine], axis=0),
            )

        full = jnp.stack([whole(0), whole(rows)])
        turn_at = ctx.astype(jnp.int32).reshape(1)
        size = gain_in.shape[0]
        grad_gate, grad_up, grad_down, mid_sums = close(
            close_feed_kernel,
            turn_at,
            ffn_blocks,
            (w_gate, w_up),
            gain_two,
            w_down.shape,
            [(size, HD)],
            True,
        )
        mid_terms = jnp.sum(mid_sums, axis=1)
        mid_terms = mid_terms + lax.ppermute(mid_terms, "tp", [(0, 1), (1, 0)])
        full = jnp.where(native, full, lax.ppermute(full, PLANE, across_perm))
        full = full.astype(F32)
        grad_attn, mid_terms, full = lax.optimization_barrier((grad_attn, mid_terms, full))
        grad_query, grad_key, grad_value, grad_gate_attn, grad_out = close(
            close_attend_kernel,
            turn_at,
            owners_at_once(grad_attn),
            (w_query, w_key, w_value, w_gate_attn),
            gain_one,
            w_out.shape,
            [],
            False,
        )

        return (
            full[0],
            full[1],
            end_sums[0] / gain_one[:, 0],
            grad_query,
            grad_key,
            grad_value,
            grad_gate_attn,
            grad_out,
            end_sums[1, :head_rows],
            end_sums[1, head_rows : 2 * head_rows],
            mid_terms,
            grad_gate,
            grad_up,
            grad_down,
        )

    return shards


def solution(mesh):
    return jax.shard_map(
        make_shards(mesh),
        mesh=mesh,
        in_specs=(
            P(("shard", "ctx"), None),
            P("shard", None),
            P("shard", None),
            P("shard"),
            P("shard", "tp"),
            P("shard", "tp"),
            P("shard", "tp"),
            P("shard", "tp"),
            P("tp", "shard"),
            P("shard"),
            P("shard"),
            P("shard"),
            P("shard", "tp"),
            P("shard", "tp"),
            P("tp", "shard"),
            P(("shard", "ctx"), None),
        ),
        out_specs=(
            P(("shard", "ctx"), None),
            P(("shard", "ctx"), None),
            P("shard"),
            P("shard", "tp"),
            P("shard", "tp"),
            P("shard", "tp"),
            P("shard", "tp"),
            P("tp", "shard"),
            P("shard"),
            P("shard"),
            P("shard"),
            P("shard", "tp"),
            P("shard", "tp"),
            P("tp", "shard"),
        ),
        check_vma=False,
    )
```

```python
import math

import jax
import jax.numpy as jnp
from jax import lax
from jax.experimental import pallas as pl
from jax.experimental.pallas import tpu as pltpu
from jax.sharding import PartitionSpec as P

HD = 128
EPS = 1e-06
BASE = 1000000.0
NEG = -1e30
F32 = jnp.float32
BF16 = jnp.bfloat16
PLANE = ("shard", "tp")
SCALE = 1.0 / math.sqrt(HD)
VMEM = 48 << 20
ALL_VMEM = 60 << 20


def lookup(onehot, table):
    return jnp.sum(onehot * table[None, :], axis=1)


def tree_layout(lengths, parents, places):
    labels = jnp.arange(lengths.shape[0], dtype=jnp.int32)
    ends = jnp.cumsum(lengths)
    starts = ends - lengths
    parent_hot = (parents[:, None] == labels[None, :]).astype(jnp.int32)
    grand = lookup(parent_hot, parents)
    parent_len = lookup(parent_hot, lengths)
    grand_hot = (grand[:, None] == labels[None, :]).astype(jnp.int32)
    grand_len = lookup(grand_hot, lengths)
    before = jnp.where(labels == 0, 0, parent_len + jnp.where(parents == 0, 0, grand_len))
    segment = jnp.sum((places[:, None] >= ends[None, :]).astype(jnp.int32), axis=1)
    token_hot = (segment[:, None] == labels[None, :]).astype(jnp.int32)
    position = places - lookup(token_hot, starts) + lookup(token_hot, before)
    return (segment, lookup(token_hot, parents), lookup(token_hot, grand), position)


def rope_tables(position, columns):
    halfway = columns // 2
    frequency = jnp.exp(jnp.arange(halfway, dtype=F32) * (-2.0 * math.log(BASE) / columns))
    angles = position.astype(F32)[:, None] * frequency[None, :]
    angles = jnp.concatenate([angles, angles], axis=1)
    return (jnp.cos(angles), jnp.sin(angles))


def rms_scale(inputs):
    return lax.rsqrt(jnp.mean(inputs * inputs, axis=-1, keepdims=True) + EPS)


def dot(left, right):
    return jnp.dot(left, right, preferred_element_type=F32)


def dot_rows(left, right):
    return lax.dot_general(left, right, (((0,), (0,)), ((), ())), preferred_element_type=F32)


def dot_back(left, right):
    return lax.dot_general(left, right, (((1,), (1,)), ((), ())), preferred_element_type=F32)


def turn(inputs):
    halfway = inputs.shape[-1] // 2
    return jnp.concatenate([-inputs[:, halfway:], inputs[:, :halfway]], axis=-1)


def unturn(inputs):
    halfway = inputs.shape[-1] // 2
    return jnp.concatenate([inputs[:, halfway:], -inputs[:, :halfway]], axis=-1)


def head(number):
    return slice(number * HD, (number + 1) * HD)


def call(
    kernel, grid, in_specs, out_specs, out_shape, flops, scratch=(), moved=8 << 20, behind=(), vmem=VMEM
):
    count = len(in_specs)

    def body(*refs):
        kernel(*refs[:count], *refs[count + len(behind) :])

    built = pl.pallas_call(
        body,
        grid=grid,
        in_specs=list(in_specs) + [pl.BlockSpec(memory_space=pl.ANY)] * len(behind),
        out_specs=out_specs,
        out_shape=out_shape,
        scratch_shapes=scratch,
        compiler_params=pltpu.CompilerParams(
            dimension_semantics=("arbitrary",) * len(grid), vmem_limit_bytes=vmem
        ),
        cost_estimate=pl.CostEstimate(flops=flops, bytes_accessed=moved, transcendentals=0),
    )
    return lambda *operands: built(*operands, *behind)


def struct(shape, dtype):
    return jax.ShapeDtypeStruct(shape, dtype)


def fixed(shape):
    return pl.BlockSpec(shape, lambda i: (0,) * len(shape))


def rowed(rows, columns):
    return pl.BlockSpec((rows, columns), lambda i: (i, 0))


def piled(shape, which):
    return pl.BlockSpec((shape[0], shape[1] // 2, shape[2]), lambda i: (0, which, 0))


def flat(value):
    return value.reshape((-1,) + value.shape[2:])


def project_kernel(xa, xb, w, gains, cosine, sine, xn, pre, low, gate):
    x = flat(jnp.where(pl.program_id(0) == 0, xa[...], xb[...])).astype(F32)
    normed = (x * rms_scale(x)).astype(BF16)
    xn[...] = normed
    out = dot(normed, w[...])
    for place in range(3):
        raw = out[:, head(place)]
        pre[:, head(place)] = raw
        unit = raw * rms_scale(raw) * gains[place // 2 : place // 2 + 1, :]
        low[:, head(place)] = (unit * cosine[...] + turn(unit) * sine[...]).astype(BF16)
    low[:, head(3)] = out[:, head(3)].astype(BF16)
    gate[...] = out[:, 4 * HD :]


def project(xa, xb, w, gains, cosine, sine):
    half, width = xa.shape[0] * xa.shape[1] // 2, xa.shape[2]
    return call(
        project_kernel,
        (2,),
        [
            piled(xa.shape, 0),
            piled(xb.shape, 0),
            fixed((width, 6 * HD)),
            fixed(gains.shape),
            rowed(half, HD),
            rowed(half, HD),
        ],
        [
            rowed(half, width),
            rowed(half, 3 * HD),
            rowed(half, 4 * HD),
            rowed(half, 2 * HD),
        ],
        [
            struct((2 * half, width), BF16),
            struct((2 * half, 3 * HD), F32),
            struct((2 * half, 4 * HD), BF16),
            struct((2 * half, 2 * HD), F32),
        ],
        2 * 2 * half * width * 6 * HD,
    )(xa, xb, w, gains, cosine, sine)


def attend_kernel(low, gate, w_out, of_row, of_column, probs, attended, gated, mine, other):
    step = pl.program_id(0)
    half = probs.shape[1]
    rows = pl.ds(step * half, half)
    key, value = low[:, head(2)], low[:, head(3)]
    seg, par, grand, place = (of_row[rows, n : n + 1] for n in range(4))
    key_seg, key_place = of_column[0:1, :], of_column[1:2, :]
    allowed = ((key_seg == seg) | (key_seg == par) | (key_seg == grand)) & (key_place <= place)
    for number in range(2):
        scores = dot_back(low[rows, head(number)], key) * SCALE
        scores = jnp.where(allowed, scores, NEG)
        raised = jnp.exp(scores - jnp.max(scores, axis=-1, keepdims=True))
        share = raised / jnp.sum(raised, axis=-1, keepdims=True)
        probs[number] = share
        seen = dot(share.astype(BF16), value)
        attended[:, head(number)] = seen
        gated[:, head(number)] = (seen * jax.nn.sigmoid(gate[:, head(number)])).astype(BF16)
    out = dot_back(gated[...], w_out[...])

    @pl.when(step == 0)
    def _():
        mine[...] = out.astype(BF16)

    @pl.when(step == 1)
    def _():
        other[...] = out.astype(BF16)


def attend(low, gate, w, of_row, of_column):
    length = low.shape[0]
    half, width = length // 2, w.shape[0]
    return call(
        attend_kernel,
        (2,),
        [
            fixed((length, 4 * HD)),
            rowed(half, 2 * HD),
            pl.BlockSpec((width, 2 * HD), lambda i: (0, 3)),
            fixed((length, 4)),
            fixed((2, length)),
        ],
        [
            pl.BlockSpec((2, half, length), lambda i: (0, i, 0)),
            rowed(half, 2 * HD),
            rowed(half, 2 * HD),
            fixed((half, width)),
            fixed((half, width)),
        ],
        [
            struct((2, length, length), F32),
            struct((length, 2 * HD), F32),
            struct((length, 2 * HD), BF16),
            struct((half, width), BF16),
            struct((half, width), BF16),
        ],
        2 * length * width * 2 * HD + 8 * length * length * HD,
    )(low, gate, w, of_row, of_column)


def flip_kernel(pieces, out):
    at = 0
    for piece in pieces:
        out[:, at : at + piece.shape[0]] = piece[...].T
        at += piece.shape[0]


def flip(*pieces):
    length, width = sum(piece.shape[0] for piece in pieces), pieces[0].shape[1]
    chunk = 2 * HD
    return call(
        lambda *refs: flip_kernel(refs[:-1], refs[-1]),
        (width // chunk,),
        [pl.BlockSpec((piece.shape[0], chunk), lambda i: (0, i)) for piece in pieces],
        rowed(chunk, length),
        struct((width, length), BF16),
        1 << 20,
    )(*pieces)


FEED_STEPS = 3


def feed_kernel(
    ua, ub, ca, cb, wg, wu, wd, u_flip, sa, sb, hidden, d_gate, d_up, out, flipped
):
    step = pl.program_id(0)
    half, chunk, units = ua.shape[0], wg.shape[1], hidden.shape[1]

    @pl.when(step < FEED_STEPS)
    def _():
        columns = pl.ds(pl.multiple_of(step * chunk, chunk), chunk)
        for number, (u, cot) in enumerate(((ua, ca), (ub, cb))):
            rows = slice(number * half, (number + 1) * half)
            gate, up = dot(u[...], wg[...]), dot(u[...], wu[...])
            d_hidden = dot(flat(cot[...]), wd[...])
            sig = jax.nn.sigmoid(gate)
            silu = gate * sig
            hidden[rows, columns] = (silu * up).astype(BF16)
            d_gate[rows, columns] = (d_hidden * up * sig * (1.0 + gate * (1.0 - sig))).astype(BF16)
            d_up[rows, columns] = (d_hidden * silu).astype(BF16)

    @pl.when(step == FEED_STEPS)
    def _():
        flipped[...] = hidden[...].T

    @pl.when(step >= FEED_STEPS)
    def _():
        out[:, :units] = dot(u_flip[...], d_gate[...]).astype(BF16)
        out[:, units : 2 * units] = dot(u_flip[...], d_up[...]).astype(BF16)
        cot = jnp.concatenate([flat(sa[...]), flat(sb[...])], axis=0)
        spread_blocks(flipped[...], cot, out, 2 * units)


def feed(ua, ub, ca, cb, w, u_flip):
    half, width = ua.shape
    length, units = 2 * half, w.shape[1] // 3
    chunk, slab = units // FEED_STEPS, 4 * HD
    early = lambda i: jnp.minimum(i, FEED_STEPS - 1)
    late = lambda i: jnp.maximum(i - FEED_STEPS, 0)
    column = lambda shift: pl.BlockSpec(
        (width, chunk), lambda i: (0, shift * FEED_STEPS + early(i))
    )
    piece = pl.BlockSpec((ca.shape[0], ca.shape[1] // 2, slab), lambda i: (0, 1, late(i)))
    return call(
        feed_kernel,
        (FEED_STEPS + width // slab,),
        [fixed((half, width))] * 2
        + [piled(ca.shape, 1)] * 2
        + [column(0), column(1), column(2)]
        + [pl.BlockSpec((slab, length), lambda i: (late(i), 0)), piece, piece],
        [fixed((length, units))] * 3 + [pl.BlockSpec((slab, 3 * units), lambda i: (late(i), 0))],
        [struct((length, units), BF16)] * 3 + [struct((width, 3 * units), BF16)],
        2 * length * width * units * 6,
        scratch=[pltpu.VMEM((units, length), BF16)],
        vmem=60 << 20,
    )(ua, ub, ca, cb, w, w, w, u_flip, ca, cb)


def feed_back_kernel(d_gate, d_up, wg, wu, mine, other):
    half = mine.shape[0]
    out = dot_back(d_gate[...], wg[...]) + dot_back(d_up[...], wu[...])
    mine[...] = out[:half, :].astype(BF16)
    other[...] = out[half:, :].astype(BF16)


def feed_back(d_gate, d_up, w, behind):
    length, units = d_gate.shape
    half, width = length // 2, w.shape[0]
    chunk = 4 * HD
    slab = pl.BlockSpec((half, chunk), lambda i: (0, i))
    return call(
        feed_back_kernel,
        (width // chunk,),
        [fixed((length, units))] * 2
        + [
            pl.BlockSpec((chunk, units), lambda i: (i, 0)),
            pl.BlockSpec((chunk, units), lambda i: (i, 1)),
        ],
        [slab, slab],
        [struct((half, width), BF16), struct((half, width), BF16)],
        2 * length * width * units * 2,
        behind=behind,
        vmem=48 << 20,
    )(d_gate, d_up, w, w)


def down_kernel(hidden, w, mine, other):
    out = dot_back(hidden[...], w[...])

    @pl.when(pl.program_id(0) == 0)
    def _():
        mine[...] = out.astype(BF16)

    @pl.when(pl.program_id(0) == 1)
    def _():
        other[...] = out.astype(BF16)


def down_product(left, w, place, behind):
    length, units = left.shape
    half, width = length // 2, w.shape[0]
    return call(
        down_kernel,
        (2,),
        [rowed(half, units), pl.BlockSpec((width, units), lambda i: (0, place))],
        [fixed((half, width)), fixed((half, width))],
        [struct((half, width), BF16), struct((half, width), BF16)],
        2 * length * width * units,
        behind=behind,
    )(left, w)


def spread_blocks(flipped, right, out, start):
    term = dot(flipped, right).astype(BF16)
    for place in range(flipped.shape[0] // HD):
        for owner in range(right.shape[1] // HD):
            at = start + place * HD
            out[owner * HD : (owner + 1) * HD, at : at + HD] = term[head(place), head(owner)]


def gate_back_kernel(da, db, w_out, gate, attended, d_attended, d_gate):
    half = da.shape[0]
    for number, low in enumerate((da, db)):
        rows = slice(number * half, (number + 1) * half)
        d_gated = dot(low[...], w_out[...])
        sig = jax.nn.sigmoid(gate[rows, :])
        d_attended[rows, :] = (d_gated * sig).astype(BF16)
        d_gate[rows, :] = (d_gated * attended[rows, :] * sig * (1.0 - sig)).astype(BF16)


def gate_back(da, db, w, gate, attended):
    half, width = da.shape
    wide = (2 * half, 2 * HD)
    return call(
        gate_back_kernel,
        (1,),
        [fixed((half, width))] * 2
        + [pl.BlockSpec((width, 2 * HD), lambda i: (0, 3)), fixed(wide), fixed(wide)],
        [fixed(wide), fixed(wide)],
        [struct(wide, BF16), struct(wide, BF16)],
        2 * 2 * half * width * 2 * HD,
    )(da, db, w, gate, attended)


def head_back(grads, inputs, gain):
    factor = rms_scale(inputs)
    scaled = gain * grads
    back = factor * scaled - inputs * factor**3 * jnp.mean(scaled * inputs, axis=-1, keepdims=True)
    return back.astype(BF16), jnp.sum(grads * inputs * factor, axis=0, keepdims=True)


def attend_back_kernel(
    probs, low, d_attended, pre, gains, cosine, sine, out, terms, d_key, d_value
):
    step = pl.program_id(0)
    half = probs.shape[1]
    start = pl.multiple_of(step * half, half)
    rows = pl.ds(start, half)
    key, value = low[:, head(2)], low[:, head(3)]
    cos_rows, sin_rows = cosine[rows, :], sine[rows, :]

    @pl.when(step == 0)
    def _():
        d_key[...] = jnp.zeros_like(d_key)
        d_value[...] = jnp.zeros_like(d_value)
        terms[...] = jnp.zeros_like(terms)

    for number in range(2):
        share = probs[number]
        d_seen = d_attended[:, head(number)]
        d_share = dot_back(d_seen, value)
        d_scores = share * (d_share - jnp.sum(share * d_share, axis=-1, keepdims=True))
        d_scores = d_scores.astype(BF16)
        d_query = dot(d_scores, key) * SCALE
        d_key[...] += dot_rows(d_scores, low[rows, head(number)])
        d_value[...] += dot_rows(share.astype(BF16), d_seen)
        grads = d_query * cos_rows + unturn(d_query * sin_rows)
        back, term = head_back(grads, pre[rows, head(number)], gains[0:1, :])
        out[rows, head(number)] = back
        terms[0:1, :] += term

    @pl.when(step == 1)
    def _():
        grads = d_key[...] * SCALE
        grads = grads * cosine[...] + unturn(grads * sine[...])
        back, term = head_back(grads, pre[:, head(2)], gains[1:2, :])
        out[:, head(2)] = back
        terms[1:2, :] = term
        out[:, head(3)] = d_value[...].astype(BF16)


def attend_back(probs, low, d_attended, pre, gains, cosine, sine, behind):
    length = low.shape[0]
    half = length // 2
    return call(
        attend_back_kernel,
        (2,),
        [
            pl.BlockSpec((2, half, length), lambda i: (0, i, 0)),
            fixed((length, 4 * HD)),
            rowed(half, 2 * HD),
            fixed((length, 3 * HD)),
            fixed((8, HD)),
            fixed((length, HD)),
            fixed((length, HD)),
        ],
        [fixed((length, 4 * HD)), fixed((8, HD))],
        [struct((length, 4 * HD), BF16), struct((8, HD), F32)],
        20 * length * length * HD,
        scratch=[pltpu.VMEM((length, HD), F32), pltpu.VMEM((length, HD), F32)],
        behind=behind,
    )(probs, low, d_attended, pre, gains, cosine, sine)


def input_back_kernel(d_qkv, d_gate, w, mine, other):
    out = dot_back(d_qkv[...], w[:, : 4 * HD]) + dot_back(d_gate[...], w[:, 4 * HD :])

    @pl.when(pl.program_id(0) == 0)
    def _():
        mine[...] = out.astype(BF16)

    @pl.when(pl.program_id(0) == 1)
    def _():
        other[...] = out.astype(BF16)


def input_back(d_qkv, d_gate, w, behind):
    length = d_qkv.shape[0]
    half, width = length // 2, w.shape[0]
    return call(
        input_back_kernel,
        (2,),
        [rowed(half, 4 * HD), rowed(half, 2 * HD), fixed((width, 6 * HD))],
        [fixed((half, width)), fixed((half, width))],
        [struct((half, width), BF16), struct((half, width), BF16)],
        2 * length * width * 6 * HD,
        behind=behind,
    )(d_qkv, d_gate, w)


def attend_grads_kernel(x_flip, da, db, d_qkv, d_gate, gated, out, flipped):
    @pl.when(pl.program_id(0) == 0)
    def _():
        flipped[...] = gated[...].T

    inner, split = d_qkv.shape[1], d_gate.shape[1]
    out[:, :inner] = dot(x_flip[...], d_qkv[...]).astype(BF16)
    out[:, inner : inner + split] = dot(x_flip[...], d_gate[...]).astype(BF16)
    spread_blocks(
        flipped[...], jnp.concatenate([da[...], db[...]], axis=0), out, inner + split
    )


def attend_grads(x_flip, da, db, d_qkv, d_gate, gated, behind):
    width, length = x_flip.shape
    columns = d_qkv.shape[1] + d_gate.shape[1] + gated.shape[1]
    chunk = 4 * HD
    slab = pl.BlockSpec((length // 2, chunk), lambda i: (0, i))
    return call(
        attend_grads_kernel,
        (width // chunk,),
        [
            rowed(chunk, length),
            slab,
            slab,
            fixed(d_qkv.shape),
            fixed(d_gate.shape),
            fixed(gated.shape),
        ],
        rowed(chunk, columns),
        struct((width, columns), BF16),
        2 * length * width * columns,
        scratch=[pltpu.VMEM(gated.shape[::-1], BF16)],
        behind=behind,
    )(x_flip, da, db, d_qkv, d_gate, gated)


def middle_kernel(parts, x, middle, spread):
    total = x[...].astype(F32) + jnp.sum(parts[...].astype(F32), axis=0)
    middle[...] = total
    low = (total * rms_scale(total)).astype(BF16)
    for number in range(spread.shape[0]):
        spread[number] = low


def middle_step(parts, x, behind):
    shape = x.shape
    return call(
        middle_kernel,
        (1,),
        [fixed(parts.shape), fixed(shape)],
        [fixed(shape), fixed(parts.shape)],
        [struct(shape, F32), struct(parts.shape, BF16)],
        1 << 20,
        behind=behind,
    )(parts, x)


def norm_back(grads, inputs):
    factor = rms_scale(inputs)
    return factor * grads - inputs * factor**3 * jnp.mean(grads * inputs, axis=-1, keepdims=True)


def d_middle_kernel(parts, middle, cot, d_middle, spread):
    grads = jnp.sum(parts[...].astype(F32), axis=0)
    total = cot[...].astype(F32) + norm_back(grads, middle[...])
    d_middle[...] = total
    for number in range(spread.shape[0]):
        spread[number] = total.astype(BF16)


def d_middle_step(parts, middle, cot):
    shape = cot.shape
    return call(
        d_middle_kernel,
        (1,),
        [fixed(parts.shape), fixed(shape), fixed(shape)],
        [fixed(shape), fixed(parts.shape)],
        [struct(shape, F32), struct(parts.shape, BF16)],
        1 << 20,
    )(parts, middle, cot)


def ends_kernel(parts, middle, d_middle, x, out, terms):
    rows = x.shape[0]
    total = sum(part[...].astype(F32) for part in parts)
    out[:rows, :] = (middle[...] + total[:rows, :]).astype(BF16)
    inputs = x[...].astype(F32)
    grads = total[rows:, :]
    out[rows:, :] = (d_middle[...] + norm_back(grads, inputs)).astype(BF16)
    found = jnp.sum(grads * inputs * rms_scale(inputs), axis=0, keepdims=True)
    terms[...] = jnp.broadcast_to(found, terms.shape)


def ends_step(parts, middle, d_middle, x, behind):
    shape, wide = x.shape, parts[0].shape
    count = len(parts)
    return call(
        lambda *refs: ends_kernel(refs[:count], *refs[count:]),
        (1,),
        [fixed(wide)] * count + [fixed(shape)] * 3,
        [fixed(wide), fixed((8, shape[1]))],
        [struct(wide, BF16), struct((8, shape[1]), F32)],
        1 << 20,
        behind=behind,
    )(*parts, middle, d_middle, x)


def prefetched(kernel, grid, in_specs, out_specs, out_shape, vmem=VMEM):
    return pl.pallas_call(
        kernel,
        grid_spec=pltpu.PrefetchScalarGridSpec(
            num_scalar_prefetch=1, grid=grid, in_specs=in_specs, out_specs=out_specs
        ),
        out_shape=out_shape,
        compiler_params=pltpu.CompilerParams(
            dimension_semantics=("arbitrary",) * len(grid), vmem_limit_bytes=vmem
        ),
        cost_estimate=pl.CostEstimate(flops=1 << 20, bytes_accessed=8 << 20, transcendentals=0),
    )


def copy_kernel(core, source, out):
    out[...] = source[...]


def sibling_part(core, found):
    pairs, _, rows, columns = found.shape
    return prefetched(
        copy_kernel,
        (pairs // 2,),
        [pl.BlockSpec((2, None, rows, columns), lambda i, at: (i, 1 - at[0], 0, 0))],
        pl.BlockSpec((2, rows, columns), lambda i, at: (i, 0, 0)),
        struct((pairs, rows, columns), found.dtype),
    )(core, found)


def join_kernel(core, mine, other, out):
    out[:, core[0]] = mine[...]
    out[:, 1 - core[0]] = other[...]


def join_cores(core, found, other):
    pairs, _, rows, columns = found.shape
    return prefetched(
        join_kernel,
        (pairs // 2,),
        [
            pl.BlockSpec((2, None, rows, columns), lambda i, at: (i, at[0], 0, 0)),
            pl.BlockSpec((2, rows, columns), lambda i, at: (i, 0, 0)),
        ],
        pl.BlockSpec((2, 2, rows, columns), lambda i, at: (i, 0, 0, 0)),
        struct(found.shape, found.dtype),
    )(core, found, other)


def lanes(value):
    return sum(value[:, start : start + HD] for start in range(0, value.shape[1], HD))


def pick(blocks):
    step = pl.program_id(0)
    value = blocks[0][...]
    for number in range(1, len(blocks)):
        value = jnp.where(step == number, blocks[number][...], value)
    return value.astype(F32)


def close_feed_kernel(turn_at, b0, b1, b2, b3, w_gate, w_up, gain, g_gate, g_up, g_down, sums):
    raw = pick((b0, b1, b2, b3))
    units = w_gate.shape[1]
    raw_gate, raw_up = raw[:, :units], raw[:, units : 2 * units]
    g_gate[...] = raw_gate * gain[...]
    g_up[...] = raw_up * gain[...]
    for place in range(units // HD):
        g_down[head(place), :] = raw[:, 2 * units + place * HD : 2 * units + (place + 1) * HD]
    term = lanes(raw_gate * w_gate[...].astype(F32)) + lanes(raw_up * w_up[...].astype(F32))

    @pl.when(pl.program_id(0) == 0)
    def _():
        sums[...] = term

    @pl.when(pl.program_id(0) > 0)
    def _():
        sums[...] += term


def close_attend_kernel(turn_at, b0, b1, b2, b3, gain, gq, gk, gv, gg, go):
    found, scale = pick((b0, b1, b2, b3)), gain[...]
    gq[...], gk[...] = found[:, : 2 * HD] * scale, found[:, head(2)] * scale
    gv[...], gg[...] = found[:, head(3)] * scale, found[:, 4 * HD : 6 * HD] * scale
    go[...] = jnp.concatenate([found[:, head(6)], found[:, head(7)]], axis=0)


def close(kernel, turn_at, blocks, weights, gain, out_rows, extra, read):
    quarters = 4
    place = lambda i, at: (at[0] + quarters - i) % quarters
    whole = lambda value: pl.BlockSpec(value.shape, lambda i, at: (0, 0))
    columns = lambda w: pl.BlockSpec(
        (w.shape[0], w.shape[1] // quarters), lambda i, at: (0, place(i, at))
    )
    rows, width = out_rows
    operands = weights if read else ()
    in_specs = [whole(b) for b in blocks] + [columns(w) for w in operands] + [whole(gain)]
    out_specs = [columns(w) for w in weights]
    out_specs += [pl.BlockSpec((rows // quarters, width), lambda i, at: (place(i, at), 0))]
    out_specs += [pl.BlockSpec(shape, lambda i, at: (0, 0)) for shape in extra]
    out_shape = [struct(w.shape, F32) for w in weights] + [struct(out_rows, F32)]
    out_shape += [struct(shape, F32) for shape in extra]
    return prefetched(kernel, (quarters,), in_specs, out_specs, out_shape, vmem=ALL_VMEM)(
        turn_at, *blocks, *operands, gain
    )


def column(row):
    shape = (HD, HD)
    there = lax.broadcasted_iota(jnp.int32, shape, 0) == lax.broadcasted_iota(jnp.int32, shape, 1)
    return jnp.sum(jnp.where(there, jnp.broadcast_to(row, shape), 0.0), axis=1, keepdims=True)


def first_kernel(at, wq, wk, wv, wg, wo, gain, out):
    scale = column(gain[...].astype(F32))
    start = 0
    for w in (wq, wk, wv, wg):
        stop = start + w.shape[1]
        out[:, start:stop] = (w[...].astype(F32) * scale).astype(BF16)
        start = stop
    out[:, start:] = wo[...].T


def first_columns(at, wq, wk, wv, wg, wo, gain):
    quarter = lambda w: pl.BlockSpec((w.shape[0], w.shape[1] // 4), lambda i, at: (0, at[0]))
    rows = wq.shape[0]
    heads = wo.shape[0] // 4
    columns = sum(w.shape[1] // 4 for w in (wq, wk, wv, wg)) + heads
    return prefetched(
        first_kernel,
        (1,),
        [quarter(w) for w in (wq, wk, wv, wg)]
        + [pl.BlockSpec((heads, rows), lambda i, at: (at[0], 0))]
        + [pl.BlockSpec(gain.shape, lambda i, at: (0, 0))],
        pl.BlockSpec((rows, columns), lambda i, at: (0, 0)),
        struct((rows, columns), BF16),
        vmem=ALL_VMEM,
    )(at, wq, wk, wv, wg, wo, gain)


def make_shards(mesh):
    n_shard, n_ctx, n_tp = mesh.shape["shard"], mesh.shape["ctx"], mesh.shape["tp"]
    pairs = n_shard // 2

    def joint(pair, core, tp):
        return (pair * 2 + core) * n_tp + tp

    core_perm = [(i, i ^ 1) for i in range(n_shard)]
    planes = [
        [joint(pair, core, tp) for pair in range(pairs) for tp in range(n_tp)] for core in range(2)
    ]
    swap_perm = [
        edge
        for pair in range(pairs)
        for edge in (
            (joint(pair, 1, 0), joint(pair, 0, 1)),
            (joint(pair, 0, 1), joint(pair, 1, 0)),
        )
    ]
    across_perm = [(joint(pair, t, t), joint(pair, t, 1 - t)) for pair in range(pairs) for t in range(2)]

    def spot(pair, core, ctx, tp):
        return ((pair * 2 + core) * n_ctx + ctx) * n_tp + tp

    owner_perms = [
        [
            (spot(pair, core, ctx, tp), spot(pair, tp, (ctx + by) % n_ctx, core))
            for pair in range(pairs)
            for core in range(2)
            for ctx in range(n_ctx)
            for tp in range(n_tp)
            if by > 0 or core != tp
        ]
        for by in range(n_ctx)
    ]

    def core_swap(value):
        return lax.ppermute(value, "shard", core_perm)

    def ctx_exchange(value):
        return lax.all_to_all(value, "ctx", 0, 0)

    def ctx_turn(value, by):
        return lax.ppermute(value, "ctx", [(i, (i + by) % n_ctx) for i in range(n_ctx)])

    def tree_rows(spread, *before):
        mine = ctx_exchange(spread)
        if before:
            mine, *before = lax.optimization_barrier((mine, *before))
        return mine, core_swap(mine), *before

    def tree_half(mine, other):
        half = (mine.astype(F32) + core_swap(other).astype(F32)).astype(BF16)
        return half.reshape((n_ctx, -1) + half.shape[1:])

    def plane_gather(value):
        return lax.all_gather(value, PLANE, axis=0, tiled=True, axis_index_groups=planes)

    def plane_scatter(value):
        return lax.psum_scatter(
            value, PLANE, scatter_dimension=0, tiled=True, axis_index_groups=planes
        )

    def shards(
        tokens,
        seg_lengths,
        seg_parents,
        gain_in,
        w_query,
        w_key,
        w_value,
        w_gate_attn,
        w_out,
        gain_query,
        gain_key,
        gain_mid,
        w_gate,
        w_up,
        w_down,
        cotangent,
    ):
        core = lax.axis_index("shard") % 2
        tp = lax.axis_index("tp")
        ctx = lax.axis_index("ctx")
        native = core == tp
        rows = tokens.shape[0] // 2

        def swapped(value):
            return jnp.where(native, value, lax.ppermute(value, PLANE, swap_perm))

        def quarter(weight, axis):
            size = weight.shape[axis] // n_ctx
            return lax.dynamic_slice_in_dim(weight, ctx * size, size, axis)

        gain_one = gain_in.astype(F32)[:, None]
        gain_two = gain_mid.astype(F32)[:, None]
        head_rows = gain_query.shape[0]
        first = first_columns(
            ctx.astype(jnp.int32).reshape(1), w_query, w_key, w_value, w_gate_attn, w_out, gain_in[None]
        )
        found = plane_gather(first)
        both_gains = jnp.pad(jnp.stack([gain_query, gain_key]), ((0, 6), (0, HD - head_rows)))
        both_gains = lax.all_to_all(
            jnp.broadcast_to(both_gains[None], (n_shard, 8, HD)), "shard", 0, 0
        )

        def half_rows(place):
            pieces = [lax.dynamic_slice_in_dim(v, place * rows, rows, 0) for v in (tokens, cotangent)]
            return jnp.concatenate(pieces, axis=0)

        own = jnp.where(native, half_rows(core), core_swap(half_rows(1 - core)))
        tree = jnp.concatenate([seg_lengths, seg_parents], axis=0)
        tree = jnp.where(native, tree, core_swap(tree))
        own, both_gains = lax.optimization_barrier((own, both_gains))
        own_x, own_cot = own[:rows], own[rows:]
        xa, xb = tree_rows(jnp.broadcast_to(own[None], (n_ctx,) + own.shape))

        second = jnp.concatenate([quarter(w_gate, 1), quarter(w_up, 1)], axis=1)
        second = (second.astype(F32) * gain_two).astype(BF16)
        second = jnp.concatenate([second, quarter(w_down, 0).T], axis=1)
        moved = lax.ppermute(second, PLANE, swap_perm)
        moved, xa = lax.optimization_barrier((moved, xa))
        w2 = plane_gather(jnp.where(native, second, moved))

        gains = both_gains[:, :, :head_rows].astype(F32).transpose(1, 0, 2).reshape(8, HD)
        half_at = jnp.where(jnp.arange(2) == 0, core, 1 - core) * rows
        places = (
            half_at[:, None, None]
            + jnp.arange(n_ctx, dtype=jnp.int32)[None, :, None] * (2 * rows)
            + jnp.arange(rows, dtype=jnp.int32)[None, None, :]
        ).reshape(-1)
        segment, parent_seg, grand_seg, position = tree_layout(tree[0], tree[1], places)
        of_row = jnp.stack([segment, parent_seg, grand_seg, places], axis=1)
        of_column = jnp.stack([segment, places], axis=0)
        cosine, sine = rope_tables(position, HD)

        found, xa, xb, of_row, of_column, cosine, sine = lax.optimization_barrier(
            (found, xa, xb, of_row, of_column, cosine, sine)
        )
        found = found.reshape(pairs, n_tp, gain_in.shape[0], -1)
        core_at = core.astype(jnp.int32).reshape(1)
        other = core_swap(sibling_part(core_at, found))
        w1 = join_cores(core_at, found, other).reshape(-1, first.shape[1])

        xn, pre, low, gate = project(xa, xb, w1, gains, cosine, sine)
        probs, attended, gated, mine, other = attend(low, gate, w1, of_row, of_column)
        x_flip = flip(xn)
        middle, spread = middle_step(ctx_exchange(tree_half(mine, other)), own_x, (x_flip,))
        ua, ub = (flat(v) for v in tree_rows(spread))
        u_flip = flip(ua, ub)

        hidden, d_gate, d_up, ffn = feed(ua, ub, xa, xb, w2, u_flip)
        half = tree_half(*feed_back(d_gate, d_up, w2, ()))
        d_middle, spread = d_middle_step(ctx_exchange(half), middle, own_cot)
        layer_mine, layer_other = down_product(hidden, w2, 2, (half,))
        da, db, layer_mine, layer_other = tree_rows(spread, layer_mine, layer_other)
        da, db = flat(da), flat(db)
        grad_ffn = plane_scatter(ffn)

        d_attended, d_gate_pre = gate_back(da, db, w1, gate, attended)
        d_qkv, terms = attend_back(probs, low, d_attended, pre, gains, cosine, sine, ())

        attn = attend_grads(x_flip, da, db, d_qkv, d_gate_pre, gated, ())
        in_mine, in_other = input_back(d_qkv, d_gate_pre, w1, (attn,))
        layer_half, in_half = tree_half(layer_mine, layer_other), tree_half(in_mine, in_other)
        grad_attn = plane_scatter(attn)
        layer_half, in_half, grad_ffn = lax.optimization_barrier((layer_half, in_half, grad_ffn))

        def owners(block):
            block = swapped(block)
            return [block] + [ctx_turn(block, by) for by in range(1, n_ctx)]

        def owners_at_once(block):
            moved = [lax.ppermute(block, ("shard", "ctx", "tp"), perm) for perm in owner_perms]
            return [jnp.where(native, block, moved[0])] + moved[1:]


        both = jnp.concatenate(
            [layer_half, in_half], axis=1
        )
        parts = [lax.dynamic_index_in_dim(both, ctx, 0, False)] + [
            ctx_turn(lax.dynamic_index_in_dim(both, (ctx + by) % n_ctx, 0, False), by)
            for by in range(1, n_ctx)
        ]
        ffn_blocks = owners(grad_ffn)
        ends, in_terms = ends_step(parts, middle, d_middle, own_x, (ffn_blocks[0],))
        ends, in_terms, ffn_blocks[1] = lax.optimization_barrier((ends, in_terms, ffn_blocks[1]))
        pieces = jnp.concatenate(
            [terms[0].reshape(n_shard, -1), terms[1].reshape(n_shard, -1)], axis=1
        )
        pieces = jnp.pad(pieces, ((0, 0), (0, HD - pieces.shape[1])))
        pieces = jnp.stack([in_terms[0].reshape(n_shard, HD), pieces], axis=1).astype(BF16)
        copies = n_ctx * n_tp
        pieces = jnp.broadcast_to(
            jnp.pad(pieces, ((0, 0), (0, 6), (0, 0)))[:, None], (n_shard, copies, 8, HD)
        )
        pieces = lax.all_to_all(
            pieces.reshape(n_shard * copies, 8, HD), ("shard", "ctx", "tp"), 0, 0
        )
        end_sums = jnp.sum(pieces.astype(F32), axis=0)
        sibling = core_swap(ends)

        def whole(start):
            mine, other = ends[start : start + rows], sibling[start : start + rows]
            return jnp.where(
                core == 0,
                jnp.concatenate([mine, other], axis=0),
                jnp.concatenate([other, mine], axis=0),
            )

        full = jnp.stack([whole(0), whole(rows)])
        turn_at = ctx.astype(jnp.int32).reshape(1)
        size = gain_in.shape[0]
        grad_gate, grad_up, grad_down, mid_sums = close(
            close_feed_kernel,
            turn_at,
            ffn_blocks,
            (w_gate, w_up),
            gain_two,
            w_down.shape,
            [(size, HD)],
            True,
        )
        mid_terms = jnp.sum(mid_sums, axis=1)
        grad_attn, mid_terms = lax.optimization_barrier((grad_attn, mid_terms))
        full = jnp.where(native, full, lax.ppermute(full, PLANE, across_perm))
        outputs = [full[0].astype(F32), full[1].astype(F32)]
        attn_blocks = owners_at_once(grad_attn)
        attn_blocks[1], mid_terms = lax.optimization_barrier((attn_blocks[1], mid_terms))
        mid_terms = mid_terms + lax.ppermute(mid_terms, "tp", [(0, 1), (1, 0)])
        *outputs, attn_blocks[3], end_sums = lax.optimization_barrier(
            (*outputs, attn_blocks[3], end_sums)
        )
        grad_query, grad_key, grad_value, grad_gate_attn, grad_out = close(
            close_attend_kernel,
            turn_at,
            attn_blocks,
            (w_query, w_key, w_value, w_gate_attn),
            gain_one,
            w_out.shape,
            [],
            False,
        )

        return (
            *outputs,
            end_sums[0] / gain_one[:, 0],
            grad_query,
            grad_key,
            grad_value,
            grad_gate_attn,
            grad_out,
            end_sums[1, :head_rows],
            end_sums[1, head_rows : 2 * head_rows],
            mid_terms,
            grad_gate,
            grad_up,
            grad_down,
        )

    return shards


def solution(mesh):
    return jax.shard_map(
        make_shards(mesh),
        mesh=mesh,
        in_specs=(
            P(("shard", "ctx"), None),
            P("shard", None),
            P("shard", None),
            P("shard"),
            P("shard", "tp"),
            P("shard", "tp"),
            P("shard", "tp"),
            P("shard", "tp"),
            P("tp", "shard"),
            P("shard"),
            P("shard"),
            P("shard"),
            P("shard", "tp"),
            P("shard", "tp"),
            P("tp", "shard"),
            P(("shard", "ctx"), None),
        ),
        out_specs=(
            P(("shard", "ctx"), None),
            P(("shard", "ctx"), None),
            P("shard"),
            P("shard", "tp"),
            P("shard", "tp"),
            P("shard", "tp"),
            P("shard", "tp"),
            P("tp", "shard"),
            P("shard"),
            P("shard"),
            P("shard"),
            P("shard", "tp"),
            P("shard", "tp"),
            P("tp", "shard"),
        ),
        check_vma=False,
    )
```

```python
import math

import jax
import jax.numpy as jnp
from jax import lax
from jax.experimental import pallas as pl
from jax.experimental.pallas import tpu as pltpu
from jax.sharding import PartitionSpec as P

HD = 128
EPS = 1e-06
BASE = 1000000.0
NEG = -1e30
F32 = jnp.float32
BF16 = jnp.bfloat16
PLANE = ("shard", "tp")
SCALE = 1.0 / math.sqrt(HD)
VMEM = 48 << 20
ALL_VMEM = 60 << 20


def lookup(onehot, table):
    return jnp.sum(onehot * table[None, :], axis=1)


def tree_layout(lengths, parents, places):
    labels = jnp.arange(lengths.shape[0], dtype=jnp.int32)
    ends = jnp.cumsum(lengths)
    starts = ends - lengths
    parent_hot = (parents[:, None] == labels[None, :]).astype(jnp.int32)
    grand = lookup(parent_hot, parents)
    parent_len = lookup(parent_hot, lengths)
    grand_hot = (grand[:, None] == labels[None, :]).astype(jnp.int32)
    grand_len = lookup(grand_hot, lengths)
    before = jnp.where(labels == 0, 0, parent_len + jnp.where(parents == 0, 0, grand_len))
    segment = jnp.sum((places[:, None] >= ends[None, :]).astype(jnp.int32), axis=1)
    token_hot = (segment[:, None] == labels[None, :]).astype(jnp.int32)
    position = places - lookup(token_hot, starts) + lookup(token_hot, before)
    return (segment, lookup(token_hot, parents), lookup(token_hot, grand), position)


def rope_tables(position, columns):
    halfway = columns // 2
    frequency = jnp.exp(jnp.arange(halfway, dtype=F32) * (-2.0 * math.log(BASE) / columns))
    angles = position.astype(F32)[:, None] * frequency[None, :]
    angles = jnp.concatenate([angles, angles], axis=1)
    return (jnp.cos(angles), jnp.sin(angles))


def rms_scale(inputs):
    return lax.rsqrt(jnp.mean(inputs * inputs, axis=-1, keepdims=True) + EPS)


def dot(left, right):
    return jnp.dot(left, right, preferred_element_type=F32)


def dot_rows(left, right):
    return lax.dot_general(left, right, (((0,), (0,)), ((), ())), preferred_element_type=F32)


def dot_back(left, right):
    return lax.dot_general(left, right, (((1,), (1,)), ((), ())), preferred_element_type=F32)


def turn(inputs):
    halfway = inputs.shape[-1] // 2
    return jnp.concatenate([-inputs[:, halfway:], inputs[:, :halfway]], axis=-1)


def unturn(inputs):
    halfway = inputs.shape[-1] // 2
    return jnp.concatenate([inputs[:, halfway:], -inputs[:, :halfway]], axis=-1)


def head(number):
    return slice(number * HD, (number + 1) * HD)


def call(
    kernel, grid, in_specs, out_specs, out_shape, flops, scratch=(), moved=8 << 20, behind=(), vmem=VMEM
):
    count = len(in_specs)

    def body(*refs):
        kernel(*refs[:count], *refs[count + len(behind) :])

    built = pl.pallas_call(
        body,
        grid=grid,
        in_specs=list(in_specs) + [pl.BlockSpec(memory_space=pl.ANY)] * len(behind),
        out_specs=out_specs,
        out_shape=out_shape,
        scratch_shapes=scratch,
        compiler_params=pltpu.CompilerParams(
            dimension_semantics=("arbitrary",) * len(grid), vmem_limit_bytes=vmem
        ),
        cost_estimate=pl.CostEstimate(flops=flops, bytes_accessed=moved, transcendentals=0),
    )
    return lambda *operands: built(*operands, *behind)


def struct(shape, dtype):
    return jax.ShapeDtypeStruct(shape, dtype)


def fixed(shape):
    return pl.BlockSpec(shape, lambda i: (0,) * len(shape))


def rowed(rows, columns):
    return pl.BlockSpec((rows, columns), lambda i: (i, 0))


def piled(shape, which):
    return pl.BlockSpec((shape[0], shape[1] // 2, shape[2]), lambda i: (0, which, 0))


def flat(value):
    return value.reshape((-1,) + value.shape[2:])


def project_kernel(xa, xb, w, gains, cosine, sine, xn, pre, low, gate):
    x = flat(jnp.where(pl.program_id(0) == 0, xa[...], xb[...])).astype(F32)
    normed = (x * rms_scale(x)).astype(BF16)
    xn[...] = normed
    out = dot(normed, w[...])
    for place in range(3):
        raw = out[:, head(place)]
        pre[:, head(place)] = raw
        unit = raw * rms_scale(raw) * gains[place // 2 : place // 2 + 1, :]
        low[:, head(place)] = (unit * cosine[...] + turn(unit) * sine[...]).astype(BF16)
    low[:, head(3)] = out[:, head(3)].astype(BF16)
    gate[...] = out[:, 4 * HD :]


def project(xa, xb, w, gains, cosine, sine):
    half, width = xa.shape[0] * xa.shape[1] // 2, xa.shape[2]
    return call(
        project_kernel,
        (2,),
        [
            piled(xa.shape, 0),
            piled(xb.shape, 0),
            fixed((width, 6 * HD)),
            fixed(gains.shape),
            rowed(half, HD),
            rowed(half, HD),
        ],
        [
            rowed(half, width),
            rowed(half, 3 * HD),
            rowed(half, 4 * HD),
            rowed(half, 2 * HD),
        ],
        [
            struct((2 * half, width), BF16),
            struct((2 * half, 3 * HD), F32),
            struct((2 * half, 4 * HD), BF16),
            struct((2 * half, 2 * HD), F32),
        ],
        2 * 2 * half * width * 6 * HD,
    )(xa, xb, w, gains, cosine, sine)


def attend_kernel(low, gate, w_out, of_row, of_column, probs, attended, gated, mine, other):
    step = pl.program_id(0)
    half = probs.shape[1]
    rows = pl.ds(step * half, half)
    key, value = low[:, head(2)], low[:, head(3)]
    seg, par, grand, place = (of_row[rows, n : n + 1] for n in range(4))
    key_seg, key_place = of_column[0:1, :], of_column[1:2, :]
    allowed = ((key_seg == seg) | (key_seg == par) | (key_seg == grand)) & (key_place <= place)
    for number in range(2):
        scores = dot_back(low[rows, head(number)], key) * SCALE
        scores = jnp.where(allowed, scores, NEG)
        raised = jnp.exp(scores - jnp.max(scores, axis=-1, keepdims=True))
        share = raised / jnp.sum(raised, axis=-1, keepdims=True)
        probs[number] = share
        seen = dot(share.astype(BF16), value)
        attended[:, head(number)] = seen
        gated[:, head(number)] = (seen * jax.nn.sigmoid(gate[:, head(number)])).astype(BF16)
    out = dot_back(gated[...], w_out[...])

    @pl.when(step == 0)
    def _():
        mine[...] = out.astype(BF16)

    @pl.when(step == 1)
    def _():
        other[...] = out.astype(BF16)


def attend(low, gate, w, of_row, of_column):
    length = low.shape[0]
    half, width = length // 2, w.shape[0]
    return call(
        attend_kernel,
        (2,),
        [
            fixed((length, 4 * HD)),
            rowed(half, 2 * HD),
            pl.BlockSpec((width, 2 * HD), lambda i: (0, 3)),
            fixed((length, 4)),
            fixed((2, length)),
        ],
        [
            pl.BlockSpec((2, half, length), lambda i: (0, i, 0)),
            rowed(half, 2 * HD),
            rowed(half, 2 * HD),
            fixed((half, width)),
            fixed((half, width)),
        ],
        [
            struct((2, length, length), F32),
            struct((length, 2 * HD), F32),
            struct((length, 2 * HD), BF16),
            struct((half, width), BF16),
            struct((half, width), BF16),
        ],
        2 * length * width * 2 * HD + 8 * length * length * HD,
    )(low, gate, w, of_row, of_column)


def flip_kernel(pieces, out):
    at = 0
    for piece in pieces:
        out[:, at : at + piece.shape[0]] = piece[...].T
        at += piece.shape[0]


def flip(*pieces):
    length, width = sum(piece.shape[0] for piece in pieces), pieces[0].shape[1]
    chunk = 2 * HD
    return call(
        lambda *refs: flip_kernel(refs[:-1], refs[-1]),
        (width // chunk,),
        [pl.BlockSpec((piece.shape[0], chunk), lambda i: (0, i)) for piece in pieces],
        rowed(chunk, length),
        struct((width, length), BF16),
        1 << 20,
    )(*pieces)


FEED_STEPS = 3


def feed_kernel(
    ua, ub, ca, cb, wg, wu, wd, u_flip, sa, sb, hidden, d_gate, d_up, out, flipped
):
    step = pl.program_id(0)
    half, chunk, units = ua.shape[0], wg.shape[1], hidden.shape[1]

    @pl.when(step < FEED_STEPS)
    def _():
        columns = pl.ds(pl.multiple_of(step * chunk, chunk), chunk)
        for number, (u, cot) in enumerate(((ua, ca), (ub, cb))):
            rows = slice(number * half, (number + 1) * half)
            gate, up = dot(u[...], wg[...]), dot(u[...], wu[...])
            d_hidden = dot(flat(cot[...]), wd[...])
            sig = jax.nn.sigmoid(gate)
            silu = gate * sig
            hidden[rows, columns] = (silu * up).astype(BF16)
            d_gate[rows, columns] = (d_hidden * up * sig * (1.0 + gate * (1.0 - sig))).astype(BF16)
            d_up[rows, columns] = (d_hidden * silu).astype(BF16)

    @pl.when(step == FEED_STEPS)
    def _():
        flipped[...] = hidden[...].T

    @pl.when(step >= FEED_STEPS)
    def _():
        out[:, :units] = dot(u_flip[...], d_gate[...]).astype(BF16)
        out[:, units : 2 * units] = dot(u_flip[...], d_up[...]).astype(BF16)
        cot = jnp.concatenate([flat(sa[...]), flat(sb[...])], axis=0)
        spread_blocks(flipped[...], cot, out, 2 * units)


def feed(ua, ub, ca, cb, w, u_flip):
    half, width = ua.shape
    length, units = 2 * half, w.shape[1] // 3
    chunk, slab = units // FEED_STEPS, 4 * HD
    early = lambda i: jnp.minimum(i, FEED_STEPS - 1)
    late = lambda i: jnp.maximum(i - FEED_STEPS, 0)
    column = lambda shift: pl.BlockSpec(
        (width, chunk), lambda i: (0, shift * FEED_STEPS + early(i))
    )
    piece = pl.BlockSpec((ca.shape[0], ca.shape[1] // 2, slab), lambda i: (0, 1, late(i)))
    return call(
        feed_kernel,
        (FEED_STEPS + width // slab,),
        [fixed((half, width))] * 2
        + [piled(ca.shape, 1)] * 2
        + [column(0), column(1), column(2)]
        + [pl.BlockSpec((slab, length), lambda i: (late(i), 0)), piece, piece],
        [fixed((length, units))] * 3 + [pl.BlockSpec((slab, 3 * units), lambda i: (late(i), 0))],
        [struct((length, units), BF16)] * 3 + [struct((width, 3 * units), BF16)],
        2 * length * width * units * 6,
        scratch=[pltpu.VMEM((units, length), BF16)],
        vmem=60 << 20,
    )(ua, ub, ca, cb, w, w, w, u_flip, ca, cb)


def feed_back_kernel(d_gate, d_up, wg, wu, mine, other):
    half = mine.shape[0]
    out = dot_back(d_gate[...], wg[...]) + dot_back(d_up[...], wu[...])
    mine[...] = out[:half, :].astype(BF16)
    other[...] = out[half:, :].astype(BF16)


def feed_back(d_gate, d_up, w, behind):
    length, units = d_gate.shape
    half, width = length // 2, w.shape[0]
    chunk = 4 * HD
    slab = pl.BlockSpec((half, chunk), lambda i: (0, i))
    return call(
        feed_back_kernel,
        (width // chunk,),
        [fixed((length, units))] * 2
        + [
            pl.BlockSpec((chunk, units), lambda i: (i, 0)),
            pl.BlockSpec((chunk, units), lambda i: (i, 1)),
        ],
        [slab, slab],
        [struct((half, width), BF16), struct((half, width), BF16)],
        2 * length * width * units * 2,
        behind=behind,
        vmem=48 << 20,
    )(d_gate, d_up, w, w)


def down_kernel(hidden, w, mine, other):
    out = dot_back(hidden[...], w[...])

    @pl.when(pl.program_id(0) == 0)
    def _():
        mine[...] = out.astype(BF16)

    @pl.when(pl.program_id(0) == 1)
    def _():
        other[...] = out.astype(BF16)


def down_product(left, w, place, behind):
    length, units = left.shape
    half, width = length // 2, w.shape[0]
    return call(
        down_kernel,
        (2,),
        [rowed(half, units), pl.BlockSpec((width, units), lambda i: (0, place))],
        [fixed((half, width)), fixed((half, width))],
        [struct((half, width), BF16), struct((half, width), BF16)],
        2 * length * width * units,
        behind=behind,
    )(left, w)


def spread_blocks(flipped, right, out, start):
    term = dot(flipped, right).astype(BF16)
    for place in range(flipped.shape[0] // HD):
        for owner in range(right.shape[1] // HD):
            at = start + place * HD
            out[owner * HD : (owner + 1) * HD, at : at + HD] = term[head(place), head(owner)]


def gate_back_kernel(da, db, w_out, gate, attended, d_attended, d_gate):
    half = da.shape[0]
    for number, low in enumerate((da, db)):
        rows = slice(number * half, (number + 1) * half)
        d_gated = dot(low[...], w_out[...])
        sig = jax.nn.sigmoid(gate[rows, :])
        d_attended[rows, :] = (d_gated * sig).astype(BF16)
        d_gate[rows, :] = (d_gated * attended[rows, :] * sig * (1.0 - sig)).astype(BF16)


def gate_back(da, db, w, gate, attended):
    half, width = da.shape
    wide = (2 * half, 2 * HD)
    return call(
        gate_back_kernel,
        (1,),
        [fixed((half, width))] * 2
        + [pl.BlockSpec((width, 2 * HD), lambda i: (0, 3)), fixed(wide), fixed(wide)],
        [fixed(wide), fixed(wide)],
        [struct(wide, BF16), struct(wide, BF16)],
        2 * 2 * half * width * 2 * HD,
    )(da, db, w, gate, attended)


def head_back(grads, inputs, gain):
    factor = rms_scale(inputs)
    scaled = gain * grads
    back = factor * scaled - inputs * factor**3 * jnp.mean(scaled * inputs, axis=-1, keepdims=True)
    return back.astype(BF16), jnp.sum(grads * inputs * factor, axis=0, keepdims=True)


def attend_back_kernel(
    probs, low, d_attended, pre, gains, cosine, sine, out, terms, d_key, d_value
):
    step = pl.program_id(0)
    half = probs.shape[1]
    start = pl.multiple_of(step * half, half)
    rows = pl.ds(start, half)
    key, value = low[:, head(2)], low[:, head(3)]
    cos_rows, sin_rows = cosine[rows, :], sine[rows, :]

    @pl.when(step == 0)
    def _():
        d_key[...] = jnp.zeros_like(d_key)
        d_value[...] = jnp.zeros_like(d_value)
        terms[...] = jnp.zeros_like(terms)

    for number in range(2):
        share = probs[number]
        d_seen = d_attended[:, head(number)]
        d_share = dot_back(d_seen, value)
        d_scores = share * (d_share - jnp.sum(share * d_share, axis=-1, keepdims=True))
        d_scores = d_scores.astype(BF16)
        d_query = dot(d_scores, key) * SCALE
        d_key[...] += dot_rows(d_scores, low[rows, head(number)])
        d_value[...] += dot_rows(share.astype(BF16), d_seen)
        grads = d_query * cos_rows + unturn(d_query * sin_rows)
        back, term = head_back(grads, pre[rows, head(number)], gains[0:1, :])
        out[rows, head(number)] = back
        terms[0:1, :] += term

    @pl.when(step == 1)
    def _():
        grads = d_key[...] * SCALE
        grads = grads * cosine[...] + unturn(grads * sine[...])
        back, term = head_back(grads, pre[:, head(2)], gains[1:2, :])
        out[:, head(2)] = back
        terms[1:2, :] = term
        out[:, head(3)] = d_value[...].astype(BF16)


def attend_back(probs, low, d_attended, pre, gains, cosine, sine, behind):
    length = low.shape[0]
    half = length // 2
    return call(
        attend_back_kernel,
        (2,),
        [
            pl.BlockSpec((2, half, length), lambda i: (0, i, 0)),
            fixed((length, 4 * HD)),
            rowed(half, 2 * HD),
            fixed((length, 3 * HD)),
            fixed((8, HD)),
            fixed((length, HD)),
            fixed((length, HD)),
        ],
        [fixed((length, 4 * HD)), fixed((8, HD))],
        [struct((length, 4 * HD), BF16), struct((8, HD), F32)],
        20 * length * length * HD,
        scratch=[pltpu.VMEM((length, HD), F32), pltpu.VMEM((length, HD), F32)],
        behind=behind,
    )(probs, low, d_attended, pre, gains, cosine, sine)


def input_back_kernel(d_qkv, d_gate, w, mine, other):
    out = dot_back(d_qkv[...], w[:, : 4 * HD]) + dot_back(d_gate[...], w[:, 4 * HD :])

    @pl.when(pl.program_id(0) == 0)
    def _():
        mine[...] = out.astype(BF16)

    @pl.when(pl.program_id(0) == 1)
    def _():
        other[...] = out.astype(BF16)


def input_back(d_qkv, d_gate, w, behind):
    length = d_qkv.shape[0]
    half, width = length // 2, w.shape[0]
    return call(
        input_back_kernel,
        (2,),
        [rowed(half, 4 * HD), rowed(half, 2 * HD), fixed((width, 6 * HD))],
        [fixed((half, width)), fixed((half, width))],
        [struct((half, width), BF16), struct((half, width), BF16)],
        2 * length * width * 6 * HD,
        behind=behind,
    )(d_qkv, d_gate, w)


def attend_grads_kernel(x_flip, da, db, d_qkv, d_gate, gated, out, flipped):
    @pl.when(pl.program_id(0) == 0)
    def _():
        flipped[...] = gated[...].T

    inner, split = d_qkv.shape[1], d_gate.shape[1]
    out[:, :inner] = dot(x_flip[...], d_qkv[...]).astype(BF16)
    out[:, inner : inner + split] = dot(x_flip[...], d_gate[...]).astype(BF16)
    spread_blocks(
        flipped[...], jnp.concatenate([da[...], db[...]], axis=0), out, inner + split
    )


def attend_grads(x_flip, da, db, d_qkv, d_gate, gated, behind):
    width, length = x_flip.shape
    columns = d_qkv.shape[1] + d_gate.shape[1] + gated.shape[1]
    chunk = 4 * HD
    slab = pl.BlockSpec((length // 2, chunk), lambda i: (0, i))
    return call(
        attend_grads_kernel,
        (width // chunk,),
        [
            rowed(chunk, length),
            slab,
            slab,
            fixed(d_qkv.shape),
            fixed(d_gate.shape),
            fixed(gated.shape),
        ],
        rowed(chunk, columns),
        struct((width, columns), BF16),
        2 * length * width * columns,
        scratch=[pltpu.VMEM(gated.shape[::-1], BF16)],
        behind=behind,
    )(x_flip, da, db, d_qkv, d_gate, gated)


def middle_kernel(parts, x, middle, spread):
    total = x[...].astype(F32) + jnp.sum(parts[...].astype(F32), axis=0)
    middle[...] = total
    low = (total * rms_scale(total)).astype(BF16)
    for number in range(spread.shape[0]):
        spread[number] = low


def middle_step(parts, x, behind):
    shape = x.shape
    return call(
        middle_kernel,
        (1,),
        [fixed(parts.shape), fixed(shape)],
        [fixed(shape), fixed(parts.shape)],
        [struct(shape, F32), struct(parts.shape, BF16)],
        1 << 20,
        behind=behind,
    )(parts, x)


def norm_back(grads, inputs):
    factor = rms_scale(inputs)
    return factor * grads - inputs * factor**3 * jnp.mean(grads * inputs, axis=-1, keepdims=True)


def d_middle_kernel(parts, middle, cot, d_middle, spread):
    grads = jnp.sum(parts[...].astype(F32), axis=0)
    total = cot[...].astype(F32) + norm_back(grads, middle[...])
    d_middle[...] = total
    for number in range(spread.shape[0]):
        spread[number] = total.astype(BF16)


def d_middle_step(parts, middle, cot):
    shape = cot.shape
    return call(
        d_middle_kernel,
        (1,),
        [fixed(parts.shape), fixed(shape), fixed(shape)],
        [fixed(shape), fixed(parts.shape)],
        [struct(shape, F32), struct(parts.shape, BF16)],
        1 << 20,
    )(parts, middle, cot)


def ends_kernel(parts, middle, d_middle, x, out, terms):
    rows = x.shape[0]
    total = sum(part[...].astype(F32) for part in parts)
    out[:rows, :] = (middle[...] + total[:rows, :]).astype(BF16)
    inputs = x[...].astype(F32)
    grads = total[rows:, :]
    out[rows:, :] = (d_middle[...] + norm_back(grads, inputs)).astype(BF16)
    found = jnp.sum(grads * inputs * rms_scale(inputs), axis=0, keepdims=True)
    terms[...] = jnp.broadcast_to(found, terms.shape)


def ends_step(parts, middle, d_middle, x, behind):
    shape, wide = x.shape, parts[0].shape
    count = len(parts)
    return call(
        lambda *refs: ends_kernel(refs[:count], *refs[count:]),
        (1,),
        [fixed(wide)] * count + [fixed(shape)] * 3,
        [fixed(wide), fixed((8, shape[1]))],
        [struct(wide, BF16), struct((8, shape[1]), F32)],
        1 << 20,
        behind=behind,
    )(*parts, middle, d_middle, x)


def prefetched(kernel, grid, in_specs, out_specs, out_shape, vmem=VMEM):
    return pl.pallas_call(
        kernel,
        grid_spec=pltpu.PrefetchScalarGridSpec(
            num_scalar_prefetch=1, grid=grid, in_specs=in_specs, out_specs=out_specs
        ),
        out_shape=out_shape,
        compiler_params=pltpu.CompilerParams(
            dimension_semantics=("arbitrary",) * len(grid), vmem_limit_bytes=vmem
        ),
        cost_estimate=pl.CostEstimate(flops=1 << 20, bytes_accessed=8 << 20, transcendentals=0),
    )


def copy_kernel(core, source, out):
    out[...] = source[...]


def sibling_part(core, found):
    pairs, _, rows, columns = found.shape
    return prefetched(
        copy_kernel,
        (pairs // 2,),
        [pl.BlockSpec((2, None, rows, columns), lambda i, at: (i, 1 - at[0], 0, 0))],
        pl.BlockSpec((2, rows, columns), lambda i, at: (i, 0, 0)),
        struct((pairs, rows, columns), found.dtype),
    )(core, found)


def join_kernel(core, mine, other, out):
    out[:, core[0]] = mine[...]
    out[:, 1 - core[0]] = other[...]


def join_cores(core, found, other):
    pairs, _, rows, columns = found.shape
    return prefetched(
        join_kernel,
        (pairs // 2,),
        [
            pl.BlockSpec((2, None, rows, columns), lambda i, at: (i, at[0], 0, 0)),
            pl.BlockSpec((2, rows, columns), lambda i, at: (i, 0, 0)),
        ],
        pl.BlockSpec((2, 2, rows, columns), lambda i, at: (i, 0, 0, 0)),
        struct(found.shape, found.dtype),
    )(core, found, other)


def lanes(value):
    return sum(value[:, start : start + HD] for start in range(0, value.shape[1], HD))


def pick(blocks):
    step = pl.program_id(0)
    value = blocks[0][...]
    for number in range(1, len(blocks)):
        value = jnp.where(step == number, blocks[number][...], value)
    return value.astype(F32)


def close_feed_kernel(turn_at, b0, b1, b2, b3, w_gate, w_up, gain, g_gate, g_up, g_down, sums):
    raw = pick((b0, b1, b2, b3))
    units = w_gate.shape[1]
    raw_gate, raw_up = raw[:, :units], raw[:, units : 2 * units]
    g_gate[...] = raw_gate * gain[...]
    g_up[...] = raw_up * gain[...]
    for place in range(units // HD):
        g_down[head(place), :] = raw[:, 2 * units + place * HD : 2 * units + (place + 1) * HD]
    term = lanes(raw_gate * w_gate[...].astype(F32)) + lanes(raw_up * w_up[...].astype(F32))

    @pl.when(pl.program_id(0) == 0)
    def _():
        sums[...] = term

    @pl.when(pl.program_id(0) > 0)
    def _():
        sums[...] += term


def close_attend_kernel(turn_at, b0, b1, b2, b3, gain, gq, gk, gv, gg, go):
    found, scale = pick((b0, b1, b2, b3)), gain[...]
    gq[...], gk[...] = found[:, : 2 * HD] * scale, found[:, head(2)] * scale
    gv[...], gg[...] = found[:, head(3)] * scale, found[:, 4 * HD : 6 * HD] * scale
    go[...] = jnp.concatenate([found[:, head(6)], found[:, head(7)]], axis=0)


def close(kernel, turn_at, blocks, weights, gain, out_rows, extra, read):
    quarters = 4
    place = lambda i, at: (at[0] + quarters - i) % quarters
    whole = lambda value: pl.BlockSpec(value.shape, lambda i, at: (0, 0))
    columns = lambda w: pl.BlockSpec(
        (w.shape[0], w.shape[1] // quarters), lambda i, at: (0, place(i, at))
    )
    rows, width = out_rows
    operands = weights if read else ()
    in_specs = [whole(b) for b in blocks] + [columns(w) for w in operands] + [whole(gain)]
    out_specs = [columns(w) for w in weights]
    out_specs += [pl.BlockSpec((rows // quarters, width), lambda i, at: (place(i, at), 0))]
    out_specs += [pl.BlockSpec(shape, lambda i, at: (0, 0)) for shape in extra]
    out_shape = [struct(w.shape, F32) for w in weights] + [struct(out_rows, F32)]
    out_shape += [struct(shape, F32) for shape in extra]
    return prefetched(kernel, (quarters,), in_specs, out_specs, out_shape, vmem=ALL_VMEM)(
        turn_at, *blocks, *operands, gain
    )


def column(row):
    shape = (HD, HD)
    there = lax.broadcasted_iota(jnp.int32, shape, 0) == lax.broadcasted_iota(jnp.int32, shape, 1)
    return jnp.sum(jnp.where(there, jnp.broadcast_to(row, shape), 0.0), axis=1, keepdims=True)


def first_kernel(at, wq, wk, wv, wg, wo, gain, out):
    scale = column(gain[...].astype(F32))
    start = 0
    for w in (wq, wk, wv, wg):
        stop = start + w.shape[1]
        out[:, start:stop] = (w[...].astype(F32) * scale).astype(BF16)
        start = stop
    out[:, start:] = wo[...].T


def first_columns(at, wq, wk, wv, wg, wo, gain):
    quarter = lambda w: pl.BlockSpec((w.shape[0], w.shape[1] // 4), lambda i, at: (0, at[0]))
    rows = wq.shape[0]
    heads = wo.shape[0] // 4
    columns = sum(w.shape[1] // 4 for w in (wq, wk, wv, wg)) + heads
    return prefetched(
        first_kernel,
        (1,),
        [quarter(w) for w in (wq, wk, wv, wg)]
        + [pl.BlockSpec((heads, rows), lambda i, at: (at[0], 0))]
        + [pl.BlockSpec(gain.shape, lambda i, at: (0, 0))],
        pl.BlockSpec((rows, columns), lambda i, at: (0, 0)),
        struct((rows, columns), BF16),
        vmem=ALL_VMEM,
    )(at, wq, wk, wv, wg, wo, gain)


def make_shards(mesh):
    n_shard, n_ctx, n_tp = mesh.shape["shard"], mesh.shape["ctx"], mesh.shape["tp"]
    pairs = n_shard // 2

    def joint(pair, core, tp):
        return (pair * 2 + core) * n_tp + tp

    core_perm = [(i, i ^ 1) for i in range(n_shard)]
    planes = [
        [joint(pair, core, tp) for pair in range(pairs) for tp in range(n_tp)] for core in range(2)
    ]
    swap_perm = [
        edge
        for pair in range(pairs)
        for edge in (
            (joint(pair, 1, 0), joint(pair, 0, 1)),
            (joint(pair, 0, 1), joint(pair, 1, 0)),
        )
    ]
    across_perm = [(joint(pair, t, t), joint(pair, t, 1 - t)) for pair in range(pairs) for t in range(2)]

    def spot(pair, core, ctx, tp):
        return ((pair * 2 + core) * n_ctx + ctx) * n_tp + tp

    owner_perms = [
        [
            (spot(pair, core, ctx, tp), spot(pair, tp, (ctx + by) % n_ctx, core))
            for pair in range(pairs)
            for core in range(2)
            for ctx in range(n_ctx)
            for tp in range(n_tp)
            if by > 0 or core != tp
        ]
        for by in range(n_ctx)
    ]

    def core_swap(value):
        return lax.ppermute(value, "shard", core_perm)

    def ctx_exchange(value):
        return lax.all_to_all(value, "ctx", 0, 0)

    def ctx_turn(value, by):
        return lax.ppermute(value, "ctx", [(i, (i + by) % n_ctx) for i in range(n_ctx)])

    def tree_rows(spread, *before):
        mine = ctx_exchange(spread)
        if before:
            mine, *before = lax.optimization_barrier((mine, *before))
        return mine, core_swap(mine), *before

    def tree_half(mine, other):
        half = (mine.astype(F32) + core_swap(other).astype(F32)).astype(BF16)
        return half.reshape((n_ctx, -1) + half.shape[1:])

    def plane_gather(value):
        return lax.all_gather(value, PLANE, axis=0, tiled=True, axis_index_groups=planes)

    def plane_scatter(value):
        return lax.psum_scatter(
            value, PLANE, scatter_dimension=0, tiled=True, axis_index_groups=planes
        )

    def shards(
        tokens,
        seg_lengths,
        seg_parents,
        gain_in,
        w_query,
        w_key,
        w_value,
        w_gate_attn,
        w_out,
        gain_query,
        gain_key,
        gain_mid,
        w_gate,
        w_up,
        w_down,
        cotangent,
    ):
        core = lax.axis_index("shard") % 2
        tp = lax.axis_index("tp")
        ctx = lax.axis_index("ctx")
        native = core == tp
        rows = tokens.shape[0] // 2

        def swapped(value):
            return jnp.where(native, value, lax.ppermute(value, PLANE, swap_perm))

        def quarter(weight, axis):
            size = weight.shape[axis] // n_ctx
            return lax.dynamic_slice_in_dim(weight, ctx * size, size, axis)

        gain_one = gain_in.astype(F32)[:, None]
        gain_two = gain_mid.astype(F32)[:, None]
        head_rows = gain_query.shape[0]
        first = first_columns(
            ctx.astype(jnp.int32).reshape(1), w_query, w_key, w_value, w_gate_attn, w_out, gain_in[None]
        )
        found = plane_gather(first)
        both_gains = jnp.pad(jnp.stack([gain_query, gain_key]), ((0, 6), (0, HD - head_rows)))
        both_gains = lax.all_to_all(
            jnp.broadcast_to(both_gains[None], (n_shard, 8, HD)), "shard", 0, 0
        )

        def half_rows(place):
            pieces = [lax.dynamic_slice_in_dim(v, place * rows, rows, 0) for v in (tokens, cotangent)]
            return jnp.concatenate(pieces, axis=0)

        own = jnp.where(native, half_rows(core), core_swap(half_rows(1 - core)))
        tree = jnp.concatenate([seg_lengths, seg_parents], axis=0)
        tree = jnp.where(native, tree, core_swap(tree))
        own, both_gains = lax.optimization_barrier((own, both_gains))
        own_x, own_cot = own[:rows], own[rows:]
        xa, xb = tree_rows(jnp.broadcast_to(own[None], (n_ctx,) + own.shape))

        second = jnp.concatenate([quarter(w_gate, 1), quarter(w_up, 1)], axis=1)
        second = (second.astype(F32) * gain_two).astype(BF16)
        second = jnp.concatenate([second, quarter(w_down, 0).T], axis=1)
        moved = lax.ppermute(second, PLANE, swap_perm)
        moved, xa = lax.optimization_barrier((moved, xa))
        w2 = plane_gather(jnp.where(native, second, moved))

        gains = both_gains[:, :, :head_rows].astype(F32).transpose(1, 0, 2).reshape(8, HD)
        half_at = jnp.where(jnp.arange(2) == 0, core, 1 - core) * rows
        places = (
            half_at[:, None, None]
            + jnp.arange(n_ctx, dtype=jnp.int32)[None, :, None] * (2 * rows)
            + jnp.arange(rows, dtype=jnp.int32)[None, None, :]
        ).reshape(-1)
        segment, parent_seg, grand_seg, position = tree_layout(tree[0], tree[1], places)
        of_row = jnp.stack([segment, parent_seg, grand_seg, places], axis=1)
        of_column = jnp.stack([segment, places], axis=0)
        cosine, sine = rope_tables(position, HD)

        found, xa, xb, of_row, of_column, cosine, sine = lax.optimization_barrier(
            (found, xa, xb, of_row, of_column, cosine, sine)
        )
        found = found.reshape(pairs, n_tp, gain_in.shape[0], -1)
        core_at = core.astype(jnp.int32).reshape(1)
        other = core_swap(sibling_part(core_at, found))
        w1 = join_cores(core_at, found, other).reshape(-1, first.shape[1])

        xn, pre, low, gate = project(xa, xb, w1, gains, cosine, sine)
        probs, attended, gated, mine, other = attend(low, gate, w1, of_row, of_column)
        x_flip = flip(xn)
        middle, spread = middle_step(ctx_exchange(tree_half(mine, other)), own_x, (x_flip,))
        ua, ub = (flat(v) for v in tree_rows(spread))
        u_flip = flip(ua, ub)

        hidden, d_gate, d_up, ffn = feed(ua, ub, xa, xb, w2, u_flip)
        half = tree_half(*feed_back(d_gate, d_up, w2, ()))
        d_middle, spread = d_middle_step(ctx_exchange(half), middle, own_cot)
        layer_mine, layer_other = down_product(hidden, w2, 2, (half,))
        da, db, layer_mine, layer_other = tree_rows(spread, layer_mine, layer_other)
        da, db = flat(da), flat(db)
        grad_ffn = plane_scatter(ffn)

        d_attended, d_gate_pre = gate_back(da, db, w1, gate, attended)
        d_qkv, terms = attend_back(probs, low, d_attended, pre, gains, cosine, sine, ())

        attn = attend_grads(x_flip, da, db, d_qkv, d_gate_pre, gated, ())
        in_mine, in_other = input_back(d_qkv, d_gate_pre, w1, (attn,))
        layer_half, in_half = tree_half(layer_mine, layer_other), tree_half(in_mine, in_other)
        grad_attn = plane_scatter(attn)
        layer_half, in_half, grad_ffn = lax.optimization_barrier((layer_half, in_half, grad_ffn))

        def owners(block):
            block = swapped(block)
            return [block] + [ctx_turn(block, by) for by in range(1, n_ctx)]

        def owners_at_once(block):
            moved = [lax.ppermute(block, ("shard", "ctx", "tp"), perm) for perm in owner_perms]
            return [jnp.where(native, block, moved[0])] + moved[1:]


        both = jnp.concatenate(
            [layer_half, in_half], axis=1
        )
        parts = [lax.dynamic_index_in_dim(both, ctx, 0, False)] + [
            ctx_turn(lax.dynamic_index_in_dim(both, (ctx + by) % n_ctx, 0, False), by)
            for by in range(1, n_ctx)
        ]
        ffn_blocks = owners(grad_ffn)
        ends, in_terms = ends_step(parts, middle, d_middle, own_x, (ffn_blocks[0],))
        ends, in_terms, ffn_blocks[1] = lax.optimization_barrier((ends, in_terms, ffn_blocks[1]))
        pieces = jnp.concatenate(
            [terms[0].reshape(n_shard, -1), terms[1].reshape(n_shard, -1)], axis=1
        )
        pieces = jnp.pad(pieces, ((0, 0), (0, HD - pieces.shape[1])))
        pieces = jnp.stack([in_terms[0].reshape(n_shard, HD), pieces], axis=1).astype(BF16)
        copies = n_ctx * n_tp
        pieces = jnp.broadcast_to(
            jnp.pad(pieces, ((0, 0), (0, 6), (0, 0)))[:, None], (n_shard, copies, 8, HD)
        )
        pieces = lax.all_to_all(
            pieces.reshape(n_shard * copies, 8, HD), ("shard", "ctx", "tp"), 0, 0
        )
        end_sums = jnp.sum(pieces.astype(F32), axis=0)
        sibling = core_swap(ends)

        def whole(start):
            mine, other = ends[start : start + rows], sibling[start : start + rows]
            return jnp.where(
                core == 0,
                jnp.concatenate([mine, other], axis=0),
                jnp.concatenate([other, mine], axis=0),
            )

        full = jnp.stack([whole(0), whole(rows)])
        turn_at = ctx.astype(jnp.int32).reshape(1)
        size = gain_in.shape[0]
        grad_gate, grad_up, grad_down, mid_sums = close(
            close_feed_kernel,
            turn_at,
            ffn_blocks,
            (w_gate, w_up),
            gain_two,
            w_down.shape,
            [(size, HD)],
            True,
        )
        mid_terms = jnp.sum(mid_sums, axis=1)
        mid_terms = mid_terms + lax.ppermute(mid_terms, "tp", [(0, 1), (1, 0)])
        grad_attn, mid_terms = lax.optimization_barrier((grad_attn, mid_terms))
        full = jnp.where(native, full, lax.ppermute(full, PLANE, across_perm))
        outputs = [full[0].astype(F32), full[1].astype(F32)]
        attn_blocks = owners_at_once(grad_attn)
        *outputs, attn_blocks[3], end_sums = lax.optimization_barrier(
            (*outputs, attn_blocks[3], end_sums)
        )
        grad_query, grad_key, grad_value, grad_gate_attn, grad_out = close(
            close_attend_kernel,
            turn_at,
            attn_blocks,
            (w_query, w_key, w_value, w_gate_attn),
            gain_one,
            w_out.shape,
            [],
            False,
        )

        return (
            *outputs,
            end_sums[0] / gain_one[:, 0],
            grad_query,
            grad_key,
            grad_value,
            grad_gate_attn,
            grad_out,
            end_sums[1, :head_rows],
            end_sums[1, head_rows : 2 * head_rows],
            mid_terms,
            grad_gate,
            grad_up,
            grad_down,
        )

    return shards


def solution(mesh):
    return jax.shard_map(
        make_shards(mesh),
        mesh=mesh,
        in_specs=(
            P(("shard", "ctx"), None),
            P("shard", None),
            P("shard", None),
            P("shard"),
            P("shard", "tp"),
            P("shard", "tp"),
            P("shard", "tp"),
            P("shard", "tp"),
            P("tp", "shard"),
            P("shard"),
            P("shard"),
            P("shard"),
            P("shard", "tp"),
            P("shard", "tp"),
            P("tp", "shard"),
            P(("shard", "ctx"), None),
        ),
        out_specs=(
            P(("shard", "ctx"), None),
            P(("shard", "ctx"), None),
            P("shard"),
            P("shard", "tp"),
            P("shard", "tp"),
            P("shard", "tp"),
            P("shard", "tp"),
            P("tp", "shard"),
            P("shard"),
            P("shard"),
            P("shard"),
            P("shard", "tp"),
            P("shard", "tp"),
            P("tp", "shard"),
        ),
        check_vma=False,
    )
```

```python
import math

import jax
import jax.numpy as jnp
from jax import lax
from jax.experimental import pallas as pl
from jax.experimental.pallas import tpu as pltpu
from jax.sharding import PartitionSpec as P

HD = 128
EPS = 1e-06
BASE = 1000000.0
NEG = -1e30
F32 = jnp.float32
BF16 = jnp.bfloat16
PLANE = ("shard", "tp")
SCALE = 1.0 / math.sqrt(HD)
VMEM = 48 << 20
ALL_VMEM = 60 << 20


def lookup(onehot, table):
    return jnp.sum(onehot * table[None, :], axis=1)


def tree_layout(lengths, parents, places):
    labels = jnp.arange(lengths.shape[0], dtype=jnp.int32)
    ends = jnp.cumsum(lengths)
    starts = ends - lengths
    parent_hot = (parents[:, None] == labels[None, :]).astype(jnp.int32)
    grand = lookup(parent_hot, parents)
    parent_len = lookup(parent_hot, lengths)
    grand_hot = (grand[:, None] == labels[None, :]).astype(jnp.int32)
    grand_len = lookup(grand_hot, lengths)
    before = jnp.where(labels == 0, 0, parent_len + jnp.where(parents == 0, 0, grand_len))
    segment = jnp.sum((places[:, None] >= ends[None, :]).astype(jnp.int32), axis=1)
    token_hot = (segment[:, None] == labels[None, :]).astype(jnp.int32)
    position = places - lookup(token_hot, starts) + lookup(token_hot, before)
    return (segment, lookup(token_hot, parents), lookup(token_hot, grand), position)


def rope_tables(position, columns):
    halfway = columns // 2
    frequency = jnp.exp(jnp.arange(halfway, dtype=F32) * (-2.0 * math.log(BASE) / columns))
    angles = position.astype(F32)[:, None] * frequency[None, :]
    angles = jnp.concatenate([angles, angles], axis=1)
    return (jnp.cos(angles), jnp.sin(angles))


def rms_scale(inputs):
    return lax.rsqrt(jnp.mean(inputs * inputs, axis=-1, keepdims=True) + EPS)


def dot(left, right):
    return jnp.dot(left, right, preferred_element_type=F32)


def dot_rows(left, right):
    return lax.dot_general(left, right, (((0,), (0,)), ((), ())), preferred_element_type=F32)


def dot_back(left, right):
    return lax.dot_general(left, right, (((1,), (1,)), ((), ())), preferred_element_type=F32)


def turn(inputs):
    halfway = inputs.shape[-1] // 2
    return jnp.concatenate([-inputs[:, halfway:], inputs[:, :halfway]], axis=-1)


def unturn(inputs):
    halfway = inputs.shape[-1] // 2
    return jnp.concatenate([inputs[:, halfway:], -inputs[:, :halfway]], axis=-1)


def head(number):
    return slice(number * HD, (number + 1) * HD)


def call(
    kernel, grid, in_specs, out_specs, out_shape, flops, scratch=(), moved=8 << 20, behind=(), vmem=VMEM
):
    count = len(in_specs)

    def body(*refs):
        kernel(*refs[:count], *refs[count + len(behind) :])

    built = pl.pallas_call(
        body,
        grid=grid,
        in_specs=list(in_specs) + [pl.BlockSpec(memory_space=pl.ANY)] * len(behind),
        out_specs=out_specs,
        out_shape=out_shape,
        scratch_shapes=scratch,
        compiler_params=pltpu.CompilerParams(
            dimension_semantics=("arbitrary",) * len(grid), vmem_limit_bytes=vmem
        ),
        cost_estimate=pl.CostEstimate(flops=flops, bytes_accessed=moved, transcendentals=0),
    )
    return lambda *operands: built(*operands, *behind)


def struct(shape, dtype):
    return jax.ShapeDtypeStruct(shape, dtype)


def fixed(shape):
    return pl.BlockSpec(shape, lambda i: (0,) * len(shape))


def rowed(rows, columns):
    return pl.BlockSpec((rows, columns), lambda i: (i, 0))


def piled(shape, which):
    return pl.BlockSpec((shape[0], shape[1] // 2, shape[2]), lambda i: (0, which, 0))


def flat(value):
    return value.reshape((-1,) + value.shape[2:])


def project_kernel(xa, xb, w, gains, cosine, sine, xn, pre, low, gate):
    x = flat(jnp.where(pl.program_id(0) == 0, xa[...], xb[...])).astype(F32)
    normed = (x * rms_scale(x)).astype(BF16)
    xn[...] = normed
    out = dot(normed, w[...])
    for place in range(3):
        raw = out[:, head(place)]
        pre[:, head(place)] = raw
        unit = raw * rms_scale(raw) * gains[place // 2 : place // 2 + 1, :]
        low[:, head(place)] = (unit * cosine[...] + turn(unit) * sine[...]).astype(BF16)
    low[:, head(3)] = out[:, head(3)].astype(BF16)
    gate[...] = out[:, 4 * HD :]


def project(xa, xb, w, gains, cosine, sine):
    half, width = xa.shape[0] * xa.shape[1] // 2, xa.shape[2]
    return call(
        project_kernel,
        (2,),
        [
            piled(xa.shape, 0),
            piled(xb.shape, 0),
            fixed((width, 6 * HD)),
            fixed(gains.shape),
            rowed(half, HD),
            rowed(half, HD),
        ],
        [
            rowed(half, width),
            rowed(half, 3 * HD),
            rowed(half, 4 * HD),
            rowed(half, 2 * HD),
        ],
        [
            struct((2 * half, width), BF16),
            struct((2 * half, 3 * HD), F32),
            struct((2 * half, 4 * HD), BF16),
            struct((2 * half, 2 * HD), F32),
        ],
        2 * 2 * half * width * 6 * HD,
    )(xa, xb, w, gains, cosine, sine)


def attend_kernel(low, gate, w_out, of_row, of_column, probs, attended, gated, mine, other):
    step = pl.program_id(0)
    half = probs.shape[1]
    rows = pl.ds(step * half, half)
    key, value = low[:, head(2)], low[:, head(3)]
    seg, par, grand, place = (of_row[rows, n : n + 1] for n in range(4))
    key_seg, key_place = of_column[0:1, :], of_column[1:2, :]
    allowed = ((key_seg == seg) | (key_seg == par) | (key_seg == grand)) & (key_place <= place)
    for number in range(2):
        scores = dot_back(low[rows, head(number)], key) * SCALE
        scores = jnp.where(allowed, scores, NEG)
        raised = jnp.exp(scores - jnp.max(scores, axis=-1, keepdims=True))
        share = raised / jnp.sum(raised, axis=-1, keepdims=True)
        probs[number] = share
        seen = dot(share.astype(BF16), value)
        attended[:, head(number)] = seen
        gated[:, head(number)] = (seen * jax.nn.sigmoid(gate[:, head(number)])).astype(BF16)
    out = dot_back(gated[...], w_out[...])

    @pl.when(step == 0)
    def _():
        mine[...] = out.astype(BF16)

    @pl.when(step == 1)
    def _():
        other[...] = out.astype(BF16)


def attend(low, gate, w, of_row, of_column):
    length = low.shape[0]
    half, width = length // 2, w.shape[0]
    return call(
        attend_kernel,
        (2,),
        [
            fixed((length, 4 * HD)),
            rowed(half, 2 * HD),
            pl.BlockSpec((width, 2 * HD), lambda i: (0, 3)),
            fixed((length, 4)),
            fixed((2, length)),
        ],
        [
            pl.BlockSpec((2, half, length), lambda i: (0, i, 0)),
            rowed(half, 2 * HD),
            rowed(half, 2 * HD),
            fixed((half, width)),
            fixed((half, width)),
        ],
        [
            struct((2, length, length), F32),
            struct((length, 2 * HD), F32),
            struct((length, 2 * HD), BF16),
            struct((half, width), BF16),
            struct((half, width), BF16),
        ],
        2 * length * width * 2 * HD + 8 * length * length * HD,
    )(low, gate, w, of_row, of_column)


def flip_kernel(pieces, out):
    at = 0
    for piece in pieces:
        out[:, at : at + piece.shape[0]] = piece[...].T
        at += piece.shape[0]


def flip(*pieces):
    length, width = sum(piece.shape[0] for piece in pieces), pieces[0].shape[1]
    chunk = 2 * HD
    return call(
        lambda *refs: flip_kernel(refs[:-1], refs[-1]),
        (width // chunk,),
        [pl.BlockSpec((piece.shape[0], chunk), lambda i: (0, i)) for piece in pieces],
        rowed(chunk, length),
        struct((width, length), BF16),
        1 << 20,
    )(*pieces)


FEED_STEPS = 3


def feed_kernel(
    ua, ub, ca, cb, wg, wu, wd, u_flip, sa, sb, hidden, d_gate, d_up, out, flipped
):
    step = pl.program_id(0)
    half, chunk, units = ua.shape[0], wg.shape[1], hidden.shape[1]

    @pl.when(step < FEED_STEPS)
    def _():
        columns = pl.ds(pl.multiple_of(step * chunk, chunk), chunk)
        for number, (u, cot) in enumerate(((ua, ca), (ub, cb))):
            rows = slice(number * half, (number + 1) * half)
            gate, up = dot(u[...], wg[...]), dot(u[...], wu[...])
            d_hidden = dot(flat(cot[...]), wd[...])
            sig = jax.nn.sigmoid(gate)
            silu = gate * sig
            hidden[rows, columns] = (silu * up).astype(BF16)
            d_gate[rows, columns] = (d_hidden * up * sig * (1.0 + gate * (1.0 - sig))).astype(BF16)
            d_up[rows, columns] = (d_hidden * silu).astype(BF16)

    @pl.when(step == FEED_STEPS)
    def _():
        flipped[...] = hidden[...].T

    @pl.when(step >= FEED_STEPS)
    def _():
        out[:, :units] = dot(u_flip[...], d_gate[...]).astype(BF16)
        out[:, units : 2 * units] = dot(u_flip[...], d_up[...]).astype(BF16)
        cot = jnp.concatenate([flat(sa[...]), flat(sb[...])], axis=0)
        spread_blocks(flipped[...], cot, out, 2 * units)


def feed(ua, ub, ca, cb, w, u_flip):
    half, width = ua.shape
    length, units = 2 * half, w.shape[1] // 3
    chunk, slab = units // FEED_STEPS, 8 * HD
    early = lambda i: jnp.minimum(i, FEED_STEPS - 1)
    late = lambda i: jnp.maximum(i - FEED_STEPS, 0)
    column = lambda shift: pl.BlockSpec(
        (width, chunk), lambda i: (0, shift * FEED_STEPS + early(i))
    )
    piece = pl.BlockSpec((ca.shape[0], ca.shape[1] // 2, slab), lambda i: (0, 1, late(i)))
    return call(
        feed_kernel,
        (FEED_STEPS + width // slab,),
        [fixed((half, width))] * 2
        + [piled(ca.shape, 1)] * 2
        + [column(0), column(1), column(2)]
        + [pl.BlockSpec((slab, length), lambda i: (late(i), 0)), piece, piece],
        [fixed((length, units))] * 3 + [pl.BlockSpec((slab, 3 * units), lambda i: (late(i), 0))],
        [struct((length, units), BF16)] * 3 + [struct((width, 3 * units), BF16)],
        2 * length * width * units * 6,
        scratch=[pltpu.VMEM((units, length), BF16)],
        vmem=60 << 20,
    )(ua, ub, ca, cb, w, w, w, u_flip, ca, cb)


def feed_back_kernel(d_gate, d_up, wg, wu, mine, other):
    half = mine.shape[0]
    out = dot_back(d_gate[...], wg[...]) + dot_back(d_up[...], wu[...])
    mine[...] = out[:half, :].astype(BF16)
    other[...] = out[half:, :].astype(BF16)


def feed_back(d_gate, d_up, w, behind):
    length, units = d_gate.shape
    half, width = length // 2, w.shape[0]
    chunk = 4 * HD
    slab = pl.BlockSpec((half, chunk), lambda i: (0, i))
    return call(
        feed_back_kernel,
        (width // chunk,),
        [fixed((length, units))] * 2
        + [
            pl.BlockSpec((chunk, units), lambda i: (i, 0)),
            pl.BlockSpec((chunk, units), lambda i: (i, 1)),
        ],
        [slab, slab],
        [struct((half, width), BF16), struct((half, width), BF16)],
        2 * length * width * units * 2,
        behind=behind,
        vmem=48 << 20,
    )(d_gate, d_up, w, w)


def down_kernel(hidden, w, mine, other):
    out = dot_back(hidden[...], w[...])

    @pl.when(pl.program_id(0) == 0)
    def _():
        mine[...] = out.astype(BF16)

    @pl.when(pl.program_id(0) == 1)
    def _():
        other[...] = out.astype(BF16)


def down_product(left, w, place, behind):
    length, units = left.shape
    half, width = length // 2, w.shape[0]
    return call(
        down_kernel,
        (2,),
        [rowed(half, units), pl.BlockSpec((width, units), lambda i: (0, place))],
        [fixed((half, width)), fixed((half, width))],
        [struct((half, width), BF16), struct((half, width), BF16)],
        2 * length * width * units,
        behind=behind,
    )(left, w)


def spread_blocks(flipped, right, out, start):
    term = dot(flipped, right).astype(BF16)
    for place in range(flipped.shape[0] // HD):
        for owner in range(right.shape[1] // HD):
            at = start + place * HD
            out[owner * HD : (owner + 1) * HD, at : at + HD] = term[head(place), head(owner)]


def gate_back_kernel(da, db, w_out, gate, attended, d_attended, d_gate):
    half = da.shape[0]
    for number, low in enumerate((da, db)):
        rows = slice(number * half, (number + 1) * half)
        d_gated = dot(low[...], w_out[...])
        sig = jax.nn.sigmoid(gate[rows, :])
        d_attended[rows, :] = (d_gated * sig).astype(BF16)
        d_gate[rows, :] = (d_gated * attended[rows, :] * sig * (1.0 - sig)).astype(BF16)


def gate_back(da, db, w, gate, attended):
    half, width = da.shape
    wide = (2 * half, 2 * HD)
    return call(
        gate_back_kernel,
        (1,),
        [fixed((half, width))] * 2
        + [pl.BlockSpec((width, 2 * HD), lambda i: (0, 3)), fixed(wide), fixed(wide)],
        [fixed(wide), fixed(wide)],
        [struct(wide, BF16), struct(wide, BF16)],
        2 * 2 * half * width * 2 * HD,
    )(da, db, w, gate, attended)


def head_back(grads, inputs, gain):
    factor = rms_scale(inputs)
    scaled = gain * grads
    back = factor * scaled - inputs * factor**3 * jnp.mean(scaled * inputs, axis=-1, keepdims=True)
    return back.astype(BF16), jnp.sum(grads * inputs * factor, axis=0, keepdims=True)


def attend_back_kernel(
    probs, low, d_attended, pre, gains, cosine, sine, out, terms, d_key, d_value
):
    step = pl.program_id(0)
    half = probs.shape[1]
    start = pl.multiple_of(step * half, half)
    rows = pl.ds(start, half)
    key, value = low[:, head(2)], low[:, head(3)]
    cos_rows, sin_rows = cosine[rows, :], sine[rows, :]

    @pl.when(step == 0)
    def _():
        d_key[...] = jnp.zeros_like(d_key)
        d_value[...] = jnp.zeros_like(d_value)
        terms[...] = jnp.zeros_like(terms)

    for number in range(2):
        share = probs[number]
        d_seen = d_attended[:, head(number)]
        d_share = dot_back(d_seen, value)
        d_scores = share * (d_share - jnp.sum(share * d_share, axis=-1, keepdims=True))
        d_scores = d_scores.astype(BF16)
        d_query = dot(d_scores, key) * SCALE
        d_key[...] += dot_rows(d_scores, low[rows, head(number)])
        d_value[...] += dot_rows(share.astype(BF16), d_seen)
        grads = d_query * cos_rows + unturn(d_query * sin_rows)
        back, term = head_back(grads, pre[rows, head(number)], gains[0:1, :])
        out[rows, head(number)] = back
        terms[0:1, :] += term

    @pl.when(step == 1)
    def _():
        grads = d_key[...] * SCALE
        grads = grads * cosine[...] + unturn(grads * sine[...])
        back, term = head_back(grads, pre[:, head(2)], gains[1:2, :])
        out[:, head(2)] = back
        terms[1:2, :] = term
        out[:, head(3)] = d_value[...].astype(BF16)


def attend_back(probs, low, d_attended, pre, gains, cosine, sine, behind):
    length = low.shape[0]
    half = length // 2
    return call(
        attend_back_kernel,
        (2,),
        [
            pl.BlockSpec((2, half, length), lambda i: (0, i, 0)),
            fixed((length, 4 * HD)),
            rowed(half, 2 * HD),
            fixed((length, 3 * HD)),
            fixed((8, HD)),
            fixed((length, HD)),
            fixed((length, HD)),
        ],
        [fixed((length, 4 * HD)), fixed((8, HD))],
        [struct((length, 4 * HD), BF16), struct((8, HD), F32)],
        20 * length * length * HD,
        scratch=[pltpu.VMEM((length, HD), F32), pltpu.VMEM((length, HD), F32)],
        behind=behind,
    )(probs, low, d_attended, pre, gains, cosine, sine)


def input_back_kernel(d_qkv, d_gate, w, mine, other):
    out = dot_back(d_qkv[...], w[:, : 4 * HD]) + dot_back(d_gate[...], w[:, 4 * HD :])

    @pl.when(pl.program_id(0) == 0)
    def _():
        mine[...] = out.astype(BF16)

    @pl.when(pl.program_id(0) == 1)
    def _():
        other[...] = out.astype(BF16)


def input_back(d_qkv, d_gate, w, behind):
    length = d_qkv.shape[0]
    half, width = length // 2, w.shape[0]
    return call(
        input_back_kernel,
        (2,),
        [rowed(half, 4 * HD), rowed(half, 2 * HD), fixed((width, 6 * HD))],
        [fixed((half, width)), fixed((half, width))],
        [struct((half, width), BF16), struct((half, width), BF16)],
        2 * length * width * 6 * HD,
        behind=behind,
    )(d_qkv, d_gate, w)


def attend_grads_kernel(x_flip, da, db, d_qkv, d_gate, gated, out, flipped):
    @pl.when(pl.program_id(0) == 0)
    def _():
        flipped[...] = gated[...].T

    inner, split = d_qkv.shape[1], d_gate.shape[1]
    out[:, :inner] = dot(x_flip[...], d_qkv[...]).astype(BF16)
    out[:, inner : inner + split] = dot(x_flip[...], d_gate[...]).astype(BF16)
    spread_blocks(
        flipped[...], jnp.concatenate([da[...], db[...]], axis=0), out, inner + split
    )


def attend_grads(x_flip, da, db, d_qkv, d_gate, gated, behind):
    width, length = x_flip.shape
    columns = d_qkv.shape[1] + d_gate.shape[1] + gated.shape[1]
    chunk = 4 * HD
    slab = pl.BlockSpec((length // 2, chunk), lambda i: (0, i))
    return call(
        attend_grads_kernel,
        (width // chunk,),
        [
            rowed(chunk, length),
            slab,
            slab,
            fixed(d_qkv.shape),
            fixed(d_gate.shape),
            fixed(gated.shape),
        ],
        rowed(chunk, columns),
        struct((width, columns), BF16),
        2 * length * width * columns,
        scratch=[pltpu.VMEM(gated.shape[::-1], BF16)],
        behind=behind,
    )(x_flip, da, db, d_qkv, d_gate, gated)


def middle_kernel(parts, x, middle, spread):
    total = x[...].astype(F32) + jnp.sum(parts[...].astype(F32), axis=0)
    middle[...] = total
    low = (total * rms_scale(total)).astype(BF16)
    for number in range(spread.shape[0]):
        spread[number] = low


def middle_step(parts, x, behind):
    shape = x.shape
    return call(
        middle_kernel,
        (1,),
        [fixed(parts.shape), fixed(shape)],
        [fixed(shape), fixed(parts.shape)],
        [struct(shape, F32), struct(parts.shape, BF16)],
        1 << 20,
        behind=behind,
    )(parts, x)


def norm_back(grads, inputs):
    factor = rms_scale(inputs)
    return factor * grads - inputs * factor**3 * jnp.mean(grads * inputs, axis=-1, keepdims=True)


def d_middle_kernel(parts, middle, cot, d_middle, spread):
    grads = jnp.sum(parts[...].astype(F32), axis=0)
    total = cot[...].astype(F32) + norm_back(grads, middle[...])
    d_middle[...] = total
    for number in range(spread.shape[0]):
        spread[number] = total.astype(BF16)


def d_middle_step(parts, middle, cot):
    shape = cot.shape
    return call(
        d_middle_kernel,
        (1,),
        [fixed(parts.shape), fixed(shape), fixed(shape)],
        [fixed(shape), fixed(parts.shape)],
        [struct(shape, F32), struct(parts.shape, BF16)],
        1 << 20,
    )(parts, middle, cot)


def ends_kernel(parts, middle, d_middle, x, out, terms):
    rows = x.shape[0]
    total = sum(part[...].astype(F32) for part in parts)
    out[:rows, :] = (middle[...] + total[:rows, :]).astype(BF16)
    inputs = x[...].astype(F32)
    grads = total[rows:, :]
    out[rows:, :] = (d_middle[...] + norm_back(grads, inputs)).astype(BF16)
    found = jnp.sum(grads * inputs * rms_scale(inputs), axis=0, keepdims=True)
    terms[...] = jnp.broadcast_to(found, terms.shape)


def ends_step(parts, middle, d_middle, x, behind):
    shape, wide = x.shape, parts[0].shape
    count = len(parts)
    return call(
        lambda *refs: ends_kernel(refs[:count], *refs[count:]),
        (1,),
        [fixed(wide)] * count + [fixed(shape)] * 3,
        [fixed(wide), fixed((8, shape[1]))],
        [struct(wide, BF16), struct((8, shape[1]), F32)],
        1 << 20,
        behind=behind,
    )(*parts, middle, d_middle, x)


def prefetched(kernel, grid, in_specs, out_specs, out_shape, vmem=VMEM):
    return pl.pallas_call(
        kernel,
        grid_spec=pltpu.PrefetchScalarGridSpec(
            num_scalar_prefetch=1, grid=grid, in_specs=in_specs, out_specs=out_specs
        ),
        out_shape=out_shape,
        compiler_params=pltpu.CompilerParams(
            dimension_semantics=("arbitrary",) * len(grid), vmem_limit_bytes=vmem
        ),
        cost_estimate=pl.CostEstimate(flops=1 << 20, bytes_accessed=8 << 20, transcendentals=0),
    )


def copy_kernel(core, source, out):
    out[...] = source[...]


def sibling_part(core, found):
    pairs, _, rows, columns = found.shape
    return prefetched(
        copy_kernel,
        (pairs // 2,),
        [pl.BlockSpec((2, None, rows, columns), lambda i, at: (i, 1 - at[0], 0, 0))],
        pl.BlockSpec((2, rows, columns), lambda i, at: (i, 0, 0)),
        struct((pairs, rows, columns), found.dtype),
    )(core, found)


def join_kernel(core, mine, other, out):
    out[:, core[0]] = mine[...]
    out[:, 1 - core[0]] = other[...]


def join_cores(core, found, other):
    pairs, _, rows, columns = found.shape
    return prefetched(
        join_kernel,
        (pairs // 2,),
        [
            pl.BlockSpec((2, None, rows, columns), lambda i, at: (i, at[0], 0, 0)),
            pl.BlockSpec((2, rows, columns), lambda i, at: (i, 0, 0)),
        ],
        pl.BlockSpec((2, 2, rows, columns), lambda i, at: (i, 0, 0, 0)),
        struct(found.shape, found.dtype),
    )(core, found, other)


def lanes(value):
    return sum(value[:, start : start + HD] for start in range(0, value.shape[1], HD))


def pick(blocks):
    step = pl.program_id(0)
    value = blocks[0][...]
    for number in range(1, len(blocks)):
        value = jnp.where(step == number, blocks[number][...], value)
    return value.astype(F32)


def close_feed_kernel(turn_at, b0, b1, b2, b3, w_gate, w_up, gain, g_gate, g_up, g_down, sums):
    raw = pick((b0, b1, b2, b3))
    units = w_gate.shape[1]
    raw_gate, raw_up = raw[:, :units], raw[:, units : 2 * units]
    g_gate[...] = raw_gate * gain[...]
    g_up[...] = raw_up * gain[...]
    for place in range(units // HD):
        g_down[head(place), :] = raw[:, 2 * units + place * HD : 2 * units + (place + 1) * HD]
    term = lanes(raw_gate * w_gate[...].astype(F32)) + lanes(raw_up * w_up[...].astype(F32))

    @pl.when(pl.program_id(0) == 0)
    def _():
        sums[...] = term

    @pl.when(pl.program_id(0) > 0)
    def _():
        sums[...] += term


def close_attend_kernel(turn_at, b0, b1, b2, b3, gain, gq, gk, gv, gg, go):
    found, scale = pick((b0, b1, b2, b3)), gain[...]
    gq[...], gk[...] = found[:, : 2 * HD] * scale, found[:, head(2)] * scale
    gv[...], gg[...] = found[:, head(3)] * scale, found[:, 4 * HD : 6 * HD] * scale
    go[...] = jnp.concatenate([found[:, head(6)], found[:, head(7)]], axis=0)


def close(kernel, turn_at, blocks, weights, gain, out_rows, extra, read):
    quarters = 4
    place = lambda i, at: (at[0] + quarters - i) % quarters
    whole = lambda value: pl.BlockSpec(value.shape, lambda i, at: (0, 0))
    columns = lambda w: pl.BlockSpec(
        (w.shape[0], w.shape[1] // quarters), lambda i, at: (0, place(i, at))
    )
    rows, width = out_rows
    operands = weights if read else ()
    in_specs = [whole(b) for b in blocks] + [columns(w) for w in operands] + [whole(gain)]
    out_specs = [columns(w) for w in weights]
    out_specs += [pl.BlockSpec((rows // quarters, width), lambda i, at: (place(i, at), 0))]
    out_specs += [pl.BlockSpec(shape, lambda i, at: (0, 0)) for shape in extra]
    out_shape = [struct(w.shape, F32) for w in weights] + [struct(out_rows, F32)]
    out_shape += [struct(shape, F32) for shape in extra]
    return prefetched(kernel, (quarters,), in_specs, out_specs, out_shape, vmem=ALL_VMEM)(
        turn_at, *blocks, *operands, gain
    )


def column(row):
    shape = (HD, HD)
    there = lax.broadcasted_iota(jnp.int32, shape, 0) == lax.broadcasted_iota(jnp.int32, shape, 1)
    return jnp.sum(jnp.where(there, jnp.broadcast_to(row, shape), 0.0), axis=1, keepdims=True)


def first_kernel(at, wq, wk, wv, wg, wo, gain, out):
    scale = column(gain[...].astype(F32))
    start = 0
    for w in (wq, wk, wv, wg):
        stop = start + w.shape[1]
        out[:, start:stop] = (w[...].astype(F32) * scale).astype(BF16)
        start = stop
    out[:, start:] = wo[...].T


def first_columns(at, wq, wk, wv, wg, wo, gain):
    quarter = lambda w: pl.BlockSpec((w.shape[0], w.shape[1] // 4), lambda i, at: (0, at[0]))
    rows = wq.shape[0]
    heads = wo.shape[0] // 4
    columns = sum(w.shape[1] // 4 for w in (wq, wk, wv, wg)) + heads
    return prefetched(
        first_kernel,
        (1,),
        [quarter(w) for w in (wq, wk, wv, wg)]
        + [pl.BlockSpec((heads, rows), lambda i, at: (at[0], 0))]
        + [pl.BlockSpec(gain.shape, lambda i, at: (0, 0))],
        pl.BlockSpec((rows, columns), lambda i, at: (0, 0)),
        struct((rows, columns), BF16),
        vmem=ALL_VMEM,
    )(at, wq, wk, wv, wg, wo, gain)


def make_shards(mesh):
    n_shard, n_ctx, n_tp = mesh.shape["shard"], mesh.shape["ctx"], mesh.shape["tp"]
    pairs = n_shard // 2

    def joint(pair, core, tp):
        return (pair * 2 + core) * n_tp + tp

    core_perm = [(i, i ^ 1) for i in range(n_shard)]
    planes = [
        [joint(pair, core, tp) for pair in range(pairs) for tp in range(n_tp)] for core in range(2)
    ]
    swap_perm = [
        edge
        for pair in range(pairs)
        for edge in (
            (joint(pair, 1, 0), joint(pair, 0, 1)),
            (joint(pair, 0, 1), joint(pair, 1, 0)),
        )
    ]
    across_perm = [(joint(pair, t, t), joint(pair, t, 1 - t)) for pair in range(pairs) for t in range(2)]

    def spot(pair, core, ctx, tp):
        return ((pair * 2 + core) * n_ctx + ctx) * n_tp + tp

    owner_perms = [
        [
            (spot(pair, core, ctx, tp), spot(pair, tp, (ctx + by) % n_ctx, core))
            for pair in range(pairs)
            for core in range(2)
            for ctx in range(n_ctx)
            for tp in range(n_tp)
            if by > 0 or core != tp
        ]
        for by in range(n_ctx)
    ]

    def core_swap(value):
        return lax.ppermute(value, "shard", core_perm)

    def ctx_exchange(value):
        return lax.all_to_all(value, "ctx", 0, 0)

    def ctx_turn(value, by):
        return lax.ppermute(value, "ctx", [(i, (i + by) % n_ctx) for i in range(n_ctx)])

    def tree_rows(spread, *before):
        mine = ctx_exchange(spread)
        if before:
            mine, *before = lax.optimization_barrier((mine, *before))
        return mine, core_swap(mine), *before

    def tree_half(mine, other):
        half = (mine.astype(F32) + core_swap(other).astype(F32)).astype(BF16)
        return half.reshape((n_ctx, -1) + half.shape[1:])

    def plane_gather(value):
        return lax.all_gather(value, PLANE, axis=0, tiled=True, axis_index_groups=planes)

    def plane_scatter(value):
        return lax.psum_scatter(
            value, PLANE, scatter_dimension=0, tiled=True, axis_index_groups=planes
        )

    def shards(
        tokens,
        seg_lengths,
        seg_parents,
        gain_in,
        w_query,
        w_key,
        w_value,
        w_gate_attn,
        w_out,
        gain_query,
        gain_key,
        gain_mid,
        w_gate,
        w_up,
        w_down,
        cotangent,
    ):
        core = lax.axis_index("shard") % 2
        tp = lax.axis_index("tp")
        ctx = lax.axis_index("ctx")
        native = core == tp
        rows = tokens.shape[0] // 2

        def swapped(value):
            return jnp.where(native, value, lax.ppermute(value, PLANE, swap_perm))

        def quarter(weight, axis):
            size = weight.shape[axis] // n_ctx
            return lax.dynamic_slice_in_dim(weight, ctx * size, size, axis)

        gain_one = gain_in.astype(F32)[:, None]
        gain_two = gain_mid.astype(F32)[:, None]
        head_rows = gain_query.shape[0]
        first = first_columns(
            ctx.astype(jnp.int32).reshape(1), w_query, w_key, w_value, w_gate_attn, w_out, gain_in[None]
        )
        found = plane_gather(first)
        both_gains = jnp.pad(jnp.stack([gain_query, gain_key]), ((0, 6), (0, HD - head_rows)))
        both_gains = lax.all_to_all(
            jnp.broadcast_to(both_gains[None], (n_shard, 8, HD)), "shard", 0, 0
        )

        def half_rows(place):
            pieces = [lax.dynamic_slice_in_dim(v, place * rows, rows, 0) for v in (tokens, cotangent)]
            return jnp.concatenate(pieces, axis=0)

        own = jnp.where(native, half_rows(core), core_swap(half_rows(1 - core)))
        tree = jnp.concatenate([seg_lengths, seg_parents], axis=0)
        tree = jnp.where(native, tree, core_swap(tree))
        own, both_gains = lax.optimization_barrier((own, both_gains))
        own_x, own_cot = own[:rows], own[rows:]
        xa, xb = tree_rows(jnp.broadcast_to(own[None], (n_ctx,) + own.shape))

        second = jnp.concatenate([quarter(w_gate, 1), quarter(w_up, 1)], axis=1)
        second = (second.astype(F32) * gain_two).astype(BF16)
        second = jnp.concatenate([second, quarter(w_down, 0).T], axis=1)
        moved = lax.ppermute(second, PLANE, swap_perm)
        moved, xa = lax.optimization_barrier((moved, xa))
        w2 = plane_gather(jnp.where(native, second, moved))

        gains = both_gains[:, :, :head_rows].astype(F32).transpose(1, 0, 2).reshape(8, HD)
        half_at = jnp.where(jnp.arange(2) == 0, core, 1 - core) * rows
        places = (
            half_at[:, None, None]
            + jnp.arange(n_ctx, dtype=jnp.int32)[None, :, None] * (2 * rows)
            + jnp.arange(rows, dtype=jnp.int32)[None, None, :]
        ).reshape(-1)
        segment, parent_seg, grand_seg, position = tree_layout(tree[0], tree[1], places)
        of_row = jnp.stack([segment, parent_seg, grand_seg, places], axis=1)
        of_column = jnp.stack([segment, places], axis=0)
        cosine, sine = rope_tables(position, HD)

        found, xa, xb, of_row, of_column, cosine, sine = lax.optimization_barrier(
            (found, xa, xb, of_row, of_column, cosine, sine)
        )
        found = found.reshape(pairs, n_tp, gain_in.shape[0], -1)
        core_at = core.astype(jnp.int32).reshape(1)
        other = core_swap(sibling_part(core_at, found))
        w1 = join_cores(core_at, found, other).reshape(-1, first.shape[1])

        xn, pre, low, gate = project(xa, xb, w1, gains, cosine, sine)
        probs, attended, gated, mine, other = attend(low, gate, w1, of_row, of_column)
        x_flip = flip(xn)
        middle, spread = middle_step(ctx_exchange(tree_half(mine, other)), own_x, (x_flip,))
        ua, ub = (flat(v) for v in tree_rows(spread))
        u_flip = flip(ua, ub)

        hidden, d_gate, d_up, ffn = feed(ua, ub, xa, xb, w2, u_flip)
        half = tree_half(*feed_back(d_gate, d_up, w2, ()))
        d_middle, spread = d_middle_step(ctx_exchange(half), middle, own_cot)
        layer_mine, layer_other = down_product(hidden, w2, 2, (half,))
        da, db, layer_mine, layer_other = tree_rows(spread, layer_mine, layer_other)
        da, db = flat(da), flat(db)
        grad_ffn = plane_scatter(ffn)

        d_attended, d_gate_pre = gate_back(da, db, w1, gate, attended)
        d_qkv, terms = attend_back(probs, low, d_attended, pre, gains, cosine, sine, ())

        attn = attend_grads(x_flip, da, db, d_qkv, d_gate_pre, gated, ())
        in_mine, in_other = input_back(d_qkv, d_gate_pre, w1, (attn,))
        layer_half, in_half = tree_half(layer_mine, layer_other), tree_half(in_mine, in_other)
        grad_attn = plane_scatter(attn)
        layer_half, in_half, grad_ffn = lax.optimization_barrier((layer_half, in_half, grad_ffn))

        def owners(block):
            block = swapped(block)
            return [block] + [ctx_turn(block, by) for by in range(1, n_ctx)]

        def owners_at_once(block):
            moved = [lax.ppermute(block, ("shard", "ctx", "tp"), perm) for perm in owner_perms]
            return [jnp.where(native, block, moved[0])] + moved[1:]


        both = jnp.concatenate(
            [layer_half, in_half], axis=1
        )
        parts = [lax.dynamic_index_in_dim(both, ctx, 0, False)] + [
            ctx_turn(lax.dynamic_index_in_dim(both, (ctx + by) % n_ctx, 0, False), by)
            for by in range(1, n_ctx)
        ]
        ffn_blocks = owners(grad_ffn)
        ends, in_terms = ends_step(parts, middle, d_middle, own_x, (ffn_blocks[0],))
        ends, in_terms, ffn_blocks[1] = lax.optimization_barrier((ends, in_terms, ffn_blocks[1]))
        pieces = jnp.concatenate(
            [terms[0].reshape(n_shard, -1), terms[1].reshape(n_shard, -1)], axis=1
        )
        pieces = jnp.pad(pieces, ((0, 0), (0, HD - pieces.shape[1])))
        pieces = jnp.stack([in_terms[0].reshape(n_shard, HD), pieces], axis=1).astype(BF16)
        copies = n_ctx * n_tp
        pieces = jnp.broadcast_to(
            jnp.pad(pieces, ((0, 0), (0, 6), (0, 0)))[:, None], (n_shard, copies, 8, HD)
        )
        pieces = lax.all_to_all(
            pieces.reshape(n_shard * copies, 8, HD), ("shard", "ctx", "tp"), 0, 0
        )
        end_sums = jnp.sum(pieces.astype(F32), axis=0)
        sibling = core_swap(ends)

        def whole(start):
            mine, other = ends[start : start + rows], sibling[start : start + rows]
            return jnp.where(
                core == 0,
                jnp.concatenate([mine, other], axis=0),
                jnp.concatenate([other, mine], axis=0),
            )

        full = jnp.stack([whole(0), whole(rows)])
        turn_at = ctx.astype(jnp.int32).reshape(1)
        size = gain_in.shape[0]
        grad_gate, grad_up, grad_down, mid_sums = close(
            close_feed_kernel,
            turn_at,
            ffn_blocks,
            (w_gate, w_up),
            gain_two,
            w_down.shape,
            [(size, HD)],
            True,
        )
        mid_terms = jnp.sum(mid_sums, axis=1)
        grad_attn, mid_terms = lax.optimization_barrier((grad_attn, mid_terms))
        full = jnp.where(native, full, lax.ppermute(full, PLANE, across_perm))
        outputs = [full[0].astype(F32), full[1].astype(F32)]
        attn_blocks = owners_at_once(grad_attn)
        attn_blocks[1], mid_terms = lax.optimization_barrier((attn_blocks[1], mid_terms))
        mid_terms = mid_terms + lax.ppermute(mid_terms, "tp", [(0, 1), (1, 0)])
        *outputs, attn_blocks[3], end_sums = lax.optimization_barrier(
            (*outputs, attn_blocks[3], end_sums)
        )
        grad_query, grad_key, grad_value, grad_gate_attn, grad_out = close(
            close_attend_kernel,
            turn_at,
            attn_blocks,
            (w_query, w_key, w_value, w_gate_attn),
            gain_one,
            w_out.shape,
            [],
            False,
        )

        return (
            *outputs,
            end_sums[0] / gain_one[:, 0],
            grad_query,
            grad_key,
            grad_value,
            grad_gate_attn,
            grad_out,
            end_sums[1, :head_rows],
            end_sums[1, head_rows : 2 * head_rows],
            mid_terms,
            grad_gate,
            grad_up,
            grad_down,
        )

    return shards


def solution(mesh):
    return jax.shard_map(
        make_shards(mesh),
        mesh=mesh,
        in_specs=(
            P(("shard", "ctx"), None),
            P("shard", None),
            P("shard", None),
            P("shard"),
            P("shard", "tp"),
            P("shard", "tp"),
            P("shard", "tp"),
            P("shard", "tp"),
            P("tp", "shard"),
            P("shard"),
            P("shard"),
            P("shard"),
            P("shard", "tp"),
            P("shard", "tp"),
            P("tp", "shard"),
            P(("shard", "ctx"), None),
        ),
        out_specs=(
            P(("shard", "ctx"), None),
            P(("shard", "ctx"), None),
            P("shard"),
            P("shard", "tp"),
            P("shard", "tp"),
            P("shard", "tp"),
            P("shard", "tp"),
            P("tp", "shard"),
            P("shard"),
            P("shard"),
            P("shard"),
            P("shard", "tp"),
            P("shard", "tp"),
            P("tp", "shard"),
        ),
        check_vma=False,
    )
```
